128 devices in a mesh: section: 2 (over y_hi), dp: 64 (over y_lo, z, x, core).
Axes of the slice: x: 4, y: 4 (y_hi: 2, y_lo: 2; y = y_hi * 2 + y_lo), z: 4, core: 2. Of those that a mesh axis runs over, the one named last changes fastest.
Arguments:
- x_vis: bfloat16 [4, 64, 48, 768], P(None, 'dp'), may hold values from -6 to 6
- lengths: int32 [4, 64, 4], P(None, 'dp'), may hold values from 1 to 96, 192 in all within a row
- shuffle: int32 [4, 64, 192], P(None, 'dp'), may hold values from 0 to 191, each once within a row
- enc_gains: bfloat16 [2, 768], P(None, ('section', 'dp')), may hold values from 0.5 to 1.5
- enc_biases: bfloat16 [6, 768], P(None, ('section', 'dp')), may hold values from -1.75 to 1.75
- enc_qkv: bfloat16 [768, 2304], P(('section', 'dp')), may hold values from -0.21875 to 0.21875
- enc_proj: bfloat16 [768, 768], P(('section', 'dp')), may hold values from -0.625 to 0.625
- enc_up: bfloat16 [768, 3072], P(('section', 'dp')), may hold values from -0.21875 to 0.21875
- enc_up_bias: bfloat16 [3072], P(('section', 'dp')), may hold values from -1.75 to 1.75
- enc_down: bfloat16 [3072, 768], P(('section', 'dp')), may hold values from -0.109375 to 0.109375
- dec_fill: bfloat16 [2, 512], P(None, ('section', 'dp')), may hold values from -6 to 6
- dec_embed: bfloat16 [768, 512], P(('section', 'dp')), may hold values from -0.21875 to 0.21875
- dec_gains: bfloat16 [2, 512], P(None, ('section', 'dp')), may hold values from 0.5 to 1.5
- dec_biases: bfloat16 [6, 512], P(None, ('section', 'dp')), may hold values from -1.75 to 1.75
- dec_qkv: bfloat16 [512, 1536], P(('section', 'dp')), may hold values from -0.25 to 0.25
- dec_proj: bfloat16 [512, 512], P(('section', 'dp')), may hold values from -0.75 to 0.75
- dec_up: bfloat16 [512, 2048], P(('section', 'dp')), may hold values from -0.25 to 0.25
- dec_up_bias: bfloat16 [2048], P(('section', 'dp')), may hold values from -1.75 to 1.75
- dec_down: bfloat16 [2048, 512], P(('section', 'dp')), may hold values from -0.125 to 0.125
- cotangent: bfloat16 [4, 64, 192, 512], P(None, 'dp'), may hold values from -6 to 6
Outputs:
- decoded: bfloat16 [4, 64, 192, 512], P(None, 'dp', None, 'section')
- x_grad: bfloat16 [4, 64, 48, 768], P(None, 'dp', None, 'section')
- grad_enc_gains: float32 [2, 768], P(None, ('section', 'dp'))
- grad_enc_biases: float32 [6, 768], P(None, ('section', 'dp'))
- grad_enc_qkv: float32 [768, 2304], P(('section', 'dp'))
- grad_enc_proj: float32 [768, 768], P(('section', 'dp'))
- grad_enc_up: float32 [768, 3072], P(('section', 'dp'))
- grad_enc_up_bias: float32 [3072], P(('section', 'dp'))
- grad_enc_down: float32 [3072, 768], P(('section', 'dp'))
- grad_dec_fill: float32 [2, 512], P(None, ('section', 'dp'))
- grad_dec_embed: float32 [768, 512], P(('section', 'dp'))
- grad_dec_gains: float32 [2, 512], P(None, ('section', 'dp'))
- grad_dec_biases: float32 [6, 512], P(None, ('section', 'dp'))
- grad_dec_qkv: float32 [512, 1536], P(('section', 'dp'))
- grad_dec_proj: float32 [512, 512], P(('section', 'dp'))
- grad_dec_up: float32 [512, 2048], P(('section', 'dp'))
- grad_dec_up_bias: float32 [2048], P(('section', 'dp'))
- grad_dec_down: float32 [2048, 512], P(('section', 'dp'))
The draws below stay inside these ranges and needn't reach their ends.
Inputs may be any that keep to these rules, and one draw needn't show every extreme that they name: The 4 tile lengths of a pack sum to 192. `shuffle`: each pack's row is a permutation of its 192 positions.
All inputs are finite; a program needn't handle non-finite values.
Results may differ from the reference program's by a relative error of at most 0.024.
Values may be sent and summed in bfloat16 or wider, within the bound.
No kernel may reach another device: no remote copies, remote signals or barrier semaphores. Data moves between devices by JAX's collectives and lax.ppermute only.
A program may use at most 576 MiB of HBM per device.

```python
import math
import jax
import jax.numpy as jnp
import numpy as np
from jax import lax

D_ENC = 768
H_ENC = 12
FF_ENC = 3072
D_DEC = 512
H_DEC = 16
FF_DEC = 2048
SEQ = 192
VIS = 48
TILES = 4
MB = 4
PACKS = 64


def levels(own_key, dims, split, smallest, high):
    factor_of = 1.0
    for position, shards_of in split:
        steps = jax.random.uniform(jax.random.fold_in(jax.random.fold_in(own_key, 6), position), (shards_of,), jnp.float32, smallest / len(split), high / len(split))
        factor_of = factor_of * jnp.repeat(jnp.exp(steps), dims[position] // shards_of).reshape((-1,) + (1,) * (len(dims) - 1 - position))
    return factor_of


def length_profile(number_of, total, bound, slope):
    weights = [(1 << 20) // math.isqrt(rank ** slope) + 1 for rank in range(2, number_of + 1)]
    spare, counts = total - bound - (number_of - 1), [1] * (number_of - 1)
    while spare > 0:
        candidates = [i for i in range(number_of - 1) if counts[i] < bound]
        mass, budget = sum([weights[i] for i in candidates]), spare
        for i in candidates:
            extra = min(bound - counts[i], max(1, budget * weights[i] // mass), spare)
            counts[i] = counts[i] + extra
            spare = spare - extra
    return np.array([bound] + counts)


def uneven(own_key, count, total, reach, skew):
    if count == 2:
        one = jax.random.randint(own_key, (), max(1, total - reach), min(reach, total - 1) + 1)
        return jnp.stack([one, total - one])
    tallies = jnp.asarray(length_profile(count, total, reach, skew), jnp.int32)
    pairs = (count - 1) // 2
    giver, sink = tallies[1:1 + 2 * pairs:2], tallies[2:2 + 2 * pairs:2]
    margin = jnp.minimum(giver - 1, reach - sink)
    shifted = jax.random.randint(jax.random.fold_in(own_key, 1), (pairs,), 0, 1 << 20) % (margin + 1)
    tallies = tallies.at[1:1 + 2 * pairs:2].set(giver - shifted).at[2:2 + 2 * pairs:2].set(sink + shifted)
    return tallies[jax.random.permutation(jax.random.fold_in(own_key, 2), count)]


def bell_draw(key, extent, scale, limit, split=(), kind=jnp.bfloat16):
    entries = jax.random.normal(key, extent, jnp.float32) * scale
    if len(split) > 0:
        entries = levels(key, extent, split, -0.22, 0.18) * entries
    return jnp.clip(entries, min=-limit, max=limit).astype(kind)


def setup_inputs(seed: int = 0) -> dict:
    keys = jax.random.split(jax.random.key(seed), 21)
    return {
        "x_vis": bell_draw(keys[0], (MB, PACKS, VIS, D_ENC), 1.0, 6.0, ((1, 64),)),
        "lengths": jax.vmap(lambda own: uneven(own, TILES, SEQ, SEQ // 2, 2))(jax.random.split(keys[1], MB * PACKS)).reshape((MB, PACKS, TILES)).astype(jnp.int32),
        "shuffle": jax.vmap(lambda own: jax.random.permutation(own, SEQ))(jax.random.split(keys[2], MB * PACKS)).reshape((MB, PACKS, SEQ)).astype(jnp.int32),
        "enc_gains": jnp.clip(1.0 + 0.1 * jax.random.normal(keys[3], (2, D_ENC), jnp.float32), 0.5, 1.5).astype(jnp.bfloat16),
        "enc_biases": bell_draw(keys[4], (6, D_ENC), 0.3, 1.75, ((1, 128),)),
        "enc_qkv": bell_draw(keys[5], (D_ENC, 3 * D_ENC), D_ENC ** -0.5, 0.21875, ((0, 128),)),
        "enc_proj": bell_draw(keys[6], (D_ENC, D_ENC), (D_ENC // 8) ** -0.5, 0.625, ((0, 128),)),
        "enc_up": bell_draw(keys[7], (D_ENC, FF_ENC), D_ENC ** -0.5, 0.21875, ((0, 128),)),
        "enc_up_bias": bell_draw(keys[8], (FF_ENC,), 0.3, 1.75, ((0, 128),)),
        "enc_down": bell_draw(keys[9], (FF_ENC, D_ENC), FF_ENC ** -0.5, 0.109375, ((0, 128),)),
        "dec_fill": bell_draw(keys[10], (2, D_DEC), 1.0, 6.0, ((1, 128),)),
        "dec_embed": bell_draw(keys[11], (D_ENC, D_DEC), D_ENC ** -0.5, 0.21875, ((0, 128),)),
        "dec_gains": jnp.clip(1.0 + 0.1 * jax.random.normal(keys[12], (2, D_DEC), jnp.float32), 0.5, 1.5).astype(jnp.bfloat16),
        "dec_biases": bell_draw(keys[13], (6, D_DEC), 0.3, 1.75, ((1, 128),)),
        "dec_qkv": bell_draw(keys[14], (D_DEC, 3 * D_DEC), D_DEC ** -0.5, 0.25, ((0, 128),)),
        "dec_proj": bell_draw(keys[15], (D_DEC, D_DEC), (D_DEC // 8) ** -0.5, 0.75, ((0, 128),)),
        "dec_up": bell_draw(keys[16], (D_DEC, FF_DEC), D_DEC ** -0.5, 0.25, ((0, 128),)),
        "dec_up_bias": bell_draw(keys[17], (FF_DEC,), 0.3, 1.75, ((0, 128),)),
        "dec_down": bell_draw(keys[18], (FF_DEC, D_DEC), FF_DEC ** -0.5, 0.125, ((0, 128),)),
        "cotangent": bell_draw(keys[19], (MB, PACKS, SEQ, D_DEC), 1.0, 6.0, ((1, 64),)),
    }


@jax.custom_vjp
def low(v):
    return lax.optimization_barrier(v.astype(jnp.bfloat16)).astype(jnp.float32)

@jax.custom_vjp
def low_back(v):
    return v

def low_keep(v):
    return (low(v), None)

def low_pass(kept, grad):
    return (grad,)

def back_keep(v):
    return (v, None)

def back_low(kept, grad):
    return (low(grad),)
low.defvjp(low_keep, low_pass)
low_back.defvjp(back_keep, back_low)
eps_norm = 1e-06

def matmul(left, right):
    return jnp.dot(left, right, precision=lax.Precision.HIGHEST, preferred_element_type=jnp.float32)

def layer_norm(values, gain, shift):
    mean = lax.optimization_barrier(jnp.mean(values, axis=-1, keepdims=True))
    centred = values - mean
    spread = lax.optimization_barrier(jnp.mean(centred * centred, axis=-1, keepdims=True))
    return centred * lax.rsqrt(spread + eps_norm) * gain + shift

def gelu_exact(values):
    return jax.nn.gelu(values, approximate=False)

def position_table(offset, width):
    half = width // 2
    rates = jnp.exp(jnp.arange(half, dtype=jnp.float32) * (-math.log(10000.0) / half))
    angle = offset.astype(jnp.float32)[:, None] * rates[None, :]
    return jnp.concatenate([jnp.sin(angle), jnp.cos(angle)], axis=1)

def layout(length_row, order):
    length = order.shape[0]
    ends = jnp.cumsum(length_row, dtype=jnp.int32)
    places = jnp.arange(length, dtype=jnp.int32)
    passed = places[:, None] >= ends[None, :]
    segment = lax.optimization_barrier(jnp.sum(passed.astype(jnp.int32), axis=1, dtype=jnp.int32))
    offset = places - lax.optimization_barrier(jnp.sum(jnp.where(passed, length_row[None, :], 0), axis=1, dtype=jnp.int32))
    shown_pos = order[:VIS]
    shown_seg = lax.optimization_barrier(jnp.sum((shown_pos[:, None] >= ends[None, :]).astype(jnp.int32), axis=1, dtype=jnp.int32))
    onehot = (places[:, None] == shown_pos[None, :]).astype(jnp.float32)
    return (segment, offset, shown_seg, onehot)

def attention(projected, allowed, heads):
    rows = projected.shape[0]
    width = projected.shape[1] // 3
    size = width // heads
    parts = projected.reshape(rows, 3, heads, size)
    query = parts[:, 0]
    key = parts[:, 1]
    value = parts[:, 2]
    raw = jnp.einsum('qhd,khd->hqk', query, key, precision=lax.Precision.HIGHEST) * (1.0 / math.sqrt(size))
    scores = jnp.where(allowed[None], low_back(raw), -1e+30)
    shares = low(jax.nn.softmax(scores, axis=-1))
    output = jnp.einsum('hqk,khd->qhd', shares, value, precision=lax.Precision.HIGHEST)
    return output.reshape(rows, width)

def block(values, weights, allowed, heads):
    gains, biases, w_qkv, w_proj, w_up, up_bias, w_down = weights
    width = values.shape[1]
    normed = low(layer_norm(values, gains[0], biases[0]))
    qkv_bias = jnp.concatenate([biases[2], jnp.zeros((width,), jnp.float32), biases[3]])
    projected = low(low_back(matmul(normed, w_qkv)) + qkv_bias)
    attended = low(low_back(attention(projected, allowed, heads)))
    middle = values + low_back(matmul(attended, w_proj)) + biases[4]
    normed_two = low(layer_norm(middle, gains[1], biases[1]))
    hidden = low_back(matmul(normed_two, w_up)) + up_bias
    activated = low(gelu_exact(hidden))
    return middle + low_back(matmul(activated, w_down)) + biases[5]

def pack_forward(x_item, length_row, order, params):
    enc_weights = params[0:7]
    fill = params[7]
    embed = params[8]
    dec_weights = params[9:16]
    segment, offset, shown_seg, onehot = layout(length_row, order)
    encoded = block(x_item, enc_weights, shown_seg[:, None] == shown_seg[None, :], H_ENC)
    sent = low(low_back(encoded))
    embedded = low(matmul(sent, embed) + fill[0])
    filled = low_back(matmul(onehot, embedded))
    masked = 1.0 - lax.optimization_barrier(jnp.sum(onehot, axis=1))
    start = filled + masked[:, None] * fill[1][None, :] + position_table(offset, D_DEC)
    return block(start, dec_weights, segment[:, None] == segment[None, :], H_DEC)

def reference(x_vis, lengths, shuffle, enc_gains, enc_biases, enc_qkv, enc_proj, enc_up, enc_up_bias, enc_down, dec_fill, dec_embed, dec_gains, dec_biases, dec_qkv, dec_proj, dec_up, dec_up_bias, dec_down, cotangent):
    params = tuple((part.astype(jnp.float32) for part in (enc_gains, enc_biases, enc_qkv, enc_proj, enc_up, enc_up_bias, enc_down, dec_fill, dec_embed, dec_gains, dec_biases, dec_qkv, dec_proj, dec_up, dec_up_bias, dec_down)))
    x_all = x_vis.astype(jnp.float32).reshape(MB * PACKS, VIS, D_ENC)
    length_rows = lengths.reshape(MB * PACKS, TILES).astype(jnp.int32)
    orders = shuffle.reshape(MB * PACKS, SEQ).astype(jnp.int32)
    checked = jax.checkpoint(pack_forward)

    def forward(x_inputs, weights):

        def one_pack(item):
            return checked(item[0], item[1], item[2], weights)
        return lax.map(one_pack, (x_inputs, length_rows, orders))
    decoded, pull = jax.vjp(forward, x_all, params)
    x_grad, grads = pull(cotangent.astype(jnp.float32).reshape(MB * PACKS, SEQ, D_DEC))
    return (decoded.reshape(MB, PACKS, SEQ, D_DEC).astype(jnp.bfloat16), x_grad.reshape(MB, PACKS, VIS, D_ENC).astype(jnp.bfloat16), grads[0], grads[1], grads[2], grads[3], grads[4], grads[5], grads[6], grads[7], grads[8], grads[9], grads[10], grads[11], grads[12], grads[13], grads[14], grads[15])
```

```python
import math

import jax
import jax.numpy as jnp
from jax import lax
from jax.sharding import PartitionSpec as P

H_ENC = 12
H_DEC = 16
BOTH = ("section", "dp")
F32 = jnp.float32
BF16 = jnp.bfloat16
eps_norm = 1e-06
big_negative = -1e30


def layer_norm(values, gain, shift):
    mean = jnp.mean(values, axis=-1, keepdims=True)
    centred = values - mean
    spread = jnp.mean(centred * centred, axis=-1, keepdims=True)
    return centred * lax.rsqrt(spread + eps_norm) * gain + shift


def gelu_exact(values):
    return jax.nn.gelu(values, approximate=False)


def dot(left, right):
    return jnp.dot(left, right, preferred_element_type=F32)


def inner(left, right):
    return lax.dot_general(left, right, (((0,), (0,)), ((), ())), preferred_element_type=F32)


def times_back(left, right):
    return lax.dot_general(left, right, (((1,), (1,)), ((), ())), preferred_element_type=F32)


def position_table(offset, width):
    half = width // 2
    rates = jnp.exp(jnp.arange(half, dtype=F32) * (-math.log(10000.0) / half))
    angle = offset.astype(F32)[:, None] * rates[None, :]
    return jnp.concatenate([jnp.sin(angle), jnp.cos(angle)], axis=1)


def layout(length_row, order, visible):
    length = order.shape[0]
    ends = jnp.cumsum(length_row, dtype=jnp.int32)
    places = lax.broadcasted_iota(jnp.int32, (length, 1), 0)
    passed = places >= ends[None, :]
    segment = jnp.sum(passed.astype(jnp.int32), axis=1, dtype=jnp.int32)
    offset = places[:, 0] - jnp.sum(
        jnp.where(passed, length_row[None, :], 0), axis=1, dtype=jnp.int32
    )
    shown_pos = order[:visible]
    shown_seg = jnp.sum(
        (shown_pos[:, None] >= ends[None, :]).astype(jnp.int32), axis=1, dtype=jnp.int32
    )
    onehot = places == shown_pos[None, :]
    return (segment, offset, shown_seg, onehot)


def split_heads(matrix, packs, heads):
    rows, width = matrix.shape
    return matrix.reshape(packs, rows // packs, heads, width // heads)


def attend_forward(projected, allowed, heads):
    packs = allowed.shape[0]
    width = projected.shape[1] // 3
    scale = 1.0 / math.sqrt(width // heads)
    query, key, value = [
        split_heads(projected[:, i * width : (i + 1) * width], packs, heads) for i in range(3)
    ]
    scores = jnp.einsum("bqhd,bkhd->bhqk", query, key, preferred_element_type=F32) * scale
    scores = jnp.where(allowed[:, None], scores, big_negative)
    peak = jnp.max(scores, axis=-1, keepdims=True)
    powers = jnp.exp(scores - peak)
    shares = powers / jnp.sum(powers, axis=-1, keepdims=True)
    output = jnp.einsum("bhqk,bkhd->bqhd", shares.astype(BF16), value, preferred_element_type=F32)
    return output.reshape(-1, width), shares


def attend_backward(projected, shares, d_attended, heads):
    packs = shares.shape[0]
    width = projected.shape[1] // 3
    scale = 1.0 / math.sqrt(width // heads)
    query, key, value = [
        split_heads(projected[:, i * width : (i + 1) * width], packs, heads) for i in range(3)
    ]
    d_out = split_heads(d_attended, packs, heads)
    d_value = jnp.einsum(
        "bhqk,bqhd->bkhd", shares.astype(BF16), d_out, preferred_element_type=F32
    )
    d_shares = jnp.einsum("bqhd,bkhd->bhqk", d_out, value, preferred_element_type=F32)
    centre = jnp.sum(d_shares * shares, axis=-1, keepdims=True)
    d_scores = (shares * (d_shares - centre)).astype(BF16)
    d_query = jnp.einsum("bhqk,bkhd->bqhd", d_scores, key, preferred_element_type=F32) * scale
    d_key = jnp.einsum("bhqk,bqhd->bkhd", d_scores, query, preferred_element_type=F32) * scale
    return jnp.concatenate([p.reshape(-1, width) for p in (d_query, d_key, d_value)], axis=1)


def block_forward(values, weights, allowed, heads):
    gains, biases, w_qkv, w_proj, w_up, up_bias, w_down = weights
    width = values.shape[1]
    normed = layer_norm(values, gains[0], biases[0]).astype(BF16)
    qkv_bias = jnp.concatenate([biases[2], jnp.zeros((width,), biases.dtype), biases[3]])
    projected = (dot(normed, w_qkv) + qkv_bias).astype(BF16)
    attended, shares = attend_forward(projected, allowed, heads)
    attended = attended.astype(BF16)
    middle = values + dot(attended, w_proj) + biases[4]
    normed_two = layer_norm(middle, gains[1], biases[1]).astype(BF16)
    hidden = dot(normed_two, w_up) + up_bias
    activated = gelu_exact(hidden).astype(BF16)
    output = middle + dot(activated, w_down) + biases[5]
    return (output, (normed, projected, shares, attended, middle, normed_two, hidden, activated))


def block_backward(gradient, values, stored, weights, heads):
    gains, biases, w_qkv, w_proj, w_up, up_bias, w_down = weights
    normed, projected, shares, attended, middle, normed_two, hidden, activated = stored
    width = values.shape[1]
    grad_low = gradient.astype(BF16)
    d_act = times_back(grad_low, w_down)
    gelu_value, gelu_pull = jax.vjp(gelu_exact, hidden)
    d_hidden = gelu_pull(d_act)[0]
    d_hidden_low = d_hidden.astype(BF16)
    d_normed_two = times_back(d_hidden_low, w_up)
    norm_value, norm_pull = jax.vjp(
        layer_norm, middle, gains[1].astype(F32), biases[1].astype(F32)
    )
    d_mid_part, d_gain_two, d_shift_two = norm_pull(d_normed_two)
    d_middle = gradient + d_mid_part
    d_middle_low = d_middle.astype(BF16)
    d_attended = times_back(d_middle_low, w_proj).astype(BF16)
    d_projected = attend_backward(projected, shares, d_attended, heads)
    d_projected_low = d_projected.astype(BF16)
    d_normed = times_back(d_projected_low, w_qkv)
    first_value, first_pull = jax.vjp(
        layer_norm, values, gains[0].astype(F32), biases[0].astype(F32)
    )
    d_in_part, d_gain_one, d_shift_one = first_pull(d_normed)
    d_values = d_middle + d_in_part
    d_gains = jnp.stack([d_gain_one, d_gain_two])
    d_biases = jnp.stack(
        [
            d_shift_one,
            d_shift_two,
            jnp.sum(d_projected[:, :width], axis=0),
            jnp.sum(d_projected[:, 2 * width :], axis=0),
            jnp.sum(d_middle, axis=0),
            jnp.sum(gradient, axis=0),
        ]
    )
    small = (d_gains, d_biases, jnp.sum(d_hidden, axis=0))
    return d_values, grad_low, d_hidden_low, d_middle_low, d_projected_low, small


def spread_rows(devices, rows, at):
    feature = lax.broadcasted_iota(jnp.int32, (devices * rows, devices * 8), 0)
    place = lax.broadcasted_iota(jnp.int32, (devices * rows, devices * 8), 1)
    return (8 * (feature // rows) + at + feature % rows == place).astype(BF16)


SMALL = (("g", 6), ("b", 6), ("u", 24), ("f", 4), ("g", 4), ("b", 4), ("u", 16))


def vectors_in(flat, counts):
    out = []
    at = 0
    for lead, part in counts:
        piece = flat[:, at : at + lead * part].reshape(128, lead, part)
        out.append(piece.transpose(1, 0, 2).reshape(lead, 128 * part))
        at += lead * part
    return out


COUNTS = ((2, 6), (6, 6), (1, 24), (2, 4), (2, 4), (6, 4), (1, 16))


def regroup(matrix, groups):
    rows = matrix.shape[0]
    return matrix.reshape(rows, 128, groups, 8).transpose(0, 2, 1, 3).reshape(rows, -1)


def ungroup(matrix, groups):
    rows = matrix.shape[0]
    return matrix.reshape(rows, groups, 128, 8).transpose(0, 2, 1, 3).reshape(rows, -1)


def partner(block):
    return lax.ppermute(block, "section", [(0, 1), (1, 0)])


def on_device(
    x_vis,
    lengths,
    shuffle,
    enc_gains,
    enc_biases,
    enc_qkv,
    enc_proj,
    enc_up,
    enc_up_bias,
    enc_down,
    dec_fill,
    dec_embed,
    dec_gains,
    dec_biases,
    dec_qkv,
    dec_proj,
    dec_up,
    dec_up_bias,
    dec_down,
    cotangent,
):
    section = lax.axis_index("section")
    small = jnp.concatenate(
        [
            v.reshape(1, -1)
            for v in (enc_gains, enc_biases, enc_up_bias, dec_fill, dec_gains, dec_biases, dec_up_bias)
        ],
        axis=1,
    )
    enc_top = jnp.concatenate([enc_qkv, enc_proj, regroup(enc_up, 3), dec_embed], axis=1)
    small_row = jnp.pad(small, ((0, 1), (0, enc_top.shape[1] - small.shape[1])))
    enc_down_wide = enc_down.reshape(3, 8, 768).transpose(1, 0, 2).reshape(8, 2304)
    dec_top = jnp.concatenate(
        [jnp.concatenate([dec_qkv, dec_proj], axis=1), regroup(dec_up, 2)], axis=0
    )
    dec_down_wide = dec_down.reshape(2, 8, 512).transpose(1, 0, 2).reshape(8, 1024)
    shard = jnp.concatenate(
        [jnp.concatenate([enc_top, small_row], axis=0), enc_down_wide, dec_top, dec_down_wide],
        axis=1,
    )
    whole = lax.all_gather(shard, BOTH, axis=0, tiled=True)

    packs = 2
    mine = lambda a: lax.dynamic_slice_in_dim(a, section * packs, packs, 0)[:, 0]
    x_rows = mine(x_vis).reshape(packs * 48, 768).astype(F32)
    pull = mine(cotangent).reshape(packs * 192, 512).astype(F32)
    length_rows, orders = mine(lengths), mine(shuffle)
    segment, offset, shown_seg, onehot = jax.vmap(lambda a, b: layout(a, b, 48))(
        length_rows, orders
    )
    enc_allowed = shown_seg[:, :, None] == shown_seg[:, None, :]
    dec_allowed = segment[:, :, None] == segment[:, None, :]
    picker = onehot.astype(BF16)
    masked = (1.0 - jnp.sum(onehot.astype(F32), axis=2)).reshape(-1, 1)
    table = position_table(offset.reshape(-1), 512)

    to_enc = spread_rows(32, 6, 0)
    enc_mat = (
        jnp.einsum(
            "ab,gbc->gac", to_enc, whole[:, :6656].reshape(4, 256, 6656), preferred_element_type=F32
        )
        .astype(BF16)
        .reshape(768, 6656)
    )
    dec_z = whole[:, 8960:11008].reshape(4, 256, 2048)
    dec_mat = [
        jnp.einsum("ab,gbc->gac", spread_rows(32, 4, at), dec_z, preferred_element_type=F32)
        .astype(BF16)
        .reshape(512, 2048)
        for at in (0, 4)
    ]
    flat = whole[:, :128].reshape(128, 8, 128)[:, 6]
    e_gains, e_biases, e_up_bias, fill, d_gains, d_biases, d_up_bias = vectors_in(flat, COUNTS)
    e_up_bias = regroup(e_up_bias, 3)[0]
    d_up_bias = regroup(d_up_bias, 2)[0]
    enc_down_mat = jnp.concatenate([whole[:, 6656 + 768 * g : 7424 + 768 * g] for g in range(3)])
    dec_down_mat = jnp.concatenate([whole[:, 11008 + 512 * g : 11520 + 512 * g] for g in range(2)])
    enc_weights = (
        e_gains,
        e_biases,
        enc_mat[:, :2304],
        enc_mat[:, 2304:3072],
        enc_mat[:, 3072:6144],
        e_up_bias,
        enc_down_mat,
    )
    embed = enc_mat[:, 6144:6656]
    dec_weights = (
        d_gains,
        d_biases,
        dec_mat[0][:, :1536],
        dec_mat[0][:, 1536:],
        dec_mat[1],
        d_up_bias,
        dec_down_mat,
    )

    encoded, enc_stored = block_forward(x_rows, enc_weights, enc_allowed, H_ENC)
    encoded = encoded.astype(BF16)
    embedded = (dot(encoded, embed) + fill[0]).astype(BF16)
    filled = jnp.einsum(
        "bij,bjd->bid", picker, embedded.reshape(packs, 48, 512), preferred_element_type=F32
    ).reshape(-1, 512)
    start = filled + masked * fill[1] + table
    decoded, dec_stored = block_forward(start, dec_weights, dec_allowed, H_DEC)
    decoded = decoded.astype(BF16)

    d_start, d_low, d_hid, d_mid, d_p3, dec_small = block_backward(
        pull, start, dec_stored, dec_weights, H_DEC
    )
    pad_low = spread_rows(128, 4, 0)
    pad_high = spread_rows(128, 4, 4)
    dec_h1, _, _, dec_att, _, dec_h2, _, dec_act = dec_stored
    grad_dec_top = jnp.concatenate(
        [inner(dot(dec_h1, pad_low).astype(BF16), d_p3), inner(dot(dec_att, pad_low).astype(BF16), d_mid)],
        axis=1,
    ) + inner(dot(dec_h2, pad_high).astype(BF16), d_hid)
    grad_dec = jnp.concatenate(
        [grad_dec_top] + [inner(dec_act[:, g * 1024 : g * 1024 + 1024], d_low) for g in range(2)],
        axis=1,
    )
    dec_sum = lax.psum_scatter(grad_dec.astype(BF16), BOTH, scatter_dimension=0, tiled=True)
    d_mask = jnp.sum(masked * d_start, axis=0)
    d_embedded = jnp.einsum(
        "bij,bid->bjd",
        picker,
        d_start.astype(BF16).reshape(packs, 192, 512),
        preferred_element_type=F32,
    ).reshape(-1, 512)
    d_embedded_low = d_embedded.astype(BF16)
    d_encoded = times_back(d_embedded_low, embed).astype(BF16)
    d_fill = jnp.stack([jnp.sum(d_embedded, axis=0), d_mask])

    d_values, e_low, e_hid, e_mid, e_p3, enc_small = block_backward(
        d_encoded.astype(F32), x_rows, enc_stored, enc_weights, H_ENC
    )
    x_grad = d_values.astype(BF16)
    pad_enc = spread_rows(128, 6, 0)
    enc_h1, _, _, enc_att, _, enc_h2, _, enc_act = enc_stored
    widen = lambda a: dot(a, pad_enc).astype(BF16)
    small_parts = (
        enc_small[0],
        enc_small[1],
        enc_small[2][None],
        d_fill,
        dec_small[0],
        dec_small[1],
        dec_small[2][None],
    )
    small_parts = list(small_parts)
    small_parts[2] = ungroup(small_parts[2], 3)
    small_parts[6] = ungroup(small_parts[6], 2)
    small_grad = jnp.concatenate(
        [
            v.reshape(lead, 128, part).transpose(1, 0, 2).reshape(128, lead * part)
            for v, (lead, part) in zip(small_parts, COUNTS)
        ],
        axis=1,
    )
    small_rows = jnp.pad(small_grad[:, None, :], ((0, 0), (6, 1), (0, 2304 - 128))).reshape(1024, 2304)
    grad_enc = jnp.concatenate(
        [
            inner(widen(enc_h1), e_p3) + small_rows,
            inner(widen(enc_att), e_mid),
            inner(widen(enc_h2), e_hid),
            inner(widen(encoded), d_embedded_low),
        ]
        + [inner(enc_act[:, g * 1024 : g * 1024 + 1024], e_low) for g in range(3)],
        axis=1,
    )
    low_enc = grad_enc.astype(BF16)
    enc_sum = jnp.concatenate(
        [
            lax.psum_scatter(low_enc[:, a:b], BOTH, scatter_dimension=0, tiled=True)
            for a, b in ((0, 3072), (3072, 6144), (6144, 8960))
        ],
        axis=1,
    )

    enc_sum = enc_sum.astype(F32)
    dec_sum = dec_sum.astype(F32)
    flat_sum = enc_sum[6, :128]
    pieces = []
    at = 0
    for lead, part in COUNTS:
        pieces.append(flat_sum[at : at + lead * part].reshape(lead, part))
        at += lead * part
    g_enc_qkv = enc_sum[:6, :2304]
    g_enc_proj = enc_sum[:6, 2304:3072]
    g_enc_up = ungroup(enc_sum[:6, 3072:6144], 3)
    g_embed = enc_sum[:6, 6144:6656]
    g_enc_down = enc_sum[:, 6656:].reshape(8, 3, 768).transpose(1, 0, 2).reshape(24, 768)
    g_dec_qkv = dec_sum[:4, :1536]
    g_dec_proj = dec_sum[:4, 1536:2048]
    g_dec_up = ungroup(dec_sum[4:, :2048], 2)
    g_dec_down = dec_sum[:, 2048:].reshape(8, 2, 512).transpose(1, 0, 2).reshape(16, 512)

    def placed(rows, width):
        rows = rows.reshape(packs, 1, -1, width)
        half = width // 2
        keep = lax.dynamic_slice_in_dim(rows, section * half, half, 3)
        send = lax.dynamic_slice_in_dim(rows, (1 - section) * half, half, 3)
        got = partner(send)
        both = jnp.where(section == 0, jnp.concatenate([keep, got]), jnp.concatenate([got, keep]))
        return both

    return (
        placed(decoded, 512),
        placed(x_grad, 768),
        pieces[0],
        pieces[1],
        g_enc_qkv,
        g_enc_proj,
        g_enc_up,
        pieces[2][0],
        g_enc_down,
        pieces[3],
        g_embed,
        pieces[4],
        pieces[5],
        g_dec_qkv,
        g_dec_proj,
        g_dec_up,
        pieces[6][0],
        g_dec_down,
    )


def solution(mesh):
    rows = P(None, "dp", None, None)
    ids = P(None, "dp", None)
    wide = P(None, BOTH)
    tall = P(BOTH, None)
    flat = P(BOTH)
    in_specs = (rows, ids, ids, wide, wide, tall, tall, tall, flat, tall, wide, tall, wide, wide)
    in_specs += (tall, tall, tall, flat, tall, rows)
    out_rows = P(None, "dp", None, "section")
    out_specs = (out_rows, out_rows, wide, wide, tall, tall, tall, flat, tall, wide, tall, wide)
    out_specs += (wide, tall, tall, tall, flat, tall)
    return jax.shard_map(
        on_device, mesh=mesh, in_specs=in_specs, out_specs=out_specs, check_vma=False
    )
```

```python
import functools
import math

import jax
import jax.numpy as jnp
from jax import lax
from jax.experimental import pallas as pl
from jax.experimental.pallas import tpu as pltpu
from jax.sharding import PartitionSpec as P

H_ENC = 12
H_DEC = 16
BOTH = ("section", "dp")
F32 = jnp.float32
BF16 = jnp.bfloat16
EPS = 1e-06
NEVER = -1e30
MIB = 1 << 20

C_PROJ = 2304
C_UP = 3072
C_EMB = 6144
C_DOWN = 6656
C_Z = 8960
C_DDOWN = 11008
C_ALL = 12032
COUNTS = ((2, 6), (6, 6), (1, 24), (2, 4), (2, 4), (6, 4), (1, 16))


def dot(left, right):
    return jnp.dot(left, right, preferred_element_type=F32)


def dot_t(left, right):
    return lax.dot_general(left, right, (((1,), (1,)), ((), ())), preferred_element_type=F32)


def t_dot(left, right):
    return lax.dot_general(left, right, (((0,), (0,)), ((), ())), preferred_element_type=F32)


def low(values):
    return values.astype(BF16)


def norm_parts(values):
    mean = jnp.mean(values, axis=-1, keepdims=True)
    centred = values - mean
    rstd = lax.rsqrt(jnp.mean(centred * centred, axis=-1, keepdims=True) + EPS)
    return centred * rstd, rstd


def norm_back(d_normed, unit, rstd, gain):
    scaled = d_normed * gain
    part = scaled - jnp.mean(scaled, axis=-1, keepdims=True)
    part = (part - unit * jnp.mean(scaled * unit, axis=-1, keepdims=True)) * rstd
    return part, col_sum(d_normed * unit), col_sum(d_normed)


def col_sum(values):
    return jnp.sum(values, axis=0, keepdims=True)


def gelu_pair(hidden):
    share = 0.5 + 0.5 * lax.erf(hidden * math.sqrt(0.5))
    slope = share + hidden * (jnp.exp(-0.5 * hidden * hidden) * (1.0 / math.sqrt(2.0 * math.pi)))
    return hidden * share, slope


def head_stack(block, heads, rows):
    size = 128 // heads
    lane = lax.broadcasted_iota(jnp.int32, (1, 128), 1)
    fill = jnp.zeros((rows - block.shape[0], 128), BF16)
    parts = []
    for head in range(heads):
        own = ((lane >= head * size) & (lane < (head + 1) * size)).astype(BF16)
        parts += [block * own, fill]
    return jnp.concatenate(parts, axis=0)


def head_unstack(stack, heads, rows, count):
    size = 128 // heads
    lane = lax.broadcasted_iota(jnp.int32, (1, 128), 1)
    total = None
    for head in range(heads):
        own = ((lane >= head * size) & (lane < (head + 1) * size)).astype(F32)
        part = stack[head * rows : head * rows + count] * own
        total = part if total is None else total + part
    return total


def attend_group(query, key, value, bias, heads, scale, shares_out):
    rows = bias.shape[1]
    scores = dot_t(query, head_stack(key, heads, rows))
    parts = []
    for head in range(heads):
        s = scores[:, head * rows : (head + 1) * rows] * scale + bias
        powers = jnp.exp(s - jnp.max(s, axis=-1, keepdims=True))
        parts.append(powers / jnp.sum(powers, axis=-1, keepdims=True))
    shares = jnp.concatenate(parts, axis=1)
    shares_out[...] = shares
    return dot(low(shares), head_stack(value, heads, rows))


def attend_group_back(query, key, value, d_out, shares, heads, scale, rows):
    count = key.shape[0]
    d_shares = dot_t(d_out, head_stack(value, heads, rows))
    parts = []
    for head in range(heads):
        cut = slice(head * rows, (head + 1) * rows)
        p, dp = shares[:, cut], d_shares[:, cut]
        parts.append(low(p * (dp - jnp.sum(dp * p, axis=-1, keepdims=True))))
    d_scores = jnp.concatenate(parts, axis=1)
    d_query = dot(d_scores, head_stack(key, heads, rows)) * scale
    d_key = head_unstack(t_dot(d_scores, query), heads, rows, count) * scale
    d_value = head_unstack(t_dot(low(shares), d_out), heads, rows, count)
    return d_query, d_key, d_value


def widen(values, pads):
    return jnp.concatenate(
        [low(dot(values[:, :384], pads)), low(dot(values[:, 384:], pads))], axis=1
    )


def narrow(values, pads):
    return jnp.concatenate(
        [low(dot_t(values[:, :512], pads)), low(dot_t(values[:, 512:], pads))], axis=1
    )


def narrow_wide(values, pads):
    high = low(values)
    rest = low(values - high.astype(F32))
    return jnp.concatenate(
        [
            dot_t(high[:, :512], pads) + dot_t(rest[:, :512], pads),
            dot_t(high[:, 512:], pads) + dot_t(rest[:, 512:], pads),
        ],
        axis=1,
    )


def place_masks(width, part, offset):
    column = lax.broadcasted_iota(jnp.int32, (128, width), 1).astype(F32)
    line = lax.broadcasted_iota(jnp.int32, (128, width), 0).astype(F32)
    device = jnp.floor((column + 0.5) * (1.0 / part))
    own = (device == line).astype(F32)
    pick = (column - device * part + offset == line).astype(BF16)
    return own, pick


def small_plan():
    plan, at = [], 0
    for family, (lead, part) in enumerate(COUNTS):
        if part >= 16:
            for group in range(part // 8):
                plan.append((family, group, 1024, 8, at + 8 * group))
        else:
            for line in range(lead):
                plan.append((family, line, 128 * part, part, at + line * part))
        at += lead * part
    return plan


def small_in_kernel(whole_ref, enc_ref, enc_up_ref, dec_ref, dec_up_ref):
    device = lax.broadcasted_iota(jnp.int32, (128, 1024), 0)
    place = lax.broadcasted_iota(jnp.int32, (128, 1024), 1)
    table = low(dot((place == 8 * device + 6).astype(BF16), whole_ref[...]))
    enc_ref[...] = jnp.zeros_like(enc_ref)
    dec_ref[...] = jnp.zeros_like(dec_ref)
    for family, line, width, part, offset in small_plan():
        own, pick = place_masks(width, part, offset)
        vector = col_sum(own * dot(table, pick))
        if family == 2:
            enc_up_ref[:, 1024 * line : 1024 * line + 1024] = vector
        elif family == 6:
            dec_up_ref[:, 1024 * line : 1024 * line + 1024] = vector
        elif family < 2:
            enc_ref[2 * family + line : 2 * family + line + 1, :] = vector
        else:
            row = 2 * (family - 3) + line
            dec_ref[row : row + 1, :] = vector


def small_in(whole):
    return pl.pallas_call(
        small_in_kernel,
        grid=(1,),
        in_specs=[pl.BlockSpec((1024, 128), lambda i: (0, 0))],
        out_specs=[
            pl.BlockSpec((8, 768), lambda i: (0, 0)),
            pl.BlockSpec((1, 3072), lambda i: (0, 0)),
            pl.BlockSpec((16, 512), lambda i: (0, 0)),
            pl.BlockSpec((1, 2048), lambda i: (0, 0)),
        ],
        out_shape=[
            jax.ShapeDtypeStruct((8, 768), F32),
            jax.ShapeDtypeStruct((1, 3072), F32),
            jax.ShapeDtypeStruct((16, 512), F32),
            jax.ShapeDtypeStruct((1, 2048), F32),
        ],
        compiler_params=pltpu.CompilerParams(vmem_limit_bytes=32 * MIB),
        name="small_in",
    )(whole)


def small_out(enc, enc_up, dec, dec_up):
    total = jnp.zeros((128, 128), F32)
    for family, line, width, part, offset in small_plan():
        own, pick = place_masks(width, part, offset)
        if family == 2:
            vector = enc_up[:, 1024 * line : 1024 * line + 1024]
        elif family == 6:
            vector = dec_up[:, 1024 * line : 1024 * line + 1024]
        elif family < 2:
            vector = enc[2 * family + line : 2 * family + line + 1]
        else:
            row = 2 * (family - 3) + line
            vector = dec[row : row + 1]
        total = total + dot_t(low(own * vector), pick)
    return total


ENC_SAVED = (
    ("h1", (96, 768), BF16),
    ("proj3", (96, 2304), BF16),
    ("shares", (6, 96, 256), F32),
    ("attended", (96, 768), BF16),
    ("middle", (96, 768), F32),
    ("h2", (96, 768), BF16),
    ("slope", (96, 3072), F32),
    ("activated", (96, 3072), BF16),
)


def enc_forward_kernel(
    whole, x_ref, bias_ref, pads_ref, enc_ref, enc_up_ref, dec_ref,
    encoded_ref, embedded_ref, h1_ref, proj3_ref, shares_ref, attended_ref, middle_ref, h2_ref,
    slope_ref, activated_ref,
    w_qkv, w_proj, w_up, w_emb, w_down, sems,
):
    copies = [
        pltpu.make_async_copy(whole.at[:, pl.ds(at, ref.shape[1])], ref, sems.at[i])
        for i, (at, ref) in enumerate(
            ((0, w_qkv), (C_PROJ, w_proj), (C_UP, w_up), (C_DOWN, w_down), (C_EMB, w_emb))
        )
    ]
    for copy in copies:
        copy.start()
    pads = pads_ref[...]
    x = x_ref[...].astype(F32)
    unit, _ = norm_parts(x)
    h1 = low(unit * enc_ref[0:1] + enc_ref[2:3])
    h1_ref[...] = h1
    wide = widen(h1, pads)
    copies[0].wait()
    for third in range(3):
        cut = slice(768 * third, 768 * third + 768)
        part = dot(wide, w_qkv[:, cut])
        if third != 1:
            part = part + (enc_ref[4:5] if third == 0 else enc_ref[5:6])
        proj3_ref[:, cut] = low(part)
    bias = bias_ref[...]
    for group in range(6):
        cuts = [slice(768 * i + 128 * group, 768 * i + 128 * group + 128) for i in range(3)]
        out = attend_group(
            proj3_ref[:, cuts[0]], proj3_ref[:, cuts[1]], proj3_ref[:, cuts[2]],
            bias, 2, 0.125, shares_ref.at[group],
        )
        attended_ref[:, cuts[0]] = low(out)
    copies[1].wait()
    middle = x + dot(widen(attended_ref[...], pads), w_proj[...]) + enc_ref[6:7]
    middle_ref[...] = middle
    unit, _ = norm_parts(middle)
    h2 = low(unit * enc_ref[1:2] + enc_ref[3:4])
    h2_ref[...] = h2
    wide = widen(h2, pads)
    copies[2].wait()

    @pl.loop(0, 6)
    def _(tile):
        cut = pl.ds(pl.multiple_of(tile * 512, 512), 512)
        value, slope = gelu_pair(dot(wide, w_up[:, cut]) + enc_up_ref[:, cut])
        activated_ref[:, cut] = low(value)
        slope_ref[:, cut] = slope

    copies[3].wait()
    out = middle + enc_ref[7:8]
    for group in range(3):
        out = out + dot(
            activated_ref[:, 1024 * group : 1024 * group + 1024],
            w_down[:, 768 * group : 768 * group + 768],
        )
    encoded = low(out)
    encoded_ref[...] = encoded
    copies[4].wait()
    embedded_ref[...] = low(dot(widen(encoded, pads), w_emb[...]) + dec_ref[0:1])


VMEM = pl.BlockSpec(memory_space=pltpu.VMEM)
ANY = pl.BlockSpec(memory_space=pl.ANY)


def shape(dims, kind):
    return jax.ShapeDtypeStruct(dims, kind)


def params(limit):
    return pltpu.CompilerParams(vmem_limit_bytes=limit * MIB)


def enc_forward(whole, x, bias, pads, enc_vec, enc_up, dec_vec):
    outs = (("encoded", (96, 768), BF16), ("embedded", (96, 512), BF16)) + ENC_SAVED
    return pl.pallas_call(
        enc_forward_kernel,
        in_specs=[ANY] + [VMEM] * 6,
        out_specs=[VMEM] * len(outs),
        out_shape=[shape(dims, kind) for _, dims, kind in outs],
        scratch_shapes=[
            pltpu.VMEM((1024, 2304), BF16),
            pltpu.VMEM((1024, 768), BF16),
            pltpu.VMEM((1024, 3072), BF16),
            pltpu.VMEM((1024, 512), BF16),
            pltpu.VMEM((1024, 2304), BF16),
            pltpu.SemaphoreType.DMA((5,)),
        ],
        compiler_params=params(48),
        cost_estimate=pl.CostEstimate(flops=2 * 10**9, bytes_accessed=20 * 10**6, transcendentals=0),
        name="enc_forward",
    )(whole, x, bias, pads, enc_vec, enc_up, dec_vec)


DEC_SCALE = 1.0 / math.sqrt(32)


def put(staged, half, core, keep, send, rows_cols, sem):
    rows, cols = rows_cols

    @pl.when(core == half)
    def _():
        pltpu.make_async_copy(staged, keep.at[rows, cols], sem).start()

    @pl.when(core != half)
    def _():
        pltpu.make_async_copy(staged, send.at[rows, cols], sem).start()


def dec_kernel(
    core_ref, whole, embedded_ref, picker_ref, picker_t_ref, masked_ref, table_ref, bias_ref,
    pull_ref, low_ref, high_ref, low_t_ref, high_t_ref, pads_ref, dec_ref, dec_up_ref,
    decoded_ref, d_encoded_ref, d_embedded_ref, d_small_ref, d_up_small_ref,
    keep_att, send_att, keep_up, send_up, keep_down, send_down,
    w_z, w_down, w_emb, w_lo, w_hi, start_ref, proj3_ref, shares_ref, attended_ref, middle_ref,
    activated_ref, slope_ref, d_hid_ref, d_p3_ref, wide_a, wide_b, stage_down, stage_z,
    sems, out_sems,
):
    core = core_ref[0]
    copies = [
        pltpu.make_async_copy(whole.at[:, pl.ds(at, ref.shape[1])], ref, sems.at[i])
        for i, (at, ref) in enumerate(((C_Z, w_z), (C_DDOWN, w_down), (C_EMB, w_emb)))
    ]
    for copy in copies:
        copy.start()
    gain_1, gain_2 = dec_ref[2:3], dec_ref[3:4]
    start = dot(picker_ref[...], embedded_ref[...]) + masked_ref[...] * dec_ref[1:2] + table_ref[...]
    start_ref[...] = start
    unit, _ = norm_parts(start)
    h1 = low(unit * gain_1 + dec_ref[4:5])
    copies[0].wait()

    @pl.loop(0, 4)
    def _(block):
        into = pl.ds(pl.multiple_of(block * 128, 128), 128)
        source = pl.ds(pl.multiple_of(block * 256, 256), 256)
        for half in range(2):
            cut = slice(1024 * half, 1024 * half + 1024)
            rows = w_z[source, cut]
            w_lo[into, cut] = low(dot(low_ref[...], rows))
            w_hi[into, cut] = low(dot(high_ref[...], rows))

    for third in range(3):
        cut = slice(512 * third, 512 * third + 512)
        part = dot(h1, w_lo[:, cut])
        if third != 1:
            part = part + (dec_ref[6:7] if third == 0 else dec_ref[7:8])
        proj3_ref[:, cut] = low(part)

    @pl.loop(0, 8)
    def _(step):
        pack, group = step // 4, step % 4
        rows = pl.ds(pl.multiple_of(pack * 192, 192), 192)
        cuts = [pl.ds(pl.multiple_of(512 * i + 128 * group, 128), 128) for i in range(3)]
        out = attend_group(
            proj3_ref[rows, cuts[0]], proj3_ref[rows, cuts[1]], proj3_ref[rows, cuts[2]],
            bias_ref[pack], 4, DEC_SCALE, shares_ref.at[step],
        )
        attended_ref[rows, cuts[0]] = low(out)

    middle = start + dot(attended_ref[...], w_lo[:, 1536:]) + dec_ref[8:9]
    middle_ref[...] = middle
    unit_2, rstd_2 = norm_parts(middle)
    h2 = low(unit_2 * gain_2 + dec_ref[5:6])

    @pl.loop(0, 4)
    def _(tile):
        cut = pl.ds(pl.multiple_of(tile * 512, 512), 512)
        value, slope = gelu_pair(dot(h2, w_hi[:, cut]) + dec_up_ref[:, cut])
        activated_ref[:, cut] = low(value)
        slope_ref[:, cut] = slope

    copies[1].wait()
    out = middle + dec_ref[9:10]
    for group in range(2):
        out = out + dot(
            activated_ref[:, 1024 * group : 1024 * group + 1024],
            w_down[:, 512 * group : 512 * group + 512],
        )
    decoded_ref[...] = low(out)

    g_low = pull_ref[...]
    for tile in range(4):
        group, rows = tile // 2, slice(512 * (tile % 2), 512 * (tile % 2) + 512)
        cut = slice(512 * tile, 512 * tile + 512)
        d_hid = dot_t(g_low, w_down[rows, 512 * group : 512 * group + 512]) * slope_ref[:, cut]
        d_up_small_ref[:, cut] = col_sum(d_hid)
        d_hid_ref[:, cut] = low(d_hid)
        grad = low(t_dot(activated_ref[:, cut], g_low))
        for half in range(2):
            stage_down[half, rows, 256 * group : 256 * group + 256] = grad[:, 256 * half : 256 * half + 256]
    for half in range(2):
        put(
            stage_down.at[half], half, core, keep_down, send_down,
            (slice(None), pl.ds(1408, 512)), out_sems.at[half],
        )
    d_h2 = dot_t(d_hid_ref[...], w_hi[...])
    part, d_gain_2, d_shift_2 = norm_back(d_h2, unit_2, rstd_2, gain_2)
    g = g_low.astype(F32)
    d_mid = g + part
    d_mid_low = low(d_mid)
    d_att = low(dot_t(d_mid_low, w_lo[:, 1536:]))
    d_small_ref[...] = jnp.zeros_like(d_small_ref)
    d_small_ref[3:4] = d_gain_2
    d_small_ref[5:6] = d_shift_2
    d_small_ref[8:9] = col_sum(d_mid)
    d_small_ref[9:10] = col_sum(g)
    middle_ref[...] = d_mid
    d_att_ref = wide_b.at[pl.ds(0, 384), pl.ds(0, 512)]
    d_att_ref[...] = d_att

    @pl.loop(0, 8)
    def _(step):
        pack, group = step // 4, step % 4
        rows = pl.ds(pl.multiple_of(pack * 192, 192), 192)
        cuts = [pl.ds(pl.multiple_of(512 * i + 128 * group, 128), 128) for i in range(3)]
        parts = attend_group_back(
            proj3_ref[rows, cuts[0]], proj3_ref[rows, cuts[1]], proj3_ref[rows, cuts[2]],
            d_att_ref[rows, cuts[0]], shares_ref[step], 4, DEC_SCALE, 256,
        )
        for cut, part in zip(cuts, parts):
            d_p3_ref[rows, cut] = part

    d_small_ref[6:7] = col_sum(d_p3_ref[:, :512])
    d_small_ref[7:8] = col_sum(d_p3_ref[:, 1024:])
    d_p3 = low(d_p3_ref[...])
    d_h1 = dot_t(d_p3, w_lo[:, :1536])
    unit, rstd = norm_parts(start_ref[...])
    part, d_gain_1, d_shift_1 = norm_back(d_h1, unit, rstd, gain_1)
    d_start = middle_ref[...] + part
    d_small_ref[2:3] = d_gain_1
    d_small_ref[4:5] = d_shift_1
    d_small_ref[1:2] = col_sum(masked_ref[...] * d_start)
    d_embedded = dot(picker_t_ref[...], low(d_start))
    d_small_ref[0:1] = col_sum(d_embedded)
    d_embedded = low(d_embedded)
    d_embedded_ref[...] = d_embedded
    copies[2].wait()
    d_encoded_ref[...] = narrow(low(dot_t(d_embedded, w_emb[...])), pads_ref[...])

    h1 = low(unit * gain_1 + dec_ref[4:5])
    att = attended_ref[...]
    for block in range(4):
        into, cut = slice(256 * block, 256 * block + 256), slice(128 * block, 128 * block + 128)
        wide_a[into, :384] = low(dot_t(low_t_ref[...], h1[:, cut]))
        wide_b[into, :384] = low(dot_t(low_t_ref[...], att[:, cut]))
        raised = low(dot_t(high_t_ref[...], h2[:, cut]))
        wide_a[into, 384:] = raised
        wide_b[into, 384:] = raised
    for tile in range(4):
        cut = slice(512 * tile, 512 * tile + 512)
        if tile < 3:
            right = jnp.concatenate([d_p3[:, cut], d_hid_ref[:, cut]], axis=0)
            stage_z[tile] = low(dot(wide_a[...], right))
        else:
            right = jnp.concatenate([d_mid_low, d_hid_ref[:, cut]], axis=0)
            stage_z[tile] = low(dot(wide_b[...], right))
        keep, send = (keep_att, send_att) if tile < 2 else (keep_up, send_up)
        put(
            stage_z.at[tile], tile % 2, core, keep, send,
            (slice(None), pl.ds(1536, 512)), out_sems.at[2 + tile],
        )
    for half in range(2):
        pltpu.make_async_copy(
            stage_down.at[half], keep_down.at[:, pl.ds(1408, 512)], out_sems.at[half]
        ).wait()
    for tile in range(4):
        pltpu.make_async_copy(
            stage_z.at[tile], keep_att.at[:, pl.ds(1536, 512)], out_sems.at[2 + tile]
        ).wait()


def decoder(core, whole, embedded, picker, picker_t, masked, table, bias, pull, spread, pads, dec_vec, dec_up):
    outs = (
        shape((384, 512), BF16),
        shape((96, 768), BF16),
        shape((96, 512), BF16),
        shape((16, 512), F32),
        shape((1, 2048), F32),
        shape((1024, 2048), BF16),
        shape((1024, 2048), BF16),
        shape((1024, 2048), BF16),
        shape((1024, 2048), BF16),
        shape((1024, 1920), BF16),
        shape((1024, 1920), BF16),
    )
    return pl.pallas_call(
        dec_kernel,
        in_specs=[pl.BlockSpec(memory_space=pltpu.SMEM), ANY] + [VMEM] * 14,
        out_specs=[VMEM] * 5 + [ANY] * 6,
        out_shape=outs,
        scratch_shapes=[
            pltpu.VMEM((1024, 2048), BF16),
            pltpu.VMEM((1024, 1024), BF16),
            pltpu.VMEM((1024, 512), BF16),
            pltpu.VMEM((512, 2048), BF16),
            pltpu.VMEM((512, 2048), BF16),
            pltpu.VMEM((384, 512), F32),
            pltpu.VMEM((384, 1536), BF16),
            pltpu.VMEM((8, 192, 1024), F32),
            pltpu.VMEM((384, 512), BF16),
            pltpu.VMEM((384, 512), F32),
            pltpu.VMEM((384, 2048), BF16),
            pltpu.VMEM((384, 2048), F32),
            pltpu.VMEM((384, 2048), BF16),
            pltpu.VMEM((384, 1536), F32),
            pltpu.VMEM((1024, 768), BF16),
            pltpu.VMEM((1024, 768), BF16),
            pltpu.VMEM((2, 1024, 512), BF16),
            pltpu.VMEM((4, 1024, 512), BF16),
            pltpu.SemaphoreType.DMA((3,)),
            pltpu.SemaphoreType.DMA((6,)),
        ],
        compiler_params=params(58),
        cost_estimate=pl.CostEstimate(flops=12 * 10**9, bytes_accessed=16 * 10**6, transcendentals=0),
        name="decoder",
    )(
        core, whole, embedded, picker, picker_t, masked, table, bias, pull, *spread, pads, dec_vec, dec_up
    )


def enc_mlp_back_kernel(
    core_ref, whole, d_encoded_ref, d_embedded_ref, encoded_ref, h2_ref, middle_ref, slope_ref,
    activated_ref, pads_ref, enc_ref, in_keep_up, in_send_up, in_keep_down, in_send_down,
    d_middle_ref, d_small_ref, d_up_small_ref, keep_up, send_up, keep_down, send_down,
    w_up, w_down, d_hid_ref, stage_down, stage_up, sems, out_sems,
):
    core = core_ref[0]
    copies = [
        pltpu.make_async_copy(whole.at[:, pl.ds(at, ref.shape[1])], ref, sems.at[i])
        for i, (at, ref) in enumerate(((C_DOWN, w_down), (C_UP, w_up)))
    ]
    for copy in copies:
        copy.start()
    pads = pads_ref[...]
    g_low = d_encoded_ref[...]
    g = g_low.astype(F32)
    grad = low(t_dot(widen(encoded_ref[...], pads), d_embedded_ref[...]))
    for half in range(2):
        stage_down[half, :, 1152:] = grad[:, 256 * half : 256 * half + 256]
    for group in range(3):
        cut = slice(1024 * group, 1024 * group + 1024)
        grad = low(t_dot(activated_ref[:, cut], g_low))
        for half in range(2):
            stage_down[half, :, 384 * group : 384 * group + 384] = grad[:, 384 * half : 384 * half + 384]
    for half in range(2):
        put(
            stage_down.at[half], half, core, keep_down, send_down,
            (slice(None), pl.ds(0, 1408)), out_sems.at[half],
        )
    copies[0].wait()
    for group in range(3):
        cut = slice(1024 * group, 1024 * group + 1024)
        d_hid = dot_t(g_low, w_down[:, 768 * group : 768 * group + 768]) * slope_ref[:, cut]
        d_up_small_ref[:, cut] = col_sum(d_hid)
        d_hid_ref[:, cut] = low(d_hid)
    wide_t = widen(h2_ref[...], pads).T
    for half in range(2):

        @pl.loop(0, 3)
        def _(tile, half=half):
            cut = pl.ds(pl.multiple_of(1536 * half + 512 * tile, 512), 512)
            into = pl.ds(pl.multiple_of(512 * tile, 512), 512)
            stage_up[half, :, into] = low(dot(wide_t, d_hid_ref[:, cut]))

        put(
            stage_up.at[half], half, core, keep_up, send_up,
            (slice(None), pl.ds(0, 1536)), out_sems.at[2 + half],
        )
    copies[1].wait()
    d_h2 = narrow_wide(dot_t(d_hid_ref[...], w_up[...]), pads)
    unit, rstd = norm_parts(middle_ref[...])
    part, d_gain, d_shift = norm_back(d_h2, unit, rstd, enc_ref[1:2])
    d_middle = g + part
    d_middle_ref[...] = d_middle
    d_small_ref[...] = jnp.zeros_like(d_small_ref)
    d_small_ref[1:2] = d_gain
    d_small_ref[3:4] = d_shift
    d_small_ref[6:7] = col_sum(d_middle)
    d_small_ref[7:8] = col_sum(g)
    for half in range(2):
        pltpu.make_async_copy(
            stage_down.at[half], keep_down.at[:, pl.ds(0, 1408)], out_sems.at[half]
        ).wait()
        pltpu.make_async_copy(
            stage_up.at[half], keep_up.at[:, pl.ds(0, 1536)], out_sems.at[2 + half]
        ).wait()


def enc_mlp_back(core, whole, d_encoded, d_embedded, encoded, h2, middle, slope, activated, pads, enc_vec, ups_downs):
    outs = (
        shape((96, 768), F32),
        shape((8, 768), F32),
        shape((1, 3072), F32),
        shape((1024, 2048), BF16),
        shape((1024, 2048), BF16),
        shape((1024, 1920), BF16),
        shape((1024, 1920), BF16),
    )
    return pl.pallas_call(
        enc_mlp_back_kernel,
        in_specs=[pl.BlockSpec(memory_space=pltpu.SMEM), ANY] + [VMEM] * 9 + [ANY] * 4,
        out_specs=[VMEM] * 3 + [ANY] * 4,
        out_shape=outs,
        input_output_aliases={11: 3, 12: 4, 13: 5, 14: 6},
        scratch_shapes=[
            pltpu.VMEM((1024, 3072), BF16),
            pltpu.VMEM((1024, 2304), BF16),
            pltpu.VMEM((96, 3072), BF16),
            pltpu.VMEM((2, 1024, 1408), BF16),
            pltpu.VMEM((2, 1024, 1536), BF16),
            pltpu.SemaphoreType.DMA((2,)),
            pltpu.SemaphoreType.DMA((4,)),
        ],
        compiler_params=params(56),
        cost_estimate=pl.CostEstimate(flops=3 * 10**9, bytes_accessed=25 * 10**6, transcendentals=0),
        name="enc_mlp_back",
    )(core, whole, d_encoded, d_embedded, encoded, h2, middle, slope, activated, pads, enc_vec, *ups_downs)


def enc_att_back_kernel(
    core_ref, whole, d_middle_ref, x_ref, h1_ref, proj3_ref, shares_ref, attended_ref, pads_ref,
    enc_ref, d_enc_ref, d_enc_up_ref, d_dec_ref, d_dec_up_ref, in_keep, in_send,
    x_grad_ref, keep, send,
    w_qkv, w_proj, d_p3_ref, stage, sems, out_sems,
):
    core = core_ref[0]
    copies = [
        pltpu.make_async_copy(whole.at[:, pl.ds(at, ref.shape[1])], ref, sems.at[i])
        for i, (at, ref) in enumerate(((C_PROJ, w_proj), (0, w_qkv)))
    ]
    for copy in copies:
        copy.start()
    pads = pads_ref[...]
    d_middle = d_middle_ref[...]
    d_mid_low = low(d_middle)
    copies[0].wait()
    d_att = narrow(low(dot_t(d_mid_low, w_proj[...])), pads)
    for group in range(6):
        cuts = [slice(768 * i + 128 * group, 768 * i + 128 * group + 128) for i in range(3)]
        parts = attend_group_back(
            proj3_ref[:, cuts[0]], proj3_ref[:, cuts[1]], proj3_ref[:, cuts[2]],
            d_att[:, cuts[0]], shares_ref[group], 2, 0.125, 128,
        )
        for cut, part in zip(cuts, parts):
            d_p3_ref[:, cut] = part
    d_p3 = low(d_p3_ref[...])
    copies[1].wait()
    d_h1 = narrow_wide(dot_t(d_p3, w_qkv[...]), pads)
    unit, rstd = norm_parts(x_ref[...].astype(F32))
    part, d_gain, d_shift = norm_back(d_h1, unit, rstd, enc_ref[0:1])
    x_grad_ref[...] = low(d_middle + part)
    row = lax.broadcasted_iota(jnp.int32, (8, 768), 0)
    d_enc = d_enc_ref[...]
    for line, vector in (
        (0, d_gain),
        (2, d_shift),
        (4, col_sum(d_p3_ref[:, :768])),
        (5, col_sum(d_p3_ref[:, 1536:])),
    ):
        d_enc = d_enc + jnp.where(row == line, vector, 0.0)
    table = low(small_out(d_enc, d_enc_up_ref[...], d_dec_ref[...], d_dec_up_ref[...]))
    place = lax.broadcasted_iota(jnp.int32, (1024, 128), 0)
    device = lax.broadcasted_iota(jnp.int32, (1024, 128), 1)
    small = dot((place == 8 * device + 6).astype(BF16), table)
    wide_t = widen(h1_ref[...], pads).T
    wide_att_t = widen(attended_ref[...], pads).T
    for tile in range(4):
        half, into = tile // 2, slice(768 * (tile % 2), 768 * (tile % 2) + 768)
        if tile < 3:
            grad = dot(wide_t, d_p3[:, 768 * tile : 768 * tile + 768])
        else:
            grad = dot(wide_att_t, d_mid_low)
        stage[half, :, into] = low(grad)
        if tile == 0:
            stage[0, :, 0:128] = low(grad[:, 0:128] + small)
        if tile % 2 == 1:
            put(
                stage.at[half], half, core, keep, send,
                (slice(None), pl.ds(0, 1536)), out_sems.at[half],
            )
    for half in range(2):
        pltpu.make_async_copy(
            stage.at[half], keep.at[:, pl.ds(0, 1536)], out_sems.at[half]
        ).wait()


def enc_att_back(core, whole, d_middle, x, h1, proj3, shares, attended, pads, enc_vec, d_enc, d_enc_up, d_dec, d_dec_up, keep, send):
    return pl.pallas_call(
        enc_att_back_kernel,
        in_specs=[pl.BlockSpec(memory_space=pltpu.SMEM), ANY] + [VMEM] * 12 + [ANY] * 2,
        out_specs=[VMEM] + [ANY] * 2,
        out_shape=(
            shape((96, 768), BF16),
            shape((1024, 2048), BF16),
            shape((1024, 2048), BF16),
        ),
        input_output_aliases={14: 1, 15: 2},
        scratch_shapes=[
            pltpu.VMEM((1024, 2304), BF16),
            pltpu.VMEM((1024, 768), BF16),
            pltpu.VMEM((96, 2304), F32),
            pltpu.VMEM((2, 1024, 1536), BF16),
            pltpu.SemaphoreType.DMA((2,)),
            pltpu.SemaphoreType.DMA((2,)),
        ],
        compiler_params=params(48),
        cost_estimate=pl.CostEstimate(flops=3 * 10**9, bytes_accessed=20 * 10**6, transcendentals=0),
        name="enc_att_back",
    )(core, whole, d_middle, x, h1, proj3, shares, attended, pads, enc_vec, d_enc, d_enc_up, d_dec, d_dec_up, keep, send)


def regroup(matrix, groups):
    rows = matrix.shape[0]
    return matrix.reshape(rows, 128, groups, 8).transpose(0, 2, 1, 3).reshape(rows, -1)


def ungroup(matrix, groups):
    rows = matrix.shape[0]
    return matrix.reshape(rows, groups, 128, 8).transpose(0, 2, 1, 3).reshape(rows, -1)


def packed_shard(
    enc_gains, enc_biases, enc_qkv, enc_proj, enc_up, enc_up_bias, enc_down, dec_fill, dec_embed,
    dec_gains, dec_biases, dec_qkv, dec_proj, dec_up, dec_up_bias, dec_down,
):
    small = jnp.concatenate(
        [
            v.reshape(1, -1)
            for v in (enc_gains, enc_biases, enc_up_bias, dec_fill, dec_gains, dec_biases, dec_up_bias)
        ],
        axis=1,
    )
    enc_top = jnp.concatenate([enc_qkv, enc_proj, regroup(enc_up, 3), dec_embed], axis=1)
    small_row = jnp.pad(small, ((0, 1), (0, enc_top.shape[1] - small.shape[1])))
    enc_down_wide = enc_down.reshape(3, 8, 768).transpose(1, 0, 2).reshape(8, 2304)
    dec_top = jnp.concatenate(
        [jnp.concatenate([dec_qkv, dec_proj], axis=1), regroup(dec_up, 2)], axis=0
    )
    dec_down_wide = dec_down.reshape(2, 8, 512).transpose(1, 0, 2).reshape(8, 1024)
    return jnp.concatenate(
        [jnp.concatenate([enc_top, small_row], axis=0), enc_down_wide, dec_top, dec_down_wide],
        axis=1,
    )


def position_table(offset, width):
    half = width // 2
    rates = jnp.exp(jnp.arange(half, dtype=F32) * (-math.log(10000.0) / half))
    angle = offset.astype(F32)[:, None] * rates[None, :]
    return jnp.concatenate([jnp.sin(angle), jnp.cos(angle)], axis=1)


def layout(length_row, order, visible):
    length = order.shape[0]
    ends = jnp.cumsum(length_row, dtype=jnp.int32)
    places = lax.broadcasted_iota(jnp.int32, (length, 1), 0)
    passed = places >= ends[None, :]
    segment = jnp.sum(passed.astype(jnp.int32), axis=1, dtype=jnp.int32)
    offset = places[:, 0] - jnp.sum(
        jnp.where(passed, length_row[None, :], 0), axis=1, dtype=jnp.int32
    )
    shown_pos = order[:visible]
    shown_seg = jnp.sum(
        (shown_pos[:, None] >= ends[None, :]).astype(jnp.int32), axis=1, dtype=jnp.int32
    )
    onehot = places == shown_pos[None, :]
    return (segment, offset, shown_seg, onehot)


def spread_rows(devices, rows, at):
    feature = lax.broadcasted_iota(jnp.int32, (devices * rows, devices * 8), 0)
    place = lax.broadcasted_iota(jnp.int32, (devices * rows, devices * 8), 1)
    return (8 * (feature // rows) + at + feature % rows == place).astype(BF16)


def plans(length_rows, orders):
    segment, offset, shown_seg, onehot = jax.vmap(lambda a, b: layout(a, b, 48))(
        length_rows, orders
    )
    pack = jnp.arange(2, dtype=jnp.int32)[:, None] * 16
    seen = (shown_seg + pack).reshape(96)
    seen_keys = jnp.concatenate([seen, jnp.full((32,), -1, jnp.int32)])
    enc_bias = jnp.where(seen[:, None] == seen_keys[None, :], 0.0, NEVER).astype(F32)
    keys = jnp.concatenate([segment, jnp.full((2, 64), -1, jnp.int32)], axis=1)
    dec_bias = jnp.where(segment[:, :, None] == keys[:, None, :], 0.0, NEVER).astype(F32)
    hot = onehot.astype(BF16)
    none = jnp.zeros((192, 48), BF16)
    picker = jnp.concatenate(
        [jnp.concatenate([hot[0], none], axis=1), jnp.concatenate([none, hot[1]], axis=1)], axis=0
    )
    masked = (1.0 - jnp.sum(onehot.astype(F32), axis=2)).reshape(-1, 1)
    table = position_table(offset.reshape(-1), 512)
    return enc_bias, dec_bias, picker, picker.T, masked, table


def place_of(device):
    return device // 32, device // 8 % 4, device // 2 % 4, device % 2


AXES = {"y": (32, 4), "z": (8, 4), "x": (2, 4), "c": (1, 2)}


def moved(block, axis, by):
    stride, size = AXES[axis]
    route = []
    for device in range(128):
        at = device // stride % size
        route.append((device, device + ((at + by) % size - at) * stride))
    return lax.ppermute(block, BOTH, route)


def summed_along(parts, axis, at, before, final=False):
    rows, columns = parts[0].shape
    after = rows // (4 * before)
    cut = [part.reshape(before, 4, after, columns) for part in parts]

    def chunk(k):
        total = None
        for part in cut:
            piece = lax.dynamic_index_in_dim(part, k, 1, keepdims=False).astype(F32)
            total = piece if total is None else total + piece
        return total.reshape(before * after, columns)

    arrived = [moved(low(chunk((at + by) % 4)), axis, by) for by in (1, 3, 2)]
    total = chunk(at)
    for piece in arrived:
        total = total + piece.astype(F32)
    return total if final else low(total)


def on_device(
    x_vis, lengths, shuffle, enc_gains, enc_biases, enc_qkv, enc_proj, enc_up, enc_up_bias,
    enc_down, dec_fill, dec_embed, dec_gains, dec_biases, dec_qkv, dec_proj, dec_up, dec_up_bias,
    dec_down, cotangent,
):
    section = lax.axis_index("section")
    device = lax.axis_index(BOTH)
    y, z, x, core = place_of(device)
    shard = packed_shard(
        enc_gains, enc_biases, enc_qkv, enc_proj, enc_up, enc_up_bias, enc_down, dec_fill,
        dec_embed, dec_gains, dec_biases, dec_qkv, dec_proj, dec_up, dec_up_bias, dec_down,
    )
    whole = lax.all_gather(shard, BOTH, axis=0, tiled=True)

    packs = 2

    def mine(rows):
        return lax.dynamic_slice_in_dim(rows, section * packs, packs, 0)[:, 0]

    x_rows = mine(x_vis).reshape(packs * 48, 768)
    pull = mine(cotangent).reshape(packs * 192, 512)
    enc_bias, dec_bias, picker, picker_t, masked, table = plans(mine(lengths), mine(shuffle))
    pads = spread_rows(64, 6, 0)
    low_rows, high_rows = spread_rows(32, 4, 0), spread_rows(32, 4, 4)
    spread = (low_rows, high_rows, low_rows.T, high_rows.T)
    core_id = core.astype(jnp.int32).reshape(1)

    enc_vec, enc_up_vec, dec_vec, dec_up_vec = small_in(whole)
    encoded, embedded, h1, proj3, shares, attended, middle, h2, slope, activated = enc_forward(
        whole, x_rows, enc_bias, pads, enc_vec, enc_up_vec, dec_vec
    )
    decoded, d_encoded, d_embedded, d_dec, d_dec_up, *grads = decoder(
        core_id, whole, embedded, picker, picker_t, masked, table, dec_bias, pull, spread, pads,
        dec_vec, dec_up_vec,
    )
    d_middle, d_enc, d_enc_up, *mlp_grads = enc_mlp_back(
        core_id, whole, d_encoded, d_embedded, encoded, h2, middle, slope, activated, pads,
        enc_vec, grads[2:],
    )
    x_grad, keep_att, send_att = enc_att_back(
        core_id, whole, d_middle, x_rows, h1, proj3, shares, attended, pads, enc_vec, d_enc,
        d_enc_up, d_dec, d_dec_up, grads[0], grads[1],
    )
    keep_up, send_up, keep_down, send_down = mlp_grads

    down = summed_along((keep_down, moved(send_down, "c", 1)), "x", x, 16)
    up = summed_along((keep_up, moved(send_up, "c", 1)), "y", y, 1)
    att = summed_along((keep_att, moved(send_att, "c", 1)), "z", z, 4)
    down = summed_along((down,), "y", y, 1)
    up = summed_along((up,), "z", z, 1)
    att = summed_along((att,), "x", x, 4)
    down = summed_along((down,), "z", z, 1, True)
    up = summed_along((up,), "x", x, 1, True)
    att = summed_along((att,), "y", y, 1, True)
    columns = jnp.concatenate([att, up, down], axis=1).reshape(2, 8, -1)
    own = lax.dynamic_index_in_dim(columns, core, 0, keepdims=False)
    got = moved(lax.dynamic_index_in_dim(columns, 1 - core, 0, keepdims=False), "c", 1)
    halves = (jnp.where(core == 0, own, got), jnp.where(core == 0, got, own))

    def both(start, width):
        return jnp.concatenate([half[:, start : start + width] for half in halves], axis=1)

    top = both(0, 1536)
    z_att = both(1536, 512)
    enc_up_grad = both(2048, 1536)
    z_up = both(3584, 512)
    enc_down_grad = jnp.stack([both(4096 + 384 * g, 384) for g in range(3)])
    embed_grad = both(5248, 256)
    dec_down_grad = jnp.stack([both(5504 + 256 * g, 256) for g in range(2)])
    z_all = jnp.concatenate([z_att, z_up], axis=1)
    flat = top[6, :128]
    pieces = []
    at = 0
    for lead, part in COUNTS:
        pieces.append(flat[at : at + lead * part].reshape(lead, part))
        at += lead * part

    def placed(rows, width):
        rows = rows.reshape(packs, 1, -1, width)
        half = width // 2
        keep = lax.dynamic_slice_in_dim(rows, section * half, half, 3)
        send = lax.dynamic_slice_in_dim(rows, (1 - section) * half, half, 3)
        got = lax.ppermute(send, "section", [(0, 1), (1, 0)])
        return jnp.where(section == 0, jnp.concatenate([keep, got]), jnp.concatenate([got, keep]))

    return (
        placed(decoded, 512),
        placed(x_grad, 768),
        pieces[0],
        pieces[1],
        top[:6, :2304],
        top[:6, 2304:],
        ungroup(enc_up_grad[:6], 3),
        pieces[2][0],
        enc_down_grad.reshape(24, 768),
        pieces[3],
        embed_grad[:6],
        pieces[4],
        pieces[5],
        z_all[:4, :1536],
        z_all[:4, 1536:],
        ungroup(z_all[4:], 2),
        pieces[6][0],
        dec_down_grad.reshape(16, 512),
    )


def solution(mesh):
    rows = P(None, "dp", None, None)
    ids = P(None, "dp", None)
    wide = P(None, BOTH)
    tall = P(BOTH, None)
    flat = P(BOTH)
    in_specs = (rows, ids, ids, wide, wide, tall, tall, tall, flat, tall, wide, tall, wide, wide)
    in_specs += (tall, tall, tall, flat, tall, rows)
    out_rows = P(None, "dp", None, "section")
    out_specs = (out_rows, out_rows, wide, wide, tall, tall, tall, flat, tall, wide, tall, wide)
    out_specs += (wide, tall, tall, tall, flat, tall)
    return jax.shard_map(
        on_device, mesh=mesh, in_specs=in_specs, out_specs=out_specs, check_vma=False
    )
```

```python
import functools
import math

import jax
import jax.numpy as jnp
from jax import lax
from jax.experimental import pallas as pl
from jax.experimental.pallas import tpu as pltpu
from jax.sharding import PartitionSpec as P

H_ENC = 12
H_DEC = 16
BOTH = ("section", "dp")
F32 = jnp.float32
BF16 = jnp.bfloat16
EPS = 1e-06
NEVER = -1e30
MIB = 1 << 20

C_PROJ = 2304
C_UP = 3072
C_EMB = 6144
C_DOWN = 6656
C_Z = 8960
C_DDOWN = 11008
C_ALL = 12032
COUNTS = ((2, 6), (6, 6), (1, 24), (2, 4), (2, 4), (6, 4), (1, 16))


def dot(left, right):
    return jnp.dot(left, right, preferred_element_type=F32)


def dot_t(left, right):
    return lax.dot_general(left, right, (((1,), (1,)), ((), ())), preferred_element_type=F32)


def t_dot(left, right):
    return lax.dot_general(left, right, (((0,), (0,)), ((), ())), preferred_element_type=F32)


def low(values):
    return values.astype(BF16)


def norm_parts(values):
    mean = jnp.mean(values, axis=-1, keepdims=True)
    centred = values - mean
    rstd = lax.rsqrt(jnp.mean(centred * centred, axis=-1, keepdims=True) + EPS)
    return centred * rstd, rstd


def norm_back(d_normed, unit, rstd, gain):
    scaled = d_normed * gain
    part = scaled - jnp.mean(scaled, axis=-1, keepdims=True)
    part = (part - unit * jnp.mean(scaled * unit, axis=-1, keepdims=True)) * rstd
    return part, col_sum(d_normed * unit), col_sum(d_normed)


def col_sum(values):
    return jnp.sum(values, axis=0, keepdims=True)


def gelu_pair(hidden):
    share = 0.5 + 0.5 * lax.erf(hidden * math.sqrt(0.5))
    slope = share + hidden * (jnp.exp(-0.5 * hidden * hidden) * (1.0 / math.sqrt(2.0 * math.pi)))
    return hidden * share, slope


def head_stack(block, heads, rows):
    size = 128 // heads
    lane = lax.broadcasted_iota(jnp.int32, (1, 128), 1)
    fill = jnp.zeros((rows - block.shape[0], 128), BF16)
    parts = []
    for head in range(heads):
        own = ((lane >= head * size) & (lane < (head + 1) * size)).astype(BF16)
        parts += [block * own, fill]
    return jnp.concatenate(parts, axis=0)


def head_unstack(stack, heads, rows, count):
    size = 128 // heads
    lane = lax.broadcasted_iota(jnp.int32, (1, 128), 1)
    total = None
    for head in range(heads):
        own = ((lane >= head * size) & (lane < (head + 1) * size)).astype(F32)
        part = stack[head * rows : head * rows + count] * own
        total = part if total is None else total + part
    return total


def attend_group(query, key, value, bias, heads, scale, shares_out):
    rows = bias.shape[1]
    scores = dot_t(query, head_stack(key, heads, rows))
    parts = []
    for head in range(heads):
        s = scores[:, head * rows : (head + 1) * rows] * scale + bias
        powers = jnp.exp(s - jnp.max(s, axis=-1, keepdims=True))
        parts.append(powers / jnp.sum(powers, axis=-1, keepdims=True))
    shares = jnp.concatenate(parts, axis=1)
    shares_out[...] = shares
    return dot(low(shares), head_stack(value, heads, rows))


def attend_group_back(query, key, value, d_out, shares, heads, scale, rows):
    count = key.shape[0]
    d_shares = dot_t(d_out, head_stack(value, heads, rows))
    parts = []
    for head in range(heads):
        cut = slice(head * rows, (head + 1) * rows)
        p, dp = shares[:, cut], d_shares[:, cut]
        parts.append(low(p * (dp - jnp.sum(dp * p, axis=-1, keepdims=True))))
    d_scores = jnp.concatenate(parts, axis=1)
    d_query = dot(d_scores, head_stack(key, heads, rows)) * scale
    d_key = head_unstack(t_dot(d_scores, query), heads, rows, count) * scale
    d_value = head_unstack(t_dot(low(shares), d_out), heads, rows, count)
    return d_query, d_key, d_value


def widen(values, pads):
    return jnp.concatenate(
        [low(dot(values[:, :384], pads)), low(dot(values[:, 384:], pads))], axis=1
    )


def narrow(values, pads):
    return jnp.concatenate(
        [low(dot_t(values[:, :512], pads)), low(dot_t(values[:, 512:], pads))], axis=1
    )


def narrow_wide(values, pads):
    high = low(values)
    rest = low(values - high.astype(F32))
    return jnp.concatenate(
        [
            dot_t(high[:, :512], pads) + dot_t(rest[:, :512], pads),
            dot_t(high[:, 512:], pads) + dot_t(rest[:, 512:], pads),
        ],
        axis=1,
    )


def place_masks(width, part, offset):
    column = lax.broadcasted_iota(jnp.int32, (128, width), 1).astype(F32)
    line = lax.broadcasted_iota(jnp.int32, (128, width), 0).astype(F32)
    device = jnp.floor((column + 0.5) * (1.0 / part))
    own = (device == line).astype(F32)
    pick = (column - device * part + offset == line).astype(BF16)
    return own, pick


def small_plan():
    plan, at = [], 0
    for family, (lead, part) in enumerate(COUNTS):
        if part >= 16:
            for group in range(part // 8):
                plan.append((family, group, 1024, 8, at + 8 * group))
        else:
            for line in range(lead):
                plan.append((family, line, 128 * part, part, at + line * part))
        at += lead * part
    return plan


def small_in_kernel(whole_ref, enc_ref, enc_up_ref, dec_ref, dec_up_ref):
    device = lax.broadcasted_iota(jnp.int32, (128, 1024), 0)
    place = lax.broadcasted_iota(jnp.int32, (128, 1024), 1)
    table = low(dot((place == 8 * device + 6).astype(BF16), whole_ref[...]))
    enc_ref[...] = jnp.zeros_like(enc_ref)
    dec_ref[...] = jnp.zeros_like(dec_ref)
    for family, line, width, part, offset in small_plan():
        own, pick = place_masks(width, part, offset)
        vector = col_sum(own * dot(table, pick))
        if family == 2:
            enc_up_ref[:, 1024 * line : 1024 * line + 1024] = vector
        elif family == 6:
            dec_up_ref[:, 1024 * line : 1024 * line + 1024] = vector
        elif family < 2:
            enc_ref[2 * family + line : 2 * family + line + 1, :] = vector
        else:
            row = 2 * (family - 3) + line
            dec_ref[row : row + 1, :] = vector


def small_in(whole):
    return pl.pallas_call(
        small_in_kernel,
        grid=(1,),
        in_specs=[pl.BlockSpec((1024, 128), lambda i: (0, 0))],
        out_specs=[
            pl.BlockSpec((8, 768), lambda i: (0, 0)),
            pl.BlockSpec((1, 3072), lambda i: (0, 0)),
            pl.BlockSpec((16, 512), lambda i: (0, 0)),
            pl.BlockSpec((1, 2048), lambda i: (0, 0)),
        ],
        out_shape=[
            jax.ShapeDtypeStruct((8, 768), F32),
            jax.ShapeDtypeStruct((1, 3072), F32),
            jax.ShapeDtypeStruct((16, 512), F32),
            jax.ShapeDtypeStruct((1, 2048), F32),
        ],
        compiler_params=pltpu.CompilerParams(vmem_limit_bytes=32 * MIB),
        name="small_in",
    )(whole)


def small_out(enc, enc_up, dec, dec_up):
    total = jnp.zeros((128, 128), F32)
    for family, line, width, part, offset in small_plan():
        own, pick = place_masks(width, part, offset)
        if family == 2:
            vector = enc_up[:, 1024 * line : 1024 * line + 1024]
        elif family == 6:
            vector = dec_up[:, 1024 * line : 1024 * line + 1024]
        elif family < 2:
            vector = enc[2 * family + line : 2 * family + line + 1]
        else:
            row = 2 * (family - 3) + line
            vector = dec[row : row + 1]
        total = total + dot_t(low(own * vector), pick)
    return total


def enc_forward_kernel(
    whole, x_ref, bias_ref, pads_ref, enc_ref, enc_up_ref, dec_ref,
    embedded_ref, act_ref, h2_ref, h1_att_ref, proj3_ref, shares_ref, middle_ref, slope_ref,
    w_qkv, w_proj, w_up, w_emb, w_down, sems,
):
    copies = [
        pltpu.make_async_copy(whole.at[:, pl.ds(at, ref.shape[1])], ref, sems.at[i])
        for i, (at, ref) in enumerate(
            ((0, w_qkv), (C_PROJ, w_proj), (C_UP, w_up), (C_DOWN, w_down), (C_EMB, w_emb))
        )
    ]
    for copy in copies:
        copy.start()
    pads = pads_ref[...]
    x = x_ref[...].astype(F32)
    unit, _ = norm_parts(x)
    h1 = low(unit * enc_ref[0:1] + enc_ref[2:3])
    h1_att_ref[:, :768] = h1
    wide = widen(h1, pads)
    copies[0].wait()
    for third in range(3):
        cut = slice(768 * third, 768 * third + 768)
        part = dot(wide, w_qkv[:, cut])
        if third != 1:
            part = part + (enc_ref[4:5] if third == 0 else enc_ref[5:6])
        proj3_ref[:, cut] = low(part)
    bias = bias_ref[...]
    for group in range(6):
        cuts = [slice(768 * i + 128 * group, 768 * i + 128 * group + 128) for i in range(3)]
        out = attend_group(
            proj3_ref[:, cuts[0]], proj3_ref[:, cuts[1]], proj3_ref[:, cuts[2]],
            bias, 2, 0.125, shares_ref.at[group],
        )
        h1_att_ref[:, 768 + 128 * group : 896 + 128 * group] = low(out)
    copies[1].wait()
    middle = x + dot(widen(h1_att_ref[:, 768:], pads), w_proj[...]) + enc_ref[6:7]
    middle_ref[...] = middle
    unit, _ = norm_parts(middle)
    h2 = low(unit * enc_ref[1:2] + enc_ref[3:4])
    h2_ref[...] = h2
    wide = widen(h2, pads)
    copies[2].wait()

    @pl.loop(0, 6)
    def _(tile):
        cut = pl.ds(pl.multiple_of(tile * 512, 512), 512)
        value, slope = gelu_pair(dot(wide, w_up[:, cut]) + enc_up_ref[:, cut])
        act_ref[:, cut] = low(value)
        slope_ref[:, cut] = slope

    copies[3].wait()
    out = middle + enc_ref[7:8]
    for group in range(3):
        out = out + dot(
            act_ref[:, 1024 * group : 1024 * group + 1024],
            w_down[:, 768 * group : 768 * group + 768],
        )
    encoded = low(out)
    act_ref[:, 3072:] = encoded
    copies[4].wait()
    embedded_ref[...] = low(dot(widen(encoded, pads), w_emb[...]) + dec_ref[0:1])


VMEM = pl.BlockSpec(memory_space=pltpu.VMEM)
ANY = pl.BlockSpec(memory_space=pl.ANY)


def shape(dims, kind):
    return jax.ShapeDtypeStruct(dims, kind)


def params(limit):
    return pltpu.CompilerParams(vmem_limit_bytes=limit * MIB)


def enc_forward(whole, x, bias, pads, enc_vec, enc_up, dec_vec):
    outs = (
        shape((96, 512), BF16),
        shape((96, 3840), BF16),
        shape((96, 768), BF16),
        shape((96, 1536), BF16),
        shape((96, 2304), BF16),
        shape((6, 96, 256), F32),
        shape((96, 768), F32),
        shape((96, 3072), F32),
    )
    return pl.pallas_call(
        enc_forward_kernel,
        in_specs=[ANY] + [VMEM] * 6,
        out_specs=[VMEM] * len(outs),
        out_shape=outs,
        scratch_shapes=[
            pltpu.VMEM((1024, 2304), BF16),
            pltpu.VMEM((1024, 768), BF16),
            pltpu.VMEM((1024, 3072), BF16),
            pltpu.VMEM((1024, 512), BF16),
            pltpu.VMEM((1024, 2304), BF16),
            pltpu.SemaphoreType.DMA((5,)),
        ],
        compiler_params=params(48),
        cost_estimate=pl.CostEstimate(flops=2 * 10**9, bytes_accessed=20 * 10**6, transcendentals=0),
        name="enc_forward",
    )(whole, x, bias, pads, enc_vec, enc_up, dec_vec)


DEC_SCALE = 1.0 / math.sqrt(32)


def dec_kernel(
    whole, embedded_ref, picker_ref, picker_t_ref, masked_ref, table_ref, bias_ref,
    pull_ref, low_ref, high_ref, pads_ref, dec_ref, dec_up_ref,
    decoded_ref, d_encoded_ref, d_embedded_ref, d_small_ref, d_up_small_ref,
    activated_ref, rows_ref,
    w_z, w_down, w_emb, w_lo, w_hi, start_ref, proj3_ref, shares_ref, middle_ref, slope_ref,
    d_att_ref, d_p3_ref, sems,
):
    attended_ref, d_hid_ref = rows_ref.at[:, pl.ds(512, 512)], rows_ref.at[:, pl.ds(3584, 2048)]
    copies = [
        pltpu.make_async_copy(whole.at[:, pl.ds(at, ref.shape[1])], ref, sems.at[i])
        for i, (at, ref) in enumerate(((C_Z, w_z), (C_DDOWN, w_down), (C_EMB, w_emb)))
    ]
    for copy in copies:
        copy.start()
    gain_1, gain_2 = dec_ref[2:3], dec_ref[3:4]
    start = dot(picker_ref[...], embedded_ref[...]) + masked_ref[...] * dec_ref[1:2] + table_ref[...]
    start_ref[...] = start
    unit, _ = norm_parts(start)
    h1 = low(unit * gain_1 + dec_ref[4:5])
    rows_ref[:, :512] = h1
    copies[0].wait()

    @pl.loop(0, 4)
    def _(block):
        into = pl.ds(pl.multiple_of(block * 128, 128), 128)
        source = pl.ds(pl.multiple_of(block * 256, 256), 256)
        for half in range(2):
            cut = slice(1024 * half, 1024 * half + 1024)
            rows = w_z[source, cut]
            w_lo[into, cut] = low(dot(low_ref[...], rows))
            w_hi[into, cut] = low(dot(high_ref[...], rows))

    for third in range(3):
        cut = slice(512 * third, 512 * third + 512)
        part = dot(h1, w_lo[:, cut])
        if third != 1:
            part = part + (dec_ref[6:7] if third == 0 else dec_ref[7:8])
        proj3_ref[:, cut] = low(part)

    @pl.loop(0, 8)
    def _(step):
        pack, group = step // 4, step % 4
        rows = pl.ds(pl.multiple_of(pack * 192, 192), 192)
        cuts = [pl.ds(pl.multiple_of(512 * i + 128 * group, 128), 128) for i in range(3)]
        out = attend_group(
            proj3_ref[rows, cuts[0]], proj3_ref[rows, cuts[1]], proj3_ref[rows, cuts[2]],
            bias_ref[pack], 4, DEC_SCALE, shares_ref.at[step],
        )
        attended_ref[rows, cuts[0]] = low(out)

    middle = start + dot(attended_ref[...], w_lo[:, 1536:]) + dec_ref[8:9]
    middle_ref[...] = middle
    unit_2, rstd_2 = norm_parts(middle)
    h2 = low(unit_2 * gain_2 + dec_ref[5:6])
    rows_ref[:, 1024:1536] = h2

    @pl.loop(0, 4)
    def _(tile):
        cut = pl.ds(pl.multiple_of(tile * 512, 512), 512)
        value, slope = gelu_pair(dot(h2, w_hi[:, cut]) + dec_up_ref[:, cut])
        activated_ref[:, cut] = low(value)
        slope_ref[:, cut] = slope

    copies[1].wait()
    out = middle + dec_ref[9:10]
    for group in range(2):
        out = out + dot(
            activated_ref[:, 1024 * group : 1024 * group + 1024],
            w_down[:, 512 * group : 512 * group + 512],
        )
    decoded_ref[...] = low(out)

    g_low = pull_ref[...]
    for tile in range(4):
        group, rows = tile // 2, slice(512 * (tile % 2), 512 * (tile % 2) + 512)
        cut = slice(512 * tile, 512 * tile + 512)
        d_hid = dot_t(g_low, w_down[rows, 512 * group : 512 * group + 512]) * slope_ref[:, cut]
        d_up_small_ref[:, cut] = col_sum(d_hid)
        d_hid_ref[:, cut] = low(d_hid)
    d_h2 = dot_t(d_hid_ref[...], w_hi[...])
    part, d_gain_2, d_shift_2 = norm_back(d_h2, unit_2, rstd_2, gain_2)
    g = g_low.astype(F32)
    d_mid = g + part
    d_mid_low = low(d_mid)
    d_att = low(dot_t(d_mid_low, w_lo[:, 1536:]))
    d_small_ref[...] = jnp.zeros_like(d_small_ref)
    d_small_ref[3:4] = d_gain_2
    d_small_ref[5:6] = d_shift_2
    d_small_ref[8:9] = col_sum(d_mid)
    d_small_ref[9:10] = col_sum(g)
    rows_ref[:, 3072:3584] = d_mid_low
    middle_ref[...] = d_mid
    d_att_ref[...] = d_att

    @pl.loop(0, 8)
    def _(step):
        pack, group = step // 4, step % 4
        rows = pl.ds(pl.multiple_of(pack * 192, 192), 192)
        cuts = [pl.ds(pl.multiple_of(512 * i + 128 * group, 128), 128) for i in range(3)]
        parts = attend_group_back(
            proj3_ref[rows, cuts[0]], proj3_ref[rows, cuts[1]], proj3_ref[rows, cuts[2]],
            d_att_ref[rows, cuts[0]], shares_ref[step], 4, DEC_SCALE, 256,
        )
        for cut, part in zip(cuts, parts):
            d_p3_ref[rows, cut] = part

    d_small_ref[6:7] = col_sum(d_p3_ref[:, :512])
    d_small_ref[7:8] = col_sum(d_p3_ref[:, 1024:])
    d_p3 = low(d_p3_ref[...])
    rows_ref[:, 1536:3072] = d_p3
    d_h1 = dot_t(d_p3, w_lo[:, :1536])
    unit, rstd = norm_parts(start_ref[...])
    part, d_gain_1, d_shift_1 = norm_back(d_h1, unit, rstd, gain_1)
    d_start = middle_ref[...] + part
    d_small_ref[2:3] = d_gain_1
    d_small_ref[4:5] = d_shift_1
    d_small_ref[1:2] = col_sum(masked_ref[...] * d_start)
    d_embedded = dot(picker_t_ref[...], low(d_start))
    d_small_ref[0:1] = col_sum(d_embedded)
    d_embedded = low(d_embedded)
    d_embedded_ref[...] = d_embedded
    copies[2].wait()
    d_encoded_ref[...] = narrow(low(dot_t(d_embedded, w_emb[...])), pads_ref[...])


def decoder(whole, embedded, picker, picker_t, masked, table, bias, pull, spread, pads, dec_vec, dec_up):
    outs = (
        shape((384, 512), BF16),
        shape((96, 768), BF16),
        shape((96, 512), BF16),
        shape((16, 512), F32),
        shape((1, 2048), F32),
        shape((384, 2048), BF16),
        shape((384, 5632), BF16),
    )
    return pl.pallas_call(
        dec_kernel,
        in_specs=[ANY] + [VMEM] * 12,
        out_specs=[VMEM] * 7,
        out_shape=outs,
        scratch_shapes=[
            pltpu.VMEM((1024, 2048), BF16),
            pltpu.VMEM((1024, 1024), BF16),
            pltpu.VMEM((1024, 512), BF16),
            pltpu.VMEM((512, 2048), BF16),
            pltpu.VMEM((512, 2048), BF16),
            pltpu.VMEM((384, 512), F32),
            pltpu.VMEM((384, 1536), BF16),
            pltpu.VMEM((8, 192, 1024), F32),
            pltpu.VMEM((384, 512), F32),
            pltpu.VMEM((384, 2048), F32),
            pltpu.VMEM((384, 512), BF16),
            pltpu.VMEM((384, 1536), F32),
            pltpu.SemaphoreType.DMA((3,)),
        ],
        compiler_params=params(52),
        cost_estimate=pl.CostEstimate(flops=9 * 10**9, bytes_accessed=16 * 10**6, transcendentals=0),
        name="decoder",
    )(whole, embedded, picker, picker_t, masked, table, bias, pull, *spread, pads, dec_vec, dec_up)


def enc_mlp_back_kernel(
    whole, d_encoded_ref, middle_ref, slope_ref, pads_ref, enc_ref,
    d_middle_ref, d_small_ref, d_up_small_ref, d_hid_ref,
    w_up, w_down, sems,
):
    copies = [
        pltpu.make_async_copy(whole.at[:, pl.ds(at, ref.shape[1])], ref, sems.at[i])
        for i, (at, ref) in enumerate(((C_DOWN, w_down), (C_UP, w_up)))
    ]
    for copy in copies:
        copy.start()
    pads = pads_ref[...]
    g_low = d_encoded_ref[...]
    g = g_low.astype(F32)
    unit, rstd = norm_parts(middle_ref[...])
    copies[0].wait()
    for group in range(3):
        cut = slice(1024 * group, 1024 * group + 1024)
        d_hid = dot_t(g_low, w_down[:, 768 * group : 768 * group + 768]) * slope_ref[:, cut]
        d_up_small_ref[:, cut] = col_sum(d_hid)
        d_hid_ref[:, cut] = low(d_hid)
    copies[1].wait()
    d_h2 = narrow_wide(dot_t(d_hid_ref[...], w_up[...]), pads)
    part, d_gain, d_shift = norm_back(d_h2, unit, rstd, enc_ref[1:2])
    d_middle = g + part
    d_middle_ref[...] = d_middle
    d_small_ref[...] = jnp.zeros_like(d_small_ref)
    d_small_ref[1:2] = d_gain
    d_small_ref[3:4] = d_shift
    d_small_ref[6:7] = col_sum(d_middle)
    d_small_ref[7:8] = col_sum(g)


def enc_mlp_back(whole, d_encoded, middle, slope, pads, enc_vec):
    outs = (
        shape((96, 768), F32),
        shape((8, 768), F32),
        shape((1, 3072), F32),
        shape((96, 3072), BF16),
    )
    return pl.pallas_call(
        enc_mlp_back_kernel,
        in_specs=[ANY] + [VMEM] * 5,
        out_specs=[VMEM] * 4,
        out_shape=outs,
        scratch_shapes=[
            pltpu.VMEM((1024, 3072), BF16),
            pltpu.VMEM((1024, 2304), BF16),
            pltpu.SemaphoreType.DMA((2,)),
        ],
        compiler_params=params(32),
        cost_estimate=pl.CostEstimate(flops=2 * 10**9, bytes_accessed=12 * 10**6, transcendentals=0),
        name="enc_mlp_back",
    )(whole, d_encoded, middle, slope, pads, enc_vec)


def enc_att_back_kernel(
    whole, d_middle_ref, x_ref, proj3_ref, shares_ref, pads_ref, enc_ref, d_enc_ref, d_enc_up_ref,
    d_dec_ref, d_dec_up_ref,
    x_grad_ref, rows_ref,
    w_qkv, w_proj, d_p3_ref, sems,
):
    copies = [
        pltpu.make_async_copy(whole.at[:, pl.ds(at, ref.shape[1])], ref, sems.at[i])
        for i, (at, ref) in enumerate(((C_PROJ, w_proj), (0, w_qkv)))
    ]
    for copy in copies:
        copy.start()
    pads = pads_ref[...]
    d_middle = d_middle_ref[...]
    d_mid_low = low(d_middle)
    rows_ref[96:, :3072] = jnp.zeros((32, 3072), BF16)
    rows_ref[:96, 2304:3072] = d_mid_low
    copies[0].wait()
    d_att = narrow(low(dot_t(d_mid_low, w_proj[...])), pads)
    for group in range(6):
        cuts = [slice(768 * i + 128 * group, 768 * i + 128 * group + 128) for i in range(3)]
        parts = attend_group_back(
            proj3_ref[:, cuts[0]], proj3_ref[:, cuts[1]], proj3_ref[:, cuts[2]],
            d_att[:, cuts[0]], shares_ref[group], 2, 0.125, 128,
        )
        for cut, part in zip(cuts, parts):
            d_p3_ref[:, cut] = part
    d_p3 = low(d_p3_ref[...])
    rows_ref[:96, :2304] = d_p3
    copies[1].wait()
    d_h1 = narrow_wide(dot_t(d_p3, w_qkv[...]), pads)
    unit, rstd = norm_parts(x_ref[...].astype(F32))
    part, d_gain, d_shift = norm_back(d_h1, unit, rstd, enc_ref[0:1])
    x_grad_ref[...] = low(d_middle + part)
    row = lax.broadcasted_iota(jnp.int32, (8, 768), 0)
    d_enc = d_enc_ref[...]
    for line, vector in (
        (0, d_gain),
        (2, d_shift),
        (4, col_sum(d_p3_ref[:, :768])),
        (5, col_sum(d_p3_ref[:, 1536:])),
    ):
        d_enc = d_enc + jnp.where(row == line, vector, 0.0)
    rows_ref[:, 3072:] = low(
        small_out(d_enc, d_enc_up_ref[...], d_dec_ref[...], d_dec_up_ref[...])
    )


def enc_att_back(whole, d_middle, x, proj3, shares, pads, enc_vec, d_enc, d_enc_up, d_dec, d_dec_up):
    return pl.pallas_call(
        enc_att_back_kernel,
        in_specs=[ANY] + [VMEM] * 10,
        out_specs=[VMEM] * 2,
        out_shape=(shape((96, 768), BF16), shape((128, 3200), BF16)),
        scratch_shapes=[
            pltpu.VMEM((1024, 2304), BF16),
            pltpu.VMEM((1024, 768), BF16),
            pltpu.VMEM((96, 2304), F32),
            pltpu.SemaphoreType.DMA((2,)),
        ],
        compiler_params=params(32),
        cost_estimate=pl.CostEstimate(flops=2 * 10**9, bytes_accessed=8 * 10**6, transcendentals=0),
        name="enc_att_back",
    )(whole, d_middle, x, proj3, shares, pads, enc_vec, d_enc, d_enc_up, d_dec, d_dec_up)


def widen_t(values, pads_t):
    return jnp.concatenate(
        [low(dot_t(pads_t, values[:, :384])), low(dot_t(pads_t, values[:, 384:]))], axis=0
    )


def spread_t(values, rows_t):
    return jnp.concatenate(
        [low(dot_t(rows_t, values[:, 128 * i : 128 * i + 128])) for i in range(4)], axis=0
    )


def two(own, other, cut):
    return jnp.concatenate([own[:, cut], other[:, cut]], axis=0)


def chunk_copies(stage, place, splits, outs, sems):
    copies = []
    for split, (start, width, first) in enumerate(splits):
        send, keep = outs[2 * split], outs[2 * split + 1]
        for slot, (ref, flips) in enumerate(((send, (first, 2)), (keep, (0, 4 - first)))):
            for line, turn in enumerate(flips):
                copies.append(
                    pltpu.make_async_copy(
                        stage.at[:, place ^ turn, :, pl.ds(start, width)],
                        ref.at[line],
                        sems.at[4 * split + 2 * slot + line],
                    )
                )
    return copies


X_SPLITS = ((0, 1024, 1), (1024, 896, 3))
Y_SPLITS = ((0, 1280, 1), (1280, 1280, 3))
Z_SPLITS = ((0, 768, 1), (768, 768, 3))


def grad_x_kernel(
    place_ref, enc_ref, enc_o_ref, m_ref, m_o_ref, e_ref, e_o_ref, dec_ref, dec_o_ref, pull_ref,
    pull_o_ref, pads_t_ref, send_p, keep_p, send_q, keep_q, stage, sems,
):
    core = place_ref[3]
    copies = chunk_copies(stage, place_ref[0], X_SPLITS, (send_p, keep_p, send_q, keep_q), sems)
    for group in range(3):
        right = two(m_ref, m_o_ref, pl.ds(pl.multiple_of(384 * core, 128), 384))
        grad = low(t_dot(two(enc_ref, enc_o_ref, pl.ds(1024 * group, 1024)), right))
        stage[:, :, :, 384 * group : 384 * group + 384] = grad.reshape(16, 4, 16, 384)
    for copy in copies[:4]:
        copy.start()
    right = two(e_ref, e_o_ref, pl.ds(pl.multiple_of(256 * core, 128), 256))
    wide = widen_t(two(enc_ref, enc_o_ref, pl.ds(3072, 768)), pads_t_ref[...])
    stage[:, :, :, 1152:1408] = low(dot(wide, right)).reshape(16, 4, 16, 256)
    right = two(pull_ref, pull_o_ref, pl.ds(pl.multiple_of(256 * core, 128), 256))
    for group in range(2):
        grad = low(t_dot(two(dec_ref, dec_o_ref, pl.ds(1024 * group, 1024)), right))
        stage[:, :, :, 1408 + 256 * group : 1664 + 256 * group] = grad.reshape(16, 4, 16, 256)
    for copy in copies[4:]:
        copy.start()
    for copy in copies:
        copy.wait()


def grad_y_kernel(
    place_ref, h2_ref, h2_o_ref, hid_ref, hid_o_ref, dec_ref, dec_o_ref, pads_t_ref, low_t_ref,
    high_t_ref, send_p, keep_p, send_q, keep_q, stage, sems,
):
    core = place_ref[3]
    copies = chunk_copies(stage, place_ref[1], Y_SPLITS, (send_p, keep_p, send_q, keep_q), sems)
    wide = widen_t(two(h2_ref, h2_o_ref, slice(None)), pads_t_ref[...])
    for tile in range(3):
        cut = pl.ds(pl.multiple_of(1536 * core + 512 * tile, 128), 512)
        stage[0, :, :, 512 * tile : 512 * tile + 512] = low(
            dot(wide, two(hid_ref, hid_o_ref, cut))
        ).reshape(4, 256, 512)
    for copy in copies[:4]:
        copy.start()
    low_t = low_t_ref[...]
    raised = spread_t(two(dec_ref, dec_o_ref, slice(1024, 1536)), high_t_ref[...])
    for tile in range(2):
        left_at = 0 if tile == 0 else pl.multiple_of(512 * core, 128)
        left = spread_t(two(dec_ref, dec_o_ref, pl.ds(left_at, 512)), low_t)
        at = pl.multiple_of(1024 * tile + 512 * core, 128)
        grad = dot(left, two(dec_ref, dec_o_ref, pl.ds(1536 + at, 512)))
        grad = grad + dot(raised, two(dec_ref, dec_o_ref, pl.ds(3584 + at, 512)))
        stage[0, :, :, 1536 + 512 * tile : 2048 + 512 * tile] = low(grad).reshape(4, 256, 512)
    for copy in copies[4:]:
        copy.start()
    for copy in copies:
        copy.wait()


def grad_z_kernel(
    place_ref, h1_ref, h1_o_ref, rows_ref, rows_o_ref, pads_t_ref,
    send_p, keep_p, send_q, keep_q, stage, sems,
):
    core = place_ref[3]
    copies = chunk_copies(stage, place_ref[2], Z_SPLITS, (send_p, keep_p, send_q, keep_q), sems)
    pads_t = pads_t_ref[...]
    table = low(rows_ref[:, 3072:].astype(F32) + rows_o_ref[:, 3072:].astype(F32))
    line = lax.broadcasted_iota(jnp.int32, (1024, 128), 0)
    device = lax.broadcasted_iota(jnp.int32, (1024, 128), 1)
    small = dot(((line == 8 * device + 6) & (core == 0)).astype(BF16), table)

    def right(at):
        cut = pl.ds(pl.multiple_of(1536 * core + at, 128), 768)
        return jnp.concatenate([rows_ref[:96, cut], rows_o_ref[:96, cut]], axis=0)

    grad = dot(widen_t(two(h1_ref, h1_o_ref, pl.ds(0, 768)), pads_t), right(0))
    stage[:, :, :, :768] = low(grad).reshape(4, 4, 64, 768)
    stage[:, :, :, :128] = low(grad[:, :128] + small).reshape(4, 4, 64, 128)
    for copy in copies[:4]:
        copy.start()
    cut = pl.ds(pl.multiple_of(768 * core, 128), 768)
    grad = dot(widen_t(two(h1_ref, h1_o_ref, cut), pads_t), right(768))
    stage[:, :, :, 768:] = low(grad).reshape(4, 4, 64, 768)
    for copy in copies[4:]:
        copy.start()
    for copy in copies:
        copy.wait()


def grad_call(kernel, name, before, splits, place, *operands):
    after = 256 // before
    outs = []
    for _, width, _ in splits:
        outs += [shape((2, before, after, width), BF16)] * 2
    columns = sum(width for _, width, _ in splits)
    return pl.pallas_call(
        kernel,
        in_specs=[pl.BlockSpec(memory_space=pltpu.SMEM)] + [VMEM] * len(operands),
        out_specs=[ANY] * 4,
        out_shape=outs,
        scratch_shapes=[
            pltpu.VMEM((before, 4, after, columns), BF16),
            pltpu.SemaphoreType.DMA((8,)),
        ],
        compiler_params=params(48),
        cost_estimate=pl.CostEstimate(flops=3 * 10**9, bytes_accessed=8 * 10**6, transcendentals=0),
        name=name,
    )(place, *operands)


def fold_kernel(keep_ref, got_ref, mine_ref, send_ref):
    mine_ref[...] = low(keep_ref[0].astype(F32) + got_ref[0].astype(F32))
    send_ref[...] = low(keep_ref[1].astype(F32) + got_ref[1].astype(F32))


def fold(keep, got):
    _, rows, columns = keep.shape
    steps = max(1, rows // 64)
    block = (2, rows // steps, columns)
    return pl.pallas_call(
        fold_kernel,
        grid=(steps,),
        in_specs=[pl.BlockSpec(block, lambda i: (0, i, 0))] * 2,
        out_specs=[pl.BlockSpec(block[1:], lambda i: (i, 0))] * 2,
        out_shape=[shape((rows, columns), BF16)] * 2,
        compiler_params=params(24),
        name="fold",
    )(keep, got)


def turn_kernel(place_ref, *refs, axis, first, count):
    place = place_ref[axis]
    sources, (send_ref, keep_ref) = refs[: 2 * count], refs[2 * count :]
    for out, flips in ((send_ref, (first, 2)), (keep_ref, (0, 4 - first))):
        for line, turn in enumerate(flips):
            at = 0
            for pair in range(count):
                a, b = sources[2 * pair], sources[2 * pair + 1]
                chunk = pl.ds(place ^ turn, 1)
                total = a[:, chunk].astype(F32) + b[:, chunk].astype(F32)
                before, _, after, columns = total.shape
                out[line, :, at : at + columns] = low(total).reshape(before * after, columns)
                at += columns


def turn(place, axis, before, pairs):
    rows = pairs[0][0].shape[0]
    after = rows // (4 * before)
    operands = [a.reshape(before, 4, after, a.shape[-1]) for pair in pairs for a in pair]
    columns = sum(pair[0].shape[-1] for pair in pairs)
    out = shape((2, rows // 4, columns), BF16)
    return pl.pallas_call(
        functools.partial(turn_kernel, axis=axis, first=1, count=len(pairs)),
        in_specs=[pl.BlockSpec(memory_space=pltpu.SMEM)] + [VMEM] * len(operands),
        out_specs=[VMEM] * 2,
        out_shape=[out] * 2,
        compiler_params=params(24),
        name="turn",
    )(place, *operands)


def last_kernel(place_ref, *refs):
    core = place_ref[3]
    sources, (own_ref, other_ref) = refs[:6], refs[6:]
    at = 0
    for pair in range(3):
        total = sources[2 * pair][...].astype(F32) + sources[2 * pair + 1][...].astype(F32)
        cut = slice(at, at + total.shape[1])
        own_ref[:, cut] = jnp.where(core == 0, total[:8], total[8:])
        other_ref[:, cut] = jnp.where(core == 0, total[8:], total[:8])
        at += total.shape[1]


def last(place, pairs):
    columns = sum(pair[0].shape[-1] for pair in pairs)
    return pl.pallas_call(
        last_kernel,
        in_specs=[pl.BlockSpec(memory_space=pltpu.SMEM)] + [VMEM] * 6,
        out_specs=[VMEM] * 2,
        out_shape=[shape((8, columns), F32)] * 2,
        compiler_params=params(24),
        name="last",
    )(place, *[a for pair in pairs for a in pair])


def regroup(matrix, groups):
    rows = matrix.shape[0]
    return matrix.reshape(rows, 128, groups, 8).transpose(0, 2, 1, 3).reshape(rows, -1)


def ungroup(matrix, groups):
    rows = matrix.shape[0]
    return matrix.reshape(rows, groups, 128, 8).transpose(0, 2, 1, 3).reshape(rows, -1)


def packed_shard(
    enc_gains, enc_biases, enc_qkv, enc_proj, enc_up, enc_up_bias, enc_down, dec_fill, dec_embed,
    dec_gains, dec_biases, dec_qkv, dec_proj, dec_up, dec_up_bias, dec_down,
):
    small = jnp.concatenate(
        [
            v.reshape(1, -1)
            for v in (enc_gains, enc_biases, enc_up_bias, dec_fill, dec_gains, dec_biases, dec_up_bias)
        ],
        axis=1,
    )
    enc_top = jnp.concatenate([enc_qkv, enc_proj, regroup(enc_up, 3), dec_embed], axis=1)
    small_row = jnp.pad(small, ((0, 1), (0, enc_top.shape[1] - small.shape[1])))
    enc_down_wide = enc_down.reshape(3, 8, 768).transpose(1, 0, 2).reshape(8, 2304)
    dec_top = jnp.concatenate(
        [jnp.concatenate([dec_qkv, dec_proj], axis=1), regroup(dec_up, 2)], axis=0
    )
    dec_down_wide = dec_down.reshape(2, 8, 512).transpose(1, 0, 2).reshape(8, 1024)
    return jnp.concatenate(
        [jnp.concatenate([enc_top, small_row], axis=0), enc_down_wide, dec_top, dec_down_wide],
        axis=1,
    )


def position_table(offset, width):
    half = width // 2
    rates = jnp.exp(jnp.arange(half, dtype=F32) * (-math.log(10000.0) / half))
    angle = offset.astype(F32)[:, None] * rates[None, :]
    return jnp.concatenate([jnp.sin(angle), jnp.cos(angle)], axis=1)


def layout(length_row, order, visible):
    length = order.shape[0]
    ends = jnp.cumsum(length_row, dtype=jnp.int32)
    places = lax.broadcasted_iota(jnp.int32, (length, 1), 0)
    passed = places >= ends[None, :]
    segment = jnp.sum(passed.astype(jnp.int32), axis=1, dtype=jnp.int32)
    offset = places[:, 0] - jnp.sum(
        jnp.where(passed, length_row[None, :], 0), axis=1, dtype=jnp.int32
    )
    shown_pos = order[:visible]
    shown_seg = jnp.sum(
        (shown_pos[:, None] >= ends[None, :]).astype(jnp.int32), axis=1, dtype=jnp.int32
    )
    onehot = places == shown_pos[None, :]
    return (segment, offset, shown_seg, onehot)


def spread_rows(devices, rows, at):
    feature = lax.broadcasted_iota(jnp.int32, (devices * rows, devices * 8), 0)
    place = lax.broadcasted_iota(jnp.int32, (devices * rows, devices * 8), 1)
    return (8 * (feature // rows) + at + feature % rows == place).astype(BF16)


def plans(length_rows, orders):
    segment, offset, shown_seg, onehot = jax.vmap(lambda a, b: layout(a, b, 48))(
        length_rows, orders
    )
    pack = jnp.arange(2, dtype=jnp.int32)[:, None] * 16
    seen = (shown_seg + pack).reshape(96)
    seen_keys = jnp.concatenate([seen, jnp.full((32,), -1, jnp.int32)])
    enc_bias = jnp.where(seen[:, None] == seen_keys[None, :], 0.0, NEVER).astype(F32)
    keys = jnp.concatenate([segment, jnp.full((2, 64), -1, jnp.int32)], axis=1)
    dec_bias = jnp.where(segment[:, :, None] == keys[:, None, :], 0.0, NEVER).astype(F32)
    hot = onehot.astype(BF16)
    none = jnp.zeros((192, 48), BF16)
    picker = jnp.concatenate(
        [jnp.concatenate([hot[0], none], axis=1), jnp.concatenate([none, hot[1]], axis=1)], axis=0
    )
    masked = (1.0 - jnp.sum(onehot.astype(F32), axis=2)).reshape(-1, 1)
    table = position_table(offset.reshape(-1), 512)
    return enc_bias, dec_bias, picker, picker.T, masked, table


def place_of(device):
    return device // 2 % 4, device // 32, device // 8 % 4, device % 2


AXES = {"y": (32, 4), "z": (8, 4), "x": (2, 4), "c": (1, 2)}


def flipped(block, axis, turn):
    stride, size = AXES[axis]
    route = []
    for device in range(128):
        at = device // stride % size
        route.append((device, device + ((at ^ turn) - at) * stride))
    return lax.ppermute(block, BOTH, route)


def other_core(block):
    return flipped(block, "c", 1)


def summed(axis, first, send, keep):
    mine, onward = fold(keep, flipped(send, axis, first))
    return mine, flipped(onward, axis, 4 - first)


def summed_first(axis, outs):
    pairs = []
    for split, first in enumerate((1, 3)):
        send, keep = [a.reshape(2, 256, a.shape[-1]) for a in outs[2 * split : 2 * split + 2]]
        pairs.append(summed(axis, first, send, keep))
    return pairs


def on_device(
    x_vis, lengths, shuffle, enc_gains, enc_biases, enc_qkv, enc_proj, enc_up, enc_up_bias,
    enc_down, dec_fill, dec_embed, dec_gains, dec_biases, dec_qkv, dec_proj, dec_up, dec_up_bias,
    dec_down, cotangent,
):
    section = lax.axis_index("section")
    device = lax.axis_index(BOTH)
    x, y, z, core = place_of(device)
    shard = packed_shard(
        enc_gains, enc_biases, enc_qkv, enc_proj, enc_up, enc_up_bias, enc_down, dec_fill,
        dec_embed, dec_gains, dec_biases, dec_qkv, dec_proj, dec_up, dec_up_bias, dec_down,
    )
    whole = lax.all_gather(shard, BOTH, axis=0, tiled=True)

    packs = 2

    def mine(rows):
        return lax.dynamic_slice_in_dim(rows, section * packs, packs, 0)[:, 0]

    x_rows = mine(x_vis).reshape(packs * 48, 768)
    pull = mine(cotangent).reshape(packs * 192, 512)
    enc_bias, dec_bias, picker, picker_t, masked, table = plans(mine(lengths), mine(shuffle))
    pads = spread_rows(64, 6, 0)
    low_rows, high_rows = spread_rows(32, 4, 0), spread_rows(32, 4, 4)
    spread = (low_rows, high_rows)
    pads_t, low_t, high_t = pads.T, low_rows.T, high_rows.T
    place = jnp.stack([x, y, z, core]).astype(jnp.int32)
    pull_o = other_core(pull)

    enc_vec, enc_up_vec, dec_vec, dec_up_vec = small_in(whole)
    embedded, act, h2, h1_att, proj3, shares, middle, slope = enc_forward(
        whole, x_rows, enc_bias, pads, enc_vec, enc_up_vec, dec_vec
    )
    act_o, h2_o, h1_att_o = other_core(act), other_core(h2), other_core(h1_att)
    decoded, d_encoded, d_embedded, d_dec, d_dec_up, dec_act, dec_rows = decoder(
        whole, embedded, picker, picker_t, masked, table, dec_bias, pull, spread, pads, dec_vec,
        dec_up_vec,
    )
    dec_act_o, dec_rows_o = other_core(dec_act), other_core(dec_rows)
    d_encoded_o, d_embedded_o = other_core(d_encoded), other_core(d_embedded)
    d_middle, d_enc, d_enc_up, d_hid = enc_mlp_back(
        whole, d_encoded, middle, slope, pads, enc_vec
    )
    d_hid_o = other_core(d_hid)
    sums_x = grad_call(
        grad_x_kernel, "grad_x", 16, X_SPLITS, place, act, act_o, d_encoded, d_encoded_o,
        d_embedded, d_embedded_o, dec_act, dec_act_o, pull, pull_o, pads_t,
    )
    sums_x = summed_first("x", sums_x)
    sums_y = grad_call(
        grad_y_kernel, "grad_y", 1, Y_SPLITS, place, h2, h2_o, d_hid, d_hid_o, dec_rows,
        dec_rows_o, pads_t, low_t, high_t,
    )
    sums_y = summed_first("y", sums_y)
    x_grad, rows = enc_att_back(
        whole, d_middle, x_rows, proj3, shares, pads, enc_vec, d_enc, d_enc_up, d_dec, d_dec_up
    )
    sums_z = grad_call(
        grad_z_kernel, "grad_z", 4, Z_SPLITS, place, h1_att, h1_att_o, rows, other_core(rows), pads_t
    )
    sums_z = summed_first("z", sums_z)

    sums_x = summed("y", 1, *turn(place, 1, 1, sums_x))
    sums_y = summed("z", 1, *turn(place, 2, 1, sums_y))
    sums_z = summed("x", 1, *turn(place, 0, 4, sums_z))
    sums_x = summed("z", 1, *turn(place, 2, 1, [sums_x]))
    sums_y = summed("x", 1, *turn(place, 0, 1, [sums_y]))
    sums_z = summed("y", 1, *turn(place, 1, 1, [sums_z]))
    own, other = last(place, (sums_x, sums_y, sums_z))
    got = other_core(other)
    halves = (jnp.where(core == 0, own, got), jnp.where(core == 0, got, own))

    def both(start, width):
        return jnp.concatenate([half[:, start : start + width] for half in halves], axis=1)

    enc_down_grad = jnp.stack([both(384 * g, 384) for g in range(3)])
    embed_grad = both(1152, 256)
    dec_down_grad = jnp.stack([both(1408 + 256 * g, 256) for g in range(2)])
    enc_up_grad = both(1920, 1536)
    z_all = jnp.concatenate([both(3456, 512), both(3968, 512)], axis=1)
    top = both(4480, 1536)
    flat = top[6, :128]
    pieces = []
    at = 0
    for lead, part in COUNTS:
        pieces.append(flat[at : at + lead * part].reshape(lead, part))
        at += lead * part

    def placed(rows, width):
        rows = rows.reshape(packs, 1, -1, width)
        half = width // 2
        keep = lax.dynamic_slice_in_dim(rows, section * half, half, 3)
        send = lax.dynamic_slice_in_dim(rows, (1 - section) * half, half, 3)
        got = lax.ppermute(send, "section", [(0, 1), (1, 0)])
        return jnp.where(section == 0, jnp.concatenate([keep, got]), jnp.concatenate([got, keep]))

    return (
        placed(decoded, 512),
        placed(x_grad, 768),
        pieces[0],
        pieces[1],
        top[:6, :2304],
        top[:6, 2304:],
        ungroup(enc_up_grad[:6], 3),
        pieces[2][0],
        enc_down_grad.reshape(24, 768),
        pieces[3],
        embed_grad[:6],
        pieces[4],
        pieces[5],
        z_all[:4, :1536],
        z_all[:4, 1536:],
        ungroup(z_all[4:], 2),
        pieces[6][0],
        dec_down_grad.reshape(16, 512),
    )


def solution(mesh):
    rows = P(None, "dp", None, None)
    ids = P(None, "dp", None)
    wide = P(None, BOTH)
    tall = P(BOTH, None)
    flat = P(BOTH)
    in_specs = (rows, ids, ids, wide, wide, tall, tall, tall, flat, tall, wide, tall, wide, wide)
    in_specs += (tall, tall, tall, flat, tall, rows)
    out_rows = P(None, "dp", None, "section")
    out_specs = (out_rows, out_rows, wide, wide, tall, tall, tall, flat, tall, wide, tall, wide)
    out_specs += (wide, tall, tall, tall, flat, tall)
    return jax.shard_map(
        on_device, mesh=mesh, in_specs=in_specs, out_specs=out_specs, check_vma=False
    )
```

```python
import functools
import math

import jax
import jax.numpy as jnp
from jax import lax
from jax.experimental import pallas as pl
from jax.experimental.pallas import tpu as pltpu
from jax.sharding import Mesh
from jax.sharding import PartitionSpec as P

H_ENC = 12
H_DEC = 16
DP = ("y_low", "z", "x", "core")
BOTH = ("section", *DP)
Y_AXIS = ("section", "y_low")
F32 = jnp.float32
BF16 = jnp.bfloat16
EPS = 1e-06
NEVER = -1e30
MIB = 1 << 20

C_PROJ = 2304
C_UP = 3072
C_EMB = 6144
C_DOWN = 6656
C_Z = 8960
C_DDOWN = 11008
C_ALL = 12032
COUNTS = ((2, 6), (6, 6), (1, 24), (2, 4), (2, 4), (6, 4), (1, 16))


def dot(left, right):
    return jnp.dot(left, right, preferred_element_type=F32)


def dot_t(left, right):
    return lax.dot_general(left, right, (((1,), (1,)), ((), ())), preferred_element_type=F32)


def t_dot(left, right):
    return lax.dot_general(left, right, (((0,), (0,)), ((), ())), preferred_element_type=F32)


def low(values):
    return values.astype(BF16)


def norm_parts(values):
    mean = jnp.mean(values, axis=-1, keepdims=True)
    centred = values - mean
    rstd = lax.rsqrt(jnp.mean(centred * centred, axis=-1, keepdims=True) + EPS)
    return centred * rstd, rstd


def norm_back(d_normed, unit, rstd, gain):
    scaled = d_normed * gain
    part = scaled - jnp.mean(scaled, axis=-1, keepdims=True)
    part = (part - unit * jnp.mean(scaled * unit, axis=-1, keepdims=True)) * rstd
    return part, col_sum(d_normed * unit), col_sum(d_normed)


def col_sum(values):
    return jnp.sum(values, axis=0, keepdims=True)


def gelu_pair(hidden):
    share = 0.5 + 0.5 * lax.erf(hidden * math.sqrt(0.5))
    slope = share + hidden * (jnp.exp(-0.5 * hidden * hidden) * (1.0 / math.sqrt(2.0 * math.pi)))
    return hidden * share, slope


def head_stack(block, heads, rows):
    size = 128 // heads
    lane = lax.broadcasted_iota(jnp.int32, (1, 128), 1)
    fill = jnp.zeros((rows - block.shape[0], 128), BF16)
    parts = []
    for head in range(heads):
        own = ((lane >= head * size) & (lane < (head + 1) * size)).astype(BF16)
        parts += [block * own, fill]
    return jnp.concatenate(parts, axis=0)


def head_unstack(stack, heads, rows, count):
    size = 128 // heads
    lane = lax.broadcasted_iota(jnp.int32, (1, 128), 1)
    total = None
    for head in range(heads):
        own = ((lane >= head * size) & (lane < (head + 1) * size)).astype(F32)
        part = stack[head * rows : head * rows + count] * own
        total = part if total is None else total + part
    return total


def attend_group(query, key, value, bias, heads, scale, shares_out):
    rows = bias.shape[1]
    scores = dot_t(query, head_stack(key, heads, rows))
    parts = []
    for head in range(heads):
        s = scores[:, head * rows : (head + 1) * rows] * scale + bias
        powers = jnp.exp(s - jnp.max(s, axis=-1, keepdims=True))
        parts.append(powers / jnp.sum(powers, axis=-1, keepdims=True))
    shares = jnp.concatenate(parts, axis=1)
    shares_out[...] = shares
    return dot(low(shares), head_stack(value, heads, rows))


def attend_group_back(query, key, value, d_out, shares, heads, scale, rows):
    count = key.shape[0]
    d_shares = dot_t(d_out, head_stack(value, heads, rows))
    parts = []
    for head in range(heads):
        cut = slice(head * rows, (head + 1) * rows)
        p, dp = shares[:, cut], d_shares[:, cut]
        parts.append(low(p * (dp - jnp.sum(dp * p, axis=-1, keepdims=True))))
    d_scores = jnp.concatenate(parts, axis=1)
    d_query = dot(d_scores, head_stack(key, heads, rows)) * scale
    d_key = head_unstack(t_dot(d_scores, query), heads, rows, count) * scale
    d_value = head_unstack(t_dot(low(shares), d_out), heads, rows, count)
    return d_query, d_key, d_value


def widen(values, pads):
    return jnp.concatenate(
        [low(dot(values[:, :384], pads)), low(dot(values[:, 384:], pads))], axis=1
    )


def narrow(values, pads):
    return jnp.concatenate(
        [low(dot_t(values[:, :512], pads)), low(dot_t(values[:, 512:], pads))], axis=1
    )


def narrow_wide(values, pads):
    high = low(values)
    rest = low(values - high.astype(F32))
    return jnp.concatenate(
        [
            dot_t(high[:, :512], pads) + dot_t(rest[:, :512], pads),
            dot_t(high[:, 512:], pads) + dot_t(rest[:, 512:], pads),
        ],
        axis=1,
    )


PARTS = (6, 4, 8)


def small_rows():
    plan, at = [], 0
    for family, (lead, part) in enumerate(COUNTS):
        for value in range(lead * part):
            if part >= 16:
                plan.append((2, value // 8 + (3 if family == 6 else 0), value % 8, at))
            else:
                first = 2 if family == 1 else (0, 0, 0, 0, 2, 4)[family]
                kind = 0 if family < 2 else 1
                plan.append((kind, first + value // part, value % part, at))
            at += 1
    return plan


def strewn(kind, value):
    part = PARTS[kind]
    device = lax.broadcasted_iota(jnp.int32, (128, 128 * part), 0)
    column = lax.broadcasted_iota(jnp.int32, (128, 128 * part), 1)
    return (column == part * device + value).astype(BF16)


def small_in(columns, rows_ref, enc_ref, enc_up_ref, dec_ref, dec_up_ref):
    line = lax.broadcasted_iota(jnp.int32, (1024, 128), 0)
    device = lax.broadcasted_iota(jnp.int32, (1024, 128), 1)
    table = t_dot(columns, (line == 8 * device + 6).astype(BF16))
    rows_ref[...] = jnp.zeros_like(rows_ref)
    for kind, row, value, place in small_rows():
        rows_ref[kind, value, row : row + 1, :] = table[place : place + 1]
    whole = []
    for kind, part in enumerate(PARTS):
        total = None
        for value in range(part):
            term = dot(low(rows_ref[kind, value]), strewn(kind, value))
            total = term if total is None else total + term
        whole.append(total)
    enc_ref[...] = whole[0][:8]
    dec_ref[...] = whole[1]
    for group in range(3):
        enc_up_ref[:, 1024 * group : 1024 * group + 1024] = whole[2][group : group + 1]
    for group in range(2):
        dec_up_ref[:, 1024 * group : 1024 * group + 1024] = whole[2][3 + group : 4 + group]


def small_out(enc, enc_up, dec, dec_up, table_ref):
    ups = [enc_up[:, 1024 * g : 1024 * g + 1024] for g in range(3)]
    ups += [dec_up[:, 1024 * g : 1024 * g + 1024] for g in range(2)]
    ups += [jnp.zeros((3, 1024), F32)]
    whole = (low(enc), low(dec), low(jnp.concatenate(ups, axis=0)))
    parts = [
        [dot_t(whole[kind], strewn(kind, value)) for value in range(part)]
        for kind, part in enumerate(PARTS)
    ]
    for kind, row, value, place in small_rows():
        table_ref[place : place + 1, :] = parts[kind][value][row : row + 1]


def enc_forward_kernel(
    whole, x_ref, bias_ref, pads_ref,
    enc_ref, enc_up_ref, dec_ref, dec_up_ref, embedded_ref, rows_ref, proj3_ref, shares_ref,
    middle_ref, slope_ref, small_ref, w_qkv, w_proj, w_up, w_emb, w_down, sems,
):
    copies = [
        pltpu.make_async_copy(whole.at[:, pl.ds(at, ref.shape[1])], ref, sems.at[i])
        for i, (at, ref) in enumerate(
            ((0, w_qkv), (C_PROJ, w_proj), (C_UP, w_up), (C_DOWN, w_down), (C_EMB, w_emb))
        )
    ]
    for copy in copies:
        copy.start()
    pads = pads_ref[...]
    x = x_ref[...].astype(F32)
    unit, _ = norm_parts(x)
    copies[0].wait()
    small_in(w_qkv[:, :128], small_ref, enc_ref, enc_up_ref, dec_ref, dec_up_ref)
    h1 = low(unit * enc_ref[0:1] + enc_ref[2:3])
    rows_ref[:, 4608:5376] = h1
    wide = widen(h1, pads)
    for third in range(3):
        cut = slice(768 * third, 768 * third + 768)
        part = dot(wide, w_qkv[:, cut])
        if third != 1:
            part = part + (enc_ref[4:5] if third == 0 else enc_ref[5:6])
        proj3_ref[:, cut] = low(part)
    bias = bias_ref[...]
    for group in range(6):
        cuts = [slice(768 * i + 128 * group, 768 * i + 128 * group + 128) for i in range(3)]
        out = attend_group(
            proj3_ref[:, cuts[0]], proj3_ref[:, cuts[1]], proj3_ref[:, cuts[2]],
            bias, 2, 0.125, shares_ref.at[group],
        )
        rows_ref[:, 5376 + 128 * group : 5504 + 128 * group] = low(out)
    copies[1].wait()
    middle = x + dot(widen(rows_ref[:, 5376:], pads), w_proj[...]) + enc_ref[6:7]
    middle_ref[...] = middle
    unit, _ = norm_parts(middle)
    h2 = low(unit * enc_ref[1:2] + enc_ref[3:4])
    rows_ref[:, 3840:4608] = h2
    wide = widen(h2, pads)
    copies[2].wait()

    @pl.loop(0, 6)
    def _(tile):
        cut = pl.ds(pl.multiple_of(tile * 512, 512), 512)
        value, slope = gelu_pair(dot(wide, w_up[:, cut]) + enc_up_ref[:, cut])
        rows_ref[:, cut] = low(value)
        slope_ref[:, cut] = slope

    copies[3].wait()
    out = middle + enc_ref[7:8]
    for group in range(3):
        out = out + dot(
            rows_ref[:, 1024 * group : 1024 * group + 1024],
            w_down[:, 768 * group : 768 * group + 768],
        )
    encoded = low(out)
    rows_ref[:, 3072:3840] = encoded
    copies[4].wait()
    embedded_ref[...] = low(dot(widen(encoded, pads), w_emb[...]) + dec_ref[0:1])


VMEM = pl.BlockSpec(memory_space=pltpu.VMEM)
ANY = pl.BlockSpec(memory_space=pl.ANY)


def shape(dims, kind):
    return jax.ShapeDtypeStruct(dims, kind)


def in_hbm(array):
    return pltpu.with_memory_space_constraint(array, pltpu.HBM)


def params(limit):
    return pltpu.CompilerParams(vmem_limit_bytes=limit * MIB)


def enc_forward(whole, x, bias, pads):
    outs = (
        pltpu.HBM((8, 768), F32),
        pltpu.HBM((1, 3072), F32),
        pltpu.HBM((16, 512), F32),
        pltpu.HBM((1, 2048), F32),
        pltpu.HBM((96, 512), BF16),
        pltpu.HBM((96, 6144), BF16),
        pltpu.HBM((96, 2304), BF16),
        pltpu.HBM((6, 96, 256), F32),
        pltpu.HBM((96, 768), F32),
        pltpu.HBM((96, 3072), F32),
    )
    return pl.pallas_call(
        enc_forward_kernel,
        in_specs=[ANY] + [VMEM] * 3,
        out_specs=[VMEM] * len(outs),
        out_shape=outs,
        scratch_shapes=[
            pltpu.VMEM((3, 8, 16, 128), F32),
            pltpu.VMEM((1024, 2304), BF16),
            pltpu.VMEM((1024, 768), BF16),
            pltpu.VMEM((1024, 3072), BF16),
            pltpu.VMEM((1024, 512), BF16),
            pltpu.VMEM((1024, 2304), BF16),
            pltpu.SemaphoreType.DMA((5,)),
        ],
        compiler_params=params(36),
        cost_estimate=pl.CostEstimate(flops=10**4, bytes_accessed=10**3, transcendentals=0),
        name="enc_forward",
    )(*[in_hbm(a) for a in (whole, x, bias, pads)])


def sides(rows, side, mine_ref, theirs_ref):
    half = rows.shape[1] // 2
    mine_ref[...] = jnp.where(side == 0, rows[:, :half], rows[:, half:])
    theirs_ref[...] = jnp.where(side == 0, rows[:, half:], rows[:, :half])


DEC_SCALE = 1.0 / math.sqrt(32)


def dec_kernel(
    whole, embedded_ref, picker_ref, picker_t_ref, masked_ref, table_ref, bias_ref,
    pull_ref, low_ref, high_ref, pads_ref, dec_ref, dec_up_ref, side_ref,
    mine_ref, theirs_ref, back_ref, d_small_ref, d_up_small_ref, rows_ref,
    w_z, w_down, w_emb, w_lo, w_hi, start_ref, proj3_ref, shares_ref, middle_ref, slope_ref,
    d_att_ref, d_p3_ref, sems,
):
    attended_ref, d_hid_ref = rows_ref.at[:, pl.ds(512, 512)], rows_ref.at[:, pl.ds(3584, 2048)]
    activated_ref = rows_ref.at[:, pl.ds(5632, 2048)]
    copies = [
        pltpu.make_async_copy(whole.at[:, pl.ds(at, ref.shape[1])], ref, sems.at[i])
        for i, (at, ref) in enumerate(((C_Z, w_z), (C_DDOWN, w_down), (C_EMB, w_emb)))
    ]
    for copy in copies:
        copy.start()
    gain_1, gain_2 = dec_ref[2:3], dec_ref[3:4]
    start = dot(picker_ref[...], embedded_ref[...]) + masked_ref[...] * dec_ref[1:2] + table_ref[...]
    start_ref[...] = start
    unit, _ = norm_parts(start)
    h1 = low(unit * gain_1 + dec_ref[4:5])
    rows_ref[:, :512] = h1
    copies[0].wait()

    @pl.loop(0, 4)
    def _(block):
        into = pl.ds(pl.multiple_of(block * 128, 128), 128)
        source = pl.ds(pl.multiple_of(block * 256, 256), 256)
        for half in range(2):
            cut = slice(1024 * half, 1024 * half + 1024)
            rows = w_z[source, cut]
            w_lo[into, cut] = low(dot(low_ref[...], rows))
            w_hi[into, cut] = low(dot(high_ref[...], rows))

    for third in range(3):
        cut = slice(512 * third, 512 * third + 512)
        part = dot(h1, w_lo[:, cut])
        if third != 1:
            part = part + (dec_ref[6:7] if third == 0 else dec_ref[7:8])
        proj3_ref[:, cut] = low(part)

    @pl.loop(0, 8)
    def _(step):
        pack, group = step // 4, step % 4
        rows = pl.ds(pl.multiple_of(pack * 192, 192), 192)
        cuts = [pl.ds(pl.multiple_of(512 * i + 128 * group, 128), 128) for i in range(3)]
        out = attend_group(
            proj3_ref[rows, cuts[0]], proj3_ref[rows, cuts[1]], proj3_ref[rows, cuts[2]],
            bias_ref[pack], 4, DEC_SCALE, shares_ref.at[step],
        )
        attended_ref[rows, cuts[0]] = low(out)

    middle = start + dot(attended_ref[...], w_lo[:, 1536:]) + dec_ref[8:9]
    middle_ref[...] = middle
    unit_2, rstd_2 = norm_parts(middle)
    h2 = low(unit_2 * gain_2 + dec_ref[5:6])
    rows_ref[:, 1024:1536] = h2

    @pl.loop(0, 4)
    def _(tile):
        cut = pl.ds(pl.multiple_of(tile * 512, 512), 512)
        value, slope = gelu_pair(dot(h2, w_hi[:, cut]) + dec_up_ref[:, cut])
        activated_ref[:, cut] = low(value)
        slope_ref[:, cut] = slope

    copies[1].wait()
    out = middle + dec_ref[9:10]
    for group in range(2):
        out = out + dot(
            activated_ref[:, 1024 * group : 1024 * group + 1024],
            w_down[:, 512 * group : 512 * group + 512],
        )
    sides(low(out), side_ref[0], mine_ref, theirs_ref)

    g_low = pull_ref[...]
    for tile in range(4):
        group, rows = tile // 2, slice(512 * (tile % 2), 512 * (tile % 2) + 512)
        cut = slice(512 * tile, 512 * tile + 512)
        d_hid = dot_t(g_low, w_down[rows, 512 * group : 512 * group + 512]) * slope_ref[:, cut]
        d_up_small_ref[:, cut] = col_sum(d_hid)
        d_hid_ref[:, cut] = low(d_hid)
    d_h2 = dot_t(d_hid_ref[...], w_hi[...])
    part, d_gain_2, d_shift_2 = norm_back(d_h2, unit_2, rstd_2, gain_2)
    g = g_low.astype(F32)
    d_mid = g + part
    d_mid_low = low(d_mid)
    d_att = low(dot_t(d_mid_low, w_lo[:, 1536:]))
    d_small_ref[...] = jnp.zeros_like(d_small_ref)
    d_small_ref[3:4] = d_gain_2
    d_small_ref[5:6] = d_shift_2
    d_small_ref[8:9] = col_sum(d_mid)
    d_small_ref[9:10] = col_sum(g)
    rows_ref[:, 3072:3584] = d_mid_low
    middle_ref[...] = d_mid
    d_att_ref[...] = d_att

    @pl.loop(0, 8)
    def _(step):
        pack, group = step // 4, step % 4
        rows = pl.ds(pl.multiple_of(pack * 192, 192), 192)
        cuts = [pl.ds(pl.multiple_of(512 * i + 128 * group, 128), 128) for i in range(3)]
        parts = attend_group_back(
            proj3_ref[rows, cuts[0]], proj3_ref[rows, cuts[1]], proj3_ref[rows, cuts[2]],
            d_att_ref[rows, cuts[0]], shares_ref[step], 4, DEC_SCALE, 256,
        )
        for cut, part in zip(cuts, parts):
            d_p3_ref[rows, cut] = part

    d_small_ref[6:7] = col_sum(d_p3_ref[:, :512])
    d_small_ref[7:8] = col_sum(d_p3_ref[:, 1024:])
    d_p3 = low(d_p3_ref[...])
    rows_ref[:, 1536:3072] = d_p3
    d_h1 = dot_t(d_p3, w_lo[:, :1536])
    unit, rstd = norm_parts(start_ref[...])
    part, d_gain_1, d_shift_1 = norm_back(d_h1, unit, rstd, gain_1)
    d_start = middle_ref[...] + part
    d_small_ref[2:3] = d_gain_1
    d_small_ref[4:5] = d_shift_1
    d_small_ref[1:2] = col_sum(masked_ref[...] * d_start)
    d_embedded = dot(picker_t_ref[...], low(d_start))
    d_small_ref[0:1] = col_sum(d_embedded)
    d_embedded = low(d_embedded)
    back_ref[:, 768:] = d_embedded
    copies[2].wait()
    back_ref[:, :768] = narrow(low(dot_t(d_embedded, w_emb[...])), pads_ref[...])


def decoder(whole, embedded, picker, picker_t, masked, table, bias, pull, spread, pads, dec_vec, dec_up, side):
    outs = (
        pltpu.HBM((384, 256), BF16),
        pltpu.HBM((384, 256), BF16),
        pltpu.HBM((96, 1280), BF16),
        pltpu.HBM((16, 512), F32),
        pltpu.HBM((1, 2048), F32),
        pltpu.HBM((384, 7680), BF16),
    )
    return pl.pallas_call(
        dec_kernel,
        in_specs=[ANY] + [VMEM] * 12 + [pl.BlockSpec(memory_space=pltpu.SMEM)],
        out_specs=[VMEM] * 6,
        out_shape=outs,
        scratch_shapes=[
            pltpu.VMEM((1024, 2048), BF16),
            pltpu.VMEM((1024, 1024), BF16),
            pltpu.VMEM((1024, 512), BF16),
            pltpu.VMEM((512, 2048), BF16),
            pltpu.VMEM((512, 2048), BF16),
            pltpu.VMEM((384, 512), F32),
            pltpu.VMEM((384, 1536), BF16),
            pltpu.VMEM((8, 192, 1024), F32),
            pltpu.VMEM((384, 512), F32),
            pltpu.VMEM((384, 2048), F32),
            pltpu.VMEM((384, 512), BF16),
            pltpu.VMEM((384, 1536), F32),
            pltpu.SemaphoreType.DMA((3,)),
        ],
        compiler_params=params(42),
        cost_estimate=pl.CostEstimate(flops=10**4, bytes_accessed=10**3, transcendentals=0),
        name="decoder",
    )(*[in_hbm(a) for a in (whole, embedded, picker, picker_t, masked, table, bias, pull, *spread, pads, dec_vec, dec_up)], side)


def enc_mlp_back_kernel(
    whole, back_ref, middle_ref, slope_ref, pads_ref, enc_ref,
    d_middle_ref, d_small_ref, d_up_small_ref, rows_ref,
    w_up, w_down, sems,
):
    copies = [
        pltpu.make_async_copy(whole.at[:, pl.ds(at, ref.shape[1])], ref, sems.at[i])
        for i, (at, ref) in enumerate(((C_DOWN, w_down), (C_UP, w_up)))
    ]
    for copy in copies:
        copy.start()
    pads = pads_ref[...]
    g_low = back_ref[:, :768]
    g = g_low.astype(F32)
    unit, rstd = norm_parts(middle_ref[...])
    copies[0].wait()
    for group in range(3):
        cut = slice(1024 * group, 1024 * group + 1024)
        d_hid = dot_t(g_low, w_down[:, 768 * group : 768 * group + 768]) * slope_ref[:, cut]
        d_up_small_ref[:, cut] = col_sum(d_hid)
        rows_ref[:, cut] = low(d_hid)
    copies[1].wait()
    d_h2 = narrow_wide(dot_t(rows_ref[...], w_up[...]), pads)
    part, d_gain, d_shift = norm_back(d_h2, unit, rstd, enc_ref[1:2])
    d_middle = g + part
    d_middle_ref[...] = d_middle
    d_small_ref[...] = jnp.zeros_like(d_small_ref)
    d_small_ref[1:2] = d_gain
    d_small_ref[3:4] = d_shift
    d_small_ref[6:7] = col_sum(d_middle)
    d_small_ref[7:8] = col_sum(g)


def enc_mlp_back(whole, back, middle, slope, pads, enc_vec):
    outs = (
        pltpu.HBM((96, 768), F32),
        pltpu.HBM((8, 768), F32),
        pltpu.HBM((1, 3072), F32),
        pltpu.HBM((96, 3072), BF16),
    )
    return pl.pallas_call(
        enc_mlp_back_kernel,
        in_specs=[ANY] + [VMEM] * 5,
        out_specs=[VMEM] * 4,
        out_shape=outs,
        scratch_shapes=[
            pltpu.VMEM((1024, 3072), BF16),
            pltpu.VMEM((1024, 2304), BF16),
            pltpu.SemaphoreType.DMA((2,)),
        ],
        compiler_params=params(20),
        cost_estimate=pl.CostEstimate(flops=10**4, bytes_accessed=10**3, transcendentals=0),
        name="enc_mlp_back",
    )(*[in_hbm(a) for a in (whole, back, middle, slope, pads, enc_vec)])


def enc_att_back_kernel(
    whole, d_middle_ref, proj3_ref, shares_ref, pads_ref,
    rows_ref, d_p3_ref, w_proj, sems,
):
    copy = pltpu.make_async_copy(whole.at[:, pl.ds(C_PROJ, 768)], w_proj, sems.at[0])
    copy.start()
    pads = pads_ref[...]
    d_mid_low = low(d_middle_ref[...])
    rows_ref[:, 2304:] = d_mid_low
    copy.wait()
    d_att = narrow(low(dot_t(d_mid_low, w_proj[...])), pads)
    for group in range(6):
        cuts = [slice(768 * i + 128 * group, 768 * i + 128 * group + 128) for i in range(3)]
        parts = attend_group_back(
            proj3_ref[:, cuts[0]], proj3_ref[:, cuts[1]], proj3_ref[:, cuts[2]],
            d_att[:, cuts[0]], shares_ref[group], 2, 0.125, 128,
        )
        for cut, part in zip(cuts, parts):
            d_p3_ref[:, cut] = part
            rows_ref[:, cut] = low(part)


def enc_att_back(whole, d_middle, proj3, shares, pads):
    return pl.pallas_call(
        enc_att_back_kernel,
        in_specs=[ANY] + [VMEM] * 4,
        out_specs=[VMEM] * 2,
        out_shape=(pltpu.HBM((96, 3072), BF16), pltpu.HBM((96, 2304), F32)),
        scratch_shapes=[
            pltpu.VMEM((1024, 768), BF16),
            pltpu.SemaphoreType.DMA((1,)),
        ],
        compiler_params=params(16),
        name="enc_att_back",
    )(*[in_hbm(a) for a in (whole, d_middle, proj3, shares, pads)])


def enc_in_back_kernel(
    whole, d_middle_ref, d_p3_ref, x_ref, pads_ref, enc_ref, d_enc_ref, d_enc_up_ref, d_dec_ref,
    d_dec_up_ref, side_ref,
    mine_ref, theirs_ref, small_ref, w_qkv, table_ref, sems,
):
    copy = pltpu.make_async_copy(whole.at[:, pl.ds(0, 2304)], w_qkv, sems.at[0])
    copy.start()
    unit, rstd = norm_parts(x_ref[...].astype(F32))
    row = lax.broadcasted_iota(jnp.int32, (8, 768), 0)
    d_enc = d_enc_ref[...]
    copy.wait()
    d_h1 = narrow_wide(dot_t(low(d_p3_ref[...]), w_qkv[...]), pads_ref[...])
    part, d_gain, d_shift = norm_back(d_h1, unit, rstd, enc_ref[0:1])
    sides(low(d_middle_ref[...] + part), side_ref[0], mine_ref, theirs_ref)
    for line, vector in (
        (0, d_gain),
        (2, d_shift),
        (4, col_sum(d_p3_ref[:, :768])),
        (5, col_sum(d_p3_ref[:, 1536:])),
    ):
        d_enc = d_enc + jnp.where(row == line, vector, 0.0)
    small_out(
        d_enc, d_enc_up_ref[...], d_dec_ref[...], d_dec_up_ref[...], table_ref
    )
    small_ref[...] = low(table_ref[...])


def enc_in_back(whole, d_middle, d_p3, x, pads, enc_vec, d_enc, d_enc_up, d_dec, d_dec_up, side):
    operands = (whole, d_middle, d_p3, x, pads, enc_vec, d_enc, d_enc_up, d_dec, d_dec_up)
    return pl.pallas_call(
        enc_in_back_kernel,
        in_specs=[ANY] + [VMEM] * 9 + [pl.BlockSpec(memory_space=pltpu.SMEM)],
        out_specs=[VMEM] * 3,
        out_shape=(
            pltpu.HBM((96, 384), BF16),
            pltpu.HBM((96, 384), BF16),
            pltpu.HBM((128, 128), BF16),
        ),
        scratch_shapes=[
            pltpu.VMEM((1024, 2304), BF16),
            pltpu.VMEM((128, 128), F32),
            pltpu.SemaphoreType.DMA((1,)),
        ],
        compiler_params=params(24),
        name="enc_in_back",
    )(*[in_hbm(a) for a in operands], side)


def widen_t(values, pads_t):
    return jnp.concatenate(
        [low(dot_t(pads_t, values[:, :384])), low(dot_t(pads_t, values[:, 384:]))], axis=0
    )


def spread_t(values, rows_t):
    return jnp.concatenate(
        [low(dot_t(rows_t, values[:, 128 * i : 128 * i + 128])) for i in range(4)], axis=0
    )


def two(own, other, cut):
    return jnp.concatenate([own[:, cut], other[:, cut]], axis=0)


def chunk_copies(stage, place, splits, outs, sems):
    copies = []
    for split, (start, width, first) in enumerate(splits):
        send, keep = outs[2 * split], outs[2 * split + 1]
        for slot, (ref, flips) in enumerate(((send, (first, 2)), (keep, (0, 4 - first)))):
            for line, turn in enumerate(flips):
                copies.append(
                    pltpu.make_async_copy(
                        stage.at[:, place ^ turn, :, pl.ds(start, width)],
                        ref.at[line],
                        sems.at[4 * split + 2 * slot + line],
                    )
                )
    return copies


Y_SPLITS = ((0, 1280, 1), (1280, 1280, 3))
Z_SPLITS = ((0, 768, 1), (768, 768, 3))


def load_rows(sources, start, width, into, sems, at):
    count = sources[0].shape[0]
    return [
        pltpu.make_async_copy(
            source.at[:, pl.ds(start, width)],
            into.at[pl.ds(count * i, count), :],
            sems.at[at + i],
        )
        for i, source in enumerate(sources)
    ]


def grad_s_kernel(
    place_ref, enc_ref, enc_o_ref, m_ref, m_o_ref, pull_ref, pull_o_ref, pads_t_ref, dec, dec_o,
    sums, stage, sems, activated, load_sems,
):
    core = place_ref[3]
    loads = load_rows((dec, dec_o), 5632, 2048, activated, load_sems, 0)
    for load in loads:
        load.start()
    for group in range(3):
        right = two(m_ref, m_o_ref, pl.ds(pl.multiple_of(384 * core, 128), 384))
        grad = low(t_dot(two(enc_ref, enc_o_ref, pl.ds(1024 * group, 1024)), right))
        stage[:, :, :, 384 * group : 384 * group + 384] = grad.reshape(4, 4, 64, 384)
    right = two(m_ref, m_o_ref, pl.ds(pl.multiple_of(768 + 256 * core, 128), 256))
    wide = widen_t(two(enc_ref, enc_o_ref, pl.ds(3072, 768)), pads_t_ref[...])
    stage[:, :, :, 1152:1408] = low(dot(wide, right)).reshape(4, 4, 64, 256)
    right = two(pull_ref, pull_o_ref, pl.ds(pl.multiple_of(256 * core, 128), 256))
    for load in loads:
        load.wait()
    for group in range(2):
        grad = low(t_dot(activated[:, 1024 * group : 1024 * group + 1024], right))
        stage[:, :, :, 1408 + 256 * group : 1664 + 256 * group] = grad.reshape(4, 4, 64, 256)
    copies = [
        pltpu.make_async_copy(stage.at[:, z], sums.at[z], sems.at[z]) for z in range(4)
    ]
    for copy in copies:
        copy.start()
    for copy in copies:
        copy.wait()


def grad_y_kernel(
    place_ref, enc_ref, enc_o_ref, m_ref, m_o_ref, pads_t_ref, low_t_ref, high_t_ref, dec, dec_o,
    send_p, keep_p, send_q, keep_q, stage, sems, lefts, rights, load_sems,
):
    core = place_ref[3]
    half = pl.multiple_of(512 * core, 128)
    second = pl.multiple_of(1024 + 512 * core, 128)
    loads = []
    for i, (start, into) in enumerate(
        (
            (1024, lefts.at[0]),
            (0, lefts.at[1]),
            (1536 + half, rights.at[0]),
            (3584 + half, rights.at[1]),
            (half, lefts.at[2]),
            (1536 + second, rights.at[2]),
            (3584 + second, rights.at[3]),
        )
    ):
        loads += load_rows((dec, dec_o), start, 512, into, load_sems, 2 * i)
    for load in loads:
        load.start()
    copies = chunk_copies(stage, place_ref[1], Y_SPLITS, (send_p, keep_p, send_q, keep_q), sems)
    wide = widen_t(two(enc_ref, enc_o_ref, pl.ds(3840, 768)), pads_t_ref[...])
    for tile in range(3):
        cut = pl.ds(pl.multiple_of(1536 * core + 512 * tile, 128), 512)
        stage[0, :, :, 512 * tile : 512 * tile + 512] = low(
            dot(wide, two(m_ref, m_o_ref, cut))
        ).reshape(4, 256, 512)
    for copy in copies[:4]:
        copy.start()
    low_t = low_t_ref[...]
    for load in loads[:8]:
        load.wait()
    raised = spread_t(lefts[0], high_t_ref[...])
    for tile in range(2):
        if tile == 1:
            for load in loads[8:]:
                load.wait()
        grad = dot(spread_t(lefts[1 + tile], low_t), rights[2 * tile])
        grad = grad + dot(raised, rights[2 * tile + 1])
        stage[0, :, :, 1536 + 512 * tile : 2048 + 512 * tile] = low(grad).reshape(4, 256, 512)
    for copy in copies[4:]:
        copy.start()
    for copy in copies:
        copy.wait()


def grad_z_kernel(
    place_ref, enc_ref, enc_o_ref, rows_ref, rows_o_ref, small_ref, pads_t_ref,
    send_p, keep_p, send_q, keep_q, stage, sems,
):
    core = place_ref[3]
    copies = chunk_copies(stage, place_ref[0], Z_SPLITS, (send_p, keep_p, send_q, keep_q), sems)
    pads_t = pads_t_ref[...]
    line = lax.broadcasted_iota(jnp.int32, (1024, 128), 0)
    device = lax.broadcasted_iota(jnp.int32, (1024, 128), 1)
    small = dot_t((line == 8 * device + 6).astype(BF16), small_ref[...])
    for half, at in enumerate((0, pl.multiple_of(768 * core, 128))):
        left = widen_t(two(enc_ref, enc_o_ref, pl.ds(4608 + at, 768)), pads_t)
        cut = pl.ds(pl.multiple_of(1536 * core + 768 * half, 128), 768)
        grad = dot(left, two(rows_ref, rows_o_ref, cut))
        stage[:, :, :, 768 * half : 768 * half + 768] = low(grad).reshape(16, 4, 16, 768)
        if half == 0:
            stage[:, :, :, :128] = low(grad[:, :128] + small).reshape(16, 4, 16, 128)
        for copy in copies[4 * half : 4 * half + 4]:
            copy.start()
    for copy in copies:
        copy.wait()


def grad_call(kernel, name, staged, outs, place, small, large, scratch):
    return pl.pallas_call(
        kernel,
        in_specs=[pl.BlockSpec(memory_space=pltpu.SMEM)] + [VMEM] * len(small) + [ANY] * len(large),
        out_specs=[ANY] * len(outs),
        out_shape=[pltpu.HBM(dims, BF16) for dims in outs],
        scratch_shapes=[
            pltpu.VMEM(staged, BF16),
            pltpu.SemaphoreType.DMA((8,)),
            *scratch,
        ],
        compiler_params=params(22),
        cost_estimate=pl.CostEstimate(flops=10**4, bytes_accessed=10**3, transcendentals=0),
        name=name,
    )(place, *[in_hbm(a) for a in (*small, *large)])


def split_outs(before, splits):
    return [(2, before, 256 // before, width) for _, width, _ in splits for _ in range(2)]


def fold_kernel(keep_ref, got_ref, send_ref):
    send_ref[...] = low(keep_ref[0].astype(F32) + got_ref[0].astype(F32))


def fold(keep, got):
    _, rows, columns = keep.shape
    block = (1, rows // 2, columns)
    return pl.pallas_call(
        fold_kernel,
        grid=(2,),
        in_specs=[pl.BlockSpec(block, lambda i: (1, i, 0))] * 2,
        out_specs=pl.BlockSpec(block[1:], lambda i: (i, 0)),
        out_shape=shape((rows, columns), BF16),
        compiler_params=params(24),
        cost_estimate=pl.CostEstimate(flops=10**4, bytes_accessed=10**3, transcendentals=0),
        name="fold",
    )(keep, got)


def part_kernel(place_ref, *refs, axis, groups):
    place = place_ref[axis]
    outs = refs[sum(groups) :]
    for out, turn in zip(outs, (1, 3, 2, 0)):
        chunk = pl.ds((place + turn) % 4, 1)
        at = start = 0
        for count in groups:
            total = None
            for ref in refs[start : start + count]:
                term = (ref[0, :, chunk] if len(ref.shape) == 5 else ref[:, chunk]).astype(F32)
                total = term if total is None else total + term
            start += count
            before, _, after, columns = total.shape
            out[:, at : at + columns] = low(total).reshape(before * after, columns)
            at += columns


def parted(place, axis, before, groups):
    rows = groups[0][0].shape[-2]
    after = rows // (4 * before)
    operands, specs = [], []
    for array in (a for group in groups for a in group):
        columns = array.shape[-1]
        if array.ndim == 3:
            operands.append(array.reshape(2, before, 4, after, columns))
            specs.append(pl.BlockSpec((1, before, 4, after, columns), lambda i: (0, 0, 0, 0, 0)))
        else:
            operands.append(array.reshape(before, 4, after, columns))
            specs.append(VMEM)
    columns = sum(group[0].shape[-1] for group in groups)
    return pl.pallas_call(
        functools.partial(part_kernel, axis=axis, groups=tuple(len(g) for g in groups)),
        grid=(1,),
        in_specs=[pl.BlockSpec(memory_space=pltpu.SMEM)] + specs,
        out_specs=[VMEM] * 4,
        out_shape=[shape((rows // 4, columns), BF16)] * 4,
        compiler_params=params(24),
        cost_estimate=pl.CostEstimate(flops=10**4, bytes_accessed=10**3, transcendentals=0),
        name="parted",
    )(place, *operands)


def last_kernel(place_ref, *refs, groups):
    core = place_ref[3]
    own_ref, other_ref = refs[sum(groups) :]
    at = start = 0
    for count in groups:
        total = None
        for ref in refs[start : start + count]:
            term = ref[...].astype(F32)
            total = term if total is None else total + term
        start += count
        cut = slice(at, at + total.shape[1])
        own_ref[:, cut] = jnp.where(core == 0, total[:8], total[8:])
        other_ref[:, cut] = jnp.where(core == 0, total[8:], total[:8])
        at += total.shape[1]


def last(place, groups):
    columns = sum(group[0].shape[-1] for group in groups)
    operands = [a for group in groups for a in group]
    return pl.pallas_call(
        functools.partial(last_kernel, groups=tuple(len(g) for g in groups)),
        in_specs=[pl.BlockSpec(memory_space=pltpu.SMEM)] + [VMEM] * len(operands),
        out_specs=[VMEM] * 2,
        out_shape=[shape((8, columns), F32)] * 2,
        compiler_params=params(24),
        cost_estimate=pl.CostEstimate(flops=10**4, bytes_accessed=10**3, transcendentals=0),
        name="last",
    )(place, *operands)


def ungrouped(values, groups):
    width = 128 * groups
    line = lax.broadcasted_iota(jnp.int32, (width, width), 0)
    column = lax.broadcasted_iota(jnp.int32, (width, width), 1)
    natural = 8 * groups * ((line & 127) >> 3) + 8 * (line >> 7) + (line & 7)
    turn = (natural == column).astype(BF16)
    high = low(values)
    rest = low(values - high.astype(F32))
    parts = []
    for block in range(8):
        cuts = [slice(1024 * g + 128 * block, 1024 * g + 128 * block + 128) for g in range(groups)]
        both = [jnp.concatenate([v[:, cut] for cut in cuts], axis=1) for v in (high, rest)]
        parts.append(dot(both[0], turn) + dot(both[1], turn))
    return jnp.concatenate(parts, axis=1)


def shards_kernel(
    place_ref, own_ref, got_ref, enc_gains, enc_biases, enc_qkv, enc_proj, enc_up, enc_up_bias,
    enc_down, dec_fill, dec_embed, dec_gains, dec_biases, dec_qkv, dec_proj, dec_up, dec_up_bias,
    dec_down,
):
    core = place_ref[3]

    def halves(start, width):
        own, got = own_ref[:, start : start + width], got_ref[:, start : start + width]
        return jnp.where(core == 0, own, got), jnp.where(core == 0, got, own)

    for group in range(3):
        rows = slice(8 * group, 8 * group + 8)
        enc_down[rows, :384], enc_down[rows, 384:] = halves(384 * group, 384)
    a, b = halves(1152, 256)
    dec_embed[:, :256], dec_embed[:, 256:] = a[:6], b[:6]
    for group in range(2):
        rows = slice(8 * group, 8 * group + 8)
        dec_down[rows, :256], dec_down[rows, 256:] = halves(1408 + 256 * group, 256)
    enc_up[...] = ungrouped(jnp.concatenate(halves(3456, 1536), axis=1), 3)[:6]
    z_all = jnp.concatenate(halves(4992, 512) + halves(5504, 512), axis=1)
    dec_qkv[...] = z_all[:4, :1536]
    dec_proj[...] = z_all[:4, 1536:]
    dec_up[...] = ungrouped(z_all, 2)[4:]
    a, b = halves(1920, 1536)
    enc_qkv[:, :1536] = a[:6]
    enc_qkv[:, 1536:] = b[:6, :768]
    enc_proj[...] = b[:6, 768:]
    flat = a[6:7, :128] + b[6:7, :128]
    at = 0
    smalls = (enc_gains, enc_biases, enc_up_bias, dec_fill, dec_gains, dec_biases, dec_up_bias)
    for ref, (lead, part) in zip(smalls, COUNTS):
        for line in range(lead):
            ref[line : line + 1, :] = flat[:, at : at + part]
            at += part


def shards(place, own, got):
    dims = (
        (2, 6), (6, 6), (6, 2304), (6, 768), (6, 3072), (1, 24), (24, 768), (2, 4), (6, 512),
        (2, 4), (6, 4), (4, 1536), (4, 512), (4, 2048), (1, 16), (16, 512),
    )
    return pl.pallas_call(
        shards_kernel,
        in_specs=[pl.BlockSpec(memory_space=pltpu.SMEM)] + [VMEM] * 2,
        out_specs=[VMEM] * 16,
        out_shape=[shape(d, F32) for d in dims],
        compiler_params=params(24),
        cost_estimate=pl.CostEstimate(flops=10**4, bytes_accessed=10**3, transcendentals=0),
        name="shards",
    )(place, own, got)


def join_kernel(place_ref, dec_mine, dec_got, enc_mine, enc_got, decoded, x_grad):
    own_at = 2 * place_ref[4]
    for mine, got, out in ((dec_mine, dec_got, decoded), (enc_mine, enc_got, x_grad)):
        out[pl.ds(own_at, 2)] = mine[...]
        out[pl.ds(2 - own_at, 2)] = got[...]


def joined(place, *rows):
    return pl.pallas_call(
        join_kernel,
        in_specs=[pl.BlockSpec(memory_space=pltpu.SMEM)] + [VMEM] * 4,
        out_specs=[VMEM] * 2,
        out_shape=[pltpu.HBM((4, 192, 256), BF16), pltpu.HBM((4, 48, 384), BF16)],
        compiler_params=params(16),
        name="joined",
    )(place, *[in_hbm(a) for a in rows])


def pack_kernel(
    enc_gains, enc_biases, enc_qkv, enc_proj, enc_up, enc_up_bias, enc_down, dec_fill, dec_embed,
    dec_gains, dec_biases, dec_qkv, dec_proj, dec_up, dec_up_bias, dec_down, out,
):
    def rows(count, shift=0):
        line = lax.broadcasted_iota(jnp.int32, (8, count), 0)
        return (line == lax.broadcasted_iota(jnp.int32, (8, count), 1) + shift).astype(BF16)

    def group(start, places, source, groups):
        width = 128 * groups
        line = lax.broadcasted_iota(jnp.int32, (width, width), 0)
        column = lax.broadcasted_iota(jnp.int32, (width, width), 1)
        natural = 8 * groups * ((column & 127) >> 3) + 8 * (column >> 7) + (column & 7)
        turn = (natural == line).astype(BF16)
        for block in range(8):
            piece = low(dot(places, source[:, width * block : width * block + width]))
            piece = dot(piece, turn)
            for g in range(groups):
                at = start + 1024 * g + 128 * block
                yield at, piece[:, 128 * g : 128 * g + 128]

    smalls = (enc_gains, enc_biases, enc_up_bias, dec_fill, dec_gains, dec_biases, dec_up_bias)
    flat, at = jnp.zeros((1, 128), F32), 0
    for ref, (lead, part) in zip(smalls, COUNTS):
        values = ref[...]
        line = lax.broadcasted_iota(jnp.int32, (part, 128), 0)
        column = lax.broadcasted_iota(jnp.int32, (part, 128), 1)
        for i in range(lead):
            flat = flat + dot(values[i : i + 1], (line + at == column).astype(BF16))
            at += part
    six, four, raised = rows(6), rows(4), rows(4, 4)
    seventh = lax.broadcasted_iota(jnp.int32, (8, 128), 0) == 6
    out[:, :C_PROJ] = low(dot(six, enc_qkv[...]))
    out[:, :128] = low(dot(six, enc_qkv[:, :128]) + jnp.where(seventh, flat, 0.0))
    out[:, C_PROJ:C_UP] = low(dot(six, enc_proj[...]))
    for at, piece in group(C_UP, six, enc_up, 3):
        out[:, at : at + 128] = low(piece)
    out[:, C_EMB:C_DOWN] = low(dot(six, dec_embed[...]))
    for g in range(3):
        out[:, C_DOWN + 768 * g : C_DOWN + 768 * g + 768] = low(dot(rows(24, -8 * g), enc_down[...]))
    lower = (dec_qkv[:, :1024], jnp.concatenate([dec_qkv[:, 1024:], dec_proj[...]], axis=1))
    lower = [dot(four, values) for values in lower]
    for at, piece in group(0, raised, dec_up, 2):
        half, column = at // 1024, at % 1024
        piece = piece + lower[half][:, column : column + 128]
        out[:, C_Z + at : C_Z + at + 128] = low(piece)
    for g in range(2):
        out[:, C_DDOWN + 512 * g : C_DDOWN + 512 * g + 512] = low(dot(rows(16, -8 * g), dec_down[...]))


def pack(*weights):
    weights = [w[None] if w.ndim == 1 else w for w in weights]
    return pl.pallas_call(
        pack_kernel,
        in_specs=[VMEM] * 16,
        out_specs=VMEM,
        out_shape=pltpu.HBM((8, C_ALL), BF16),
        compiler_params=params(24),
        name="pack",
    )(*[in_hbm(w) for w in weights])


def position_table(offset, width):
    half = width // 2
    rates = jnp.exp(jnp.arange(half, dtype=F32) * (-math.log(10000.0) / half))
    angle = offset.astype(F32)[:, None] * rates[None, :]
    return jnp.concatenate([jnp.sin(angle), jnp.cos(angle)], axis=1)


def layout(length_row, order, visible):
    length = order.shape[0]
    ends = jnp.cumsum(length_row, dtype=jnp.int32)
    places = lax.broadcasted_iota(jnp.int32, (length, 1), 0)
    passed = places >= ends[None, :]
    segment = jnp.sum(passed.astype(jnp.int32), axis=1, dtype=jnp.int32)
    offset = places[:, 0] - jnp.sum(
        jnp.where(passed, length_row[None, :], 0), axis=1, dtype=jnp.int32
    )
    shown_pos = order[:visible]
    shown_seg = jnp.sum(
        (shown_pos[:, None] >= ends[None, :]).astype(jnp.int32), axis=1, dtype=jnp.int32
    )
    onehot = places == shown_pos[None, :]
    return (segment, offset, shown_seg, onehot)


def spread_rows(devices, rows, at):
    feature = lax.broadcasted_iota(jnp.int32, (devices * rows, devices * 8), 0)
    place = lax.broadcasted_iota(jnp.int32, (devices * rows, devices * 8), 1)
    return (8 * (feature // rows) + at + feature % rows == place).astype(BF16)


def plans(length_rows, orders):
    segment, offset, shown_seg, onehot = jax.vmap(lambda a, b: layout(a, b, 48))(
        length_rows, orders
    )
    pack = jnp.arange(2, dtype=jnp.int32)[:, None] * 16
    seen = (shown_seg + pack).reshape(96)
    seen_keys = jnp.concatenate([seen, jnp.full((32,), -1, jnp.int32)])
    enc_bias = jnp.where(seen[:, None] == seen_keys[None, :], 0.0, NEVER).astype(F32)
    keys = jnp.concatenate([segment, jnp.full((2, 64), -1, jnp.int32)], axis=1)
    dec_bias = jnp.where(segment[:, :, None] == keys[:, None, :], 0.0, NEVER).astype(F32)
    hot = onehot.astype(BF16)
    none = jnp.zeros((192, 48), BF16)
    picker = jnp.concatenate(
        [jnp.concatenate([hot[0], none], axis=1), jnp.concatenate([none, hot[1]], axis=1)], axis=0
    )
    masked = (1.0 - jnp.sum(onehot.astype(F32), axis=2)).reshape(-1, 1)
    table = position_table(offset.reshape(-1), 512)
    return enc_bias, dec_bias, picker, picker.T, masked, table


def place_of(device):
    return device // 2 % 4, device // 32, device // 8 % 4, device % 2


AXES = {"y": (32, 4), "z": (8, 4), "x": (2, 4), "c": (1, 2)}


def flipped(block, axis, turn):
    stride, size = AXES[axis]
    route = []
    for device in range(128):
        at = device // stride % size
        route.append((device, device + ((at ^ turn) - at) * stride))
    return lax.ppermute(block, BOTH, route)


def other_core(block):
    return flipped(block, "c", 1)


def first_sent(axis, outs):
    begun = []
    for split, first in enumerate((1, 3)):
        send, keep = [a.reshape(2, 256, a.shape[-1]) for a in outs[2 * split : 2 * split + 2]]
        begun.append((keep, flipped(send, axis, first)))
    return begun


def second_sent(axis, begun, before):
    groups = []
    for (keep, got), first in zip(begun, (1, 3)):
        onward = fold(after(keep, *before), got)
        groups.append((keep, got, flipped(onward, axis, 4 - first)))
        before = (onward,)
    return groups, before


def passed(block, axis, by):
    stride, size = AXES[axis]
    route = []
    for device in range(128):
        at = device // stride % size
        route.append((device, device + ((at + by) % size - at) * stride))
    return lax.ppermute(block, BOTH, route)


def summed(place, axis, before, groups, earlier):
    *sends, own = parted(after(place, *earlier), "xyz".index(axis), before, groups)
    return [(own, *[passed(send, axis, by) for send, by in zip(sends, (1, 3, 2))])], (own,)


def after(value, *others):
    return lax.optimization_barrier((value, *others))[0]


def on_device(
    x_vis, lengths, shuffle, enc_gains, enc_biases, enc_qkv, enc_proj, enc_up, enc_up_bias,
    enc_down, dec_fill, dec_embed, dec_gains, dec_biases, dec_qkv, dec_proj, dec_up, dec_up_bias,
    dec_down, cotangent,
):
    section = lax.axis_index("section")
    device = lax.axis_index(BOTH)
    x, y, z, core = place_of(device)
    shard = pack(
        enc_gains, enc_biases, enc_qkv, enc_proj, enc_up, enc_up_bias, enc_down, dec_fill,
        dec_embed, dec_gains, dec_biases, dec_qkv, dec_proj, dec_up, dec_up_bias, dec_down,
    )
    whole = lax.all_gather(shard, BOTH, axis=0, tiled=True)

    packs = 2

    def mine(rows):
        return lax.dynamic_slice_in_dim(rows, section * packs, packs, 0)[:, 0]

    x_rows = mine(x_vis).reshape(packs * 48, 768)
    pull = mine(cotangent).reshape(packs * 192, 512)
    enc_bias, dec_bias, picker, picker_t, masked, table = plans(mine(lengths), mine(shuffle))
    pads = spread_rows(64, 6, 0)
    low_rows, high_rows = spread_rows(32, 4, 0), spread_rows(32, 4, 4)
    spread = (low_rows, high_rows)
    pads_t, low_t, high_t = pads.T, low_rows.T, high_rows.T
    place = jnp.stack([x, y, z, core, section]).astype(jnp.int32)
    side = section.astype(jnp.int32).reshape(1)

    pull_o = other_core(pull)

    ready = (whole, x_rows, pull, pull_o, enc_bias, dec_bias, picker, picker_t, masked, table)
    ready = lax.optimization_barrier((*ready, pads, pads_t, low_t, high_t, *spread))
    whole, x_rows, pull, pull_o, enc_bias, dec_bias, picker, picker_t, masked, table = ready[:10]
    pads, pads_t, low_t, high_t, *spread = ready[10:]
    enc_vec, _, dec_vec, dec_up_vec, embedded, enc_rows, proj3, shares, middle, slope = enc_forward(
        whole, x_rows, enc_bias, pads
    )
    enc_rows_o = other_core(enc_rows)
    dec_mine, dec_theirs, back, d_dec, d_dec_up, dec_rows = decoder(
        whole, embedded, picker, picker_t, masked, table, dec_bias, pull, spread, pads, dec_vec,
        dec_up_vec, side,
    )
    back_o = other_core(back)
    dec_rows_o = other_core(after(dec_rows, enc_rows_o))
    d_middle, d_enc, d_enc_up, d_hid = enc_mlp_back(whole, back, middle, slope, pads, enc_vec)
    d_hid_o = other_core(d_hid)
    (sums_s,) = grad_call(
        grad_s_kernel, "grad_s", (4, 4, 64, 1920), [(4, 4, 64, 1920)], after(place, d_middle),
        (enc_rows, enc_rows_o, back, back_o, pull, pull_o, pads_t), (dec_rows, dec_rows_o),
        (pltpu.VMEM((768, 2048), BF16), pltpu.SemaphoreType.DMA((2,))),
    )
    att_rows, d_p3 = enc_att_back(whole, after(d_middle, sums_s), proj3, shares, pads)
    att_rows_o = other_core(att_rows)
    sums_y = grad_call(
        grad_y_kernel, "grad_y", (1, 4, 256, 2560), split_outs(1, Y_SPLITS), after(place, d_p3),
        (enc_rows, enc_rows_o, d_hid, d_hid_o, pads_t, low_t, high_t), (dec_rows, dec_rows_o),
        (
            pltpu.VMEM((3, 768, 512), BF16),
            pltpu.VMEM((4, 768, 512), BF16),
            pltpu.SemaphoreType.DMA((14,)),
        ),
    )
    enc_mine, enc_theirs, small = enc_in_back(
        whole, after(d_middle, *sums_y), d_p3, x_rows, pads, enc_vec, d_enc, d_enc_up, d_dec,
        d_dec_up, side,
    )
    sums_z = grad_call(
        grad_z_kernel, "grad_z", (16, 4, 16, 1536), split_outs(16, Z_SPLITS), place,
        (enc_rows, enc_rows_o, att_rows, att_rows_o, small, pads_t), (), (),
    )

    sums_s = lax.psum_scatter(
        sums_s.reshape(64, 16, 1920), "z", scatter_dimension=0, tiled=True
    ).reshape(256, 1920)
    sums_y = first_sent("y", sums_y)
    sums_z = first_sent("x", sums_z)
    sums_y, done = second_sent("y", sums_y, sums_z[0][:1])
    sums_s, done = summed(place, "x", 4, [(sums_s,)], done)
    sums_z, done = second_sent("x", sums_z, done)

    dec_got, enc_got = flipped(dec_theirs, "y", 2), flipped(enc_theirs, "y", 2)
    halves = [a.reshape(2, -1, a.shape[1]) for a in (dec_mine, dec_got, enc_mine, enc_got)]
    decoded, x_grad = joined(place, *halves)
    sums_y, done = summed(place, "x", 4, sums_y, done)
    sums_z, done = summed(place, "z", 4, sums_z, done)
    sums_sz, done = summed(place, "y", 1, sums_s + sums_z, (*done, decoded, x_grad))
    sums_y, done = summed(place, "z", 1, sums_y, done)
    own, other = last(place, sums_sz + sums_y)
    grads = shards(place, own, other_core(other))
    grads = [g[0] if g.shape[0] == 1 else g for g in grads]
    return (decoded[:, None], x_grad[:, None], *grads)


def solution(mesh):
    mesh = Mesh(mesh.devices.reshape(2, 2, 4, 4, 2), BOTH)
    rows = P(None, DP, None, None)
    ids = P(None, DP, None)
    wide = P(None, BOTH)
    tall = P(BOTH, None)
    flat = P(BOTH)
    in_specs = (rows, ids, ids, wide, wide, tall, tall, tall, flat, tall, wide, tall, wide, wide)
    in_specs += (tall, tall, tall, flat, tall, rows)
    out_rows = P(None, DP, None, "section")
    out_specs = (out_rows, out_rows, wide, wide, tall, tall, tall, flat, tall, wide, tall, wide)
    out_specs += (wide, tall, tall, tall, flat, tall)
    return jax.shard_map(
        on_device, mesh=mesh, in_specs=in_specs, out_specs=out_specs, check_vma=False
    )
```

```python
import functools
import math

import jax
import jax.numpy as jnp
from jax import lax
from jax.experimental import pallas as pl
from jax.experimental.pallas import tpu as pltpu
from jax.sharding import Mesh
from jax.sharding import PartitionSpec as P

H_ENC = 12
H_DEC = 16
DP = ("y_low", "z", "x", "core")
BOTH = ("section", *DP)
Y_AXIS = ("section", "y_low")
F32 = jnp.float32
BF16 = jnp.bfloat16
EPS = 1e-06
NEVER = -1e30
MIB = 1 << 20

C_PROJ = 2304
C_UP = 3072
C_EMB = 6144
C_DOWN = 6656
C_Z = 8960
C_DDOWN = 11008
C_ALL = 12032
COUNTS = ((2, 6), (6, 6), (1, 24), (2, 4), (2, 4), (6, 4), (1, 16))


def dot(left, right):
    return jnp.dot(left, right, preferred_element_type=F32)


def dot_t(left, right):
    return lax.dot_general(left, right, (((1,), (1,)), ((), ())), preferred_element_type=F32)


def t_dot(left, right):
    return lax.dot_general(left, right, (((0,), (0,)), ((), ())), preferred_element_type=F32)


def low(values):
    return values.astype(BF16)


def norm_parts(values):
    mean = jnp.mean(values, axis=-1, keepdims=True)
    centred = values - mean
    rstd = lax.rsqrt(jnp.mean(centred * centred, axis=-1, keepdims=True) + EPS)
    return centred * rstd, rstd


def norm_back(d_normed, unit, rstd, gain):
    scaled = d_normed * gain
    part = scaled - jnp.mean(scaled, axis=-1, keepdims=True)
    part = (part - unit * jnp.mean(scaled * unit, axis=-1, keepdims=True)) * rstd
    return part, col_sum(d_normed * unit), col_sum(d_normed)


def col_sum(values):
    return jnp.sum(values, axis=0, keepdims=True)


def gelu_pair(hidden):
    share = 0.5 + 0.5 * lax.erf(hidden * math.sqrt(0.5))
    slope = share + hidden * (jnp.exp(-0.5 * hidden * hidden) * (1.0 / math.sqrt(2.0 * math.pi)))
    return hidden * share, slope


def head_stack(block, heads, rows):
    size = 128 // heads
    lane = lax.broadcasted_iota(jnp.int32, (1, 128), 1)
    fill = jnp.zeros((rows - block.shape[0], 128), BF16)
    parts = []
    for head in range(heads):
        own = ((lane >= head * size) & (lane < (head + 1) * size)).astype(BF16)
        parts += [block * own, fill]
    return jnp.concatenate(parts, axis=0)


def head_unstack(stack, heads, rows, count):
    size = 128 // heads
    lane = lax.broadcasted_iota(jnp.int32, (1, 128), 1)
    total = None
    for head in range(heads):
        own = ((lane >= head * size) & (lane < (head + 1) * size)).astype(F32)
        part = stack[head * rows : head * rows + count] * own
        total = part if total is None else total + part
    return total


def attend_group(query, key, value, bias, heads, scale, shares_out):
    rows = bias.shape[1]
    scores = dot_t(query, head_stack(key, heads, rows))
    parts = []
    for head in range(heads):
        s = scores[:, head * rows : (head + 1) * rows] * scale + bias
        powers = jnp.exp(s - jnp.max(s, axis=-1, keepdims=True))
        parts.append(powers / jnp.sum(powers, axis=-1, keepdims=True))
    shares = jnp.concatenate(parts, axis=1)
    shares_out[...] = shares
    return dot(low(shares), head_stack(value, heads, rows))


def attend_group_back(query, key, value, d_out, shares, heads, scale, rows):
    count = key.shape[0]
    d_shares = dot_t(d_out, head_stack(value, heads, rows))
    parts = []
    for head in range(heads):
        cut = slice(head * rows, (head + 1) * rows)
        p, dp = shares[:, cut], d_shares[:, cut]
        parts.append(low(p * (dp - jnp.sum(dp * p, axis=-1, keepdims=True))))
    d_scores = jnp.concatenate(parts, axis=1)
    d_query = dot(d_scores, head_stack(key, heads, rows)) * scale
    d_key = head_unstack(t_dot(d_scores, query), heads, rows, count) * scale
    d_value = head_unstack(t_dot(low(shares), d_out), heads, rows, count)
    return d_query, d_key, d_value


def widen(values, pads):
    return jnp.concatenate(
        [low(dot(values[:, :384], pads)), low(dot(values[:, 384:], pads))], axis=1
    )


def narrow(values, pads):
    return jnp.concatenate(
        [low(dot_t(values[:, :512], pads)), low(dot_t(values[:, 512:], pads))], axis=1
    )


def narrow_wide(values, pads):
    high = low(values)
    rest = low(values - high.astype(F32))
    return jnp.concatenate(
        [
            dot_t(high[:, :512], pads) + dot_t(rest[:, :512], pads),
            dot_t(high[:, 512:], pads) + dot_t(rest[:, 512:], pads),
        ],
        axis=1,
    )


PARTS = (6, 4, 8)


def small_rows():
    plan, at = [], 0
    for family, (lead, part) in enumerate(COUNTS):
        for value in range(lead * part):
            if part >= 16:
                plan.append((2, value // 8 + (3 if family == 6 else 0), value % 8, at))
            else:
                first = 2 if family == 1 else (0, 0, 0, 0, 2, 4)[family]
                kind = 0 if family < 2 else 1
                plan.append((kind, first + value // part, value % part, at))
            at += 1
    return plan


def strewn(kind, value):
    part = PARTS[kind]
    device = lax.broadcasted_iota(jnp.int32, (128, 128 * part), 0)
    column = lax.broadcasted_iota(jnp.int32, (128, 128 * part), 1)
    return (column == part * device + value).astype(BF16)


def small_in(columns, rows_ref, enc_ref, enc_up_ref, dec_ref, dec_up_ref):
    line = lax.broadcasted_iota(jnp.int32, (1024, 128), 0)
    device = lax.broadcasted_iota(jnp.int32, (1024, 128), 1)
    table = t_dot(columns, (line == 8 * device + 6).astype(BF16))
    rows_ref[...] = jnp.zeros_like(rows_ref)
    for kind, row, value, place in small_rows():
        rows_ref[kind, value, row : row + 1, :] = table[place : place + 1]
    whole = []
    for kind, part in enumerate(PARTS):
        total = None
        for value in range(part):
            term = dot(low(rows_ref[kind, value]), strewn(kind, value))
            total = term if total is None else total + term
        whole.append(total)
    enc_ref[...] = whole[0][:8]
    dec_ref[...] = whole[1]
    for group in range(3):
        enc_up_ref[:, 1024 * group : 1024 * group + 1024] = whole[2][group : group + 1]
    for group in range(2):
        dec_up_ref[:, 1024 * group : 1024 * group + 1024] = whole[2][3 + group : 4 + group]


def small_out(enc, enc_up, dec, dec_up, table_ref):
    ups = [enc_up[:, 1024 * g : 1024 * g + 1024] for g in range(3)]
    ups += [dec_up[:, 1024 * g : 1024 * g + 1024] for g in range(2)]
    ups += [jnp.zeros((3, 1024), F32)]
    whole = (low(enc), low(dec), low(jnp.concatenate(ups, axis=0)))
    parts = [
        [dot_t(whole[kind], strewn(kind, value)) for value in range(part)]
        for kind, part in enumerate(PARTS)
    ]
    for kind, row, value, place in small_rows():
        table_ref[place : place + 1, :] = parts[kind][value][row : row + 1]


VMEM = pl.BlockSpec(memory_space=pltpu.VMEM)
ANY = pl.BlockSpec(memory_space=pl.ANY)


def shape(dims, kind):
    return jax.ShapeDtypeStruct(dims, kind)


def in_hbm(array):
    return pltpu.with_memory_space_constraint(array, pltpu.HBM)


def params(limit):
    return pltpu.CompilerParams(vmem_limit_bytes=limit * MIB)


def sides(rows, side, mine_ref, theirs_ref):
    half = rows.shape[1] // 2
    mine_ref[...] = jnp.where(side == 0, rows[:, :half], rows[:, half:])
    theirs_ref[...] = jnp.where(side == 0, rows[:, half:], rows[:, :half])


DEC_SCALE = 1.0 / math.sqrt(32)


def blocks_kernel(
    whole, x_ref, enc_bias_ref, pads_ref, picker_t_ref, table_ref, bias_ref, pull_ref, low_ref,
    high_ref, side_ref,
    enc_ref, mine_ref, theirs_ref, back_ref, d_small_ref, d_up_small_ref, enc_rows_out,
    enc_proj3_out, enc_shares_out, enc_middle_out, enc_slope_out, rows_out,
    enc_up_ref, dec_ref, dec_up_ref, small_ref, w_qkv, w_proj, w_up, w_emb, w_down,
    enc_rows, enc_proj3_ref, enc_shares_ref, enc_middle_ref, enc_slope_ref,
    rows_ref, w_lo, w_hi, start_ref, proj3_ref, shares_ref, middle_ref, slope_ref, d_att_ref,
    sems, out_sems,
):
    copies = [
        pltpu.make_async_copy(whole.at[:, pl.ds(at, ref.shape[1])], ref, sems.at[i])
        for i, (at, ref) in enumerate(
            ((0, w_qkv), (C_PROJ, w_proj), (C_UP, w_up), (C_DOWN, w_down), (C_EMB, w_emb))
        )
    ]
    for copy in copies:
        copy.start()
    pads = pads_ref[...]
    x = x_ref[...].astype(F32)
    unit, _ = norm_parts(x)
    copies[0].wait()
    small_in(w_qkv[:, :128], small_ref, enc_ref, enc_up_ref, dec_ref, dec_up_ref)
    h1 = low(unit * enc_ref[0:1] + enc_ref[2:3])
    enc_rows[:, 4608:5376] = h1
    wide = widen(h1, pads)
    for third in range(3):
        cut = slice(768 * third, 768 * third + 768)
        part = dot(wide, w_qkv[:, cut])
        if third != 1:
            part = part + (enc_ref[4:5] if third == 0 else enc_ref[5:6])
        enc_proj3_ref[:, cut] = low(part)
    bias = enc_bias_ref[...]
    for group in range(6):
        cuts = [slice(768 * i + 128 * group, 768 * i + 128 * group + 128) for i in range(3)]
        out = attend_group(
            enc_proj3_ref[:, cuts[0]], enc_proj3_ref[:, cuts[1]], enc_proj3_ref[:, cuts[2]],
            bias, 2, 0.125, enc_shares_ref.at[group],
        )
        enc_rows[:, 5376 + 128 * group : 5504 + 128 * group] = low(out)
    copies[1].wait()
    middle = x + dot(widen(enc_rows[:, 5376:], pads), w_proj[...]) + enc_ref[6:7]
    enc_middle_ref[...] = middle
    unit, _ = norm_parts(middle)
    h2 = low(unit * enc_ref[1:2] + enc_ref[3:4])
    enc_rows[:, 3840:4608] = h2
    wide = widen(h2, pads)
    copies[2].wait()

    @pl.loop(0, 6)
    def _(tile):
        cut = pl.ds(pl.multiple_of(tile * 512, 512), 512)
        value, slope = gelu_pair(dot(wide, w_up[:, cut]) + enc_up_ref[:, cut])
        enc_rows[:, cut] = low(value)
        enc_slope_ref[:, cut] = slope

    dec_weights = pltpu.make_async_copy(
        whole.at[:, pl.ds(C_Z, 3072)], w_up, sems.at[2]
    )
    dec_weights.start()
    copies[3].wait()
    out = middle + enc_ref[7:8]
    for group in range(3):
        out = out + dot(
            enc_rows[:, 1024 * group : 1024 * group + 1024],
            w_down[:, 768 * group : 768 * group + 768],
        )
    encoded = low(out)
    enc_rows[:, 3072:3840] = encoded
    copies[4].wait()
    embedded = low(dot(widen(encoded, pads), w_emb[...]) + dec_ref[0:1])

    attended_ref, d_hid_ref = rows_ref.at[:, pl.ds(512, 512)], rows_ref.at[:, pl.ds(3584, 2048)]
    activated_ref = rows_ref.at[:, pl.ds(5632, 2048)]
    w_z, w_ddown = w_up.at[:, pl.ds(0, 2048)], w_up.at[:, pl.ds(2048, 1024)]
    saves = [
        pltpu.make_async_copy(source, into, out_sems.at[i])
        for i, (source, into) in enumerate(
            (
                (enc_rows, enc_rows_out),
                (enc_proj3_ref, enc_proj3_out),
                (enc_shares_ref, enc_shares_out),
                (enc_middle_ref, enc_middle_out),
                (enc_slope_ref, enc_slope_out),
            )
        )
    ]
    for start, width in ((0, 1536), (5632, 2048), (3584, 2048), (1536, 2048)):
        cut = pl.ds(start, width)
        saves.append(
            pltpu.make_async_copy(rows_ref.at[:, cut], rows_out.at[:, cut], out_sems.at[len(saves)])
        )
    for save in saves[:5]:
        save.start()
    gain_1, gain_2 = dec_ref[2:3], dec_ref[3:4]
    picker_t = picker_t_ref[...]
    masked = 1.0 - t_dot(picker_t, jnp.ones((96, 512), BF16))
    start = t_dot(picker_t, embedded) + masked * dec_ref[1:2] + table_ref[...]
    start_ref[...] = start
    unit, _ = norm_parts(start)
    h1 = low(unit * gain_1 + dec_ref[4:5])
    rows_ref[:, :512] = h1
    dec_weights.wait()

    @pl.loop(0, 4)
    def _(block):
        into = pl.ds(pl.multiple_of(block * 128, 128), 128)
        source = pl.ds(pl.multiple_of(block * 256, 256), 256)
        for half in range(2):
            cut = slice(1024 * half, 1024 * half + 1024)
            rows = w_z[source, cut]
            w_lo[into, cut] = low(dot(low_ref[...], rows))
            w_hi[into, cut] = low(dot(high_ref[...], rows))

    for third in range(3):
        cut = slice(512 * third, 512 * third + 512)
        part = dot(h1, w_lo[:, cut])
        if third != 1:
            part = part + (dec_ref[6:7] if third == 0 else dec_ref[7:8])
        proj3_ref[:, cut] = low(part)

    @pl.loop(0, 8, unroll=4)
    def _(step):
        pack, group = step // 4, step % 4
        rows = pl.ds(pl.multiple_of(pack * 192, 192), 192)
        cuts = [pl.ds(pl.multiple_of(512 * i + 128 * group, 128), 128) for i in range(3)]
        out = attend_group(
            proj3_ref[rows, cuts[0]], proj3_ref[rows, cuts[1]], proj3_ref[rows, cuts[2]],
            bias_ref[pack], 4, DEC_SCALE, shares_ref.at[step],
        )
        attended_ref[rows, cuts[0]] = low(out)

    middle = start + dot(attended_ref[...], w_lo[:, 1536:]) + dec_ref[8:9]
    middle_ref[...] = middle
    unit_2, rstd_2 = norm_parts(middle)
    h2 = low(unit_2 * gain_2 + dec_ref[5:6])
    rows_ref[:, 1024:1536] = h2
    saves[5].start()

    @pl.loop(0, 4)
    def _(tile):
        cut = pl.ds(pl.multiple_of(tile * 512, 512), 512)
        value, slope = gelu_pair(dot(h2, w_hi[:, cut]) + dec_up_ref[:, cut])
        activated_ref[:, cut] = low(value)
        slope_ref[:, cut] = slope

    out = middle + dec_ref[9:10]
    for group in range(2):
        out = out + dot(
            activated_ref[:, 1024 * group : 1024 * group + 1024],
            w_ddown[:, 512 * group : 512 * group + 512],
        )
    saves[6].start()
    sides(low(out), side_ref[0], mine_ref, theirs_ref)

    g_low = pull_ref[...]
    for tile in range(4):
        group, rows = tile // 2, slice(512 * (tile % 2), 512 * (tile % 2) + 512)
        cut = slice(512 * tile, 512 * tile + 512)
        d_hid = dot_t(g_low, w_ddown[rows, 512 * group : 512 * group + 512]) * slope_ref[:, cut]
        d_up_small_ref[:, cut] = col_sum(d_hid)
        d_hid_ref[:, cut] = low(d_hid)
    saves[7].start()
    d_h2 = dot_t(d_hid_ref[...], w_hi[...])
    part, d_gain_2, d_shift_2 = norm_back(d_h2, unit_2, rstd_2, gain_2)
    g = g_low.astype(F32)
    d_mid = g + part
    d_mid_low = low(d_mid)
    d_att = low(dot_t(d_mid_low, w_lo[:, 1536:]))
    d_small_ref[...] = jnp.zeros_like(d_small_ref)
    d_small_ref[3:4] = d_gain_2
    d_small_ref[5:6] = d_shift_2
    d_small_ref[8:9] = col_sum(d_mid)
    d_small_ref[9:10] = col_sum(g)
    rows_ref[:, 3072:3584] = d_mid_low
    middle_ref[...] = d_mid
    d_att_ref[...] = d_att

    @pl.loop(0, 8, unroll=4)
    def _(step):
        pack, group = step // 4, step % 4
        rows = pl.ds(pl.multiple_of(pack * 192, 192), 192)
        cuts = [pl.ds(pl.multiple_of(512 * i + 128 * group, 128), 128) for i in range(3)]
        parts = attend_group_back(
            proj3_ref[rows, cuts[0]], proj3_ref[rows, cuts[1]], proj3_ref[rows, cuts[2]],
            d_att_ref[rows, cuts[0]], shares_ref[step], 4, DEC_SCALE, 256,
        )
        for i, part in enumerate(parts):
            at = pl.multiple_of(1536 + 512 * i + 128 * group, 128)
            rows_ref[rows, pl.ds(at, 128)] = low(part)
            if i != 1:
                d_small_ref[6 + i // 2, cuts[0]] += jnp.sum(part, axis=0)

    saves[8].start()
    d_h1 = dot_t(rows_ref[:, 1536:3072], w_lo[:, :1536])
    unit, rstd = norm_parts(start_ref[...])
    part, d_gain_1, d_shift_1 = norm_back(d_h1, unit, rstd, gain_1)
    d_start = middle_ref[...] + part
    d_small_ref[2:3] = d_gain_1
    d_small_ref[4:5] = d_shift_1
    masked = 1.0 - t_dot(picker_t_ref[...], jnp.ones((96, 512), BF16))
    d_small_ref[1:2] = col_sum(masked * d_start)
    d_embedded = dot(picker_t_ref[...], low(d_start))
    d_small_ref[0:1] = col_sum(d_embedded)
    d_embedded = low(d_embedded)
    back_ref[:, 768:] = d_embedded
    back_ref[:, :768] = narrow(low(dot_t(d_embedded, w_emb[...])), pads)
    for save in saves:
        save.wait()


def blocks(side, *operands):
    return pl.pallas_call(
        blocks_kernel,
        in_specs=[ANY] + [VMEM] * 9 + [pl.BlockSpec(memory_space=pltpu.SMEM)],
        out_specs=[VMEM] * 6 + [ANY] * 6,
        out_shape=[
            pltpu.HBM((8, 768), F32),
            pltpu.HBM((384, 256), BF16),
            pltpu.HBM((384, 256), BF16),
            shape((96, 1280), BF16),
            pltpu.HBM((16, 512), F32),
            pltpu.HBM((1, 2048), F32),
            pltpu.HBM((96, 6144), BF16),
            pltpu.HBM((96, 2304), BF16),
            pltpu.HBM((6, 96, 256), F32),
            pltpu.HBM((96, 768), F32),
            pltpu.HBM((96, 3072), F32),
            pltpu.HBM((384, 7680), BF16),
        ],
        scratch_shapes=[
            pltpu.VMEM((1, 3072), F32),
            pltpu.VMEM((16, 512), F32),
            pltpu.VMEM((1, 2048), F32),
            pltpu.VMEM((3, 8, 16, 128), F32),
            pltpu.VMEM((1024, 2304), BF16),
            pltpu.VMEM((1024, 768), BF16),
            pltpu.VMEM((1024, 3072), BF16),
            pltpu.VMEM((1024, 512), BF16),
            pltpu.VMEM((1024, 2304), BF16),
            pltpu.VMEM((96, 6144), BF16),
            pltpu.VMEM((96, 2304), BF16),
            pltpu.VMEM((6, 96, 256), F32),
            pltpu.VMEM((96, 768), F32),
            pltpu.VMEM((96, 3072), F32),
            pltpu.VMEM((384, 7680), BF16),
            pltpu.VMEM((512, 2048), BF16),
            pltpu.VMEM((512, 2048), BF16),
            pltpu.VMEM((384, 512), F32),
            pltpu.VMEM((384, 1536), BF16),
            pltpu.VMEM((8, 192, 1024), F32),
            pltpu.VMEM((384, 512), F32),
            pltpu.VMEM((384, 2048), F32),
            pltpu.VMEM((384, 512), BF16),
            pltpu.SemaphoreType.DMA((5,)),
            pltpu.SemaphoreType.DMA((9,)),
        ],
        compiler_params=params(60),
        cost_estimate=pl.CostEstimate(flops=10**4, bytes_accessed=10**3, transcendentals=0),
        name="blocks",
    )(*[in_hbm(a) for a in operands], side)


def enc_back_kernel(
    whole, back_ref, middle_ref, slope_ref, proj3_ref, shares_ref, x_ref, pads_ref, enc_ref,
    d_dec_ref, d_dec_up_ref, dec_theirs_ref, side_ref,
    rows_ref, mine_ref, theirs_ref, small_ref,
    w_down, w_up, w_proj, w_qkv, d_p3_ref, d_up_ref, table_ref, sems,
):
    copies = [
        pltpu.make_async_copy(whole.at[:, pl.ds(at, ref.shape[1])], ref, sems.at[i])
        for i, (at, ref) in enumerate(
            ((C_DOWN, w_down), (C_UP, w_up), (C_PROJ, w_proj), (0, w_qkv))
        )
    ]
    for copy in copies:
        copy.start()
    pads = pads_ref[...]
    g_low = back_ref[:, :768]
    g = g_low.astype(F32)
    unit, rstd = norm_parts(middle_ref[...])
    copies[0].wait()
    for group in range(3):
        cut = slice(1024 * group, 1024 * group + 1024)
        d_hid = dot_t(g_low, w_down[:, 768 * group : 768 * group + 768]) * slope_ref[:, cut]
        d_up_ref[:, cut] = col_sum(d_hid)
        rows_ref[:, cut] = low(d_hid)
    copies[1].wait()
    d_h2 = narrow_wide(dot_t(rows_ref[:, :3072], w_up[...]), pads)
    part, d_gain_2, d_shift_2 = norm_back(d_h2, unit, rstd, enc_ref[1:2])
    d_middle = g + part
    d_mid_low = low(d_middle)
    rows_ref[:, 5376:] = d_mid_low
    copies[2].wait()
    d_att = narrow(low(dot_t(d_mid_low, w_proj[...])), pads)
    for group in range(6):
        cuts = [slice(768 * i + 128 * group, 768 * i + 128 * group + 128) for i in range(3)]
        parts = attend_group_back(
            proj3_ref[:, cuts[0]], proj3_ref[:, cuts[1]], proj3_ref[:, cuts[2]],
            d_att[:, cuts[0]], shares_ref[group], 2, 0.125, 128,
        )
        for third, (cut, part) in enumerate(zip(cuts, parts)):
            d_p3_ref[:, cut] = part
            at = 3072 + 768 * third + 128 * group
            rows_ref[:, at : at + 128] = low(part)
    unit, rstd = norm_parts(x_ref[...].astype(F32))
    copies[3].wait()
    d_h1 = narrow_wide(dot_t(rows_ref[:, 3072:5376], w_qkv[...]), pads)
    part, d_gain_1, d_shift_1 = norm_back(d_h1, unit, rstd, enc_ref[0:1])
    theirs_ref[:384, :256] = dec_theirs_ref[...]
    theirs_ref[:384, 256:] = jnp.zeros((384, 128), BF16)
    sides(low(d_middle + part), side_ref[0], mine_ref, theirs_ref.at[pl.ds(384, 96)])
    vectors = (
        d_gain_1, d_gain_2, d_shift_1, d_shift_2, col_sum(d_p3_ref[:, :768]),
        col_sum(d_p3_ref[:, 1536:]), col_sum(d_middle), col_sum(g),
    )
    row = lax.broadcasted_iota(jnp.int32, (8, 768), 0)
    d_enc = jnp.zeros((8, 768), F32)
    for line, vector in enumerate(vectors):
        d_enc = jnp.where(row == line, vector, d_enc)
    small_out(d_enc, d_up_ref[...], d_dec_ref[...], d_dec_up_ref[...], table_ref)
    small_ref[...] = low(table_ref[...])


def enc_back(side, *operands):
    return pl.pallas_call(
        enc_back_kernel,
        in_specs=[ANY] + [VMEM] * 11 + [pl.BlockSpec(memory_space=pltpu.SMEM)],
        out_specs=[VMEM] * 4,
        out_shape=(
            shape((96, 6144), BF16),
            pltpu.HBM((96, 384), BF16),
            pltpu.HBM((480, 384), BF16),
            shape((128, 128), BF16),
        ),
        scratch_shapes=[
            pltpu.VMEM((1024, 2304), BF16),
            pltpu.VMEM((1024, 3072), BF16),
            pltpu.VMEM((1024, 768), BF16),
            pltpu.VMEM((1024, 2304), BF16),
            pltpu.VMEM((96, 2304), F32),
            pltpu.VMEM((1, 3072), F32),
            pltpu.VMEM((128, 128), F32),
            pltpu.SemaphoreType.DMA((4,)),
        ],
        compiler_params=params(36),
        name="enc_back",
    )(*[in_hbm(a) for a in operands], side)


def widen_t(values, pads_t):
    return jnp.concatenate(
        [low(dot_t(pads_t, values[:, :384])), low(dot_t(pads_t, values[:, 384:]))], axis=0
    )


def spread_t(values, rows_t):
    return jnp.concatenate(
        [low(dot_t(rows_t, values[:, 128 * i : 128 * i + 128])) for i in range(4)], axis=0
    )


def two(own, other, cut):
    return jnp.concatenate([own[:, cut], other[:, cut]], axis=0)


def chunk_copies(stage, place, splits, outs, sems):
    copies = []
    for split, (start, width, first) in enumerate(splits):
        send, keep = outs[2 * split], outs[2 * split + 1]
        for slot, (ref, flips) in enumerate(((send, (first, 2)), (keep, (0, 4 - first)))):
            for line, turn in enumerate(flips):
                copies.append(
                    pltpu.make_async_copy(
                        stage.at[:, place ^ turn, :, pl.ds(start, width)],
                        ref.at[line],
                        sems.at[4 * split + 2 * slot + line],
                    )
                )
    return copies


Y_SPLITS = ((0, 1024, 1), (1024, 1024, 3))


def load_rows(sources, start, width, into, sems, at):
    count = sources[0].shape[0]
    return [
        pltpu.make_async_copy(
            source.at[:, pl.ds(start, width)],
            into.at[pl.ds(count * i, count), :],
            sems.at[at + i],
        )
        for i, source in enumerate(sources)
    ]


def dec_tile(tile, core, dec, dec_o, lefts, rights, sems, at):
    place = pl.multiple_of(1024 * tile + 512 * core, 128)
    low_left = 0 if tile == 0 else pl.multiple_of(512 * core, 128)
    loads = []
    for i, (start, into) in enumerate(
        (
            (low_left, lefts.at[0]),
            (1024, lefts.at[1]),
            (1536 + place, rights.at[0]),
            (3584 + place, rights.at[1]),
        )
    ):
        loads += load_rows((dec, dec_o), start, 512, into, sems, at + 2 * i)
    return loads


def dec_tile_grad(lefts, rights, low_t, high_t):
    grad = dot(spread_t(lefts[0], low_t), rights[0])
    return low(grad + dot(spread_t(lefts[1], high_t), rights[1]))


def grad_s_kernel(
    place_ref, enc_ref, enc_o_ref, m_ref, m_o_ref, pull_ref, pull_o_ref, pads_t_ref, low_t_ref,
    high_t_ref, dec, dec_o,
    sums, stage, sems, activated, lefts, rights, load_sems,
):
    core = place_ref[3]
    loads = load_rows((dec, dec_o), 5632, 2048, activated, load_sems, 0)
    loads += dec_tile(0, core, dec, dec_o, lefts, rights, load_sems, 2)
    for load in loads:
        load.start()
    for group in range(3):
        right = two(m_ref, m_o_ref, pl.ds(pl.multiple_of(384 * core, 128), 384))
        grad = low(t_dot(two(enc_ref, enc_o_ref, pl.ds(1024 * group, 1024)), right))
        stage[:, :, :, 384 * group : 384 * group + 384] = grad.reshape(4, 4, 64, 384)
    right = two(m_ref, m_o_ref, pl.ds(pl.multiple_of(768 + 256 * core, 128), 256))
    wide = widen_t(two(enc_ref, enc_o_ref, pl.ds(3072, 768)), pads_t_ref[...])
    stage[:, :, :, 1152:1408] = low(dot(wide, right)).reshape(4, 4, 64, 256)
    right = two(pull_ref, pull_o_ref, pl.ds(pl.multiple_of(256 * core, 128), 256))
    for load in loads:
        load.wait()
    for group in range(2):
        grad = low(t_dot(activated[:, 1024 * group : 1024 * group + 1024], right))
        stage[:, :, :, 1408 + 256 * group : 1664 + 256 * group] = grad.reshape(4, 4, 64, 256)
    grad = dec_tile_grad(lefts, rights, low_t_ref[...], high_t_ref[...])
    stage[:, :, :, 1920:] = grad.reshape(4, 4, 64, 512)
    copies = [
        pltpu.make_async_copy(stage.at[:, z], sums.at[z], sems.at[z]) for z in range(4)
    ]
    for copy in copies:
        copy.start()
    for copy in copies:
        copy.wait()


def grad_y_kernel(
    place_ref, enc_ref, enc_o_ref, m_ref, m_o_ref, pads_t_ref, low_t_ref, high_t_ref, dec, dec_o,
    send_p, keep_p, send_q, keep_q, stage, sems, lefts, rights, load_sems,
):
    core = place_ref[3]
    loads = dec_tile(1, core, dec, dec_o, lefts, rights, load_sems, 0)
    for load in loads:
        load.start()
    copies = chunk_copies(stage, place_ref[1], Y_SPLITS, (send_p, keep_p, send_q, keep_q), sems)
    wide = widen_t(two(enc_ref, enc_o_ref, pl.ds(3840, 768)), pads_t_ref[...])
    for tile in range(3):
        cut = pl.ds(pl.multiple_of(1536 * core + 512 * tile, 128), 512)
        stage[0, :, :, 512 * tile : 512 * tile + 512] = low(
            dot(wide, two(m_ref, m_o_ref, cut))
        ).reshape(4, 256, 512)
        if tile == 1:
            for copy in copies[:4]:
                copy.start()
    for load in loads:
        load.wait()
    grad = dec_tile_grad(lefts, rights, low_t_ref[...], high_t_ref[...])
    stage[0, :, :, 1536:] = grad.reshape(4, 256, 512)
    for copy in copies[4:]:
        copy.start()
    for copy in copies:
        copy.wait()


def grad_z_kernel(
    place_ref, enc_ref, enc_o_ref, rows_ref, rows_o_ref, small_ref, pads_t_ref,
    send_1, send_3, send_2, own, stage, sems,
):
    core = place_ref[3]
    pads_t = pads_t_ref[...]
    line = lax.broadcasted_iota(jnp.int32, (1024, 128), 0)
    device = lax.broadcasted_iota(jnp.int32, (1024, 128), 1)
    small = dot_t((line == 8 * device + 6).astype(BF16), small_ref[...])
    copies = []
    for half, at in enumerate((0, pl.multiple_of(768 * core, 128))):
        left = widen_t(two(enc_ref, enc_o_ref, pl.ds(4608 + at, 768)), pads_t)
        cut = pl.ds(pl.multiple_of(3072 + 1536 * core + 768 * half, 128), 768)
        grad = dot(left, two(rows_ref, rows_o_ref, cut))
        columns = pl.ds(768 * half, 768)
        stage[:, :, :, 768 * half : 768 * half + 768] = low(grad).reshape(16, 4, 16, 768)
        if half == 0:
            stage[:, :, :, :128] = low(grad[:, :128] + small).reshape(16, 4, 16, 128)
        for i, (out, turn) in enumerate(((send_1, 1), (send_3, 3), (send_2, 2), (own, 0))):
            copies.append(
                pltpu.make_async_copy(
                    stage.at[:, (place_ref[0] + turn) % 4, :, columns],
                    out.at[:, :, columns],
                    sems.at[4 * half + i],
                )
            )
            copies[-1].start()
    for copy in copies:
        copy.wait()


def grad_call(kernel, name, staged, outs, place, small, large, scratch):
    return pl.pallas_call(
        kernel,
        in_specs=[pl.BlockSpec(memory_space=pltpu.SMEM)] + [VMEM] * len(small) + [ANY] * len(large),
        out_specs=[ANY] * len(outs),
        out_shape=[pltpu.HBM(dims, BF16) for dims in outs],
        scratch_shapes=[
            pltpu.VMEM(staged, BF16),
            pltpu.SemaphoreType.DMA((8,)),
            *scratch,
        ],
        compiler_params=params(22),
        cost_estimate=pl.CostEstimate(flops=10**4, bytes_accessed=10**3, transcendentals=0),
        name=name,
    )(place, *small, *[in_hbm(a) for a in large])


def split_outs(before, splits):
    return [(2, before, 256 // before, width) for _, width, _ in splits for _ in range(2)]


def fold_kernel(keep_ref, got_ref, send_ref):
    send_ref[...] = low(keep_ref[0].astype(F32) + got_ref[0].astype(F32))


def fold(keep, got):
    _, rows, columns = keep.shape
    block = (1, rows // 2, columns)
    return pl.pallas_call(
        fold_kernel,
        grid=(2,),
        in_specs=[pl.BlockSpec(block, lambda i: (1, i, 0))] * 2,
        out_specs=pl.BlockSpec(block[1:], lambda i: (i, 0)),
        out_shape=shape((rows, columns), BF16),
        compiler_params=params(24),
        cost_estimate=pl.CostEstimate(flops=10**4, bytes_accessed=10**3, transcendentals=0),
        name="fold",
    )(keep, got)


def part_kernel(place_ref, *refs, axis, groups):
    place = place_ref[axis]
    outs = refs[sum(groups) :]
    for out, turn in zip(outs, (1, 3, 2, 0)):
        chunk = pl.ds((place + turn) % 4, 1)
        at = start = 0
        for count in groups:
            total = None
            for ref in refs[start : start + count]:
                term = (ref[0, :, chunk] if len(ref.shape) == 5 else ref[:, chunk]).astype(F32)
                total = term if total is None else total + term
            start += count
            before, _, after, columns = total.shape
            out[:, at : at + columns] = low(total).reshape(before * after, columns)
            at += columns


def parted(place, axis, before, groups):
    rows = groups[0][0].shape[-2]
    after = rows // (4 * before)
    operands, specs = [], []
    for array in (a for group in groups for a in group):
        columns = array.shape[-1]
        if array.ndim == 3:
            operands.append(array.reshape(2, before, 4, after, columns))
            specs.append(pl.BlockSpec((1, before, 4, after, columns), lambda i: (0, 0, 0, 0, 0)))
        else:
            array = array.reshape(before, 4, after, columns)
            operands.append(in_hbm(array) if len(groups[0]) == 1 else array)
            specs.append(VMEM)
    columns = sum(group[0].shape[-1] for group in groups)
    return pl.pallas_call(
        functools.partial(part_kernel, axis=axis, groups=tuple(len(g) for g in groups)),
        grid=(1,),
        in_specs=[pl.BlockSpec(memory_space=pltpu.SMEM)] + specs,
        out_specs=[VMEM] * 4,
        out_shape=[shape((rows // 4, columns), BF16)] * 4,
        compiler_params=params(24),
        cost_estimate=pl.CostEstimate(flops=10**4, bytes_accessed=10**3, transcendentals=0),
        name="parted",
    )(place, *operands)


def last_kernel(place_ref, *refs, groups):
    core = place_ref[3]
    own_ref, other_ref = refs[sum(groups) :]
    at = start = 0
    for count in groups:
        total = None
        for ref in refs[start : start + count]:
            term = ref[...].astype(F32)
            total = term if total is None else total + term
        start += count
        cut = slice(at, at + total.shape[1])
        own_ref[:, cut] = jnp.where(core == 0, total[:8], total[8:])
        other_ref[:, cut] = jnp.where(core == 0, total[8:], total[:8])
        at += total.shape[1]


def last(place, groups):
    columns = sum(group[0].shape[-1] for group in groups)
    operands = [a for group in groups for a in group]
    return pl.pallas_call(
        functools.partial(last_kernel, groups=tuple(len(g) for g in groups)),
        in_specs=[pl.BlockSpec(memory_space=pltpu.SMEM)] + [VMEM] * len(operands),
        out_specs=[VMEM] * 2,
        out_shape=[shape((8, columns), F32)] * 2,
        compiler_params=params(24),
        cost_estimate=pl.CostEstimate(flops=10**4, bytes_accessed=10**3, transcendentals=0),
        name="last",
    )(place, *operands)


def ungrouped(values, groups):
    width = 128 * groups
    line = lax.broadcasted_iota(jnp.int32, (width, width), 0)
    column = lax.broadcasted_iota(jnp.int32, (width, width), 1)
    natural = 8 * groups * ((line & 127) >> 3) + 8 * (line >> 7) + (line & 7)
    turn = (natural == column).astype(BF16)
    high = low(values)
    rest = low(values - high.astype(F32))
    parts = []
    for block in range(8):
        cuts = [slice(1024 * g + 128 * block, 1024 * g + 128 * block + 128) for g in range(groups)]
        both = [jnp.concatenate([v[:, cut] for cut in cuts], axis=1) for v in (high, rest)]
        parts.append(dot(both[0], turn) + dot(both[1], turn))
    return jnp.concatenate(parts, axis=1)


def shards_kernel(
    place_ref, own_ref, got_ref, enc_gains, enc_biases, enc_qkv, enc_proj, enc_up, enc_up_bias,
    enc_down, dec_fill, dec_embed, dec_gains, dec_biases, dec_qkv, dec_proj, dec_up, dec_up_bias,
    dec_down,
):
    core = place_ref[3]

    def halves(start, width):
        own, got = own_ref[:, start : start + width], got_ref[:, start : start + width]
        return jnp.where(core == 0, own, got), jnp.where(core == 0, got, own)

    for group in range(3):
        rows = slice(8 * group, 8 * group + 8)
        enc_down[rows, :384], enc_down[rows, 384:] = halves(384 * group, 384)
    a, b = halves(1152, 256)
    dec_embed[:, :256], dec_embed[:, 256:] = a[:6], b[:6]
    for group in range(2):
        rows = slice(8 * group, 8 * group + 8)
        dec_down[rows, :256], dec_down[rows, 256:] = halves(1408 + 256 * group, 256)
    enc_up[...] = ungrouped(jnp.concatenate(halves(3968, 1536), axis=1), 3)[:6]
    z_all = jnp.concatenate(halves(1920, 512) + halves(5504, 512), axis=1)
    dec_qkv[...] = z_all[:4, :1536]
    dec_proj[...] = z_all[:4, 1536:]
    dec_up[...] = ungrouped(z_all, 2)[4:]
    a, b = halves(2432, 1536)
    enc_qkv[:, :1536] = a[:6]
    enc_qkv[:, 1536:] = b[:6, :768]
    enc_proj[...] = b[:6, 768:]
    flat = a[6:7, :128] + b[6:7, :128]
    at = 0
    smalls = (enc_gains, enc_biases, enc_up_bias, dec_fill, dec_gains, dec_biases, dec_up_bias)
    for ref, (lead, part) in zip(smalls, COUNTS):
        for line in range(lead):
            ref[line : line + 1, :] = flat[:, at : at + part]
            at += part


def shards(place, own, got):
    dims = (
        (2, 6), (6, 6), (6, 2304), (6, 768), (6, 3072), (1, 24), (24, 768), (2, 4), (6, 512),
        (2, 4), (6, 4), (4, 1536), (4, 512), (4, 2048), (1, 16), (16, 512),
    )
    return pl.pallas_call(
        shards_kernel,
        in_specs=[pl.BlockSpec(memory_space=pltpu.SMEM)] + [VMEM] * 2,
        out_specs=[VMEM] * 16,
        out_shape=[shape(d, F32) for d in dims],
        compiler_params=params(24),
        cost_estimate=pl.CostEstimate(flops=10**4, bytes_accessed=10**3, transcendentals=0),
        name="shards",
    )(place, own, got)


def join_kernel(place_ref, dec_mine, enc_mine, got, decoded, x_grad):
    own_at = 2 * place_ref[4]
    decoded[pl.ds(own_at, 2)] = dec_mine[...].reshape(2, 192, 256)
    decoded[pl.ds(2 - own_at, 2)] = got[:384, :256].reshape(2, 192, 256)
    x_grad[pl.ds(own_at, 2)] = enc_mine[...].reshape(2, 48, 384)
    x_grad[pl.ds(2 - own_at, 2)] = got[384:].reshape(2, 48, 384)


def joined(place, *rows):
    return pl.pallas_call(
        join_kernel,
        in_specs=[pl.BlockSpec(memory_space=pltpu.SMEM)] + [VMEM] * 3,
        out_specs=[VMEM] * 2,
        out_shape=[pltpu.HBM((4, 192, 256), BF16), pltpu.HBM((4, 48, 384), BF16)],
        compiler_params=params(16),
        name="joined",
    )(place, *[in_hbm(a) for a in rows])


def pack_kernel(
    enc_gains, enc_biases, enc_qkv, enc_proj, enc_up, enc_up_bias, enc_down, dec_fill, dec_embed,
    dec_gains, dec_biases, dec_qkv, dec_proj, dec_up, dec_up_bias, dec_down, out,
):
    def rows(count, shift=0):
        line = lax.broadcasted_iota(jnp.int32, (8, count), 0)
        return (line == lax.broadcasted_iota(jnp.int32, (8, count), 1) + shift).astype(BF16)

    def group(start, places, source, groups):
        width = 128 * groups
        line = lax.broadcasted_iota(jnp.int32, (width, width), 0)
        column = lax.broadcasted_iota(jnp.int32, (width, width), 1)
        natural = 8 * groups * ((column & 127) >> 3) + 8 * (column >> 7) + (column & 7)
        turn = (natural == line).astype(BF16)
        for block in range(8):
            piece = low(dot(places, source[:, width * block : width * block + width]))
            piece = dot(piece, turn)
            for g in range(groups):
                at = start + 1024 * g + 128 * block
                yield at, piece[:, 128 * g : 128 * g + 128]

    smalls = (enc_gains, enc_biases, enc_up_bias, dec_fill, dec_gains, dec_biases, dec_up_bias)
    flat, at = jnp.zeros((1, 128), F32), 0
    for ref, (lead, part) in zip(smalls, COUNTS):
        values = ref[...]
        line = lax.broadcasted_iota(jnp.int32, (part, 128), 0)
        column = lax.broadcasted_iota(jnp.int32, (part, 128), 1)
        for i in range(lead):
            flat = flat + dot(values[i : i + 1], (line + at == column).astype(BF16))
            at += part
    six, four, raised = rows(6), rows(4), rows(4, 4)
    seventh = lax.broadcasted_iota(jnp.int32, (8, 128), 0) == 6
    out[:, :C_PROJ] = low(dot(six, enc_qkv[...]))
    out[:, :128] = low(dot(six, enc_qkv[:, :128]) + jnp.where(seventh, flat, 0.0))
    out[:, C_PROJ:C_UP] = low(dot(six, enc_proj[...]))
    for at, piece in group(C_UP, six, enc_up, 3):
        out[:, at : at + 128] = low(piece)
    out[:, C_EMB:C_DOWN] = low(dot(six, dec_embed[...]))
    for g in range(3):
        out[:, C_DOWN + 768 * g : C_DOWN + 768 * g + 768] = low(dot(rows(24, -8 * g), enc_down[...]))
    lower = (dec_qkv[:, :1024], jnp.concatenate([dec_qkv[:, 1024:], dec_proj[...]], axis=1))
    lower = [dot(four, values) for values in lower]
    for at, piece in group(0, raised, dec_up, 2):
        half, column = at // 1024, at % 1024
        piece = piece + lower[half][:, column : column + 128]
        out[:, C_Z + at : C_Z + at + 128] = low(piece)
    for g in range(2):
        out[:, C_DDOWN + 512 * g : C_DDOWN + 512 * g + 512] = low(dot(rows(16, -8 * g), dec_down[...]))


def pack(*weights):
    weights = [w[None] if w.ndim == 1 else w for w in weights]
    return pl.pallas_call(
        pack_kernel,
        in_specs=[VMEM] * 16,
        out_specs=VMEM,
        out_shape=pltpu.HBM((8, C_ALL), BF16),
        compiler_params=params(24),
        name="pack",
    )(*[in_hbm(w) for w in weights])


def position_table(offset, width):
    half = width // 2
    rates = jnp.exp(jnp.arange(half, dtype=F32) * (-math.log(10000.0) / half))
    angle = offset.astype(F32)[:, None] * rates[None, :]
    return jnp.concatenate([jnp.sin(angle), jnp.cos(angle)], axis=1)


def layout(length_row, order, visible):
    length = order.shape[0]
    ends = jnp.cumsum(length_row, dtype=jnp.int32)
    places = lax.broadcasted_iota(jnp.int32, (length, 1), 0)
    passed = places >= ends[None, :]
    segment = jnp.sum(passed.astype(jnp.int32), axis=1, dtype=jnp.int32)
    offset = places[:, 0] - jnp.sum(
        jnp.where(passed, length_row[None, :], 0), axis=1, dtype=jnp.int32
    )
    shown_pos = order[:visible]
    shown_seg = jnp.sum(
        (shown_pos[:, None] >= ends[None, :]).astype(jnp.int32), axis=1, dtype=jnp.int32
    )
    onehot = places == shown_pos[None, :]
    return (segment, offset, shown_seg, onehot)


def spread_rows(devices, rows, at):
    feature = lax.broadcasted_iota(jnp.int32, (devices * rows, devices * 8), 0)
    place = lax.broadcasted_iota(jnp.int32, (devices * rows, devices * 8), 1)
    return (8 * (feature // rows) + at + feature % rows == place).astype(BF16)


def plans(length_rows, orders):
    segment, offset, shown_seg, onehot = jax.vmap(lambda a, b: layout(a, b, 48))(
        length_rows, orders
    )
    pack = jnp.arange(2, dtype=jnp.int32)[:, None] * 16
    seen = (shown_seg + pack).reshape(96)
    seen_keys = jnp.concatenate([seen, jnp.full((32,), -1, jnp.int32)])
    enc_bias = jnp.where(seen[:, None] == seen_keys[None, :], 0.0, NEVER).astype(F32)
    keys = jnp.concatenate([segment, jnp.full((2, 64), -1, jnp.int32)], axis=1)
    dec_bias = jnp.where(segment[:, :, None] == keys[:, None, :], 0.0, NEVER).astype(F32)
    hot = onehot.astype(BF16)
    hot = hot.transpose(0, 2, 1)
    none = jnp.zeros((48, 192), BF16)
    picker_t = jnp.concatenate(
        [jnp.concatenate([hot[0], none], axis=1), jnp.concatenate([none, hot[1]], axis=1)], axis=0
    )
    table = position_table(offset.reshape(-1), 512)
    return enc_bias, dec_bias, picker_t, table


def place_of(device):
    return device // 2 % 4, device // 32, device // 8 % 4, device % 2


AXES = {"y": (32, 4), "z": (8, 4), "x": (2, 4), "c": (1, 2)}


def flipped(block, axis, turn):
    stride, size = AXES[axis]
    route = []
    for device in range(128):
        at = device // stride % size
        route.append((device, device + ((at ^ turn) - at) * stride))
    return lax.ppermute(block, BOTH, route)


def other_core(block):
    return flipped(block, "c", 1)


def first_sent(axis, outs):
    begun = []
    for split, first in enumerate((1, 3)):
        send, keep = [a.reshape(2, 256, a.shape[-1]) for a in outs[2 * split : 2 * split + 2]]
        begun.append((keep, flipped(send, axis, first)))
    return begun


def second_sent(axis, begun, before):
    groups = []
    for (keep, got), first in zip(begun, (1, 3)):
        onward = fold(after(keep, *before), got)
        groups.append((keep, got, flipped(onward, axis, 4 - first)))
        before = (onward,)
    return groups, before


def passed(block, axis, by):
    stride, size = AXES[axis]
    route = []
    for device in range(128):
        at = device // stride % size
        route.append((device, device + ((at + by) % size - at) * stride))
    return lax.ppermute(block, BOTH, route)


def summed(place, axis, before, groups, earlier):
    *sends, own = parted(after(place, *earlier), "xyz".index(axis), before, groups)
    return [(own, *[passed(send, axis, by) for send, by in zip(sends, (1, 3, 2))])], (own,)


def after(value, *others):
    return lax.optimization_barrier((value, *others))[0]


def on_device(
    x_vis, lengths, shuffle, enc_gains, enc_biases, enc_qkv, enc_proj, enc_up, enc_up_bias,
    enc_down, dec_fill, dec_embed, dec_gains, dec_biases, dec_qkv, dec_proj, dec_up, dec_up_bias,
    dec_down, cotangent,
):
    section = lax.axis_index("section")
    device = lax.axis_index(BOTH)
    x, y, z, core = place_of(device)
    shard = pack(
        enc_gains, enc_biases, enc_qkv, enc_proj, enc_up, enc_up_bias, enc_down, dec_fill,
        dec_embed, dec_gains, dec_biases, dec_qkv, dec_proj, dec_up, dec_up_bias, dec_down,
    )
    whole = lax.all_gather(shard, BOTH, axis=0, tiled=True)

    packs = 2

    def mine(rows):
        return lax.dynamic_slice_in_dim(rows, section * packs, packs, 0)[:, 0]

    x_rows = mine(x_vis).reshape(packs * 48, 768)
    pull = mine(cotangent).reshape(packs * 192, 512)
    enc_bias, dec_bias, picker_t, table = plans(mine(lengths), mine(shuffle))
    pads = spread_rows(64, 6, 0)
    low_rows, high_rows = spread_rows(32, 4, 0), spread_rows(32, 4, 4)
    spread = (low_rows, high_rows)
    pads_t, low_t, high_t = pads.T, low_rows.T, high_rows.T
    place = jnp.stack([x, y, z, core, section]).astype(jnp.int32)
    side = section.astype(jnp.int32).reshape(1)

    pull_o = other_core(pull)

    ready = (whole, x_rows, pull, pull_o, enc_bias, dec_bias, picker_t, table)
    ready = lax.optimization_barrier((*ready, pads, pads_t, low_t, high_t, *spread))
    whole, x_rows, pull, pull_o, enc_bias, dec_bias, picker_t, table = ready[:8]
    pads, pads_t, low_t, high_t, *spread = ready[8:]
    (
        enc_vec, dec_mine, dec_theirs, back, d_dec, d_dec_up, enc_rows, proj3, shares, middle,
        slope, dec_rows,
    ) = blocks(
        side, whole, x_rows, enc_bias, pads, picker_t, table, dec_bias, pull, *spread
    )
    enc_rows_o = other_core(enc_rows)
    back_o = other_core(back)
    dec_rows_o = other_core(dec_rows)
    back_rows, enc_mine, enc_theirs, small = enc_back(
        side, whole, back, middle, slope, proj3, shares, x_rows, pads, enc_vec, d_dec, d_dec_up,
        dec_theirs,
    )
    back_rows_o = other_core(back_rows)
    (sums_s,) = grad_call(
        grad_s_kernel, "grad_s", (4, 4, 64, 2432), [(4, 4, 64, 2432)], after(place, back_rows),
        (enc_rows, enc_rows_o, back, back_o, pull, pull_o, pads_t, low_t, high_t),
        (dec_rows, dec_rows_o),
        (
            pltpu.VMEM((768, 2048), BF16),
            pltpu.VMEM((2, 768, 512), BF16),
            pltpu.VMEM((2, 768, 512), BF16),
            pltpu.SemaphoreType.DMA((10,)),
        ),
    )
    sums_y = grad_call(
        grad_y_kernel, "grad_y", (1, 4, 256, 2048), split_outs(1, Y_SPLITS), after(place, sums_s),
        (enc_rows, enc_rows_o, back_rows, back_rows_o, pads_t, low_t, high_t),
        (dec_rows, dec_rows_o),
        (
            pltpu.VMEM((2, 768, 512), BF16),
            pltpu.VMEM((2, 768, 512), BF16),
            pltpu.SemaphoreType.DMA((8,)),
        ),
    )
    sums_z = grad_call(
        grad_z_kernel, "grad_z", (16, 4, 16, 1536), [(16, 16, 1536)] * 4,
        after(place, *sums_y), (enc_rows, enc_rows_o, back_rows, back_rows_o, small, pads_t), (), (),
    )

    sums_s = lax.psum_scatter(
        sums_s.reshape(64, 16, 2432), "z", scatter_dimension=0, tiled=True
    ).reshape(256, 2432)
    sums_y = first_sent("y", sums_y)
    *sends, own = [a.reshape(256, 1536) for a in sums_z]
    sums_z = [(own, *[passed(send, "x", by) for send, by in zip(sends, (1, 3, 2))])]
    sums_y, done = second_sent("y", sums_y, (own,))
    sums_s, done = summed(place, "x", 4, [(sums_s,)], done)
    sums_z, done = summed(place, "z", 4, sums_z, done)
    sums_y, done = summed(place, "z", 1, sums_y, done)
    decoded, x_grad = joined(place, dec_mine, enc_mine, flipped(enc_theirs, "y", 2))
    sums_sz, done = summed(place, "y", 1, sums_s + sums_z, (*done, decoded, x_grad))
    sums_y, done = summed(place, "x", 1, sums_y, done)
    own, other = last(place, sums_sz + sums_y)
    grads = shards(place, own, other_core(other))
    grads = [g[0] if g.shape[0] == 1 else g for g in grads]
    return (decoded[:, None], x_grad[:, None], *grads)


def solution(mesh):
    mesh = Mesh(mesh.devices.reshape(2, 2, 4, 4, 2), BOTH)
    rows = P(None, DP, None, None)
    ids = P(None, DP, None)
    wide = P(None, BOTH)
    tall = P(BOTH, None)
    flat = P(BOTH)
    in_specs = (rows, ids, ids, wide, wide, tall, tall, tall, flat, tall, wide, tall, wide, wide)
    in_specs += (tall, tall, tall, flat, tall, rows)
    out_rows = P(None, DP, None, "section")
    out_specs = (out_rows, out_rows, wide, wide, tall, tall, tall, flat, tall, wide, tall, wide)
    out_specs += (wide, tall, tall, tall, flat, tall)
    return jax.shard_map(
        on_device, mesh=mesh, in_specs=in_specs, out_specs=out_specs, check_vma=False
    )
```

```python
import functools
import math

import jax
import jax.numpy as jnp
from jax import lax
from jax.experimental import pallas as pl
from jax.experimental.pallas import tpu as pltpu
from jax.sharding import Mesh
from jax.sharding import PartitionSpec as P

H_ENC = 12
H_DEC = 16
DP = ("y_low", "z", "x", "core")
BOTH = ("section", *DP)
Y_AXIS = ("section", "y_low")
F32 = jnp.float32
BF16 = jnp.bfloat16
EPS = 1e-06
NEVER = -1e30
MIB = 1 << 20

C_PROJ = 2304
C_UP = 3072
C_EMB = 6144
C_DOWN = 6656
C_Z = 8960
C_DDOWN = 11008
C_ALL = 12032
COUNTS = ((2, 6), (6, 6), (1, 24), (2, 4), (2, 4), (6, 4), (1, 16))


def dot(left, right):
    return jnp.dot(left, right, preferred_element_type=F32)


def dot_t(left, right):
    return lax.dot_general(left, right, (((1,), (1,)), ((), ())), preferred_element_type=F32)


def t_dot(left, right):
    return lax.dot_general(left, right, (((0,), (0,)), ((), ())), preferred_element_type=F32)


def low(values):
    return values.astype(BF16)


def norm_parts(values):
    mean = jnp.mean(values, axis=-1, keepdims=True)
    centred = values - mean
    rstd = lax.rsqrt(jnp.mean(centred * centred, axis=-1, keepdims=True) + EPS)
    return centred * rstd, rstd


def norm_back(d_normed, unit, rstd, gain):
    scaled = d_normed * gain
    part = scaled - jnp.mean(scaled, axis=-1, keepdims=True)
    part = (part - unit * jnp.mean(scaled * unit, axis=-1, keepdims=True)) * rstd
    return part, col_sum(d_normed * unit), col_sum(d_normed)


def col_sum(values):
    return jnp.sum(values, axis=0, keepdims=True)


def gelu_pair(hidden):
    share = 0.5 + 0.5 * lax.erf(hidden * math.sqrt(0.5))
    slope = share + hidden * (jnp.exp(-0.5 * hidden * hidden) * (1.0 / math.sqrt(2.0 * math.pi)))
    return hidden * share, slope


def head_stack(block, heads, rows):
    size = 128 // heads
    lane = lax.broadcasted_iota(jnp.int32, (1, 128), 1)
    fill = jnp.zeros((rows - block.shape[0], 128), BF16)
    parts = []
    for head in range(heads):
        own = ((lane >= head * size) & (lane < (head + 1) * size)).astype(BF16)
        parts += [block * own, fill]
    return jnp.concatenate(parts, axis=0)


def head_unstack(stack, heads, rows, count):
    size = 128 // heads
    lane = lax.broadcasted_iota(jnp.int32, (1, 128), 1)
    total = None
    for head in range(heads):
        own = ((lane >= head * size) & (lane < (head + 1) * size)).astype(F32)
        part = stack[head * rows : head * rows + count] * own
        total = part if total is None else total + part
    return total


def attend_group(query, key, value, bias, heads, scale, shares_out):
    rows = bias.shape[1]
    scores = dot_t(query, head_stack(key, heads, rows))
    parts = []
    for head in range(heads):
        s = scores[:, head * rows : (head + 1) * rows] * scale + bias
        powers = jnp.exp(s - jnp.max(s, axis=-1, keepdims=True))
        parts.append(powers / jnp.sum(powers, axis=-1, keepdims=True))
    shares = jnp.concatenate(parts, axis=1)
    shares_out[...] = shares
    return dot(low(shares), head_stack(value, heads, rows))


def attend_group_back(query, key, value, d_out, shares, heads, scale, rows):
    count = key.shape[0]
    d_shares = dot_t(d_out, head_stack(value, heads, rows))
    parts = []
    for head in range(heads):
        cut = slice(head * rows, (head + 1) * rows)
        p, dp = shares[:, cut], d_shares[:, cut]
        parts.append(low(p * (dp - jnp.sum(dp * p, axis=-1, keepdims=True))))
    d_scores = jnp.concatenate(parts, axis=1)
    d_query = dot(d_scores, head_stack(key, heads, rows)) * scale
    d_key = head_unstack(t_dot(d_scores, query), heads, rows, count) * scale
    d_value = head_unstack(t_dot(low(shares), d_out), heads, rows, count)
    return d_query, d_key, d_value


def widen(values, pads):
    return jnp.concatenate(
        [low(dot(values[:, :384], pads)), low(dot(values[:, 384:], pads))], axis=1
    )


def narrow(values, pads):
    return jnp.concatenate(
        [low(dot_t(values[:, :512], pads)), low(dot_t(values[:, 512:], pads))], axis=1
    )


def narrow_wide(values, pads):
    high = low(values)
    rest = low(values - high.astype(F32))
    return jnp.concatenate(
        [
            dot_t(high[:, :512], pads) + dot_t(rest[:, :512], pads),
            dot_t(high[:, 512:], pads) + dot_t(rest[:, 512:], pads),
        ],
        axis=1,
    )


PARTS = (6, 4, 8)


def small_rows():
    plan, at = [], 0
    for family, (lead, part) in enumerate(COUNTS):
        for value in range(lead * part):
            if part >= 16:
                plan.append((2, value // 8 + (3 if family == 6 else 0), value % 8, at))
            else:
                first = 2 if family == 1 else (0, 0, 0, 0, 2, 4)[family]
                kind = 0 if family < 2 else 1
                plan.append((kind, first + value // part, value % part, at))
            at += 1
    return plan


def strewn(kind, value):
    part = PARTS[kind]
    device = lax.broadcasted_iota(jnp.int32, (128, 128 * part), 0)
    column = lax.broadcasted_iota(jnp.int32, (128, 128 * part), 1)
    return (column == part * device + value).astype(BF16)


def small_in(columns, rows_ref, enc_ref, enc_up_ref, dec_ref, dec_up_ref):
    line = lax.broadcasted_iota(jnp.int32, (1024, 128), 0)
    device = lax.broadcasted_iota(jnp.int32, (1024, 128), 1)
    table = t_dot(columns, (line == 8 * device + 6).astype(BF16))
    rows_ref[...] = jnp.zeros_like(rows_ref)
    for kind, row, value, place in small_rows():
        rows_ref[kind, value, row : row + 1, :] = table[place : place + 1]
    whole = []
    for kind, part in enumerate(PARTS):
        total = None
        for value in range(part):
            term = dot(low(rows_ref[kind, value]), strewn(kind, value))
            total = term if total is None else total + term
        whole.append(total)
    enc_ref[...] = whole[0][:8]
    dec_ref[...] = whole[1]
    for group in range(3):
        enc_up_ref[:, 1024 * group : 1024 * group + 1024] = whole[2][group : group + 1]
    for group in range(2):
        dec_up_ref[:, 1024 * group : 1024 * group + 1024] = whole[2][3 + group : 4 + group]


def small_out(enc, enc_up, dec, dec_up, table_ref):
    ups = [enc_up[:, 1024 * g : 1024 * g + 1024] for g in range(3)]
    ups += [dec_up[:, 1024 * g : 1024 * g + 1024] for g in range(2)]
    ups += [jnp.zeros((3, 1024), F32)]
    whole = (low(enc), low(dec), low(jnp.concatenate(ups, axis=0)))
    parts = [
        [dot_t(whole[kind], strewn(kind, value)) for value in range(part)]
        for kind, part in enumerate(PARTS)
    ]
    for kind, row, value, place in small_rows():
        table_ref[place : place + 1, :] = parts[kind][value][row : row + 1]


VMEM = pl.BlockSpec(memory_space=pltpu.VMEM)
ANY = pl.BlockSpec(memory_space=pl.ANY)


def shape(dims, kind):
    return jax.ShapeDtypeStruct(dims, kind)


def in_hbm(array):
    return pltpu.with_memory_space_constraint(array, pltpu.HBM)


def params(limit):
    return pltpu.CompilerParams(vmem_limit_bytes=limit * MIB)


def sides(rows, side, mine_ref, theirs_ref):
    half = rows.shape[1] // 2
    mine_ref[...] = jnp.where(side == 0, rows[:, :half], rows[:, half:])
    theirs_ref[...] = jnp.where(side == 0, rows[:, half:], rows[:, :half])


DEC_SCALE = 1.0 / math.sqrt(32)


def blocks_kernel(
    whole, x_ref, enc_bias_ref, pads_ref, picker_t_ref, table_ref, bias_ref, pull_ref, low_ref,
    high_ref, side_ref,
    enc_ref, mine_ref, theirs_ref, back_ref, d_small_ref, d_up_small_ref, enc_rows_out,
    enc_proj3_out, enc_shares_out, enc_middle_out, enc_slope_out, rows_out,
    enc_up_ref, dec_ref, dec_up_ref, small_ref, w_qkv, w_proj, w_up, w_emb, w_down,
    enc_rows, enc_proj3_ref, enc_shares_ref, enc_middle_ref, enc_slope_ref,
    rows_ref, w_lo, w_hi, start_ref, proj3_ref, shares_ref, middle_ref, slope_ref, d_att_ref,
    sems, out_sems,
):
    copies = [
        pltpu.make_async_copy(whole.at[:, pl.ds(at, ref.shape[1])], ref, sems.at[i])
        for i, (at, ref) in enumerate(
            ((0, w_qkv), (C_PROJ, w_proj), (C_UP, w_up), (C_DOWN, w_down), (C_EMB, w_emb))
        )
    ]
    for copy in copies:
        copy.start()
    pads = pads_ref[...]
    x = x_ref[...].astype(F32)
    unit, _ = norm_parts(x)
    copies[0].wait()
    small_in(w_qkv[:, :128], small_ref, enc_ref, enc_up_ref, dec_ref, dec_up_ref)
    h1 = low(unit * enc_ref[0:1] + enc_ref[2:3])
    enc_rows[:, 4608:5376] = h1
    wide = widen(h1, pads)
    for third in range(3):
        cut = slice(768 * third, 768 * third + 768)
        part = dot(wide, w_qkv[:, cut])
        if third != 1:
            part = part + (enc_ref[4:5] if third == 0 else enc_ref[5:6])
        enc_proj3_ref[:, cut] = low(part)
    bias = enc_bias_ref[...]
    for group in range(6):
        cuts = [slice(768 * i + 128 * group, 768 * i + 128 * group + 128) for i in range(3)]
        out = attend_group(
            enc_proj3_ref[:, cuts[0]], enc_proj3_ref[:, cuts[1]], enc_proj3_ref[:, cuts[2]],
            bias, 2, 0.125, enc_shares_ref.at[group],
        )
        enc_rows[:, 5376 + 128 * group : 5504 + 128 * group] = low(out)
    copies[1].wait()
    middle = x + dot(widen(enc_rows[:, 5376:], pads), w_proj[...]) + enc_ref[6:7]
    enc_middle_ref[...] = middle
    unit, _ = norm_parts(middle)
    h2 = low(unit * enc_ref[1:2] + enc_ref[3:4])
    enc_rows[:, 3840:4608] = h2
    wide = widen(h2, pads)
    copies[2].wait()

    @pl.loop(0, 6)
    def _(tile):
        cut = pl.ds(pl.multiple_of(tile * 512, 512), 512)
        value, slope = gelu_pair(dot(wide, w_up[:, cut]) + enc_up_ref[:, cut])
        enc_rows[:, cut] = low(value)
        enc_slope_ref[:, cut] = slope

    dec_weights = pltpu.make_async_copy(
        whole.at[:, pl.ds(C_Z, 3072)], w_up, sems.at[2]
    )
    dec_weights.start()
    copies[3].wait()
    out = middle + enc_ref[7:8]
    for group in range(3):
        out = out + dot(
            enc_rows[:, 1024 * group : 1024 * group + 1024],
            w_down[:, 768 * group : 768 * group + 768],
        )
    encoded = low(out)
    enc_rows[:, 3072:3840] = encoded
    copies[4].wait()
    embedded = low(dot(widen(encoded, pads), w_emb[...]) + dec_ref[0:1])

    attended_ref, d_hid_ref = rows_ref.at[:, pl.ds(512, 512)], rows_ref.at[:, pl.ds(3584, 2048)]
    activated_ref = rows_ref.at[:, pl.ds(5632, 2048)]
    w_z, w_ddown = w_up.at[:, pl.ds(0, 2048)], w_up.at[:, pl.ds(2048, 1024)]
    saves = [
        pltpu.make_async_copy(source, into, out_sems.at[i])
        for i, (source, into) in enumerate(
            (
                (enc_rows, enc_rows_out),
                (enc_proj3_ref, enc_proj3_out),
                (enc_shares_ref, enc_shares_out),
                (enc_middle_ref, enc_middle_out),
                (enc_slope_ref, enc_slope_out),
            )
        )
    ]
    for start, width in ((0, 1536), (5632, 2048), (3584, 2048), (1536, 2048)):
        cut = pl.ds(start, width)
        saves.append(
            pltpu.make_async_copy(rows_ref.at[:, cut], rows_out.at[:, cut], out_sems.at[len(saves)])
        )
    for save in saves[:5]:
        save.start()
    gain_1, gain_2 = dec_ref[2:3], dec_ref[3:4]
    picker_t = picker_t_ref[...]
    masked = 1.0 - t_dot(picker_t, jnp.ones((96, 512), BF16))
    start = t_dot(picker_t, embedded) + masked * dec_ref[1:2] + table_ref[...]
    start_ref[...] = start
    unit, _ = norm_parts(start)
    h1 = low(unit * gain_1 + dec_ref[4:5])
    rows_ref[:, :512] = h1
    dec_weights.wait()

    @pl.loop(0, 4)
    def _(block):
        into = pl.ds(pl.multiple_of(block * 128, 128), 128)
        source = pl.ds(pl.multiple_of(block * 256, 256), 256)
        for half in range(2):
            cut = slice(1024 * half, 1024 * half + 1024)
            rows = w_z[source, cut]
            w_lo[into, cut] = low(dot(low_ref[...], rows))
            w_hi[into, cut] = low(dot(high_ref[...], rows))

    for third in range(3):
        cut = slice(512 * third, 512 * third + 512)
        part = dot(h1, w_lo[:, cut])
        if third != 1:
            part = part + (dec_ref[6:7] if third == 0 else dec_ref[7:8])
        proj3_ref[:, cut] = low(part)

    @pl.loop(0, 8, unroll=4)
    def _(step):
        pack, group = step // 4, step % 4
        rows = pl.ds(pl.multiple_of(pack * 192, 192), 192)
        cuts = [pl.ds(pl.multiple_of(512 * i + 128 * group, 128), 128) for i in range(3)]
        out = attend_group(
            proj3_ref[rows, cuts[0]], proj3_ref[rows, cuts[1]], proj3_ref[rows, cuts[2]],
            bias_ref[pack], 4, DEC_SCALE, shares_ref.at[step],
        )
        attended_ref[rows, cuts[0]] = low(out)

    middle = start + dot(attended_ref[...], w_lo[:, 1536:]) + dec_ref[8:9]
    middle_ref[...] = middle
    unit_2, rstd_2 = norm_parts(middle)
    h2 = low(unit_2 * gain_2 + dec_ref[5:6])
    rows_ref[:, 1024:1536] = h2
    saves[5].start()

    @pl.loop(0, 4)
    def _(tile):
        cut = pl.ds(pl.multiple_of(tile * 512, 512), 512)
        value, slope = gelu_pair(dot(h2, w_hi[:, cut]) + dec_up_ref[:, cut])
        activated_ref[:, cut] = low(value)
        slope_ref[:, cut] = slope

    out = middle + dec_ref[9:10]
    for group in range(2):
        out = out + dot(
            activated_ref[:, 1024 * group : 1024 * group + 1024],
            w_ddown[:, 512 * group : 512 * group + 512],
        )
    saves[6].start()
    sides(low(out), side_ref[0], mine_ref, theirs_ref)

    g_low = pull_ref[...]
    for tile in range(4):
        group, rows = tile // 2, slice(512 * (tile % 2), 512 * (tile % 2) + 512)
        cut = slice(512 * tile, 512 * tile + 512)
        d_hid = dot_t(g_low, w_ddown[rows, 512 * group : 512 * group + 512]) * slope_ref[:, cut]
        d_up_small_ref[:, cut] = col_sum(d_hid)
        d_hid_ref[:, cut] = low(d_hid)
    saves[7].start()
    d_h2 = dot_t(d_hid_ref[...], w_hi[...])
    part, d_gain_2, d_shift_2 = norm_back(d_h2, unit_2, rstd_2, gain_2)
    g = g_low.astype(F32)
    d_mid = g + part
    d_mid_low = low(d_mid)
    d_att = low(dot_t(d_mid_low, w_lo[:, 1536:]))
    d_small_ref[...] = jnp.zeros_like(d_small_ref)
    d_small_ref[3:4] = d_gain_2
    d_small_ref[5:6] = d_shift_2
    d_small_ref[8:9] = col_sum(d_mid)
    d_small_ref[9:10] = col_sum(g)
    rows_ref[:, 3072:3584] = d_mid_low
    middle_ref[...] = d_mid
    d_att_ref[...] = d_att

    @pl.loop(0, 8, unroll=4)
    def _(step):
        pack, group = step // 4, step % 4
        rows = pl.ds(pl.multiple_of(pack * 192, 192), 192)
        cuts = [pl.ds(pl.multiple_of(512 * i + 128 * group, 128), 128) for i in range(3)]
        parts = attend_group_back(
            proj3_ref[rows, cuts[0]], proj3_ref[rows, cuts[1]], proj3_ref[rows, cuts[2]],
            d_att_ref[rows, cuts[0]], shares_ref[step], 4, DEC_SCALE, 256,
        )
        for i, part in enumerate(parts):
            at = pl.multiple_of(1536 + 512 * i + 128 * group, 128)
            rows_ref[rows, pl.ds(at, 128)] = low(part)
            if i != 1:
                d_small_ref[6 + i // 2, cuts[0]] += jnp.sum(part, axis=0)

    saves[8].start()
    d_h1 = dot_t(rows_ref[:, 1536:3072], w_lo[:, :1536])
    unit, rstd = norm_parts(start_ref[...])
    part, d_gain_1, d_shift_1 = norm_back(d_h1, unit, rstd, gain_1)
    d_start = middle_ref[...] + part
    d_small_ref[2:3] = d_gain_1
    d_small_ref[4:5] = d_shift_1
    masked = 1.0 - t_dot(picker_t_ref[...], jnp.ones((96, 512), BF16))
    d_small_ref[1:2] = col_sum(masked * d_start)
    d_embedded = dot(picker_t_ref[...], low(d_start))
    d_small_ref[0:1] = col_sum(d_embedded)
    d_embedded = low(d_embedded)
    back_ref[:, 768:] = d_embedded
    back_ref[:, :768] = narrow(low(dot_t(d_embedded, w_emb[...])), pads)
    for save in saves:
        save.wait()


def blocks(side, *operands):
    return pl.pallas_call(
        blocks_kernel,
        in_specs=[ANY] + [VMEM] * 9 + [pl.BlockSpec(memory_space=pltpu.SMEM)],
        out_specs=[VMEM] * 6 + [ANY] * 6,
        out_shape=[
            pltpu.HBM((8, 768), F32),
            pltpu.HBM((384, 256), BF16),
            pltpu.HBM((384, 256), BF16),
            shape((96, 1280), BF16),
            pltpu.HBM((16, 512), F32),
            pltpu.HBM((1, 2048), F32),
            pltpu.HBM((96, 6144), BF16),
            pltpu.HBM((96, 2304), BF16),
            pltpu.HBM((6, 96, 256), F32),
            pltpu.HBM((96, 768), F32),
            pltpu.HBM((96, 3072), F32),
            pltpu.HBM((384, 7680), BF16),
        ],
        scratch_shapes=[
            pltpu.VMEM((1, 3072), F32),
            pltpu.VMEM((16, 512), F32),
            pltpu.VMEM((1, 2048), F32),
            pltpu.VMEM((3, 8, 16, 128), F32),
            pltpu.VMEM((1024, 2304), BF16),
            pltpu.VMEM((1024, 768), BF16),
            pltpu.VMEM((1024, 3072), BF16),
            pltpu.VMEM((1024, 512), BF16),
            pltpu.VMEM((1024, 2304), BF16),
            pltpu.VMEM((96, 6144), BF16),
            pltpu.VMEM((96, 2304), BF16),
            pltpu.VMEM((6, 96, 256), F32),
            pltpu.VMEM((96, 768), F32),
            pltpu.VMEM((96, 3072), F32),
            pltpu.VMEM((384, 7680), BF16),
            pltpu.VMEM((512, 2048), BF16),
            pltpu.VMEM((512, 2048), BF16),
            pltpu.VMEM((384, 512), F32),
            pltpu.VMEM((384, 1536), BF16),
            pltpu.VMEM((8, 192, 1024), F32),
            pltpu.VMEM((384, 512), F32),
            pltpu.VMEM((384, 2048), F32),
            pltpu.VMEM((384, 512), BF16),
            pltpu.SemaphoreType.DMA((5,)),
            pltpu.SemaphoreType.DMA((9,)),
        ],
        compiler_params=params(60),
        cost_estimate=pl.CostEstimate(flops=10**4, bytes_accessed=10**3, transcendentals=0),
        name="blocks",
    )(*[in_hbm(a) for a in operands], side)


def enc_back_kernel(
    whole, back_ref, middle_ref, slope_ref, proj3_ref, shares_ref, x_ref, pads_ref, enc_ref,
    d_dec_ref, d_dec_up_ref, dec_theirs_ref, side_ref,
    rows_ref, mine_ref, theirs_ref, small_ref,
    w_down, w_up, w_proj, w_qkv, d_p3_ref, d_up_ref, table_ref, sems,
):
    copies = [
        pltpu.make_async_copy(whole.at[:, pl.ds(at, ref.shape[1])], ref, sems.at[i])
        for i, (at, ref) in enumerate(
            ((C_DOWN, w_down), (C_UP, w_up), (C_PROJ, w_proj), (0, w_qkv))
        )
    ]
    for copy in copies:
        copy.start()
    pads = pads_ref[...]
    g_low = back_ref[:, :768]
    g = g_low.astype(F32)
    unit, rstd = norm_parts(middle_ref[...])
    copies[0].wait()
    for group in range(3):
        cut = slice(1024 * group, 1024 * group + 1024)
        d_hid = dot_t(g_low, w_down[:, 768 * group : 768 * group + 768]) * slope_ref[:, cut]
        d_up_ref[:, cut] = col_sum(d_hid)
        rows_ref[:, cut] = low(d_hid)
    copies[1].wait()
    d_h2 = narrow_wide(dot_t(rows_ref[:, :3072], w_up[...]), pads)
    part, d_gain_2, d_shift_2 = norm_back(d_h2, unit, rstd, enc_ref[1:2])
    d_middle = g + part
    d_mid_low = low(d_middle)
    rows_ref[:, 5376:] = d_mid_low
    copies[2].wait()
    d_att = narrow(low(dot_t(d_mid_low, w_proj[...])), pads)
    for group in range(6):
        cuts = [slice(768 * i + 128 * group, 768 * i + 128 * group + 128) for i in range(3)]
        parts = attend_group_back(
            proj3_ref[:, cuts[0]], proj3_ref[:, cuts[1]], proj3_ref[:, cuts[2]],
            d_att[:, cuts[0]], shares_ref[group], 2, 0.125, 128,
        )
        for third, (cut, part) in enumerate(zip(cuts, parts)):
            d_p3_ref[:, cut] = part
            at = 3072 + 768 * third + 128 * group
            rows_ref[:, at : at + 128] = low(part)
    unit, rstd = norm_parts(x_ref[...].astype(F32))
    copies[3].wait()
    d_h1 = narrow_wide(dot_t(rows_ref[:, 3072:5376], w_qkv[...]), pads)
    part, d_gain_1, d_shift_1 = norm_back(d_h1, unit, rstd, enc_ref[0:1])
    theirs_ref[:384, :256] = dec_theirs_ref[...]
    theirs_ref[:384, 256:] = jnp.zeros((384, 128), BF16)
    sides(low(d_middle + part), side_ref[0], mine_ref, theirs_ref.at[pl.ds(384, 96)])
    vectors = (
        d_gain_1, d_gain_2, d_shift_1, d_shift_2, col_sum(d_p3_ref[:, :768]),
        col_sum(d_p3_ref[:, 1536:]), col_sum(d_middle), col_sum(g),
    )
    row = lax.broadcasted_iota(jnp.int32, (8, 768), 0)
    d_enc = jnp.zeros((8, 768), F32)
    for line, vector in enumerate(vectors):
        d_enc = jnp.where(row == line, vector, d_enc)
    small_out(d_enc, d_up_ref[...], d_dec_ref[...], d_dec_up_ref[...], table_ref)
    small_ref[...] = low(table_ref[...])


def enc_back(side, *operands):
    return pl.pallas_call(
        enc_back_kernel,
        in_specs=[ANY] + [VMEM] * 11 + [pl.BlockSpec(memory_space=pltpu.SMEM)],
        out_specs=[VMEM] * 4,
        out_shape=(
            shape((96, 6144), BF16),
            pltpu.HBM((96, 384), BF16),
            pltpu.HBM((480, 384), BF16),
            shape((128, 128), BF16),
        ),
        scratch_shapes=[
            pltpu.VMEM((1024, 2304), BF16),
            pltpu.VMEM((1024, 3072), BF16),
            pltpu.VMEM((1024, 768), BF16),
            pltpu.VMEM((1024, 2304), BF16),
            pltpu.VMEM((96, 2304), F32),
            pltpu.VMEM((1, 3072), F32),
            pltpu.VMEM((128, 128), F32),
            pltpu.SemaphoreType.DMA((4,)),
        ],
        compiler_params=params(36),
        name="enc_back",
    )(*[in_hbm(a) for a in operands], side)


def widen_t(values, pads_t):
    return jnp.concatenate(
        [low(dot_t(pads_t, values[:, :384])), low(dot_t(pads_t, values[:, 384:]))], axis=0
    )


def spread_t(values, rows_t):
    return jnp.concatenate(
        [low(dot_t(rows_t, values[:, 128 * i : 128 * i + 128])) for i in range(4)], axis=0
    )


def two(own, other, cut):
    return jnp.concatenate([own[:, cut], other[:, cut]], axis=0)


def chunk_copies(stage, place, splits, outs, sems):
    copies = []
    for split, (start, width, first) in enumerate(splits):
        send, keep = outs[2 * split], outs[2 * split + 1]
        for slot, (ref, flips) in enumerate(((send, (first, 2)), (keep, (0, 4 - first)))):
            for line, turn in enumerate(flips):
                copies.append(
                    pltpu.make_async_copy(
                        stage.at[:, place ^ turn, :, pl.ds(start, width)],
                        ref.at[line],
                        sems.at[4 * split + 2 * slot + line],
                    )
                )
    return copies


Y_SPLITS = ((0, 1152, 1), (1152, 1152, 3))
Z_SPLITS = ((0, 768, 1), (768, 768, 3))


def load_rows(sources, start, width, into, sems, at):
    count = sources[0].shape[0]
    return [
        pltpu.make_async_copy(
            source.at[:, pl.ds(start, width)],
            into.at[pl.ds(count * i, count), :],
            sems.at[at + i],
        )
        for i, source in enumerate(sources)
    ]


def dec_tile(tile, core, dec, dec_o, lefts, rights, sems, at):
    place = pl.multiple_of(1024 * tile + 512 * core, 128)
    low_left = 0 if tile == 0 else pl.multiple_of(512 * core, 128)
    loads = []
    for i, (start, into) in enumerate(
        (
            (low_left, lefts.at[0]),
            (1024, lefts.at[1]),
            (1536 + place, rights.at[0]),
            (3584 + place, rights.at[1]),
        )
    ):
        loads += load_rows((dec, dec_o), start, 512, into, sems, at + 2 * i)
    return loads


def dec_tile_grad(lefts, rights, low_t, high_t):
    grad = dot(spread_t(lefts[0], low_t), rights[0])
    return low(grad + dot(spread_t(lefts[1], high_t), rights[1]))


def grad_s_kernel(
    place_ref, m_ref, m_o_ref, pull_ref, pull_o_ref, low_t_ref, high_t_ref, dec, dec_o, enc,
    enc_o,
    sums, stage, sems, enc_act, activated, lefts, rights, load_sems,
):
    core = place_ref[3]
    first = load_rows((enc, enc_o), 0, 3072, enc_act, load_sems, 10)
    for load in first:
        load.start()
    loads = load_rows((dec, dec_o), 5632, 2048, activated, load_sems, 0)
    loads += dec_tile(0, core, dec, dec_o, lefts, rights, load_sems, 2)
    for load in loads:
        load.start()
    for load in first:
        load.wait()
    for group in range(3):
        right = two(m_ref, m_o_ref, pl.ds(pl.multiple_of(384 * core, 128), 384))
        grad = low(t_dot(enc_act[:, 1024 * group : 1024 * group + 1024], right))
        stage[:, :, :, 384 * group : 384 * group + 384] = grad.reshape(4, 4, 64, 384)
    copies = []
    for i, (start, width) in enumerate(((0, 1152), (1152, 1024))):
        cut = pl.ds(start, width)
        copies += [
            pltpu.make_async_copy(stage.at[:, z, :, cut], sums.at[z, :, :, cut], sems.at[4 * i + z])
            for z in range(4)
        ]
    for copy in copies[:4]:
        copy.start()
    right = two(pull_ref, pull_o_ref, pl.ds(pl.multiple_of(256 * core, 128), 256))
    for load in loads:
        load.wait()
    for group in range(2):
        grad = low(t_dot(activated[:, 1024 * group : 1024 * group + 1024], right))
        stage[:, :, :, 1152 + 256 * group : 1408 + 256 * group] = grad.reshape(4, 4, 64, 256)
    grad = dec_tile_grad(lefts, rights, low_t_ref[...], high_t_ref[...])
    stage[:, :, :, 1664:] = grad.reshape(4, 4, 64, 512)
    for copy in copies[4:]:
        copy.start()
    for copy in copies:
        copy.wait()


def grad_y_kernel(
    place_ref, m_ref, m_o_ref, back_ref, back_o_ref, pads_t_ref, low_t_ref, high_t_ref, dec, dec_o,
    enc, enc_o,
    send_p, keep_p, send_q, keep_q, stage, sems, enc_h2, lefts, rights, load_sems,
):
    core = place_ref[3]
    first = load_rows((enc, enc_o), 3072, 1536, enc_h2, load_sems, 8)
    for load in first:
        load.start()
    loads = dec_tile(1, core, dec, dec_o, lefts, rights, load_sems, 0)
    for load in loads:
        load.start()
    copies = chunk_copies(stage, place_ref[1], Y_SPLITS, (send_p, keep_p, send_q, keep_q), sems)
    for load in first:
        load.wait()
    wide = widen_t(enc_h2[:, 768:], pads_t_ref[...])
    for tile in range(3):
        cut = pl.ds(pl.multiple_of(1536 * core + 512 * tile, 128), 512)
        stage[0, :, :, 512 * tile : 512 * tile + 512] = low(
            dot(wide, two(m_ref, m_o_ref, cut))
        ).reshape(4, 256, 512)
        if tile == 2:
            for copy in copies[:4]:
                copy.start()
    right = two(back_ref, back_o_ref, pl.ds(pl.multiple_of(768 + 256 * core, 128), 256))
    wide = widen_t(enc_h2[:, :768], pads_t_ref[...])
    stage[0, :, :, 2048:] = low(dot(wide, right)).reshape(4, 256, 256)
    for load in loads:
        load.wait()
    grad = dec_tile_grad(lefts, rights, low_t_ref[...], high_t_ref[...])
    stage[0, :, :, 1536:2048] = grad.reshape(4, 256, 512)
    for copy in copies[4:]:
        copy.start()
    for copy in copies:
        copy.wait()


def grad_z_kernel(
    place_ref, rows_ref, rows_o_ref, small_ref, pads_t_ref, enc, enc_o,
    send_p, keep_p, send_q, keep_q, stage, sems, enc_h1, load_sems,
):
    core = place_ref[3]
    first = load_rows((enc, enc_o), 4608, 1536, enc_h1, load_sems, 0)
    for load in first:
        load.start()
    copies = chunk_copies(stage, place_ref[0], Z_SPLITS, (send_p, keep_p, send_q, keep_q), sems)
    pads_t = pads_t_ref[...]
    line = lax.broadcasted_iota(jnp.int32, (1024, 128), 0)
    device = lax.broadcasted_iota(jnp.int32, (1024, 128), 1)
    small = dot_t((line == 8 * device + 6).astype(BF16), small_ref[...])
    for load in first:
        load.wait()
    for half, at in enumerate((0, pl.multiple_of(768 * core, 128))):
        left = widen_t(enc_h1[:, pl.ds(at, 768)], pads_t)
        cut = pl.ds(pl.multiple_of(3072 + 1536 * core + 768 * half, 128), 768)
        grad = dot(left, two(rows_ref, rows_o_ref, cut))
        stage[:, :, :, 768 * half : 768 * half + 768] = low(grad).reshape(16, 4, 16, 768)
        if half == 0:
            stage[:, :, :, :128] = low(grad[:, :128] + small).reshape(16, 4, 16, 128)
        for copy in copies[4 * half : 4 * half + 4]:
            copy.start()
    for copy in copies:
        copy.wait()


def grad_call(kernel, name, staged, outs, place, small, large, scratch):
    return pl.pallas_call(
        kernel,
        in_specs=[pl.BlockSpec(memory_space=pltpu.SMEM)] + [VMEM] * len(small) + [ANY] * len(large),
        out_specs=[ANY] * len(outs),
        out_shape=[pltpu.HBM(dims, BF16) for dims in outs],
        scratch_shapes=[
            pltpu.VMEM(staged, BF16),
            pltpu.SemaphoreType.DMA((8,)),
            *scratch,
        ],
        compiler_params=params(22),
        cost_estimate=pl.CostEstimate(flops=10**4, bytes_accessed=10**3, transcendentals=0),
        name=name,
    )(place, *small, *[in_hbm(a) for a in large])


def split_outs(before, splits):
    return [(2, before, 256 // before, width) for _, width, _ in splits for _ in range(2)]


def fold_kernel(keep_ref, got_ref, send_ref):
    send_ref[...] = low(keep_ref[0].astype(F32) + got_ref[0].astype(F32))


def fold(keep, got):
    _, rows, columns = keep.shape
    block = (1, rows // 2, columns)
    return pl.pallas_call(
        fold_kernel,
        grid=(2,),
        in_specs=[pl.BlockSpec(block, lambda i: (1, i, 0))] * 2,
        out_specs=pl.BlockSpec(block[1:], lambda i: (i, 0)),
        out_shape=shape((rows, columns), BF16),
        compiler_params=params(24),
        cost_estimate=pl.CostEstimate(flops=10**4, bytes_accessed=10**3, transcendentals=0),
        name="fold",
    )(in_hbm(keep) if rows * columns > 1 << 18 else keep, got)


def part_kernel(place_ref, *refs, axis, groups, turns):
    place = place_ref[axis]
    outs = refs[sum(groups) :]
    if turns is None:
        parts = [(out, (place + turn) % 4) for out, turn in zip(outs, (1, 3, 2, 0))]
    else:
        parts = [(outs[i // 2].at[i % 2], place ^ turn) for i, turn in enumerate(turns)]
    for out, chunk in parts:
        chunk = pl.ds(chunk, 1)
        at = start = 0
        for count in groups:
            total = None
            for ref in refs[start : start + count]:
                term = (ref[0, :, chunk] if len(ref.shape) == 5 else ref[:, chunk]).astype(F32)
                total = term if total is None else total + term
            start += count
            before, _, after, columns = total.shape
            out[:, at : at + columns] = low(total).reshape(before * after, columns)
            at += columns


def parted(place, axis, before, groups, first=None):
    rows = groups[0][0].shape[-2]
    after = rows // (4 * before)
    operands, specs = [], []
    for array in (a for group in groups for a in group):
        columns = array.shape[-1]
        if array.ndim == 3:
            array = array.reshape(2, before, 4, after, columns)
            kept = rows * columns > 1 << 18 and len(operands) % 3 == 0
            operands.append(in_hbm(array) if kept else array)
            specs.append(pl.BlockSpec((1, before, 4, after, columns), lambda i: (0, 0, 0, 0, 0)))
        else:
            array = array.reshape(before, 4, after, columns)
            operands.append(in_hbm(array) if len(groups[0]) == 1 else array)
            specs.append(VMEM)
    columns = sum(group[0].shape[-1] for group in groups)
    return pl.pallas_call(
        functools.partial(
            part_kernel,
            axis=axis,
            groups=tuple(len(g) for g in groups),
            turns=None if first is None else (first, 2, 0, 4 - first),
        ),
        grid=(1,),
        in_specs=[pl.BlockSpec(memory_space=pltpu.SMEM)] + specs,
        out_specs=[VMEM] * (4 if first is None else 2),
        out_shape=[shape((rows // 4, columns), BF16)] * 4
        if first is None
        else [shape((2, rows // 4, columns), BF16)] * 2,
        compiler_params=params(24),
        cost_estimate=pl.CostEstimate(flops=10**4, bytes_accessed=10**3, transcendentals=0),
        name="parted",
    )(place, *operands)


def last_kernel(place_ref, *refs, groups):
    core = place_ref[3]
    own_ref, other_ref = refs[sum(groups) :]
    at = start = 0
    for count in groups:
        total = None
        for ref in refs[start : start + count]:
            term = ref[...].astype(F32)
            total = term if total is None else total + term
        start += count
        cut = slice(at, at + total.shape[1])
        own_ref[:, cut] = jnp.where(core == 0, total[:8], total[8:])
        other_ref[:, cut] = jnp.where(core == 0, total[8:], total[:8])
        at += total.shape[1]


def last(place, groups):
    columns = sum(group[0].shape[-1] for group in groups)
    operands = [a for group in groups for a in group]
    return pl.pallas_call(
        functools.partial(last_kernel, groups=tuple(len(g) for g in groups)),
        in_specs=[pl.BlockSpec(memory_space=pltpu.SMEM)] + [VMEM] * len(operands),
        out_specs=[VMEM] * 2,
        out_shape=[shape((8, columns), F32)] * 2,
        compiler_params=params(24),
        cost_estimate=pl.CostEstimate(flops=10**4, bytes_accessed=10**3, transcendentals=0),
        name="last",
    )(place, *operands)


def ungrouped(values, groups):
    width = 128 * groups
    line = lax.broadcasted_iota(jnp.int32, (width, width), 0)
    column = lax.broadcasted_iota(jnp.int32, (width, width), 1)
    natural = 8 * groups * ((line & 127) >> 3) + 8 * (line >> 7) + (line & 7)
    turn = (natural == column).astype(BF16)
    high = low(values)
    rest = low(values - high.astype(F32))
    parts = []
    for block in range(8):
        cuts = [slice(1024 * g + 128 * block, 1024 * g + 128 * block + 128) for g in range(groups)]
        both = [jnp.concatenate([v[:, cut] for cut in cuts], axis=1) for v in (high, rest)]
        parts.append(dot(both[0], turn) + dot(both[1], turn))
    return jnp.concatenate(parts, axis=1)


def shards_kernel(
    place_ref, own_ref, got_ref, enc_gains, enc_biases, enc_qkv, enc_proj, enc_up, enc_up_bias,
    enc_down, dec_fill, dec_embed, dec_gains, dec_biases, dec_qkv, dec_proj, dec_up, dec_up_bias,
    dec_down,
):
    core = place_ref[3]

    def halves(start, width):
        own, got = own_ref[:, start : start + width], got_ref[:, start : start + width]
        return jnp.where(core == 0, own, got), jnp.where(core == 0, got, own)

    for group in range(3):
        rows = slice(8 * group, 8 * group + 8)
        enc_down[rows, :384], enc_down[rows, 384:] = halves(384 * group, 384)
    a, b = halves(5760, 256)
    dec_embed[:, :256], dec_embed[:, 256:] = a[:6], b[:6]
    for group in range(2):
        rows = slice(8 * group, 8 * group + 8)
        dec_down[rows, :256], dec_down[rows, 256:] = halves(1152 + 256 * group, 256)
    enc_up[...] = ungrouped(jnp.concatenate(halves(3712, 1536), axis=1), 3)[:6]
    z_all = jnp.concatenate(halves(1664, 512) + halves(5248, 512), axis=1)
    dec_qkv[...] = z_all[:4, :1536]
    dec_proj[...] = z_all[:4, 1536:]
    dec_up[...] = ungrouped(z_all, 2)[4:]
    a, b = halves(2176, 1536)
    enc_qkv[:, :1536] = a[:6]
    enc_qkv[:, 1536:] = b[:6, :768]
    enc_proj[...] = b[:6, 768:]
    flat = a[6:7, :128] + b[6:7, :128]
    at = 0
    smalls = (enc_gains, enc_biases, enc_up_bias, dec_fill, dec_gains, dec_biases, dec_up_bias)
    for ref, (lead, part) in zip(smalls, COUNTS):
        for line in range(lead):
            values = flat[:, at : at + part]
            if ref is dec_biases:
                ref[:, line : line + 1] = values.T
            else:
                ref[line : line + 1, :] = values
            at += part


def shards(place, own, got):
    dims = (
        (2, 6), (6, 6), (6, 2304), (6, 768), (6, 3072), (1, 24), (24, 768), (2, 4), (6, 512),
        (2, 4), (4, 6), (4, 1536), (4, 512), (4, 2048), (1, 16), (16, 512),
    )
    return pl.pallas_call(
        shards_kernel,
        in_specs=[pl.BlockSpec(memory_space=pltpu.SMEM)] + [VMEM] * 2,
        out_specs=[VMEM] * 16,
        out_shape=[shape(d, F32) for d in dims],
        compiler_params=params(24),
        cost_estimate=pl.CostEstimate(flops=10**4, bytes_accessed=10**3, transcendentals=0),
        name="shards",
    )(place, own, got)


def join_kernel(place_ref, dec_mine, enc_mine, got, decoded, x_grad):
    own_at = 2 * place_ref[4]
    decoded[pl.ds(own_at, 2)] = dec_mine[...].reshape(2, 192, 256)
    decoded[pl.ds(2 - own_at, 2)] = got[:384, :256].reshape(2, 192, 256)
    x_grad[pl.ds(own_at, 2)] = enc_mine[...].reshape(2, 48, 384)
    x_grad[pl.ds(2 - own_at, 2)] = got[384:].reshape(2, 48, 384)


def joined(place, *rows):
    return pl.pallas_call(
        join_kernel,
        in_specs=[pl.BlockSpec(memory_space=pltpu.SMEM)] + [VMEM] * 3,
        out_specs=[VMEM] * 2,
        out_shape=[pltpu.HBM((4, 192, 256), BF16), pltpu.HBM((4, 48, 384), BF16)],
        compiler_params=params(16),
        name="joined",
    )(place, *[in_hbm(a) for a in rows])


def pack_kernel(
    enc_gains, enc_biases, enc_qkv, enc_proj, enc_up, enc_up_bias, enc_down, dec_fill, dec_embed,
    dec_gains, dec_biases, dec_qkv, dec_proj, dec_up, dec_up_bias, dec_down, out,
):
    def rows(count, shift=0):
        line = lax.broadcasted_iota(jnp.int32, (8, count), 0)
        return (line == lax.broadcasted_iota(jnp.int32, (8, count), 1) + shift).astype(BF16)

    def group(start, places, source, groups):
        width = 128 * groups
        line = lax.broadcasted_iota(jnp.int32, (width, width), 0)
        column = lax.broadcasted_iota(jnp.int32, (width, width), 1)
        natural = 8 * groups * ((column & 127) >> 3) + 8 * (column >> 7) + (column & 7)
        turn = (natural == line).astype(BF16)
        for block in range(8):
            piece = low(dot(places, source[:, width * block : width * block + width]))
            piece = dot(piece, turn)
            for g in range(groups):
                at = start + 1024 * g + 128 * block
                yield at, piece[:, 128 * g : 128 * g + 128]

    smalls = (enc_gains, enc_biases, enc_up_bias, dec_fill, dec_gains, dec_biases, dec_up_bias)
    flat, at = jnp.zeros((1, 128), F32), 0
    for ref, (lead, part) in zip(smalls, COUNTS):
        values = ref[...]
        line = lax.broadcasted_iota(jnp.int32, (part, 128), 0)
        column = lax.broadcasted_iota(jnp.int32, (part, 128), 1)
        for i in range(lead):
            places = (line + at == column).astype(BF16)
            if ref is dec_biases:
                flat = flat + t_dot(values[:, i : i + 1], places)
            else:
                flat = flat + dot(values[i : i + 1], places)
            at += part
    six, four, raised = rows(6), rows(4), rows(4, 4)
    seventh = lax.broadcasted_iota(jnp.int32, (8, 128), 0) == 6
    out[:, :C_PROJ] = low(dot(six, enc_qkv[...]))
    out[:, :128] = low(dot(six, enc_qkv[:, :128]) + jnp.where(seventh, flat, 0.0))
    out[:, C_PROJ:C_UP] = low(dot(six, enc_proj[...]))
    for at, piece in group(C_UP, six, enc_up, 3):
        out[:, at : at + 128] = low(piece)
    out[:, C_EMB:C_DOWN] = low(dot(six, dec_embed[...]))
    for g in range(3):
        out[:, C_DOWN + 768 * g : C_DOWN + 768 * g + 768] = low(dot(rows(24, -8 * g), enc_down[...]))
    lower = (dec_qkv[:, :1024], jnp.concatenate([dec_qkv[:, 1024:], dec_proj[...]], axis=1))
    lower = [dot(four, values) for values in lower]
    for at, piece in group(0, raised, dec_up, 2):
        half, column = at // 1024, at % 1024
        piece = piece + lower[half][:, column : column + 128]
        out[:, C_Z + at : C_Z + at + 128] = low(piece)
    for g in range(2):
        out[:, C_DDOWN + 512 * g : C_DDOWN + 512 * g + 512] = low(dot(rows(16, -8 * g), dec_down[...]))


def pack(*weights):
    weights = [w[None] if w.ndim == 1 else w for w in weights]
    weights[10] = weights[10].T
    return pl.pallas_call(
        pack_kernel,
        in_specs=[VMEM] * 16,
        out_specs=VMEM,
        out_shape=pltpu.HBM((8, C_ALL), BF16),
        compiler_params=params(24),
        name="pack",
    )(*[in_hbm(w) for w in weights])


def position_table(offset, width):
    half = width // 2
    rates = jnp.exp(jnp.arange(half, dtype=F32) * (-math.log(10000.0) / half))
    angle = offset.astype(F32)[:, None] * rates[None, :]
    return jnp.concatenate([jnp.sin(angle), jnp.cos(angle)], axis=1)


def layout(length_row, order, visible):
    length = order.shape[0]
    ends = jnp.cumsum(length_row, dtype=jnp.int32)
    places = lax.broadcasted_iota(jnp.int32, (length, 1), 0)
    passed = places >= ends[None, :]
    segment = jnp.sum(passed.astype(jnp.int32), axis=1, dtype=jnp.int32)
    offset = places[:, 0] - jnp.sum(
        jnp.where(passed, length_row[None, :], 0), axis=1, dtype=jnp.int32
    )
    shown_pos = order[:visible]
    shown_seg = jnp.sum(
        (shown_pos[:, None] >= ends[None, :]).astype(jnp.int32), axis=1, dtype=jnp.int32
    )
    onehot = places == shown_pos[None, :]
    return (segment, offset, shown_seg, onehot)


def spread_rows(devices, rows, at):
    feature = lax.broadcasted_iota(jnp.int32, (devices * rows, devices * 8), 0)
    place = lax.broadcasted_iota(jnp.int32, (devices * rows, devices * 8), 1)
    return (8 * (feature // rows) + at + feature % rows == place).astype(BF16)


def plans(length_rows, orders):
    segment, offset, shown_seg, onehot = jax.vmap(lambda a, b: layout(a, b, 48))(
        length_rows, orders
    )
    pack = jnp.arange(2, dtype=jnp.int32)[:, None] * 16
    seen = (shown_seg + pack).reshape(96)
    seen_keys = jnp.concatenate([seen, jnp.full((32,), -1, jnp.int32)])
    enc_bias = jnp.where(seen[:, None] == seen_keys[None, :], 0.0, NEVER).astype(F32)
    keys = jnp.concatenate([segment, jnp.full((2, 64), -1, jnp.int32)], axis=1)
    dec_bias = jnp.where(segment[:, :, None] == keys[:, None, :], 0.0, NEVER).astype(F32)
    hot = onehot.astype(BF16)
    hot = hot.transpose(0, 2, 1)
    none = jnp.zeros((48, 192), BF16)
    picker_t = jnp.concatenate(
        [jnp.concatenate([hot[0], none], axis=1), jnp.concatenate([none, hot[1]], axis=1)], axis=0
    )
    table = position_table(offset.reshape(-1), 512)
    return enc_bias, dec_bias, picker_t, table


def place_of(device):
    return device // 2 % 4, device // 32, device // 8 % 4, device % 2


AXES = {"y": (32, 4), "z": (8, 4), "x": (2, 4), "c": (1, 2)}


def flipped(block, axis, turn):
    stride, size = AXES[axis]
    route = []
    for device in range(128):
        at = device // stride % size
        route.append((device, device + ((at ^ turn) - at) * stride))
    return lax.ppermute(block, BOTH, route)


def other_core(block):
    return flipped(block, "c", 1)


def first_sent(axis, outs):
    begun = []
    for split, first in enumerate((1, 3)):
        send, keep = [a.reshape(2, 256, a.shape[-1]) for a in outs[2 * split : 2 * split + 2]]
        begun.append((keep, flipped(send, axis, first)))
    return begun


def second_sent(axis, begun, before):
    groups = []
    for (keep, got), first in zip(begun, (1, 3)):
        onward = fold(after(keep, *before), got)
        groups.append((keep, got, flipped(onward, axis, 4 - first)))
        before = (onward,)
    return groups, before


def passed(block, axis, by):
    stride, size = AXES[axis]
    route = []
    for device in range(128):
        at = device // stride % size
        route.append((device, device + ((at + by) % size - at) * stride))
    return lax.ppermute(block, BOTH, route)


def summed(place, axis, before, groups, earlier):
    *sends, own = parted(after(place, *earlier), "xyz".index(axis), before, groups)
    return [(own, *[passed(send, axis, by) for send, by in zip(sends, (1, 3, 2))])], (own,)


def paired(place, axis, before, groups, first, earlier):
    send, keep = parted(after(place, *earlier), "xyz".index(axis), before, groups, first)
    return (axis, first, keep, flipped(send, axis, first)), (keep,)


def paired_end(begun, earlier):
    axis, first, keep, got = begun
    onward = fold(after(keep, *earlier), got)
    return [(keep, got, flipped(onward, axis, 4 - first))], (onward,)


def after(value, *others):
    return lax.optimization_barrier((value, *others))[0]


def on_device(
    x_vis, lengths, shuffle, enc_gains, enc_biases, enc_qkv, enc_proj, enc_up, enc_up_bias,
    enc_down, dec_fill, dec_embed, dec_gains, dec_biases, dec_qkv, dec_proj, dec_up, dec_up_bias,
    dec_down, cotangent,
):
    section = lax.axis_index("section")
    device = lax.axis_index(BOTH)
    x, y, z, core = place_of(device)
    shard = pack(
        enc_gains, enc_biases, enc_qkv, enc_proj, enc_up, enc_up_bias, enc_down, dec_fill,
        dec_embed, dec_gains, dec_biases, dec_qkv, dec_proj, dec_up, dec_up_bias, dec_down,
    )
    whole = lax.all_gather(shard, BOTH, axis=0, tiled=True)

    packs = 2

    def mine(rows):
        return lax.dynamic_slice_in_dim(rows, section * packs, packs, 0)[:, 0]

    x_rows = mine(x_vis).reshape(packs * 48, 768)
    pull = mine(cotangent).reshape(packs * 192, 512)
    enc_bias, dec_bias, picker_t, table = plans(mine(lengths), mine(shuffle))
    pads = spread_rows(64, 6, 0)
    low_rows, high_rows = spread_rows(32, 4, 0), spread_rows(32, 4, 4)
    spread = (low_rows, high_rows)
    pads_t, low_t, high_t = pads.T, low_rows.T, high_rows.T
    place = jnp.stack([x, y, z, core, section]).astype(jnp.int32)
    side = section.astype(jnp.int32).reshape(1)

    pull_o = other_core(pull)

    ready = (whole, x_rows, pull, pull_o, enc_bias, dec_bias, picker_t, table)
    ready = lax.optimization_barrier((*ready, pads, pads_t, low_t, high_t, *spread))
    whole, x_rows, pull, pull_o, enc_bias, dec_bias, picker_t, table = ready[:8]
    pads, pads_t, low_t, high_t, *spread = ready[8:]
    (
        enc_vec, dec_mine, dec_theirs, back, d_dec, d_dec_up, enc_rows, proj3, shares, middle,
        slope, dec_rows,
    ) = blocks(
        side, whole, x_rows, enc_bias, pads, picker_t, table, dec_bias, pull, *spread
    )
    enc_rows_o = other_core(enc_rows)
    back_o = other_core(back)
    dec_rows_o = other_core(dec_rows)
    back_rows, enc_mine, enc_theirs, small = enc_back(
        side, whole, back, middle, slope, proj3, shares, x_rows, pads, enc_vec, d_dec, d_dec_up,
        dec_theirs,
    )
    back_rows_o = other_core(back_rows)
    (sums_s,) = grad_call(
        grad_s_kernel, "grad_s", (4, 4, 64, 2176), [(4, 4, 64, 2176)], after(place, back_rows),
        (back, back_o, pull, pull_o, low_t, high_t),
        (dec_rows, dec_rows_o, enc_rows, enc_rows_o),
        (
            pltpu.VMEM((192, 3072), BF16),
            pltpu.VMEM((768, 2048), BF16),
            pltpu.VMEM((2, 768, 512), BF16),
            pltpu.VMEM((2, 768, 512), BF16),
            pltpu.SemaphoreType.DMA((12,)),
        ),
    )
    sums_y = grad_call(
        grad_y_kernel, "grad_y", (1, 4, 256, 2304), split_outs(1, Y_SPLITS), after(place, sums_s),
        (back_rows, back_rows_o, back, back_o, pads_t, low_t, high_t),
        (dec_rows, dec_rows_o, enc_rows, enc_rows_o),
        (
            pltpu.VMEM((192, 1536), BF16),
            pltpu.VMEM((2, 768, 512), BF16),
            pltpu.VMEM((2, 768, 512), BF16),
            pltpu.SemaphoreType.DMA((10,)),
        ),
    )
    sums_z = grad_call(
        grad_z_kernel, "grad_z", (16, 4, 16, 1536), split_outs(16, Z_SPLITS),
        after(place, *sums_y), (back_rows, back_rows_o, small, pads_t), (enc_rows, enc_rows_o),
        (pltpu.VMEM((192, 1536), BF16), pltpu.SemaphoreType.DMA((2,))),
    )

    sums_s = lax.psum_scatter(
        sums_s.reshape(64, 16, 2176), "z", scatter_dimension=0, tiled=True
    ).reshape(256, 2176)
    sums_y = first_sent("y", sums_y)
    sums_z = first_sent("x", sums_z)
    sums_y, done = second_sent("y", sums_y, sums_z[0][:1])
    sums_z, done = second_sent("x", sums_z, done)
    sums_s, done = paired(place, "x", 4, [(sums_s,)], 1, done)
    sums_y, done = paired(place, "z", 1, sums_y, 1, done)
    sums_z, done = paired(place, "z", 4, sums_z, 3, done)
    sums_s, done = paired_end(sums_s, done)
    sums_y, done = paired_end(sums_y, done)
    sums_z, done = paired_end(sums_z, done)
    sums_sz, done = summed(place, "y", 1, sums_s + sums_z, done)
    sums_y, done = summed(place, "x", 1, sums_y, done)
    decoded, x_grad = joined(place, dec_mine, enc_mine, flipped(enc_theirs, "y", 2))
    own, other = last(after(place, decoded, x_grad), sums_sz + sums_y)
    grads = shards(place, own, other_core(other))
    grads = [g[0] if g.shape[0] == 1 else g for g in grads]
    grads[10] = grads[10].T
    return (decoded[:, None], x_grad[:, None], *grads)


def solution(mesh):
    mesh = Mesh(mesh.devices.reshape(2, 2, 4, 4, 2), BOTH)
    rows = P(None, DP, None, None)
    ids = P(None, DP, None)
    wide = P(None, BOTH)
    tall = P(BOTH, None)
    flat = P(BOTH)
    in_specs = (rows, ids, ids, wide, wide, tall, tall, tall, flat, tall, wide, tall, wide, wide)
    in_specs += (tall, tall, tall, flat, tall, rows)
    out_rows = P(None, DP, None, "section")
    out_specs = (out_rows, out_rows, wide, wide, tall, tall, tall, flat, tall, wide, tall, wide)
    out_specs += (wide, tall, tall, tall, flat, tall)
    return jax.shard_map(
        on_device, mesh=mesh, in_specs=in_specs, out_specs=out_specs, check_vma=False
    )
```

```python
import functools
import math

import jax
import jax.numpy as jnp
from jax import lax
from jax.experimental import pallas as pl
from jax.experimental.pallas import tpu as pltpu
from jax.sharding import Mesh
from jax.sharding import PartitionSpec as P

H_ENC = 12
H_DEC = 16
DP = ("y_low", "z", "x", "core")
BOTH = ("section", *DP)
Y_AXIS = ("section", "y_low")
F32 = jnp.float32
BF16 = jnp.bfloat16
EPS = 1e-06
NEVER = -1e30
MIB = 1 << 20

C_PROJ = 2304
C_UP = 3072
C_EMB = 6144
C_DOWN = 6656
C_Z = 8960
C_DDOWN = 11008
C_ALL = 12032
COUNTS = ((2, 6), (6, 6), (1, 24), (2, 4), (2, 4), (6, 4), (1, 16))


def dot(left, right):
    return jnp.dot(left, right, preferred_element_type=F32)


def dot_t(left, right):
    return lax.dot_general(left, right, (((1,), (1,)), ((), ())), preferred_element_type=F32)


def t_dot(left, right):
    return lax.dot_general(left, right, (((0,), (0,)), ((), ())), preferred_element_type=F32)


def low(values):
    return values.astype(BF16)


def norm_parts(values):
    mean = jnp.mean(values, axis=-1, keepdims=True)
    centred = values - mean
    rstd = lax.rsqrt(jnp.mean(centred * centred, axis=-1, keepdims=True) + EPS)
    return centred * rstd, rstd


def norm_back(d_normed, unit, rstd, gain):
    scaled = d_normed * gain
    part = scaled - jnp.mean(scaled, axis=-1, keepdims=True)
    part = (part - unit * jnp.mean(scaled * unit, axis=-1, keepdims=True)) * rstd
    return part, col_sum(d_normed * unit), col_sum(d_normed)


def col_sum(values):
    return jnp.sum(values, axis=0, keepdims=True)


def gelu_pair(hidden):
    share = 0.5 + 0.5 * lax.erf(hidden * math.sqrt(0.5))
    slope = share + hidden * (jnp.exp(-0.5 * hidden * hidden) * (1.0 / math.sqrt(2.0 * math.pi)))
    return hidden * share, slope


def head_stack(block, heads, rows):
    size = 128 // heads
    lane = lax.broadcasted_iota(jnp.int32, (1, 128), 1)
    fill = jnp.zeros((rows - block.shape[0], 128), BF16)
    parts = []
    for head in range(heads):
        own = ((lane >= head * size) & (lane < (head + 1) * size)).astype(BF16)
        parts += [block * own, fill]
    return jnp.concatenate(parts, axis=0)


def head_unstack(stack, heads, rows, count):
    size = 128 // heads
    lane = lax.broadcasted_iota(jnp.int32, (1, 128), 1)
    total = None
    for head in range(heads):
        own = ((lane >= head * size) & (lane < (head + 1) * size)).astype(F32)
        part = stack[head * rows : head * rows + count] * own
        total = part if total is None else total + part
    return total


def attend_group(query, key, value, bias, heads, scale, shares_out):
    rows = bias.shape[1]
    scores = dot_t(query, head_stack(key, heads, rows))
    parts = []
    for head in range(heads):
        s = scores[:, head * rows : (head + 1) * rows] * scale + bias
        powers = jnp.exp(s - jnp.max(s, axis=-1, keepdims=True))
        parts.append(powers / jnp.sum(powers, axis=-1, keepdims=True))
    shares = jnp.concatenate(parts, axis=1)
    shares_out[...] = shares
    return dot(low(shares), head_stack(value, heads, rows))


def attend_group_back(query, key, value, d_out, shares, heads, scale, rows):
    count = key.shape[0]
    d_shares = dot_t(d_out, head_stack(value, heads, rows))
    parts = []
    for head in range(heads):
        cut = slice(head * rows, (head + 1) * rows)
        p, dp = shares[:, cut], d_shares[:, cut]
        parts.append(low(p * (dp - jnp.sum(dp * p, axis=-1, keepdims=True))))
    d_scores = jnp.concatenate(parts, axis=1)
    d_query = dot(d_scores, head_stack(key, heads, rows)) * scale
    d_key = head_unstack(t_dot(d_scores, query), heads, rows, count) * scale
    d_value = head_unstack(t_dot(low(shares), d_out), heads, rows, count)
    return d_query, d_key, d_value


def widen(values, pads):
    return jnp.concatenate(
        [low(dot(values[:, :384], pads)), low(dot(values[:, 384:], pads))], axis=1
    )


def narrow(values, pads):
    return jnp.concatenate(
        [low(dot_t(values[:, :512], pads)), low(dot_t(values[:, 512:], pads))], axis=1
    )


def narrow_wide(values, pads):
    high = low(values)
    rest = low(values - high.astype(F32))
    return jnp.concatenate(
        [
            dot_t(high[:, :512], pads) + dot_t(rest[:, :512], pads),
            dot_t(high[:, 512:], pads) + dot_t(rest[:, 512:], pads),
        ],
        axis=1,
    )


PARTS = (6, 4, 8)


def small_rows():
    plan, at = [], 0
    for family, (lead, part) in enumerate(COUNTS):
        for value in range(lead * part):
            if part >= 16:
                plan.append((2, value // 8 + (3 if family == 6 else 0), value % 8, at))
            else:
                first = 2 if family == 1 else (0, 0, 0, 0, 2, 4)[family]
                kind = 0 if family < 2 else 1
                plan.append((kind, first + value // part, value % part, at))
            at += 1
    return plan


def strewn(kind, value):
    part = PARTS[kind]
    device = lax.broadcasted_iota(jnp.int32, (128, 128 * part), 0)
    column = lax.broadcasted_iota(jnp.int32, (128, 128 * part), 1)
    return (column == part * device + value).astype(BF16)


def small_in(columns, rows_ref, enc_ref, enc_up_ref, dec_ref, dec_up_ref):
    line = lax.broadcasted_iota(jnp.int32, (1024, 128), 0)
    device = lax.broadcasted_iota(jnp.int32, (1024, 128), 1)
    table = t_dot(columns, (line == 8 * device + 6).astype(BF16))
    rows_ref[...] = jnp.zeros_like(rows_ref)
    for kind, row, value, place in small_rows():
        rows_ref[kind, value, row : row + 1, :] = table[place : place + 1]
    whole = []
    for kind, part in enumerate(PARTS):
        total = None
        for value in range(part):
            term = dot(low(rows_ref[kind, value]), strewn(kind, value))
            total = term if total is None else total + term
        whole.append(total)
    enc_ref[...] = whole[0][:8]
    dec_ref[...] = whole[1]
    for group in range(3):
        enc_up_ref[:, 1024 * group : 1024 * group + 1024] = whole[2][group : group + 1]
    for group in range(2):
        dec_up_ref[:, 1024 * group : 1024 * group + 1024] = whole[2][3 + group : 4 + group]


def small_out(enc, enc_up, dec, dec_up, table_ref):
    ups = [enc_up[:, 1024 * g : 1024 * g + 1024] for g in range(3)]
    ups += [dec_up[:, 1024 * g : 1024 * g + 1024] for g in range(2)]
    ups += [jnp.zeros((3, 1024), F32)]
    whole = (low(enc), low(dec), low(jnp.concatenate(ups, axis=0)))
    parts = [
        [dot_t(whole[kind], strewn(kind, value)) for value in range(part)]
        for kind, part in enumerate(PARTS)
    ]
    for kind, row, value, place in small_rows():
        table_ref[place : place + 1, :] = parts[kind][value][row : row + 1]


VMEM = pl.BlockSpec(memory_space=pltpu.VMEM)
ANY = pl.BlockSpec(memory_space=pl.ANY)


def shape(dims, kind):
    return jax.ShapeDtypeStruct(dims, kind)


def in_hbm(array):
    return pltpu.with_memory_space_constraint(array, pltpu.HBM)


def params(limit):
    return pltpu.CompilerParams(vmem_limit_bytes=limit * MIB)


def sides(rows, side, mine_ref, theirs_ref):
    half = rows.shape[1] // 2
    mine_ref[...] = jnp.where(side == 0, rows[:, :half], rows[:, half:])
    theirs_ref[...] = jnp.where(side == 0, rows[:, half:], rows[:, :half])


DEC_SCALE = 1.0 / math.sqrt(32)


def blocks_kernel(
    whole, x_ref, enc_bias_ref, pads_ref, picker_t_ref, table_ref, bias_ref, pull_ref, low_ref,
    high_ref, side_ref,
    enc_ref, mine_ref, theirs_ref, back_ref, d_small_ref, d_up_small_ref, enc_rows_out,
    enc_proj3_out, enc_shares_out, enc_middle_out, enc_slope_out, rows_out,
    enc_up_ref, dec_ref, dec_up_ref, small_ref, w_qkv, w_proj, w_up, w_emb, w_down,
    enc_rows, enc_proj3_ref, enc_shares_ref, enc_middle_ref, enc_slope_ref,
    rows_ref, w_lo, w_hi, start_ref, proj3_ref, shares_ref, middle_ref, slope_ref, d_att_ref,
    sems, out_sems,
):
    copies = [
        pltpu.make_async_copy(whole.at[:, pl.ds(at, ref.shape[1])], ref, sems.at[i])
        for i, (at, ref) in enumerate(
            ((0, w_qkv), (C_PROJ, w_proj), (C_UP, w_up), (C_DOWN, w_down), (C_EMB, w_emb))
        )
    ]
    for copy in copies:
        copy.start()
    pads = pads_ref[...]
    x = x_ref[...].astype(F32)
    unit, _ = norm_parts(x)
    copies[0].wait()
    small_in(w_qkv[:, :128], small_ref, enc_ref, enc_up_ref, dec_ref, dec_up_ref)
    h1 = low(unit * enc_ref[0:1] + enc_ref[2:3])
    enc_rows[:, 4608:5376] = h1
    wide = widen(h1, pads)
    for third in range(3):
        cut = slice(768 * third, 768 * third + 768)
        part = dot(wide, w_qkv[:, cut])
        if third != 1:
            part = part + (enc_ref[4:5] if third == 0 else enc_ref[5:6])
        enc_proj3_ref[:, cut] = low(part)
    bias = enc_bias_ref[...]
    for group in range(6):
        cuts = [slice(768 * i + 128 * group, 768 * i + 128 * group + 128) for i in range(3)]
        out = attend_group(
            enc_proj3_ref[:, cuts[0]], enc_proj3_ref[:, cuts[1]], enc_proj3_ref[:, cuts[2]],
            bias, 2, 0.125, enc_shares_ref.at[group],
        )
        enc_rows[:, 5376 + 128 * group : 5504 + 128 * group] = low(out)
    copies[1].wait()
    middle = x + dot(widen(enc_rows[:, 5376:], pads), w_proj[...]) + enc_ref[6:7]
    enc_middle_ref[...] = middle
    unit, _ = norm_parts(middle)
    h2 = low(unit * enc_ref[1:2] + enc_ref[3:4])
    enc_rows[:, 3840:4608] = h2
    wide = widen(h2, pads)
    copies[2].wait()

    @pl.loop(0, 6)
    def _(tile):
        cut = pl.ds(pl.multiple_of(tile * 512, 512), 512)
        value, slope = gelu_pair(dot(wide, w_up[:, cut]) + enc_up_ref[:, cut])
        enc_rows[:, cut] = low(value)
        enc_slope_ref[:, cut] = slope

    dec_weights = pltpu.make_async_copy(
        whole.at[:, pl.ds(C_Z, 3072)], w_up, sems.at[2]
    )
    dec_weights.start()
    copies[3].wait()
    out = middle + enc_ref[7:8]
    for group in range(3):
        out = out + dot(
            enc_rows[:, 1024 * group : 1024 * group + 1024],
            w_down[:, 768 * group : 768 * group + 768],
        )
    encoded = low(out)
    enc_rows[:, 3072:3840] = encoded
    copies[4].wait()
    embedded = low(dot(widen(encoded, pads), w_emb[...]) + dec_ref[0:1])

    attended_ref, d_hid_ref = rows_ref.at[:, pl.ds(512, 512)], rows_ref.at[:, pl.ds(3584, 2048)]
    activated_ref = rows_ref.at[:, pl.ds(5632, 2048)]
    w_z, w_ddown = w_up.at[:, pl.ds(0, 2048)], w_up.at[:, pl.ds(2048, 1024)]
    saves = [
        pltpu.make_async_copy(source, into, out_sems.at[i])
        for i, (source, into) in enumerate(
            (
                (enc_rows, enc_rows_out),
                (enc_proj3_ref, enc_proj3_out),
                (enc_shares_ref, enc_shares_out),
                (enc_middle_ref, enc_middle_out),
                (enc_slope_ref, enc_slope_out),
            )
        )
    ]
    for start, width in ((0, 1536), (5632, 2048), (3584, 2048), (1536, 2048)):
        cut = pl.ds(start, width)
        saves.append(
            pltpu.make_async_copy(rows_ref.at[:, cut], rows_out.at[:, cut], out_sems.at[len(saves)])
        )
    for save in saves[:5]:
        save.start()
    gain_1, gain_2 = dec_ref[2:3], dec_ref[3:4]
    picker_t = picker_t_ref[...]
    masked = 1.0 - t_dot(picker_t, jnp.ones((96, 512), BF16))
    start = t_dot(picker_t, embedded) + masked * dec_ref[1:2] + table_ref[...]
    start_ref[...] = start
    unit, _ = norm_parts(start)
    h1 = low(unit * gain_1 + dec_ref[4:5])
    rows_ref[:, :512] = h1
    dec_weights.wait()

    @pl.loop(0, 4)
    def _(block):
        into = pl.ds(pl.multiple_of(block * 128, 128), 128)
        source = pl.ds(pl.multiple_of(block * 256, 256), 256)
        for half in range(2):
            cut = slice(1024 * half, 1024 * half + 1024)
            rows = w_z[source, cut]
            w_lo[into, cut] = low(dot(low_ref[...], rows))
            w_hi[into, cut] = low(dot(high_ref[...], rows))

    for third in range(3):
        cut = slice(512 * third, 512 * third + 512)
        part = dot(h1, w_lo[:, cut])
        if third != 1:
            part = part + (dec_ref[6:7] if third == 0 else dec_ref[7:8])
        proj3_ref[:, cut] = low(part)

    @pl.loop(0, 8, unroll=4)
    def _(step):
        pack, group = step // 4, step % 4
        rows = pl.ds(pl.multiple_of(pack * 192, 192), 192)
        cuts = [pl.ds(pl.multiple_of(512 * i + 128 * group, 128), 128) for i in range(3)]
        out = attend_group(
            proj3_ref[rows, cuts[0]], proj3_ref[rows, cuts[1]], proj3_ref[rows, cuts[2]],
            bias_ref[pack], 4, DEC_SCALE, shares_ref.at[step],
        )
        attended_ref[rows, cuts[0]] = low(out)

    middle = start + dot(attended_ref[...], w_lo[:, 1536:]) + dec_ref[8:9]
    middle_ref[...] = middle
    unit_2, rstd_2 = norm_parts(middle)
    h2 = low(unit_2 * gain_2 + dec_ref[5:6])
    rows_ref[:, 1024:1536] = h2
    saves[5].start()

    @pl.loop(0, 4)
    def _(tile):
        cut = pl.ds(pl.multiple_of(tile * 512, 512), 512)
        value, slope = gelu_pair(dot(h2, w_hi[:, cut]) + dec_up_ref[:, cut])
        activated_ref[:, cut] = low(value)
        slope_ref[:, cut] = slope

    out = middle + dec_ref[9:10]
    for group in range(2):
        out = out + dot(
            activated_ref[:, 1024 * group : 1024 * group + 1024],
            w_ddown[:, 512 * group : 512 * group + 512],
        )
    saves[6].start()
    sides(low(out), side_ref[0], mine_ref, theirs_ref)

    g_low = pull_ref[...]
    for tile in range(4):
        group, rows = tile // 2, slice(512 * (tile % 2), 512 * (tile % 2) + 512)
        cut = slice(512 * tile, 512 * tile + 512)
        d_hid = dot_t(g_low, w_ddown[rows, 512 * group : 512 * group + 512]) * slope_ref[:, cut]
        d_up_small_ref[:, cut] = col_sum(d_hid)
        d_hid_ref[:, cut] = low(d_hid)
    saves[7].start()
    d_h2 = dot_t(d_hid_ref[...], w_hi[...])
    part, d_gain_2, d_shift_2 = norm_back(d_h2, unit_2, rstd_2, gain_2)
    g = g_low.astype(F32)
    d_mid = g + part
    d_mid_low = low(d_mid)
    d_att = low(dot_t(d_mid_low, w_lo[:, 1536:]))
    d_small_ref[...] = jnp.zeros_like(d_small_ref)
    d_small_ref[3:4] = d_gain_2
    d_small_ref[5:6] = d_shift_2
    d_small_ref[8:9] = col_sum(d_mid)
    d_small_ref[9:10] = col_sum(g)
    rows_ref[:, 3072:3584] = d_mid_low
    middle_ref[...] = d_mid
    d_att_ref[...] = d_att

    @pl.loop(0, 8, unroll=4)
    def _(step):
        pack, group = step // 4, step % 4
        rows = pl.ds(pl.multiple_of(pack * 192, 192), 192)
        cuts = [pl.ds(pl.multiple_of(512 * i + 128 * group, 128), 128) for i in range(3)]
        parts = attend_group_back(
            proj3_ref[rows, cuts[0]], proj3_ref[rows, cuts[1]], proj3_ref[rows, cuts[2]],
            d_att_ref[rows, cuts[0]], shares_ref[step], 4, DEC_SCALE, 256,
        )
        for i, part in enumerate(parts):
            at = pl.multiple_of(1536 + 512 * i + 128 * group, 128)
            rows_ref[rows, pl.ds(at, 128)] = low(part)
            if i != 1:
                d_small_ref[6 + i // 2, cuts[0]] += jnp.sum(part, axis=0)

    saves[8].start()
    d_h1 = dot_t(rows_ref[:, 1536:3072], w_lo[:, :1536])
    unit, rstd = norm_parts(start_ref[...])
    part, d_gain_1, d_shift_1 = norm_back(d_h1, unit, rstd, gain_1)
    d_start = middle_ref[...] + part
    d_small_ref[2:3] = d_gain_1
    d_small_ref[4:5] = d_shift_1
    masked = 1.0 - t_dot(picker_t_ref[...], jnp.ones((96, 512), BF16))
    d_small_ref[1:2] = col_sum(masked * d_start)
    d_embedded = dot(picker_t_ref[...], low(d_start))
    d_small_ref[0:1] = col_sum(d_embedded)
    d_embedded = low(d_embedded)
    back_ref[:, 768:] = d_embedded
    back_ref[:, :768] = narrow(low(dot_t(d_embedded, w_emb[...])), pads)
    for save in saves:
        save.wait()


def blocks(side, *operands):
    return pl.pallas_call(
        blocks_kernel,
        in_specs=[ANY] + [VMEM] * 9 + [pl.BlockSpec(memory_space=pltpu.SMEM)],
        out_specs=[VMEM] * 6 + [ANY] * 6,
        out_shape=[
            pltpu.HBM((8, 768), F32),
            pltpu.HBM((384, 256), BF16),
            pltpu.HBM((384, 256), BF16),
            shape((96, 1280), BF16),
            pltpu.HBM((16, 512), F32),
            pltpu.HBM((1, 2048), F32),
            pltpu.HBM((96, 6144), BF16),
            pltpu.HBM((96, 2304), BF16),
            pltpu.HBM((6, 96, 256), F32),
            pltpu.HBM((96, 768), F32),
            pltpu.HBM((96, 3072), F32),
            pltpu.HBM((384, 7680), BF16),
        ],
        scratch_shapes=[
            pltpu.VMEM((1, 3072), F32),
            pltpu.VMEM((16, 512), F32),
            pltpu.VMEM((1, 2048), F32),
            pltpu.VMEM((3, 8, 16, 128), F32),
            pltpu.VMEM((1024, 2304), BF16),
            pltpu.VMEM((1024, 768), BF16),
            pltpu.VMEM((1024, 3072), BF16),
            pltpu.VMEM((1024, 512), BF16),
            pltpu.VMEM((1024, 2304), BF16),
            pltpu.VMEM((96, 6144), BF16),
            pltpu.VMEM((96, 2304), BF16),
            pltpu.VMEM((6, 96, 256), F32),
            pltpu.VMEM((96, 768), F32),
            pltpu.VMEM((96, 3072), F32),
            pltpu.VMEM((384, 7680), BF16),
            pltpu.VMEM((512, 2048), BF16),
            pltpu.VMEM((512, 2048), BF16),
            pltpu.VMEM((384, 512), F32),
            pltpu.VMEM((384, 1536), BF16),
            pltpu.VMEM((8, 192, 1024), F32),
            pltpu.VMEM((384, 512), F32),
            pltpu.VMEM((384, 2048), F32),
            pltpu.VMEM((384, 512), BF16),
            pltpu.SemaphoreType.DMA((5,)),
            pltpu.SemaphoreType.DMA((9,)),
        ],
        compiler_params=params(60),
        cost_estimate=pl.CostEstimate(flops=10**4, bytes_accessed=10**3, transcendentals=0),
        name="blocks",
    )(*[in_hbm(a) for a in operands], side)


def enc_back_kernel(
    whole, back_ref, middle_ref, slope_ref, proj3_ref, shares_ref, x_ref, pads_ref, enc_ref,
    d_dec_ref, d_dec_up_ref, dec_theirs_ref, side_ref,
    rows_ref, mine_ref, theirs_ref, small_ref,
    w_down, w_up, w_proj, w_qkv, d_p3_ref, d_up_ref, table_ref, sems,
):
    copies = [
        pltpu.make_async_copy(whole.at[:, pl.ds(at, ref.shape[1])], ref, sems.at[i])
        for i, (at, ref) in enumerate(
            ((C_DOWN, w_down), (C_UP, w_up), (C_PROJ, w_proj), (0, w_qkv))
        )
    ]
    for copy in copies:
        copy.start()
    pads = pads_ref[...]
    g_low = back_ref[:, :768]
    g = g_low.astype(F32)
    unit, rstd = norm_parts(middle_ref[...])
    copies[0].wait()
    for group in range(3):
        cut = slice(1024 * group, 1024 * group + 1024)
        d_hid = dot_t(g_low, w_down[:, 768 * group : 768 * group + 768]) * slope_ref[:, cut]
        d_up_ref[:, cut] = col_sum(d_hid)
        rows_ref[:, cut] = low(d_hid)
    copies[1].wait()
    d_h2 = narrow_wide(dot_t(rows_ref[:, :3072], w_up[...]), pads)
    part, d_gain_2, d_shift_2 = norm_back(d_h2, unit, rstd, enc_ref[1:2])
    d_middle = g + part
    d_mid_low = low(d_middle)
    rows_ref[:, 5376:] = d_mid_low
    copies[2].wait()
    d_att = narrow(low(dot_t(d_mid_low, w_proj[...])), pads)
    for group in range(6):
        cuts = [slice(768 * i + 128 * group, 768 * i + 128 * group + 128) for i in range(3)]
        parts = attend_group_back(
            proj3_ref[:, cuts[0]], proj3_ref[:, cuts[1]], proj3_ref[:, cuts[2]],
            d_att[:, cuts[0]], shares_ref[group], 2, 0.125, 128,
        )
        for third, (cut, part) in enumerate(zip(cuts, parts)):
            d_p3_ref[:, cut] = part
            at = 3072 + 768 * third + 128 * group
            rows_ref[:, at : at + 128] = low(part)
    unit, rstd = norm_parts(x_ref[...].astype(F32))
    copies[3].wait()
    d_h1 = narrow_wide(dot_t(rows_ref[:, 3072:5376], w_qkv[...]), pads)
    part, d_gain_1, d_shift_1 = norm_back(d_h1, unit, rstd, enc_ref[0:1])
    theirs_ref[:384, :256] = dec_theirs_ref[...]
    theirs_ref[:384, 256:] = jnp.zeros((384, 128), BF16)
    sides(low(d_middle + part), side_ref[0], mine_ref, theirs_ref.at[pl.ds(384, 96)])
    vectors = (
        d_gain_1, d_gain_2, d_shift_1, d_shift_2, col_sum(d_p3_ref[:, :768]),
        col_sum(d_p3_ref[:, 1536:]), col_sum(d_middle), col_sum(g),
    )
    row = lax.broadcasted_iota(jnp.int32, (8, 768), 0)
    d_enc = jnp.zeros((8, 768), F32)
    for line, vector in enumerate(vectors):
        d_enc = jnp.where(row == line, vector, d_enc)
    small_out(d_enc, d_up_ref[...], d_dec_ref[...], d_dec_up_ref[...], table_ref)
    small_ref[...] = low(table_ref[...])


def enc_back(side, *operands):
    return pl.pallas_call(
        enc_back_kernel,
        in_specs=[ANY] + [VMEM] * 11 + [pl.BlockSpec(memory_space=pltpu.SMEM)],
        out_specs=[VMEM] * 4,
        out_shape=(
            shape((96, 6144), BF16),
            pltpu.HBM((96, 384), BF16),
            pltpu.HBM((480, 384), BF16),
            shape((128, 128), BF16),
        ),
        scratch_shapes=[
            pltpu.VMEM((1024, 2304), BF16),
            pltpu.VMEM((1024, 3072), BF16),
            pltpu.VMEM((1024, 768), BF16),
            pltpu.VMEM((1024, 2304), BF16),
            pltpu.VMEM((96, 2304), F32),
            pltpu.VMEM((1, 3072), F32),
            pltpu.VMEM((128, 128), F32),
            pltpu.SemaphoreType.DMA((4,)),
        ],
        compiler_params=params(36),
        name="enc_back",
    )(*[in_hbm(a) for a in operands], side)


def widen_t(values, pads_t):
    return jnp.concatenate(
        [low(dot_t(pads_t, values[:, :384])), low(dot_t(pads_t, values[:, 384:]))], axis=0
    )


def spread_t(values, rows_t):
    return jnp.concatenate(
        [low(dot_t(rows_t, values[:, 128 * i : 128 * i + 128])) for i in range(4)], axis=0
    )


def two(own, other, cut):
    return jnp.concatenate([own[:, cut], other[:, cut]], axis=0)


def chunk_copies(stage, place, splits, outs, sems):
    copies = []
    for split, (start, width, first) in enumerate(splits):
        send, keep = outs[2 * split], outs[2 * split + 1]
        for slot, (ref, flips) in enumerate(((send, (first, 2)), (keep, (0, 4 - first)))):
            for line, turn in enumerate(flips):
                copies.append(
                    pltpu.make_async_copy(
                        stage.at[:, place ^ turn, :, pl.ds(start, width)],
                        ref.at[line],
                        sems.at[4 * split + 2 * slot + line],
                    )
                )
    return copies


Y_SPLITS = ((0, 1024, 1), (1024, 1024, 3))
Z_SPLITS = ((0, 896, 1), (896, 896, 3))


def load_rows(sources, start, width, into, sems, at):
    count = sources[0].shape[0]
    return [
        pltpu.make_async_copy(
            source.at[:, pl.ds(start, width)],
            into.at[pl.ds(count * i, count), :],
            sems.at[at + i],
        )
        for i, source in enumerate(sources)
    ]


def dec_tile(tile, core, dec, dec_o, lefts, rights, sems, at):
    place = pl.multiple_of(1024 * tile + 512 * core, 128)
    low_left = 0 if tile == 0 else pl.multiple_of(512 * core, 128)
    loads = []
    for i, (start, into) in enumerate(
        (
            (low_left, lefts.at[0]),
            (1024, lefts.at[1]),
            (1536 + place, rights.at[0]),
            (3584 + place, rights.at[1]),
        )
    ):
        loads += load_rows((dec, dec_o), start, 512, into, sems, at + 2 * i)
    return loads


def dec_tile_grad(lefts, rights, low_t, high_t):
    grad = dot(spread_t(lefts[0], low_t), rights[0])
    return low(grad + dot(spread_t(lefts[1], high_t), rights[1]))


def grad_s_kernel(
    place_ref, m_ref, m_o_ref, pull_ref, pull_o_ref, low_t_ref, high_t_ref, dec, dec_o, enc,
    enc_o,
    sums, stage, sems, enc_act, activated, lefts, rights, load_sems,
):
    core = place_ref[3]
    first = load_rows((enc, enc_o), 0, 3072, enc_act, load_sems, 10)
    for load in first:
        load.start()
    loads = load_rows((dec, dec_o), 5632, 2048, activated, load_sems, 0)
    loads += dec_tile(0, core, dec, dec_o, lefts, rights, load_sems, 2)
    for load in loads:
        load.start()
    for load in first:
        load.wait()
    for group in range(3):
        right = two(m_ref, m_o_ref, pl.ds(pl.multiple_of(384 * core, 128), 384))
        grad = low(t_dot(enc_act[:, 1024 * group : 1024 * group + 1024], right))
        stage[:, :, :, 384 * group : 384 * group + 384] = grad.reshape(4, 4, 64, 384)
    copies = []
    for i, (start, width) in enumerate(((0, 1152), (1152, 1024))):
        cut = pl.ds(start, width)
        copies += [
            pltpu.make_async_copy(stage.at[:, z, :, cut], sums.at[z, :, :, cut], sems.at[4 * i + z])
            for z in range(4)
        ]
    for copy in copies[:4]:
        copy.start()
    right = two(pull_ref, pull_o_ref, pl.ds(pl.multiple_of(256 * core, 128), 256))
    for load in loads:
        load.wait()
    for group in range(2):
        grad = low(t_dot(activated[:, 1024 * group : 1024 * group + 1024], right))
        stage[:, :, :, 1152 + 256 * group : 1408 + 256 * group] = grad.reshape(4, 4, 64, 256)
    grad = dec_tile_grad(lefts, rights, low_t_ref[...], high_t_ref[...])
    stage[:, :, :, 1664:] = grad.reshape(4, 4, 64, 512)
    for copy in copies[4:]:
        copy.start()
    for copy in copies:
        copy.wait()


def grad_y_kernel(
    place_ref, m_ref, m_o_ref, pads_t_ref, low_t_ref, high_t_ref, dec, dec_o, enc, enc_o,
    send_p, keep_p, send_q, keep_q, stage, sems, enc_h2, lefts, rights, load_sems,
):
    core = place_ref[3]
    first = load_rows((enc, enc_o), 3840, 768, enc_h2, load_sems, 8)
    for load in first:
        load.start()
    loads = dec_tile(1, core, dec, dec_o, lefts, rights, load_sems, 0)
    for load in loads:
        load.start()
    copies = chunk_copies(stage, place_ref[1], Y_SPLITS, (send_p, keep_p, send_q, keep_q), sems)
    for load in first:
        load.wait()
    wide = widen_t(enc_h2[...], pads_t_ref[...])
    for tile in range(3):
        cut = pl.ds(pl.multiple_of(1536 * core + 512 * tile, 128), 512)
        stage[0, :, :, 512 * tile : 512 * tile + 512] = low(
            dot(wide, two(m_ref, m_o_ref, cut))
        ).reshape(4, 256, 512)
        if tile == 1:
            for copy in copies[:4]:
                copy.start()
    for load in loads:
        load.wait()
    grad = dec_tile_grad(lefts, rights, low_t_ref[...], high_t_ref[...])
    stage[0, :, :, 1536:] = grad.reshape(4, 256, 512)
    for copy in copies[4:]:
        copy.start()
    for copy in copies:
        copy.wait()


def grad_z_kernel(
    place_ref, rows_ref, rows_o_ref, back_ref, back_o_ref, small_ref, pads_t_ref, enc, enc_o,
    send_p, keep_p, send_q, keep_q, stage, sems, enc_h1, encoded, load_sems,
):
    core = place_ref[3]
    first = load_rows((enc, enc_o), 4608, 1536, enc_h1, load_sems, 0)
    first += load_rows((enc, enc_o), 3072, 768, encoded, load_sems, 2)
    for load in first:
        load.start()
    copies = chunk_copies(stage, place_ref[0], Z_SPLITS, (send_p, keep_p, send_q, keep_q), sems)
    pads_t = pads_t_ref[...]
    line = lax.broadcasted_iota(jnp.int32, (1024, 128), 0)
    device = lax.broadcasted_iota(jnp.int32, (1024, 128), 1)
    small = dot_t((line == 8 * device + 6).astype(BF16), small_ref[...])
    for load in first:
        load.wait()
    for half, at in enumerate((0, pl.multiple_of(768 * core, 128))):
        left = widen_t(enc_h1[:, pl.ds(at, 768)], pads_t)
        cut = pl.ds(pl.multiple_of(3072 + 1536 * core + 768 * half, 128), 768)
        grad = dot(left, two(rows_ref, rows_o_ref, cut))
        stage[:, :, :, 768 * half : 768 * half + 768] = low(grad).reshape(16, 4, 16, 768)
        if half == 0:
            stage[:, :, :, :128] = low(grad[:, :128] + small).reshape(16, 4, 16, 128)
    for copy in copies[:4]:
        copy.start()
    right = two(back_ref, back_o_ref, pl.ds(pl.multiple_of(768 + 256 * core, 128), 256))
    grad = dot(widen_t(encoded[...], pads_t), right)
    stage[:, :, :, 1536:] = low(grad).reshape(16, 4, 16, 256)
    for copy in copies[4:]:
        copy.start()
    for copy in copies:
        copy.wait()


def grad_call(kernel, name, staged, outs, place, small, large, scratch):
    return pl.pallas_call(
        kernel,
        in_specs=[pl.BlockSpec(memory_space=pltpu.SMEM)] + [VMEM] * len(small) + [ANY] * len(large),
        out_specs=[ANY] * len(outs),
        out_shape=[pltpu.HBM(dims, BF16) for dims in outs],
        scratch_shapes=[
            pltpu.VMEM(staged, BF16),
            pltpu.SemaphoreType.DMA((8,)),
            *scratch,
        ],
        compiler_params=params(22),
        cost_estimate=pl.CostEstimate(flops=10**4, bytes_accessed=10**3, transcendentals=0),
        name=name,
    )(place, *small, *[in_hbm(a) for a in large])


def split_outs(before, splits):
    return [(2, before, 256 // before, width) for _, width, _ in splits for _ in range(2)]


def fold_kernel(keep_ref, got_ref, send_ref):
    send_ref[...] = low(keep_ref[0].astype(F32) + got_ref[0].astype(F32))


def fold(keep, got):
    _, rows, columns = keep.shape
    block = (1, rows // 2, columns)
    return pl.pallas_call(
        fold_kernel,
        grid=(2,),
        in_specs=[pl.BlockSpec(block, lambda i: (1, i, 0))] * 2,
        out_specs=pl.BlockSpec(block[1:], lambda i: (i, 0)),
        out_shape=shape((rows, columns), BF16),
        compiler_params=params(24),
        cost_estimate=pl.CostEstimate(flops=10**4, bytes_accessed=10**3, transcendentals=0),
        name="fold",
    )(in_hbm(keep) if rows * columns > 1 << 18 else keep, got)


def part_kernel(place_ref, *refs, axis, groups, turns):
    place = place_ref[axis]
    outs = refs[sum(groups) :]
    if turns is None:
        parts = [(out, (place + turn) % 4) for out, turn in zip(outs, (1, 3, 2, 0))]
    else:
        parts = [(outs[i // 2].at[i % 2], place ^ turn) for i, turn in enumerate(turns)]
    for out, chunk in parts:
        chunk = pl.ds(chunk, 1)
        at = start = 0
        for count in groups:
            total = None
            for ref in refs[start : start + count]:
                term = (ref[0, :, chunk] if len(ref.shape) == 5 else ref[:, chunk]).astype(F32)
                total = term if total is None else total + term
            start += count
            before, _, after, columns = total.shape
            out[:, at : at + columns] = low(total).reshape(before * after, columns)
            at += columns


def parted(place, axis, before, groups, first=None):
    rows = groups[0][0].shape[-2]
    after = rows // (4 * before)
    operands, specs = [], []
    for array in (a for group in groups for a in group):
        columns = array.shape[-1]
        if array.ndim == 3:
            array = array.reshape(2, before, 4, after, columns)
            kept = rows * columns > 1 << 18 and len(operands) % 3 == 0
            operands.append(in_hbm(array) if kept else array)
            specs.append(pl.BlockSpec((1, before, 4, after, columns), lambda i: (0, 0, 0, 0, 0)))
        else:
            array = array.reshape(before, 4, after, columns)
            operands.append(in_hbm(array) if len(groups[0]) == 1 else array)
            specs.append(VMEM)
    columns = sum(group[0].shape[-1] for group in groups)
    return pl.pallas_call(
        functools.partial(
            part_kernel,
            axis=axis,
            groups=tuple(len(g) for g in groups),
            turns=None if first is None else (first, 2, 0, 4 - first),
        ),
        grid=(1,),
        in_specs=[pl.BlockSpec(memory_space=pltpu.SMEM)] + specs,
        out_specs=[VMEM] * (4 if first is None else 2),
        out_shape=[shape((rows // 4, columns), BF16)] * 4
        if first is None
        else [shape((2, rows // 4, columns), BF16)] * 2,
        compiler_params=params(24),
        cost_estimate=pl.CostEstimate(flops=10**4, bytes_accessed=10**3, transcendentals=0),
        name="parted",
    )(place, *operands)


def last_kernel(place_ref, *refs, groups):
    core = place_ref[3]
    own_ref, other_ref = refs[sum(groups) :]
    at = start = 0
    for count in groups:
        total = None
        for ref in refs[start : start + count]:
            term = ref[...].astype(F32)
            total = term if total is None else total + term
        start += count
        cut = slice(at, at + total.shape[1])
        own_ref[:, cut] = jnp.where(core == 0, total[:8], total[8:])
        other_ref[:, cut] = jnp.where(core == 0, total[8:], total[:8])
        at += total.shape[1]


def last(place, groups):
    columns = sum(group[0].shape[-1] for group in groups)
    operands = [a for group in groups for a in group]
    return pl.pallas_call(
        functools.partial(last_kernel, groups=tuple(len(g) for g in groups)),
        in_specs=[pl.BlockSpec(memory_space=pltpu.SMEM)] + [VMEM] * len(operands),
        out_specs=[VMEM] * 2,
        out_shape=[shape((8, columns), F32)] * 2,
        compiler_params=params(24),
        cost_estimate=pl.CostEstimate(flops=10**4, bytes_accessed=10**3, transcendentals=0),
        name="last",
    )(place, *operands)


def ungrouped(values, groups):
    width = 128 * groups
    line = lax.broadcasted_iota(jnp.int32, (width, width), 0)
    column = lax.broadcasted_iota(jnp.int32, (width, width), 1)
    natural = 8 * groups * ((line & 127) >> 3) + 8 * (line >> 7) + (line & 7)
    turn = (natural == column).astype(BF16)
    high = low(values)
    rest = low(values - high.astype(F32))
    parts = []
    for block in range(8):
        cuts = [slice(1024 * g + 128 * block, 1024 * g + 128 * block + 128) for g in range(groups)]
        both = [jnp.concatenate([v[:, cut] for cut in cuts], axis=1) for v in (high, rest)]
        parts.append(dot(both[0], turn) + dot(both[1], turn))
    return jnp.concatenate(parts, axis=1)


def shards_kernel(
    place_ref, own_ref, got_ref, enc_gains, enc_biases, enc_qkv, enc_proj, enc_up, enc_up_bias,
    enc_down, dec_fill, dec_embed, dec_gains, dec_biases, dec_qkv, dec_proj, dec_up, dec_up_bias,
    dec_down,
):
    core = place_ref[3]

    def halves(start, width):
        own, got = own_ref[:, start : start + width], got_ref[:, start : start + width]
        return jnp.where(core == 0, own, got), jnp.where(core == 0, got, own)

    for group in range(3):
        rows = slice(8 * group, 8 * group + 8)
        enc_down[rows, :384], enc_down[rows, 384:] = halves(384 * group, 384)
    a, b = halves(3712, 256)
    dec_embed[:, :256], dec_embed[:, 256:] = a[:6], b[:6]
    for group in range(2):
        rows = slice(8 * group, 8 * group + 8)
        dec_down[rows, :256], dec_down[rows, 256:] = halves(1152 + 256 * group, 256)
    enc_up[...] = ungrouped(jnp.concatenate(halves(3968, 1536), axis=1), 3)[:6]
    z_all = jnp.concatenate(halves(1664, 512) + halves(5504, 512), axis=1)
    dec_qkv[...] = z_all[:4, :1536]
    dec_proj[...] = z_all[:4, 1536:]
    dec_up[...] = ungrouped(z_all, 2)[4:]
    a, b = halves(2176, 1536)
    enc_qkv[:, :1536] = a[:6]
    enc_qkv[:, 1536:] = b[:6, :768]
    enc_proj[...] = b[:6, 768:]
    flat = a[6:7, :128] + b[6:7, :128]
    at = 0
    smalls = (enc_gains, enc_biases, enc_up_bias, dec_fill, dec_gains, dec_biases, dec_up_bias)
    for ref, (lead, part) in zip(smalls, COUNTS):
        for line in range(lead):
            values = flat[:, at : at + part]
            if ref is dec_biases:
                ref[:, line : line + 1] = values.T
            else:
                ref[line : line + 1, :] = values
            at += part


def shards(place, own, got):
    dims = (
        (2, 6), (6, 6), (6, 2304), (6, 768), (6, 3072), (1, 24), (24, 768), (2, 4), (6, 512),
        (2, 4), (4, 6), (4, 1536), (4, 512), (4, 2048), (1, 16), (16, 512),
    )
    return pl.pallas_call(
        shards_kernel,
        in_specs=[pl.BlockSpec(memory_space=pltpu.SMEM)] + [VMEM] * 2,
        out_specs=[VMEM] * 16,
        out_shape=[shape(d, F32) for d in dims],
        compiler_params=params(24),
        cost_estimate=pl.CostEstimate(flops=10**4, bytes_accessed=10**3, transcendentals=0),
        name="shards",
    )(place, own, got)


def join_kernel(place_ref, dec_mine, enc_mine, got, decoded, x_grad):
    own_at = 2 * place_ref[4]
    decoded[pl.ds(own_at, 2)] = dec_mine[...].reshape(2, 192, 256)
    decoded[pl.ds(2 - own_at, 2)] = got[:384, :256].reshape(2, 192, 256)
    x_grad[pl.ds(own_at, 2)] = enc_mine[...].reshape(2, 48, 384)
    x_grad[pl.ds(2 - own_at, 2)] = got[384:].reshape(2, 48, 384)


def joined(place, *rows):
    return pl.pallas_call(
        join_kernel,
        in_specs=[pl.BlockSpec(memory_space=pltpu.SMEM)] + [VMEM] * 3,
        out_specs=[VMEM] * 2,
        out_shape=[pltpu.HBM((4, 192, 256), BF16), pltpu.HBM((4, 48, 384), BF16)],
        compiler_params=params(16),
        name="joined",
    )(place, *[in_hbm(a) for a in rows])


def pack_kernel(
    enc_gains, enc_biases, enc_qkv, enc_proj, enc_up, enc_up_bias, enc_down, dec_fill, dec_embed,
    dec_gains, dec_biases, dec_qkv, dec_proj, dec_up, dec_up_bias, dec_down, out,
):
    def rows(count, shift=0):
        line = lax.broadcasted_iota(jnp.int32, (8, count), 0)
        return (line == lax.broadcasted_iota(jnp.int32, (8, count), 1) + shift).astype(BF16)

    def group(start, places, source, groups):
        width = 128 * groups
        line = lax.broadcasted_iota(jnp.int32, (width, width), 0)
        column = lax.broadcasted_iota(jnp.int32, (width, width), 1)
        natural = 8 * groups * ((column & 127) >> 3) + 8 * (column >> 7) + (column & 7)
        turn = (natural == line).astype(BF16)
        for block in range(8):
            piece = low(dot(places, source[:, width * block : width * block + width]))
            piece = dot(piece, turn)
            for g in range(groups):
                at = start + 1024 * g + 128 * block
                yield at, piece[:, 128 * g : 128 * g + 128]

    smalls = (enc_gains, enc_biases, enc_up_bias, dec_fill, dec_gains, dec_biases, dec_up_bias)
    flat, at = jnp.zeros((1, 128), F32), 0
    for ref, (lead, part) in zip(smalls, COUNTS):
        values = ref[...]
        line = lax.broadcasted_iota(jnp.int32, (part, 128), 0)
        column = lax.broadcasted_iota(jnp.int32, (part, 128), 1)
        for i in range(lead):
            places = (line + at == column).astype(BF16)
            if ref is dec_biases:
                flat = flat + t_dot(values[:, i : i + 1], places)
            else:
                flat = flat + dot(values[i : i + 1], places)
            at += part
    six, four, raised = rows(6), rows(4), rows(4, 4)
    seventh = lax.broadcasted_iota(jnp.int32, (8, 128), 0) == 6
    out[:, :C_PROJ] = low(dot(six, enc_qkv[...]))
    out[:, :128] = low(dot(six, enc_qkv[:, :128]) + jnp.where(seventh, flat, 0.0))
    out[:, C_PROJ:C_UP] = low(dot(six, enc_proj[...]))
    for at, piece in group(C_UP, six, enc_up, 3):
        out[:, at : at + 128] = low(piece)
    out[:, C_EMB:C_DOWN] = low(dot(six, dec_embed[...]))
    for g in range(3):
        out[:, C_DOWN + 768 * g : C_DOWN + 768 * g + 768] = low(dot(rows(24, -8 * g), enc_down[...]))
    lower = (dec_qkv[:, :1024], jnp.concatenate([dec_qkv[:, 1024:], dec_proj[...]], axis=1))
    lower = [dot(four, values) for values in lower]
    for at, piece in group(0, raised, dec_up, 2):
        half, column = at // 1024, at % 1024
        piece = piece + lower[half][:, column : column + 128]
        out[:, C_Z + at : C_Z + at + 128] = low(piece)
    for g in range(2):
        out[:, C_DDOWN + 512 * g : C_DDOWN + 512 * g + 512] = low(dot(rows(16, -8 * g), dec_down[...]))


def pack(*weights):
    weights = [w[None] if w.ndim == 1 else w for w in weights]
    weights[10] = weights[10].T
    return pl.pallas_call(
        pack_kernel,
        in_specs=[VMEM] * 16,
        out_specs=VMEM,
        out_shape=pltpu.HBM((8, C_ALL), BF16),
        compiler_params=params(24),
        name="pack",
    )(*[in_hbm(w) for w in weights])


def position_table(offset, width):
    half = width // 2
    rates = jnp.exp(jnp.arange(half, dtype=F32) * (-math.log(10000.0) / half))
    angle = offset.astype(F32)[:, None] * rates[None, :]
    return jnp.concatenate([jnp.sin(angle), jnp.cos(angle)], axis=1)


def layout(length_row, order, visible):
    length = order.shape[0]
    ends = jnp.cumsum(length_row, dtype=jnp.int32)
    places = lax.broadcasted_iota(jnp.int32, (length, 1), 0)
    passed = places >= ends[None, :]
    segment = jnp.sum(passed.astype(jnp.int32), axis=1, dtype=jnp.int32)
    offset = places[:, 0] - jnp.sum(
        jnp.where(passed, length_row[None, :], 0), axis=1, dtype=jnp.int32
    )
    shown_pos = order[:visible]
    shown_seg = jnp.sum(
        (shown_pos[:, None] >= ends[None, :]).astype(jnp.int32), axis=1, dtype=jnp.int32
    )
    onehot = places == shown_pos[None, :]
    return (segment, offset, shown_seg, onehot)


def spread_rows(devices, rows, at):
    feature = lax.broadcasted_iota(jnp.int32, (devices * rows, devices * 8), 0)
    place = lax.broadcasted_iota(jnp.int32, (devices * rows, devices * 8), 1)
    return (8 * (feature // rows) + at + feature % rows == place).astype(BF16)


def plans(length_rows, orders):
    segment, offset, shown_seg, onehot = jax.vmap(lambda a, b: layout(a, b, 48))(
        length_rows, orders
    )
    pack = jnp.arange(2, dtype=jnp.int32)[:, None] * 16
    seen = (shown_seg + pack).reshape(96)
    seen_keys = jnp.concatenate([seen, jnp.full((32,), -1, jnp.int32)])
    enc_bias = jnp.where(seen[:, None] == seen_keys[None, :], 0.0, NEVER).astype(F32)
    keys = jnp.concatenate([segment, jnp.full((2, 64), -1, jnp.int32)], axis=1)
    dec_bias = jnp.where(segment[:, :, None] == keys[:, None, :], 0.0, NEVER).astype(F32)
    hot = onehot.astype(BF16)
    hot = hot.transpose(0, 2, 1)
    none = jnp.zeros((48, 192), BF16)
    picker_t = jnp.concatenate(
        [jnp.concatenate([hot[0], none], axis=1), jnp.concatenate([none, hot[1]], axis=1)], axis=0
    )
    table = position_table(offset.reshape(-1), 512)
    return enc_bias, dec_bias, picker_t, table


def place_of(device):
    return device // 2 % 4, device // 32, device // 8 % 4, device % 2


AXES = {"y": (32, 4), "z": (8, 4), "x": (2, 4), "c": (1, 2)}


def flipped(block, axis, turn):
    stride, size = AXES[axis]
    route = []
    for device in range(128):
        at = device // stride % size
        route.append((device, device + ((at ^ turn) - at) * stride))
    return lax.ppermute(block, BOTH, route)


def other_core(block):
    return flipped(block, "c", 1)


def first_sent(axis, outs):
    begun = []
    for split, first in enumerate((1, 3)):
        send, keep = [a.reshape(2, 256, a.shape[-1]) for a in outs[2 * split : 2 * split + 2]]
        begun.append((keep, flipped(send, axis, first)))
    return begun


def second_sent(axis, begun, before):
    groups = []
    for (keep, got), first in zip(begun, (1, 3)):
        onward = fold(after(keep, *before), got)
        groups.append((keep, got, flipped(onward, axis, 4 - first)))
        before = (onward,)
    return groups, before


def passed(block, axis, by):
    stride, size = AXES[axis]
    route = []
    for device in range(128):
        at = device // stride % size
        route.append((device, device + ((at + by) % size - at) * stride))
    return lax.ppermute(block, BOTH, route)


def summed(place, axis, before, groups, earlier):
    *sends, own = parted(after(place, *earlier), "xyz".index(axis), before, groups)
    return [(own, *[passed(send, axis, by) for send, by in zip(sends, (1, 3, 2))])], (own,)


def paired(place, axis, before, groups, first, earlier):
    send, keep = parted(after(place, *earlier), "xyz".index(axis), before, groups, first)
    return (axis, first, keep, flipped(send, axis, first)), (keep,)


def paired_end(begun, earlier):
    axis, first, keep, got = begun
    onward = fold(after(keep, *earlier), got)
    return [(keep, got, flipped(onward, axis, 4 - first))], (onward,)


def after(value, *others):
    return lax.optimization_barrier((value, *others))[0]


def on_device(
    x_vis, lengths, shuffle, enc_gains, enc_biases, enc_qkv, enc_proj, enc_up, enc_up_bias,
    enc_down, dec_fill, dec_embed, dec_gains, dec_biases, dec_qkv, dec_proj, dec_up, dec_up_bias,
    dec_down, cotangent,
):
    section = lax.axis_index("section")
    device = lax.axis_index(BOTH)
    x, y, z, core = place_of(device)
    shard = pack(
        enc_gains, enc_biases, enc_qkv, enc_proj, enc_up, enc_up_bias, enc_down, dec_fill,
        dec_embed, dec_gains, dec_biases, dec_qkv, dec_proj, dec_up, dec_up_bias, dec_down,
    )
    whole = lax.all_gather(shard, BOTH, axis=0, tiled=True)

    packs = 2

    def mine(rows):
        return lax.dynamic_slice_in_dim(rows, section * packs, packs, 0)[:, 0]

    x_rows = mine(x_vis).reshape(packs * 48, 768)
    pull = mine(cotangent).reshape(packs * 192, 512)
    enc_bias, dec_bias, picker_t, table = plans(mine(lengths), mine(shuffle))
    pads = spread_rows(64, 6, 0)
    low_rows, high_rows = spread_rows(32, 4, 0), spread_rows(32, 4, 4)
    spread = (low_rows, high_rows)
    pads_t, low_t, high_t = pads.T, low_rows.T, high_rows.T
    place = jnp.stack([x, y, z, core, section]).astype(jnp.int32)
    side = section.astype(jnp.int32).reshape(1)

    pull_o = other_core(pull)

    ready = (whole, x_rows, pull, pull_o, enc_bias, dec_bias, picker_t, table)
    ready = lax.optimization_barrier((*ready, pads, pads_t, low_t, high_t, *spread))
    whole, x_rows, pull, pull_o, enc_bias, dec_bias, picker_t, table = ready[:8]
    pads, pads_t, low_t, high_t, *spread = ready[8:]
    (
        enc_vec, dec_mine, dec_theirs, back, d_dec, d_dec_up, enc_rows, proj3, shares, middle,
        slope, dec_rows,
    ) = blocks(
        side, whole, x_rows, enc_bias, pads, picker_t, table, dec_bias, pull, *spread
    )
    enc_rows_o = other_core(enc_rows)
    back_o = other_core(back)
    dec_rows_o = other_core(dec_rows)
    back_rows, enc_mine, enc_theirs, small = enc_back(
        side, whole, back, middle, slope, proj3, shares, x_rows, pads, enc_vec, d_dec, d_dec_up,
        dec_theirs,
    )
    back_rows_o = other_core(back_rows)
    (sums_s,) = grad_call(
        grad_s_kernel, "grad_s", (4, 4, 64, 2176), [(4, 4, 64, 2176)], after(place, back_rows),
        (back, back_o, pull, pull_o, low_t, high_t),
        (dec_rows, dec_rows_o, enc_rows, enc_rows_o),
        (
            pltpu.VMEM((192, 3072), BF16),
            pltpu.VMEM((768, 2048), BF16),
            pltpu.VMEM((2, 768, 512), BF16),
            pltpu.VMEM((2, 768, 512), BF16),
            pltpu.SemaphoreType.DMA((12,)),
        ),
    )
    sums_y = grad_call(
        grad_y_kernel, "grad_y", (1, 4, 256, 2048), split_outs(1, Y_SPLITS), after(place, sums_s),
        (back_rows, back_rows_o, pads_t, low_t, high_t),
        (dec_rows, dec_rows_o, enc_rows, enc_rows_o),
        (
            pltpu.VMEM((192, 768), BF16),
            pltpu.VMEM((2, 768, 512), BF16),
            pltpu.VMEM((2, 768, 512), BF16),
            pltpu.SemaphoreType.DMA((10,)),
        ),
    )
    sums_z = grad_call(
        grad_z_kernel, "grad_z", (16, 4, 16, 1792), split_outs(16, Z_SPLITS),
        after(place, *sums_y), (back_rows, back_rows_o, back, back_o, small, pads_t),
        (enc_rows, enc_rows_o),
        (
            pltpu.VMEM((192, 1536), BF16),
            pltpu.VMEM((192, 768), BF16),
            pltpu.SemaphoreType.DMA((4,)),
        ),
    )

    sums_s = lax.psum_scatter(
        sums_s.reshape(64, 16, 2176), "z", scatter_dimension=0, tiled=True
    ).reshape(256, 2176)
    sums_y = first_sent("y", sums_y)
    sums_z = first_sent("x", sums_z)
    sums_y, done = second_sent("y", sums_y, sums_z[0][:1])
    sums_z, done = second_sent("x", sums_z, done)
    sums_s, done = paired(place, "x", 4, [(sums_s,)], 1, done)
    sums_y, done = paired(place, "z", 1, sums_y, 1, done)
    sums_z, done = paired(place, "z", 4, sums_z, 3, done)
    sums_s, done = paired_end(sums_s, done)
    sums_y, done = paired_end(sums_y, done)
    sums_z, done = paired_end(sums_z, done)
    sums_sz, done = summed(place, "y", 1, sums_s + sums_z, done)
    sums_y, done = summed(place, "x", 1, sums_y, done)
    decoded, x_grad = joined(place, dec_mine, enc_mine, flipped(enc_theirs, "y", 2))
    own, other = last(after(place, decoded, x_grad), sums_sz + sums_y)
    grads = shards(place, own, other_core(other))
    grads = [g[0] if g.shape[0] == 1 else g for g in grads]
    grads[10] = grads[10].T
    return (decoded[:, None], x_grad[:, None], *grads)


def solution(mesh):
    mesh = Mesh(mesh.devices.reshape(2, 2, 4, 4, 2), BOTH)
    rows = P(None, DP, None, None)
    ids = P(None, DP, None)
    wide = P(None, BOTH)
    tall = P(BOTH, None)
    flat = P(BOTH)
    in_specs = (rows, ids, ids, wide, wide, tall, tall, tall, flat, tall, wide, tall, wide, wide)
    in_specs += (tall, tall, tall, flat, tall, rows)
    out_rows = P(None, DP, None, "section")
    out_specs = (out_rows, out_rows, wide, wide, tall, tall, tall, flat, tall, wide, tall, wide)
    out_specs += (wide, tall, tall, tall, flat, tall)
    return jax.shard_map(
        on_device, mesh=mesh, in_specs=in_specs, out_specs=out_specs, check_vma=False
    )
```

```python
import functools
import math

import jax
import jax.numpy as jnp
from jax import lax
from jax.experimental import pallas as pl
from jax.experimental.pallas import tpu as pltpu
from jax.sharding import Mesh
from jax.sharding import PartitionSpec as P

H_ENC = 12
H_DEC = 16
DP = ("y_low", "z", "x", "core")
BOTH = ("section", *DP)
Y_AXIS = ("section", "y_low")
F32 = jnp.float32
BF16 = jnp.bfloat16
EPS = 1e-06
NEVER = -1e30
MIB = 1 << 20

C_PROJ = 2304
C_UP = 3072
C_EMB = 6144
C_DOWN = 6656
C_Z = 8960
C_DDOWN = 11008
C_ALL = 12032
COUNTS = ((2, 6), (6, 6), (1, 24), (2, 4), (2, 4), (6, 4), (1, 16))


def dot(left, right):
    return jnp.dot(left, right, preferred_element_type=F32)


def dot_t(left, right):
    return lax.dot_general(left, right, (((1,), (1,)), ((), ())), preferred_element_type=F32)


def t_dot(left, right):
    return lax.dot_general(left, right, (((0,), (0,)), ((), ())), preferred_element_type=F32)


def low(values):
    return values.astype(BF16)


def norm_parts(values):
    mean = jnp.mean(values, axis=-1, keepdims=True)
    centred = values - mean
    rstd = lax.rsqrt(jnp.mean(centred * centred, axis=-1, keepdims=True) + EPS)
    return centred * rstd, rstd


def norm_back(d_normed, unit, rstd, gain):
    scaled = d_normed * gain
    part = scaled - jnp.mean(scaled, axis=-1, keepdims=True)
    part = (part - unit * jnp.mean(scaled * unit, axis=-1, keepdims=True)) * rstd
    return part, col_sum(d_normed * unit), col_sum(d_normed)


def col_sum(values):
    return jnp.sum(values, axis=0, keepdims=True)


def gelu_pair(hidden):
    share = 0.5 + 0.5 * lax.erf(hidden * math.sqrt(0.5))
    slope = share + hidden * (jnp.exp(-0.5 * hidden * hidden) * (1.0 / math.sqrt(2.0 * math.pi)))
    return hidden * share, slope


def head_stack(block, heads, rows):
    size = 128 // heads
    lane = lax.broadcasted_iota(jnp.int32, (1, 128), 1)
    fill = jnp.zeros((rows - block.shape[0], 128), BF16)
    parts = []
    for head in range(heads):
        own = ((lane >= head * size) & (lane < (head + 1) * size)).astype(BF16)
        parts += [block * own, fill]
    return jnp.concatenate(parts, axis=0)


def head_unstack(stack, heads, rows, count):
    size = 128 // heads
    lane = lax.broadcasted_iota(jnp.int32, (1, 128), 1)
    total = None
    for head in range(heads):
        own = ((lane >= head * size) & (lane < (head + 1) * size)).astype(F32)
        part = stack[head * rows : head * rows + count] * own
        total = part if total is None else total + part
    return total


def attend_group(query, key, value, bias, heads, scale, shares_out):
    rows = bias.shape[1]
    scores = dot_t(query, head_stack(key, heads, rows))
    parts = []
    for head in range(heads):
        s = scores[:, head * rows : (head + 1) * rows] * scale + bias
        powers = jnp.exp(s - jnp.max(s, axis=-1, keepdims=True))
        parts.append(powers / jnp.sum(powers, axis=-1, keepdims=True))
    shares = jnp.concatenate(parts, axis=1)
    shares_out[...] = shares
    return dot(low(shares), head_stack(value, heads, rows))


def attend_group_back(query, key, value, d_out, shares, heads, scale, rows):
    count = key.shape[0]
    d_shares = dot_t(d_out, head_stack(value, heads, rows))
    parts = []
    for head in range(heads):
        cut = slice(head * rows, (head + 1) * rows)
        p, dp = shares[:, cut], d_shares[:, cut]
        parts.append(low(p * (dp - jnp.sum(dp * p, axis=-1, keepdims=True))))
    d_scores = jnp.concatenate(parts, axis=1)
    d_query = dot(d_scores, head_stack(key, heads, rows)) * scale
    d_key = head_unstack(t_dot(d_scores, query), heads, rows, count) * scale
    d_value = head_unstack(t_dot(low(shares), d_out), heads, rows, count)
    return d_query, d_key, d_value


def widen(values, pads):
    return jnp.concatenate(
        [low(dot(values[:, :384], pads)), low(dot(values[:, 384:], pads))], axis=1
    )


def narrow(values, pads):
    return jnp.concatenate(
        [low(dot_t(values[:, :512], pads)), low(dot_t(values[:, 512:], pads))], axis=1
    )


def narrow_wide(values, pads):
    high = low(values)
    rest = low(values - high.astype(F32))
    return jnp.concatenate(
        [
            dot_t(high[:, :512], pads) + dot_t(rest[:, :512], pads),
            dot_t(high[:, 512:], pads) + dot_t(rest[:, 512:], pads),
        ],
        axis=1,
    )


PARTS = (6, 4, 8)


def small_rows():
    plan, at = [], 0
    for family, (lead, part) in enumerate(COUNTS):
        for value in range(lead * part):
            if part >= 16:
                plan.append((2, value // 8 + (3 if family == 6 else 0), value % 8, at))
            else:
                first = 2 if family == 1 else (0, 0, 0, 0, 2, 4)[family]
                kind = 0 if family < 2 else 1
                plan.append((kind, first + value // part, value % part, at))
            at += 1
    return plan


def strewn(kind, value):
    part = PARTS[kind]
    device = lax.broadcasted_iota(jnp.int32, (128, 128 * part), 0)
    column = lax.broadcasted_iota(jnp.int32, (128, 128 * part), 1)
    return (column == part * device + value).astype(BF16)


def small_in(columns, rows_ref, enc_ref, enc_up_ref, dec_ref, dec_up_ref):
    line = lax.broadcasted_iota(jnp.int32, (1024, 128), 0)
    device = lax.broadcasted_iota(jnp.int32, (1024, 128), 1)
    table = t_dot(columns, (line == 8 * device + 6).astype(BF16))
    rows_ref[...] = jnp.zeros_like(rows_ref)
    for kind, row, value, place in small_rows():
        rows_ref[kind, value, row : row + 1, :] = table[place : place + 1]
    whole = []
    for kind, part in enumerate(PARTS):
        total = None
        for value in range(part):
            term = dot(low(rows_ref[kind, value]), strewn(kind, value))
            total = term if total is None else total + term
        whole.append(total)
    enc_ref[...] = whole[0][:8]
    dec_ref[...] = whole[1]
    for group in range(3):
        enc_up_ref[:, 1024 * group : 1024 * group + 1024] = whole[2][group : group + 1]
    for group in range(2):
        dec_up_ref[:, 1024 * group : 1024 * group + 1024] = whole[2][3 + group : 4 + group]


def small_out(enc, enc_up, dec, dec_up, table_ref):
    ups = [enc_up[:, 1024 * g : 1024 * g + 1024] for g in range(3)]
    ups += [dec_up[:, 1024 * g : 1024 * g + 1024] for g in range(2)]
    ups += [jnp.zeros((3, 1024), F32)]
    whole = (low(enc), low(dec), low(jnp.concatenate(ups, axis=0)))
    parts = [
        [dot_t(whole[kind], strewn(kind, value)) for value in range(part)]
        for kind, part in enumerate(PARTS)
    ]
    for kind, row, value, place in small_rows():
        table_ref[place : place + 1, :] = parts[kind][value][row : row + 1]


VMEM = pl.BlockSpec(memory_space=pltpu.VMEM)
ANY = pl.BlockSpec(memory_space=pl.ANY)


def shape(dims, kind):
    return jax.ShapeDtypeStruct(dims, kind)


def in_hbm(array):
    return pltpu.with_memory_space_constraint(array, pltpu.HBM)


def params(limit):
    return pltpu.CompilerParams(vmem_limit_bytes=limit * MIB)


def sides(rows, side, mine_ref, theirs_ref):
    half = rows.shape[1] // 2
    mine_ref[...] = jnp.where(side == 0, rows[:, :half], rows[:, half:])
    theirs_ref[...] = jnp.where(side == 0, rows[:, half:], rows[:, :half])


DEC_SCALE = 1.0 / math.sqrt(32)


def blocks_kernel(
    whole, x_ref, enc_bias_ref, pads_ref, picker_t_ref, table_ref, bias_ref, pull_ref, low_ref,
    high_ref, side_ref,
    enc_ref, mine_ref, theirs_ref, back_ref, d_small_ref, d_up_small_ref, enc_rows_out,
    enc_proj3_out, enc_shares_out, enc_middle_out, enc_slope_out, rows_out,
    enc_up_ref, dec_ref, dec_up_ref, small_ref, w_qkv, w_proj, w_up, w_emb, w_down,
    enc_rows, enc_proj3_ref, enc_shares_ref, enc_middle_ref, enc_slope_ref,
    rows_ref, w_lo, w_hi, start_ref, proj3_ref, shares_ref, middle_ref, slope_ref, d_att_ref,
    sems, out_sems,
):
    copies = [
        pltpu.make_async_copy(whole.at[:, pl.ds(at, ref.shape[1])], ref, sems.at[i])
        for i, (at, ref) in enumerate(
            ((0, w_qkv), (C_PROJ, w_proj), (C_UP, w_up), (C_DOWN, w_down), (C_EMB, w_emb))
        )
    ]
    for copy in copies:
        copy.start()
    pads = pads_ref[...]
    x = x_ref[...].astype(F32)
    unit, _ = norm_parts(x)
    copies[0].wait()
    small_in(w_qkv[:, :128], small_ref, enc_ref, enc_up_ref, dec_ref, dec_up_ref)
    h1 = low(unit * enc_ref[0:1] + enc_ref[2:3])
    enc_rows[:, 4608:5376] = h1
    wide = widen(h1, pads)
    for third in range(3):
        cut = slice(768 * third, 768 * third + 768)
        part = dot(wide, w_qkv[:, cut])
        if third != 1:
            part = part + (enc_ref[4:5] if third == 0 else enc_ref[5:6])
        enc_proj3_ref[:, cut] = low(part)
    bias = enc_bias_ref[...]
    for group in range(6):
        cuts = [slice(768 * i + 128 * group, 768 * i + 128 * group + 128) for i in range(3)]
        out = attend_group(
            enc_proj3_ref[:, cuts[0]], enc_proj3_ref[:, cuts[1]], enc_proj3_ref[:, cuts[2]],
            bias, 2, 0.125, enc_shares_ref.at[group],
        )
        enc_rows[:, 5376 + 128 * group : 5504 + 128 * group] = low(out)
    copies[1].wait()
    middle = x + dot(widen(enc_rows[:, 5376:], pads), w_proj[...]) + enc_ref[6:7]
    enc_middle_ref[...] = middle
    unit, _ = norm_parts(middle)
    h2 = low(unit * enc_ref[1:2] + enc_ref[3:4])
    enc_rows[:, 3840:4608] = h2
    wide = widen(h2, pads)
    copies[2].wait()

    @pl.loop(0, 6, unroll=3)
    def _(tile):
        cut = pl.ds(pl.multiple_of(tile * 512, 512), 512)
        value, slope = gelu_pair(dot(wide, w_up[:, cut]) + enc_up_ref[:, cut])
        enc_rows[:, cut] = low(value)
        enc_slope_ref[:, cut] = slope

    dec_weights = pltpu.make_async_copy(
        whole.at[:, pl.ds(C_Z, 3072)], w_up, sems.at[2]
    )
    dec_weights.start()
    copies[3].wait()
    out = middle + enc_ref[7:8]
    for group in range(3):
        out = out + dot(
            enc_rows[:, 1024 * group : 1024 * group + 1024],
            w_down[:, 768 * group : 768 * group + 768],
        )
    encoded = low(out)
    enc_rows[:, 3072:3840] = encoded
    copies[4].wait()
    embedded = low(dot(widen(encoded, pads), w_emb[...]) + dec_ref[0:1])

    attended_ref, d_hid_ref = rows_ref.at[:, pl.ds(512, 512)], rows_ref.at[:, pl.ds(3584, 2048)]
    activated_ref = rows_ref.at[:, pl.ds(5632, 2048)]
    w_z, w_ddown = w_up.at[:, pl.ds(0, 2048)], w_up.at[:, pl.ds(2048, 1024)]
    saves = [
        pltpu.make_async_copy(source, into, out_sems.at[i])
        for i, (source, into) in enumerate(
            (
                (enc_rows, enc_rows_out),
                (enc_proj3_ref, enc_proj3_out),
                (enc_shares_ref, enc_shares_out),
                (enc_middle_ref, enc_middle_out),
                (enc_slope_ref, enc_slope_out),
            )
        )
    ]
    for start, width in ((0, 1536), (5632, 2048), (3584, 2048), (1536, 2048)):
        cut = pl.ds(start, width)
        saves.append(
            pltpu.make_async_copy(rows_ref.at[:, cut], rows_out.at[:, cut], out_sems.at[len(saves)])
        )
    for save in saves[:5]:
        save.start()
    gain_1, gain_2 = dec_ref[2:3], dec_ref[3:4]
    picker_t = picker_t_ref[...]
    masked = 1.0 - t_dot(picker_t, jnp.ones((96, 512), BF16))
    start = t_dot(picker_t, embedded) + masked * dec_ref[1:2] + table_ref[...]
    start_ref[...] = start
    unit, _ = norm_parts(start)
    h1 = low(unit * gain_1 + dec_ref[4:5])
    rows_ref[:, :512] = h1
    dec_weights.wait()

    @pl.loop(0, 4, unroll=4)
    def _(block):
        into = pl.ds(pl.multiple_of(block * 128, 128), 128)
        source = pl.ds(pl.multiple_of(block * 256, 256), 256)
        for half in range(2):
            cut = slice(1024 * half, 1024 * half + 1024)
            rows = w_z[source, cut]
            w_lo[into, cut] = low(dot(low_ref[...], rows))
            w_hi[into, cut] = low(dot(high_ref[...], rows))

    for third in range(3):
        cut = slice(512 * third, 512 * third + 512)
        part = dot(h1, w_lo[:, cut])
        if third != 1:
            part = part + (dec_ref[6:7] if third == 0 else dec_ref[7:8])
        proj3_ref[:, cut] = low(part)

    @pl.loop(0, 8, unroll=4)
    def _(step):
        pack, group = step // 4, step % 4
        rows = pl.ds(pl.multiple_of(pack * 192, 192), 192)
        cuts = [pl.ds(pl.multiple_of(512 * i + 128 * group, 128), 128) for i in range(3)]
        out = attend_group(
            proj3_ref[rows, cuts[0]], proj3_ref[rows, cuts[1]], proj3_ref[rows, cuts[2]],
            bias_ref[pack], 4, DEC_SCALE, shares_ref.at[step],
        )
        attended_ref[rows, cuts[0]] = low(out)

    middle = start + dot(attended_ref[...], w_lo[:, 1536:]) + dec_ref[8:9]
    middle_ref[...] = middle
    unit_2, rstd_2 = norm_parts(middle)
    h2 = low(unit_2 * gain_2 + dec_ref[5:6])
    rows_ref[:, 1024:1536] = h2
    saves[5].start()

    @pl.loop(0, 4, unroll=4)
    def _(tile):
        cut = pl.ds(pl.multiple_of(tile * 512, 512), 512)
        value, slope = gelu_pair(dot(h2, w_hi[:, cut]) + dec_up_ref[:, cut])
        activated_ref[:, cut] = low(value)
        slope_ref[:, cut] = slope

    out = middle + dec_ref[9:10]
    for group in range(2):
        out = out + dot(
            activated_ref[:, 1024 * group : 1024 * group + 1024],
            w_ddown[:, 512 * group : 512 * group + 512],
        )
    saves[6].start()
    sides(low(out), side_ref[0], mine_ref, theirs_ref)

    g_low = pull_ref[...]
    for tile in range(4):
        group, rows = tile // 2, slice(512 * (tile % 2), 512 * (tile % 2) + 512)
        cut = slice(512 * tile, 512 * tile + 512)
        d_hid = dot_t(g_low, w_ddown[rows, 512 * group : 512 * group + 512]) * slope_ref[:, cut]
        d_up_small_ref[:, cut] = col_sum(d_hid)
        d_hid_ref[:, cut] = low(d_hid)
    saves[7].start()
    d_h2 = dot_t(d_hid_ref[...], w_hi[...])
    part, d_gain_2, d_shift_2 = norm_back(d_h2, unit_2, rstd_2, gain_2)
    g = g_low.astype(F32)
    d_mid = g + part
    d_mid_low = low(d_mid)
    d_att = low(dot_t(d_mid_low, w_lo[:, 1536:]))
    d_small_ref[...] = jnp.zeros_like(d_small_ref)
    d_small_ref[3:4] = d_gain_2
    d_small_ref[5:6] = d_shift_2
    d_small_ref[8:9] = col_sum(d_mid)
    d_small_ref[9:10] = col_sum(g)
    rows_ref[:, 3072:3584] = d_mid_low
    middle_ref[...] = d_mid
    d_att_ref[...] = d_att

    @pl.loop(0, 8, unroll=4)
    def _(step):
        pack, group = step // 4, step % 4
        rows = pl.ds(pl.multiple_of(pack * 192, 192), 192)
        cuts = [pl.ds(pl.multiple_of(512 * i + 128 * group, 128), 128) for i in range(3)]
        parts = attend_group_back(
            proj3_ref[rows, cuts[0]], proj3_ref[rows, cuts[1]], proj3_ref[rows, cuts[2]],
            d_att_ref[rows, cuts[0]], shares_ref[step], 4, DEC_SCALE, 256,
        )
        for i, part in enumerate(parts):
            at = pl.multiple_of(1536 + 512 * i + 128 * group, 128)
            rows_ref[rows, pl.ds(at, 128)] = low(part)
            if i != 1:
                d_small_ref[6 + i // 2, cuts[0]] += jnp.sum(part, axis=0)

    saves[8].start()
    d_h1 = dot_t(rows_ref[:, 1536:3072], w_lo[:, :1536])
    unit, rstd = norm_parts(start_ref[...])
    part, d_gain_1, d_shift_1 = norm_back(d_h1, unit, rstd, gain_1)
    d_start = middle_ref[...] + part
    d_small_ref[2:3] = d_gain_1
    d_small_ref[4:5] = d_shift_1
    masked = 1.0 - t_dot(picker_t_ref[...], jnp.ones((96, 512), BF16))
    d_small_ref[1:2] = col_sum(masked * d_start)
    d_embedded = dot(picker_t_ref[...], low(d_start))
    d_small_ref[0:1] = col_sum(d_embedded)
    d_embedded = low(d_embedded)
    back_ref[:, 768:] = d_embedded
    back_ref[:, :768] = narrow(low(dot_t(d_embedded, w_emb[...])), pads)
    for save in saves:
        save.wait()


def blocks(side, *operands):
    return pl.pallas_call(
        blocks_kernel,
        in_specs=[ANY] + [VMEM] * 9 + [pl.BlockSpec(memory_space=pltpu.SMEM)],
        out_specs=[VMEM] * 6 + [ANY] * 6,
        out_shape=[
            pltpu.HBM((8, 768), F32),
            pltpu.HBM((384, 256), BF16),
            pltpu.HBM((384, 256), BF16),
            shape((96, 1280), BF16),
            pltpu.HBM((16, 512), F32),
            pltpu.HBM((1, 2048), F32),
            pltpu.HBM((96, 6144), BF16),
            pltpu.HBM((96, 2304), BF16),
            pltpu.HBM((6, 96, 256), F32),
            pltpu.HBM((96, 768), F32),
            pltpu.HBM((96, 3072), F32),
            pltpu.HBM((384, 7680), BF16),
        ],
        scratch_shapes=[
            pltpu.VMEM((1, 3072), F32),
            pltpu.VMEM((16, 512), F32),
            pltpu.VMEM((1, 2048), F32),
            pltpu.VMEM((3, 8, 16, 128), F32),
            pltpu.VMEM((1024, 2304), BF16),
            pltpu.VMEM((1024, 768), BF16),
            pltpu.VMEM((1024, 3072), BF16),
            pltpu.VMEM((1024, 512), BF16),
            pltpu.VMEM((1024, 2304), BF16),
            pltpu.VMEM((96, 6144), BF16),
            pltpu.VMEM((96, 2304), BF16),
            pltpu.VMEM((6, 96, 256), F32),
            pltpu.VMEM((96, 768), F32),
            pltpu.VMEM((96, 3072), F32),
            pltpu.VMEM((384, 7680), BF16),
            pltpu.VMEM((512, 2048), BF16),
            pltpu.VMEM((512, 2048), BF16),
            pltpu.VMEM((384, 512), F32),
            pltpu.VMEM((384, 1536), BF16),
            pltpu.VMEM((8, 192, 1024), F32),
            pltpu.VMEM((384, 512), F32),
            pltpu.VMEM((384, 2048), F32),
            pltpu.VMEM((384, 512), BF16),
            pltpu.SemaphoreType.DMA((5,)),
            pltpu.SemaphoreType.DMA((9,)),
        ],
        compiler_params=params(60),
        cost_estimate=pl.CostEstimate(flops=10**4, bytes_accessed=10**3, transcendentals=0),
        name="blocks",
    )(*[in_hbm(a) for a in operands], side)


def enc_back_kernel(
    whole, back_ref, middle_ref, slope_ref, proj3_ref, shares_ref, x_ref, pads_ref, enc_ref,
    d_dec_ref, d_dec_up_ref, dec_theirs_ref, side_ref,
    hid_ref, rows_ref, mine_ref, theirs_ref, small_ref,
    w_down, w_up, w_proj, w_qkv, d_p3_ref, d_up_ref, table_ref, sems,
):
    copies = [
        pltpu.make_async_copy(whole.at[:, pl.ds(at, ref.shape[1])], ref, sems.at[i])
        for i, (at, ref) in enumerate(
            ((C_DOWN, w_down), (C_UP, w_up), (C_PROJ, w_proj), (0, w_qkv))
        )
    ]
    for copy in copies:
        copy.start()
    pads = pads_ref[...]
    g_low = back_ref[:, :768]
    g = g_low.astype(F32)
    unit, rstd = norm_parts(middle_ref[...])
    copies[0].wait()
    for group in range(3):
        cut = slice(1024 * group, 1024 * group + 1024)
        d_hid = dot_t(g_low, w_down[:, 768 * group : 768 * group + 768]) * slope_ref[:, cut]
        d_up_ref[:, cut] = col_sum(d_hid)
        hid_ref[:, cut] = low(d_hid)
    copies[1].wait()
    d_h2 = narrow_wide(dot_t(hid_ref[...], w_up[...]), pads)
    part, d_gain_2, d_shift_2 = norm_back(d_h2, unit, rstd, enc_ref[1:2])
    d_middle = g + part
    d_mid_low = low(d_middle)
    rows_ref[:, 2304:] = d_mid_low
    copies[2].wait()
    d_att = narrow(low(dot_t(d_mid_low, w_proj[...])), pads)
    for group in range(6):
        cuts = [slice(768 * i + 128 * group, 768 * i + 128 * group + 128) for i in range(3)]
        parts = attend_group_back(
            proj3_ref[:, cuts[0]], proj3_ref[:, cuts[1]], proj3_ref[:, cuts[2]],
            d_att[:, cuts[0]], shares_ref[group], 2, 0.125, 128,
        )
        for third, (cut, part) in enumerate(zip(cuts, parts)):
            d_p3_ref[:, cut] = part
            at = 768 * third + 128 * group
            rows_ref[:, at : at + 128] = low(part)
    unit, rstd = norm_parts(x_ref[...].astype(F32))
    copies[3].wait()
    d_h1 = narrow_wide(dot_t(rows_ref[:, :2304], w_qkv[...]), pads)
    part, d_gain_1, d_shift_1 = norm_back(d_h1, unit, rstd, enc_ref[0:1])
    theirs_ref[:384, :256] = dec_theirs_ref[...]
    theirs_ref[:384, 256:] = jnp.zeros((384, 128), BF16)
    sides(low(d_middle + part), side_ref[0], mine_ref, theirs_ref.at[pl.ds(384, 96)])
    vectors = (
        d_gain_1, d_gain_2, d_shift_1, d_shift_2, col_sum(d_p3_ref[:, :768]),
        col_sum(d_p3_ref[:, 1536:]), col_sum(d_middle), col_sum(g),
    )
    row = lax.broadcasted_iota(jnp.int32, (8, 768), 0)
    d_enc = jnp.zeros((8, 768), F32)
    for line, vector in enumerate(vectors):
        d_enc = jnp.where(row == line, vector, d_enc)
    small_out(d_enc, d_up_ref[...], d_dec_ref[...], d_dec_up_ref[...], table_ref)
    small_ref[...] = low(table_ref[...])


def enc_back(side, *operands):
    return pl.pallas_call(
        enc_back_kernel,
        in_specs=[ANY] + [VMEM] * 11 + [pl.BlockSpec(memory_space=pltpu.SMEM)],
        out_specs=[VMEM] * 5,
        out_shape=(
            shape((96, 3072), BF16),
            shape((96, 3072), BF16),
            pltpu.HBM((96, 384), BF16),
            pltpu.HBM((480, 384), BF16),
            shape((128, 128), BF16),
        ),
        scratch_shapes=[
            pltpu.VMEM((1024, 2304), BF16),
            pltpu.VMEM((1024, 3072), BF16),
            pltpu.VMEM((1024, 768), BF16),
            pltpu.VMEM((1024, 2304), BF16),
            pltpu.VMEM((96, 2304), F32),
            pltpu.VMEM((1, 3072), F32),
            pltpu.VMEM((128, 128), F32),
            pltpu.SemaphoreType.DMA((4,)),
        ],
        compiler_params=params(36),
        name="enc_back",
    )(*[in_hbm(a) for a in operands], side)


def widen_t(values, pads_t):
    return jnp.concatenate(
        [low(dot_t(pads_t, values[:, :384])), low(dot_t(pads_t, values[:, 384:]))], axis=0
    )


def spread_t(values, rows_t):
    return jnp.concatenate(
        [low(dot_t(rows_t, values[:, 128 * i : 128 * i + 128])) for i in range(4)], axis=0
    )


def two(own, other, cut):
    return jnp.concatenate([own[:, cut], other[:, cut]], axis=0)


def chunk_copies(stage, place, splits, outs, sems):
    copies = []
    for split, (start, width, first) in enumerate(splits):
        send, keep = outs[2 * split], outs[2 * split + 1]
        for slot, (ref, flips) in enumerate(((send, (first, 2)), (keep, (0, 4 - first)))):
            for line, turn in enumerate(flips):
                copies.append(
                    pltpu.make_async_copy(
                        stage.at[:, place ^ turn, :, pl.ds(start, width)],
                        ref.at[line],
                        sems.at[4 * split + 2 * slot + line],
                    )
                )
    return copies


Y_SPLITS = ((0, 1024, 1), (1024, 1024, 3))
Z_SPLITS = ((0, 896, 1), (896, 896, 3))


def load_rows(sources, start, width, into, sems, at):
    count = sources[0].shape[0]
    return [
        pltpu.make_async_copy(
            source.at[:, pl.ds(start, width)],
            into.at[pl.ds(count * i, count), :],
            sems.at[at + i],
        )
        for i, source in enumerate(sources)
    ]


def dec_tile(tile, core, dec, dec_o, lefts, rights, sems, at):
    place = pl.multiple_of(1024 * tile + 512 * core, 128)
    low_left = 0 if tile == 0 else pl.multiple_of(512 * core, 128)
    loads = []
    for i, (start, into) in enumerate(
        (
            (low_left, lefts.at[0]),
            (1024, lefts.at[1]),
            (1536 + place, rights.at[0]),
            (3584 + place, rights.at[1]),
        )
    ):
        loads += load_rows((dec, dec_o), start, 512, into, sems, at + 2 * i)
    return loads


def dec_tile_grad(lefts, rights, low_t, high_t):
    grad = dot(spread_t(lefts[0], low_t), rights[0])
    return low(grad + dot(spread_t(lefts[1], high_t), rights[1]))


def grad_s_kernel(
    place_ref, m_ref, m_o_ref, pull_ref, pull_o_ref, low_t_ref, high_t_ref, dec, dec_o, enc,
    enc_o,
    sums, stage, sems, enc_act, activated, lefts, rights, load_sems,
):
    core = place_ref[3]
    first = load_rows((enc, enc_o), 0, 3072, enc_act, load_sems, 10)
    for load in first:
        load.start()
    loads = load_rows((dec, dec_o), 5632, 2048, activated, load_sems, 0)
    loads += dec_tile(0, core, dec, dec_o, lefts, rights, load_sems, 2)
    for load in loads:
        load.start()
    for load in first:
        load.wait()
    for group in range(3):
        right = two(m_ref, m_o_ref, pl.ds(pl.multiple_of(384 * core, 128), 384))
        grad = low(t_dot(enc_act[:, 1024 * group : 1024 * group + 1024], right))
        stage[:, :, :, 384 * group : 384 * group + 384] = grad.reshape(4, 4, 64, 384)
    copies = []
    for i, (start, width) in enumerate(((0, 1152), (1152, 1024))):
        cut = pl.ds(start, width)
        copies += [
            pltpu.make_async_copy(stage.at[:, z, :, cut], sums.at[z, :, :, cut], sems.at[4 * i + z])
            for z in range(4)
        ]
    for copy in copies[:4]:
        copy.start()
    right = two(pull_ref, pull_o_ref, pl.ds(pl.multiple_of(256 * core, 128), 256))
    for load in loads:
        load.wait()
    for group in range(2):
        grad = low(t_dot(activated[:, 1024 * group : 1024 * group + 1024], right))
        stage[:, :, :, 1152 + 256 * group : 1408 + 256 * group] = grad.reshape(4, 4, 64, 256)
    grad = dec_tile_grad(lefts, rights, low_t_ref[...], high_t_ref[...])
    stage[:, :, :, 1664:] = grad.reshape(4, 4, 64, 512)
    for copy in copies[4:]:
        copy.start()
    for copy in copies:
        copy.wait()


def grad_y_kernel(
    place_ref, m_ref, m_o_ref, pads_t_ref, low_t_ref, high_t_ref, dec, dec_o, enc, enc_o,
    send_p, keep_p, send_q, keep_q, stage, sems, enc_h2, lefts, rights, load_sems,
):
    core = place_ref[3]
    first = load_rows((enc, enc_o), 3840, 768, enc_h2, load_sems, 8)
    for load in first:
        load.start()
    loads = dec_tile(1, core, dec, dec_o, lefts, rights, load_sems, 0)
    for load in loads:
        load.start()
    copies = chunk_copies(stage, place_ref[1], Y_SPLITS, (send_p, keep_p, send_q, keep_q), sems)
    for load in first:
        load.wait()
    wide = widen_t(enc_h2[...], pads_t_ref[...])
    for tile in range(3):
        cut = pl.ds(pl.multiple_of(1536 * core + 512 * tile, 128), 512)
        stage[0, :, :, 512 * tile : 512 * tile + 512] = low(
            dot(wide, two(m_ref, m_o_ref, cut))
        ).reshape(4, 256, 512)
        if tile == 1:
            for copy in copies[:4]:
                copy.start()
    for load in loads:
        load.wait()
    grad = dec_tile_grad(lefts, rights, low_t_ref[...], high_t_ref[...])
    stage[0, :, :, 1536:] = grad.reshape(4, 256, 512)
    for copy in copies[4:]:
        copy.start()
    for copy in copies:
        copy.wait()


def grad_z_kernel(
    place_ref, rows_ref, rows_o_ref, back_ref, back_o_ref, small_ref, pads_t_ref, enc, enc_o,
    send_p, keep_p, send_q, keep_q, stage, sems, enc_h1, encoded, load_sems,
):
    core = place_ref[3]
    first = load_rows((enc, enc_o), 4608, 1536, enc_h1, load_sems, 0)
    first += load_rows((enc, enc_o), 3072, 768, encoded, load_sems, 2)
    for load in first:
        load.start()
    copies = chunk_copies(stage, place_ref[0], Z_SPLITS, (send_p, keep_p, send_q, keep_q), sems)
    pads_t = pads_t_ref[...]
    line = lax.broadcasted_iota(jnp.int32, (1024, 128), 0)
    device = lax.broadcasted_iota(jnp.int32, (1024, 128), 1)
    small = dot_t((line == 8 * device + 6).astype(BF16), small_ref[...])
    for load in first:
        load.wait()
    for half, at in enumerate((0, pl.multiple_of(768 * core, 128))):
        left = widen_t(enc_h1[:, pl.ds(at, 768)], pads_t)
        cut = pl.ds(pl.multiple_of(1536 * core + 768 * half, 128), 768)
        grad = dot(left, two(rows_ref, rows_o_ref, cut))
        stage[:, :, :, 768 * half : 768 * half + 768] = low(grad).reshape(16, 4, 16, 768)
        if half == 0:
            stage[:, :, :, :128] = low(grad[:, :128] + small).reshape(16, 4, 16, 128)
    for copy in copies[:4]:
        copy.start()
    right = two(back_ref, back_o_ref, pl.ds(pl.multiple_of(768 + 256 * core, 128), 256))
    grad = dot(widen_t(encoded[...], pads_t), right)
    stage[:, :, :, 1536:] = low(grad).reshape(16, 4, 16, 256)
    for copy in copies[4:]:
        copy.start()
    for copy in copies:
        copy.wait()


def grad_call(kernel, name, staged, outs, place, small, large, scratch):
    return pl.pallas_call(
        kernel,
        in_specs=[pl.BlockSpec(memory_space=pltpu.SMEM)] + [VMEM] * len(small) + [ANY] * len(large),
        out_specs=[ANY] * len(outs),
        out_shape=[pltpu.HBM(dims, BF16) for dims in outs],
        scratch_shapes=[
            pltpu.VMEM(staged, BF16),
            pltpu.SemaphoreType.DMA((8,)),
            *scratch,
        ],
        compiler_params=params(22),
        cost_estimate=pl.CostEstimate(flops=10**4, bytes_accessed=10**3, transcendentals=0),
        name=name,
    )(
        place,
        *[in_hbm(a) if a.shape[0] == 512 else a for a in small],
        *[in_hbm(a) for a in large],
    )


def split_outs(before, splits):
    return [(2, before, 256 // before, width) for _, width, _ in splits for _ in range(2)]


def fold_kernel(keep_ref, got_ref, send_ref):
    send_ref[...] = low(keep_ref[0].astype(F32) + got_ref[0].astype(F32))


def fold(keep, got):
    _, rows, columns = keep.shape
    block = (1, rows // 2, columns)
    return pl.pallas_call(
        fold_kernel,
        grid=(2,),
        in_specs=[pl.BlockSpec(block, lambda i: (1, i, 0))] * 2,
        out_specs=pl.BlockSpec(block[1:], lambda i: (i, 0)),
        out_shape=shape((rows, columns), BF16),
        compiler_params=params(24),
        cost_estimate=pl.CostEstimate(flops=10**4, bytes_accessed=10**3, transcendentals=0),
        name="fold",
    )(in_hbm(keep) if rows * columns > 1 << 18 else keep, got)


def part_kernel(place_ref, *refs, axis, groups, turns):
    place = place_ref[axis]
    outs = refs[sum(groups) :]
    if turns is None:
        parts = [(out, (place + turn) % 4) for out, turn in zip(outs, (1, 3, 2, 0))]
    else:
        parts = [(outs[i // 2].at[i % 2], place ^ turn) for i, turn in enumerate(turns)]
    for out, chunk in parts:
        chunk = pl.ds(chunk, 1)
        at = start = 0
        for count in groups:
            total = None
            for ref in refs[start : start + count]:
                term = (ref[0, :, chunk] if len(ref.shape) == 5 else ref[:, chunk]).astype(F32)
                total = term if total is None else total + term
            start += count
            before, _, after, columns = total.shape
            out[:, at : at + columns] = low(total).reshape(before * after, columns)
            at += columns


def parted(place, axis, before, groups, first=None):
    rows = groups[0][0].shape[-2]
    after = rows // (4 * before)
    operands, specs = [], []
    for array in (a for group in groups for a in group):
        columns = array.shape[-1]
        if array.ndim == 3:
            array = array.reshape(2, before, 4, after, columns)
            kept = rows == 256 and len(operands) % 3 == 0
            operands.append(in_hbm(array) if kept else array)
            specs.append(pl.BlockSpec((1, before, 4, after, columns), lambda i: (0, 0, 0, 0, 0)))
        else:
            array = array.reshape(before, 4, after, columns)
            operands.append(in_hbm(array) if len(groups[0]) == 1 else array)
            specs.append(VMEM)
    columns = sum(group[0].shape[-1] for group in groups)
    return pl.pallas_call(
        functools.partial(
            part_kernel,
            axis=axis,
            groups=tuple(len(g) for g in groups),
            turns=None if first is None else (first, 2, 0, 4 - first),
        ),
        grid=(1,),
        in_specs=[pl.BlockSpec(memory_space=pltpu.SMEM)] + specs,
        out_specs=[VMEM] * (4 if first is None else 2),
        out_shape=[shape((rows // 4, columns), BF16)] * 4
        if first is None
        else [shape((2, rows // 4, columns), BF16)] * 2,
        compiler_params=params(24),
        cost_estimate=pl.CostEstimate(flops=10**4, bytes_accessed=10**3, transcendentals=0),
        name="parted",
    )(place, *operands)


def last_kernel(place_ref, *refs, groups):
    core = place_ref[3]
    own_ref, other_ref = refs[sum(groups) :]
    at = start = 0
    for count in groups:
        total = None
        for ref in refs[start : start + count]:
            term = ref[...].astype(F32)
            total = term if total is None else total + term
        start += count
        cut = slice(at, at + total.shape[1])
        own_ref[:, cut] = jnp.where(core == 0, total[:8], total[8:])
        other_ref[:, cut] = jnp.where(core == 0, total[8:], total[:8])
        at += total.shape[1]


def last(place, groups):
    columns = sum(group[0].shape[-1] for group in groups)
    operands = [a for group in groups for a in group]
    return pl.pallas_call(
        functools.partial(last_kernel, groups=tuple(len(g) for g in groups)),
        in_specs=[pl.BlockSpec(memory_space=pltpu.SMEM)] + [VMEM] * len(operands),
        out_specs=[VMEM] * 2,
        out_shape=[shape((8, columns), F32)] * 2,
        compiler_params=params(24),
        cost_estimate=pl.CostEstimate(flops=10**4, bytes_accessed=10**3, transcendentals=0),
        name="last",
    )(place, *operands)


def ungrouped(values, groups):
    width = 128 * groups
    line = lax.broadcasted_iota(jnp.int32, (width, width), 0)
    column = lax.broadcasted_iota(jnp.int32, (width, width), 1)
    natural = 8 * groups * ((line & 127) >> 3) + 8 * (line >> 7) + (line & 7)
    turn = (natural == column).astype(BF16)
    high = low(values)
    rest = low(values - high.astype(F32))
    parts = []
    for block in range(8):
        cuts = [slice(1024 * g + 128 * block, 1024 * g + 128 * block + 128) for g in range(groups)]
        both = [jnp.concatenate([v[:, cut] for cut in cuts], axis=1) for v in (high, rest)]
        parts.append(dot(both[0], turn) + dot(both[1], turn))
    return jnp.concatenate(parts, axis=1)


def shards_kernel(
    place_ref, own_ref, got_ref, enc_gains, enc_biases, enc_qkv, enc_proj, enc_up, enc_up_bias,
    enc_down, dec_fill, dec_embed, dec_gains, dec_biases, dec_qkv, dec_proj, dec_up, dec_up_bias,
    dec_down,
):
    core = place_ref[3]

    def halves(start, width):
        own, got = own_ref[:, start : start + width], got_ref[:, start : start + width]
        return jnp.where(core == 0, own, got), jnp.where(core == 0, got, own)

    for group in range(3):
        rows = slice(8 * group, 8 * group + 8)
        enc_down[rows, :384], enc_down[rows, 384:] = halves(384 * group, 384)
    a, b = halves(3712, 256)
    dec_embed[:, :256], dec_embed[:, 256:] = a[:6], b[:6]
    for group in range(2):
        rows = slice(8 * group, 8 * group + 8)
        dec_down[rows, :256], dec_down[rows, 256:] = halves(1152 + 256 * group, 256)
    enc_up[...] = ungrouped(jnp.concatenate(halves(3968, 1536), axis=1), 3)[:6]
    z_all = jnp.concatenate(halves(1664, 512) + halves(5504, 512), axis=1)
    dec_qkv[...] = z_all[:4, :1536]
    dec_proj[...] = z_all[:4, 1536:]
    dec_up[...] = ungrouped(z_all, 2)[4:]
    a, b = halves(2176, 1536)
    enc_qkv[:, :1536] = a[:6]
    enc_qkv[:, 1536:] = b[:6, :768]
    enc_proj[...] = b[:6, 768:]
    flat = a[6:7, :128] + b[6:7, :128]
    at = 0
    smalls = (enc_gains, enc_biases, enc_up_bias, dec_fill, dec_gains, dec_biases, dec_up_bias)
    for ref, (lead, part) in zip(smalls, COUNTS):
        for line in range(lead):
            values = flat[:, at : at + part]
            if ref is dec_biases:
                ref[:, line : line + 1] = values.T
            else:
                ref[line : line + 1, :] = values
            at += part


def shards(place, own, got):
    dims = (
        (2, 6), (6, 6), (6, 2304), (6, 768), (6, 3072), (1, 24), (24, 768), (2, 4), (6, 512),
        (2, 4), (4, 6), (4, 1536), (4, 512), (4, 2048), (1, 16), (16, 512),
    )
    return pl.pallas_call(
        shards_kernel,
        in_specs=[pl.BlockSpec(memory_space=pltpu.SMEM)] + [VMEM] * 2,
        out_specs=[VMEM] * 16,
        out_shape=[shape(d, F32) for d in dims],
        compiler_params=params(24),
        cost_estimate=pl.CostEstimate(flops=10**4, bytes_accessed=10**3, transcendentals=0),
        name="shards",
    )(place, own, got)


def join_kernel(place_ref, dec_mine, enc_mine, got, decoded, x_grad):
    own_at = 2 * place_ref[4]
    decoded[pl.ds(own_at, 2)] = dec_mine[...].reshape(2, 192, 256)
    decoded[pl.ds(2 - own_at, 2)] = got[:384, :256].reshape(2, 192, 256)
    x_grad[pl.ds(own_at, 2)] = enc_mine[...].reshape(2, 48, 384)
    x_grad[pl.ds(2 - own_at, 2)] = got[384:].reshape(2, 48, 384)


def joined(place, *rows):
    return pl.pallas_call(
        join_kernel,
        in_specs=[pl.BlockSpec(memory_space=pltpu.SMEM)] + [VMEM] * 3,
        out_specs=[VMEM] * 2,
        out_shape=[pltpu.HBM((4, 192, 256), BF16), pltpu.HBM((4, 48, 384), BF16)],
        compiler_params=params(16),
        name="joined",
    )(place, *[in_hbm(a) for a in rows])


def pack_kernel(
    enc_gains, enc_biases, enc_qkv, enc_proj, enc_up, enc_up_bias, enc_down, dec_fill, dec_embed,
    dec_gains, dec_biases, dec_qkv, dec_proj, dec_up, dec_up_bias, dec_down, out,
):
    def rows(count, shift=0):
        line = lax.broadcasted_iota(jnp.int32, (8, count), 0)
        return (line == lax.broadcasted_iota(jnp.int32, (8, count), 1) + shift).astype(BF16)

    def group(start, places, source, groups):
        width = 128 * groups
        line = lax.broadcasted_iota(jnp.int32, (width, width), 0)
        column = lax.broadcasted_iota(jnp.int32, (width, width), 1)
        natural = 8 * groups * ((column & 127) >> 3) + 8 * (column >> 7) + (column & 7)
        turn = (natural == line).astype(BF16)
        for block in range(8):
            piece = low(dot(places, source[:, width * block : width * block + width]))
            piece = dot(piece, turn)
            for g in range(groups):
                at = start + 1024 * g + 128 * block
                yield at, piece[:, 128 * g : 128 * g + 128]

    smalls = (enc_gains, enc_biases, enc_up_bias, dec_fill, dec_gains, dec_biases, dec_up_bias)
    flat, at = jnp.zeros((1, 128), F32), 0
    for ref, (lead, part) in zip(smalls, COUNTS):
        values = ref[...]
        line = lax.broadcasted_iota(jnp.int32, (part, 128), 0)
        column = lax.broadcasted_iota(jnp.int32, (part, 128), 1)
        for i in range(lead):
            places = (line + at == column).astype(BF16)
            if ref is dec_biases:
                flat = flat + t_dot(values[:, i : i + 1], places)
            else:
                flat = flat + dot(values[i : i + 1], places)
            at += part
    six, four, raised = rows(6), rows(4), rows(4, 4)
    seventh = lax.broadcasted_iota(jnp.int32, (8, 128), 0) == 6
    out[:, :C_PROJ] = low(dot(six, enc_qkv[...]))
    out[:, :128] = low(dot(six, enc_qkv[:, :128]) + jnp.where(seventh, flat, 0.0))
    out[:, C_PROJ:C_UP] = low(dot(six, enc_proj[...]))
    for at, piece in group(C_UP, six, enc_up, 3):
        out[:, at : at + 128] = low(piece)
    out[:, C_EMB:C_DOWN] = low(dot(six, dec_embed[...]))
    for g in range(3):
        out[:, C_DOWN + 768 * g : C_DOWN + 768 * g + 768] = low(dot(rows(24, -8 * g), enc_down[...]))
    lower = (dec_qkv[:, :1024], jnp.concatenate([dec_qkv[:, 1024:], dec_proj[...]], axis=1))
    lower = [dot(four, values) for values in lower]
    for at, piece in group(0, raised, dec_up, 2):
        half, column = at // 1024, at % 1024
        piece = piece + lower[half][:, column : column + 128]
        out[:, C_Z + at : C_Z + at + 128] = low(piece)
    for g in range(2):
        out[:, C_DDOWN + 512 * g : C_DDOWN + 512 * g + 512] = low(dot(rows(16, -8 * g), dec_down[...]))


def pack(*weights):
    weights = [w[None] if w.ndim == 1 else w for w in weights]
    weights[10] = weights[10].T
    return pl.pallas_call(
        pack_kernel,
        in_specs=[VMEM] * 16,
        out_specs=VMEM,
        out_shape=pltpu.HBM((8, C_ALL), BF16),
        compiler_params=params(24),
        name="pack",
    )(*[in_hbm(w) for w in weights])


def position_table(offset, width):
    half = width // 2
    rates = jnp.exp(jnp.arange(half, dtype=F32) * (-math.log(10000.0) / half))
    angle = offset.astype(F32)[:, None] * rates[None, :]
    return jnp.concatenate([jnp.sin(angle), jnp.cos(angle)], axis=1)


def layout(length_row, order, visible):
    length = order.shape[0]
    ends = jnp.cumsum(length_row, dtype=jnp.int32)
    places = lax.broadcasted_iota(jnp.int32, (length, 1), 0)
    passed = places >= ends[None, :]
    segment = jnp.sum(passed.astype(jnp.int32), axis=1, dtype=jnp.int32)
    offset = places[:, 0] - jnp.sum(
        jnp.where(passed, length_row[None, :], 0), axis=1, dtype=jnp.int32
    )
    shown_pos = order[:visible]
    shown_seg = jnp.sum(
        (shown_pos[:, None] >= ends[None, :]).astype(jnp.int32), axis=1, dtype=jnp.int32
    )
    onehot = places == shown_pos[None, :]
    return (segment, offset, shown_seg, onehot)


def spread_rows(devices, rows, at):
    feature = lax.broadcasted_iota(jnp.int32, (devices * rows, devices * 8), 0)
    place = lax.broadcasted_iota(jnp.int32, (devices * rows, devices * 8), 1)
    return (8 * (feature // rows) + at + feature % rows == place).astype(BF16)


def plans(length_rows, orders):
    segment, offset, shown_seg, onehot = jax.vmap(lambda a, b: layout(a, b, 48))(
        length_rows, orders
    )
    pack = jnp.arange(2, dtype=jnp.int32)[:, None] * 16
    seen = (shown_seg + pack).reshape(96)
    seen_keys = jnp.concatenate([seen, jnp.full((32,), -1, jnp.int32)])
    enc_bias = jnp.where(seen[:, None] == seen_keys[None, :], 0.0, NEVER).astype(F32)
    keys = jnp.concatenate([segment, jnp.full((2, 64), -1, jnp.int32)], axis=1)
    dec_bias = jnp.where(segment[:, :, None] == keys[:, None, :], 0.0, NEVER).astype(F32)
    hot = onehot.astype(BF16)
    hot = hot.transpose(0, 2, 1)
    none = jnp.zeros((48, 192), BF16)
    picker_t = jnp.concatenate(
        [jnp.concatenate([hot[0], none], axis=1), jnp.concatenate([none, hot[1]], axis=1)], axis=0
    )
    table = position_table(offset.reshape(-1), 512)
    return enc_bias, dec_bias, picker_t, table


def place_of(device):
    return device // 2 % 4, device // 32, device // 8 % 4, device % 2


AXES = {"y": (32, 4), "z": (8, 4), "x": (2, 4), "c": (1, 2)}


def flipped(block, axis, turn):
    stride, size = AXES[axis]
    route = []
    for device in range(128):
        at = device // stride % size
        route.append((device, device + ((at ^ turn) - at) * stride))
    return lax.ppermute(block, BOTH, route)


def other_core(block):
    return flipped(block, "c", 1)


def first_sent(axis, outs):
    begun = []
    for split, first in enumerate((1, 3)):
        send, keep = [a.reshape(2, 256, a.shape[-1]) for a in outs[2 * split : 2 * split + 2]]
        begun.append((keep, flipped(send, axis, first)))
    return begun


def second_sent(axis, begun, before):
    groups = []
    for (keep, got), first in zip(begun, (1, 3)):
        onward = fold(after(keep, *before), got)
        groups.append((keep, got, flipped(onward, axis, 4 - first)))
        before = (onward,)
    return groups, before


def passed(block, axis, by):
    stride, size = AXES[axis]
    route = []
    for device in range(128):
        at = device // stride % size
        route.append((device, device + ((at + by) % size - at) * stride))
    return lax.ppermute(block, BOTH, route)


def summed(place, axis, before, groups, earlier):
    *sends, own = parted(after(place, *earlier), "xyz".index(axis), before, groups)
    return [(own, *[passed(send, axis, by) for send, by in zip(sends, (1, 3, 2))])], (own,)


def paired(place, axis, before, groups, first, earlier):
    send, keep = parted(after(place, *earlier), "xyz".index(axis), before, groups, first)
    return (axis, first, keep, flipped(send, axis, first)), (keep,)


def paired_end(begun, earlier):
    axis, first, keep, got = begun
    onward = fold(after(keep, *earlier), got)
    return [(keep, got, flipped(onward, axis, 4 - first))], (onward,)


def after(value, *others):
    return lax.optimization_barrier((value, *others))[0]


def on_device(
    x_vis, lengths, shuffle, enc_gains, enc_biases, enc_qkv, enc_proj, enc_up, enc_up_bias,
    enc_down, dec_fill, dec_embed, dec_gains, dec_biases, dec_qkv, dec_proj, dec_up, dec_up_bias,
    dec_down, cotangent,
):
    section = lax.axis_index("section")
    device = lax.axis_index(BOTH)
    x, y, z, core = place_of(device)
    shard = pack(
        enc_gains, enc_biases, enc_qkv, enc_proj, enc_up, enc_up_bias, enc_down, dec_fill,
        dec_embed, dec_gains, dec_biases, dec_qkv, dec_proj, dec_up, dec_up_bias, dec_down,
    )
    whole = lax.all_gather(shard, BOTH, axis=0, tiled=True)

    packs = 2

    def mine(rows):
        return lax.dynamic_slice_in_dim(rows, section * packs, packs, 0)[:, 0]

    x_rows = mine(x_vis).reshape(packs * 48, 768)
    pull = mine(cotangent).reshape(packs * 192, 512)
    enc_bias, dec_bias, picker_t, table = plans(mine(lengths), mine(shuffle))
    pads = spread_rows(64, 6, 0)
    low_rows, high_rows = spread_rows(32, 4, 0), spread_rows(32, 4, 4)
    spread = (low_rows, high_rows)
    pads_t, low_t, high_t = pads.T, low_rows.T, high_rows.T
    place = jnp.stack([x, y, z, core, section]).astype(jnp.int32)
    side = section.astype(jnp.int32).reshape(1)

    pull_o = other_core(pull)

    ready = (whole, x_rows, pull, pull_o, enc_bias, dec_bias, picker_t, table)
    ready = lax.optimization_barrier((*ready, pads, pads_t, low_t, high_t, *spread))
    whole, x_rows, pull, pull_o, enc_bias, dec_bias, picker_t, table = ready[:8]
    pads, pads_t, low_t, high_t, *spread = ready[8:]
    (
        enc_vec, dec_mine, dec_theirs, back, d_dec, d_dec_up, enc_rows, proj3, shares, middle,
        slope, dec_rows,
    ) = blocks(
        side, whole, x_rows, enc_bias, pads, picker_t, table, dec_bias, pull, *spread
    )
    enc_rows_o = other_core(enc_rows)
    back_o = other_core(back)
    dec_rows_o = other_core(dec_rows)
    hid_rows, att_rows, enc_mine, enc_theirs, small = enc_back(
        side, whole, back, middle, slope, proj3, shares, x_rows, pads, enc_vec, d_dec, d_dec_up,
        dec_theirs,
    )
    hid_rows_o, att_rows_o = other_core(hid_rows), other_core(att_rows)
    (sums_s,) = grad_call(
        grad_s_kernel, "grad_s", (4, 4, 64, 2176), [(4, 4, 64, 2176)], after(place, hid_rows),
        (back, back_o, pull, pull_o, low_t, high_t),
        (dec_rows, dec_rows_o, enc_rows, enc_rows_o),
        (
            pltpu.VMEM((192, 3072), BF16),
            pltpu.VMEM((768, 2048), BF16),
            pltpu.VMEM((2, 768, 512), BF16),
            pltpu.VMEM((2, 768, 512), BF16),
            pltpu.SemaphoreType.DMA((12,)),
        ),
    )
    sums_y = grad_call(
        grad_y_kernel, "grad_y", (1, 4, 256, 2048), split_outs(1, Y_SPLITS), after(place, sums_s),
        (hid_rows, hid_rows_o, pads_t, low_t, high_t),
        (dec_rows, dec_rows_o, enc_rows, enc_rows_o),
        (
            pltpu.VMEM((192, 768), BF16),
            pltpu.VMEM((2, 768, 512), BF16),
            pltpu.VMEM((2, 768, 512), BF16),
            pltpu.SemaphoreType.DMA((10,)),
        ),
    )
    sums_z = grad_call(
        grad_z_kernel, "grad_z", (16, 4, 16, 1792), split_outs(16, Z_SPLITS),
        after(place, *sums_y), (att_rows, att_rows_o, back, back_o, small, pads_t),
        (enc_rows, enc_rows_o),
        (
            pltpu.VMEM((192, 1536), BF16),
            pltpu.VMEM((192, 768), BF16),
            pltpu.SemaphoreType.DMA((4,)),
        ),
    )

    sums_s = lax.psum_scatter(
        sums_s.reshape(64, 16, 2176), "z", scatter_dimension=0, tiled=True
    ).reshape(256, 2176)
    sums_y = first_sent("y", sums_y)
    sums_z = first_sent("x", sums_z)
    sums_y, done = second_sent("y", sums_y, sums_z[0][:1])
    sums_z, done = second_sent("x", sums_z, done)
    sums_s, done = paired(place, "x", 4, [(sums_s,)], 1, done)
    sums_y, done = paired(place, "z", 1, sums_y, 1, done)
    sums_z, done = paired(place, "z", 4, sums_z, 3, done)
    sums_s, done = paired_end(sums_s, done)
    sums_y, done = paired_end(sums_y, done)
    sums_z, done = paired_end(sums_z, done)
    sums_sz, done = summed(place, "y", 1, sums_s + sums_z, done)
    sums_y, done = summed(place, "x", 1, sums_y, done)
    decoded, x_grad = joined(place, dec_mine, enc_mine, flipped(enc_theirs, "y", 2))
    own, other = last(after(place, decoded, x_grad), sums_sz + sums_y)
    grads = shards(place, own, other_core(other))
    grads = [g[0] if g.shape[0] == 1 else g for g in grads]
    grads[10] = grads[10].T
    return (decoded[:, None], x_grad[:, None], *grads)


def solution(mesh):
    mesh = Mesh(mesh.devices.reshape(2, 2, 4, 4, 2), BOTH)
    rows = P(None, DP, None, None)
    ids = P(None, DP, None)
    wide = P(None, BOTH)
    tall = P(BOTH, None)
    flat = P(BOTH)
    in_specs = (rows, ids, ids, wide, wide, tall, tall, tall, flat, tall, wide, tall, wide, wide)
    in_specs += (tall, tall, tall, flat, tall, rows)
    out_rows = P(None, DP, None, "section")
    out_specs = (out_rows, out_rows, wide, wide, tall, tall, tall, flat, tall, wide, tall, wide)
    out_specs += (wide, tall, tall, tall, flat, tall)
    return jax.shard_map(
        on_device, mesh=mesh, in_specs=in_specs, out_specs=out_specs, check_vma=False
    )
```
